32 devices in a mesh: blk: 8 (over y, x, core), seq: 4 (over z).
Axes of the slice: x: 2, y: 2, z: 4, core: 2. Of those that a mesh axis runs over, the one named last changes fastest.
Arguments:
- tokens: bfloat16 [64, 512, 768], P('blk', 'seq'), may hold values from -6 to 6
- lengths: int32 [64, 4], P('blk'), may hold values from 1 to 509, as said below
- pair_ids: int32 [128], P(('blk', 'seq')), may hold values from 0 to 127, each once
- w_query: bfloat16 [768, 768], P(('blk', 'seq')), may hold values from -0.21875 to 0.21875
- b_query: bfloat16 [768], P(('blk', 'seq')), may hold values from -1.75 to 1.75
- w_key: bfloat16 [768, 768], P(('blk', 'seq')), may hold values from -0.21875 to 0.21875
- w_value: bfloat16 [768, 768], P(('blk', 'seq')), may hold values from -0.21875 to 0.21875
- b_value: bfloat16 [768], P(('blk', 'seq')), may hold values from -1.75 to 1.75
- w_out: bfloat16 [768, 768], P(('blk', 'seq')), may hold values from -0.875 to 0.875
- b_out: bfloat16 [768], P(('blk', 'seq')), may hold values from -1.75 to 1.75
- norm1_gain: bfloat16 [768], P(('blk', 'seq')), may hold values from 0.5 to 1.5
- norm1_bias: bfloat16 [768], P(('blk', 'seq')), may hold values from -1.75 to 1.75
- w_in: bfloat16 [768, 3072], P(('blk', 'seq')), may hold values from -0.21875 to 0.21875
- b_in: bfloat16 [3072], P(('blk', 'seq')), may hold values from -1.75 to 1.75
- w_down: bfloat16 [3072, 768], P(('blk', 'seq')), may hold values from -0.109375 to 0.109375
- b_down: bfloat16 [768], P(('blk', 'seq')), may hold values from -1.75 to 1.75
- norm2_gain: bfloat16 [768], P(('blk', 'seq')), may hold values from 0.5 to 1.5
- norm2_bias: bfloat16 [768], P(('blk', 'seq')), may hold values from -0.75 to 0.75
Outputs:
- hidden_out: bfloat16 [64, 512, 768], P('blk', 'seq')
- query_loss: float32 [128], P(('blk', 'seq'))
- grad_tokens: float32 [64, 512, 768], P('blk', 'seq')
- grad_w_query: float32 [768, 768], P(('blk', 'seq'))
- grad_b_query: float32 [768], P(('blk', 'seq'))
- grad_w_key: float32 [768, 768], P(('blk', 'seq'))
- grad_w_value: float32 [768, 768], P(('blk', 'seq'))
- grad_b_value: float32 [768], P(('blk', 'seq'))
- grad_w_out: float32 [768, 768], P(('blk', 'seq'))
- grad_b_out: float32 [768], P(('blk', 'seq'))
- grad_norm1_gain: float32 [768], P(('blk', 'seq'))
- grad_norm1_bias: float32 [768], P(('blk', 'seq'))
- grad_w_in: float32 [768, 3072], P(('blk', 'seq'))
- grad_b_in: float32 [3072], P(('blk', 'seq'))
- grad_w_down: float32 [3072, 768], P(('blk', 'seq'))
- grad_b_down: float32 [768], P(('blk', 'seq'))
- grad_norm2_gain: float32 [768], P(('blk', 'seq'))
- grad_norm2_bias: float32 [768], P(('blk', 'seq'))
The draws below stay inside these ranges and needn't reach their ends.
Inputs may be any that keep to these rules, and one draw needn't show every extreme that they name: `lengths`: in each row one segment, at a place drawn from the seed, covers all but at most 127 of the row's tokens; the others have 1 to 32 tokens; fewer than 32 tokens at the row's end are padding. `pair_ids`: each document is paired with exactly one query.
All inputs are finite; a program needn't handle non-finite values.
Results may differ from the reference program's by a relative error of at most 0.015.
Values may be sent and summed in bfloat16 or wider, within the bound.
A program may use at most 256 MiB of HBM per device.

```python
import math
from functools import partial
import jax
import jax.numpy as jnp
from jax import lax

D = 768
HEADS = 12
HEAD_DIM = 64
FF = 3072
L = 512
NQ = 2
SEGS = 4
ROWS = 64
QUERIES = 128
SHORT = 32


def draw_lengths(key, part):
    key = jax.random.fold_in(key, 11)
    long_key, short_key, pad_key, row_key = jax.random.split(key, 4)
    long_slot = jax.random.randint(long_key, (ROWS, 1), 0, SEGS)
    shorts = jax.random.randint(short_key, (ROWS, SEGS), 1, SHORT + 1)
    padding = jax.random.randint(pad_key, (ROWS, 1), 0, SHORT)
    chosen_row = jax.random.randint(row_key, (), 0, ROWS)
    is_chosen = jnp.arange(ROWS)[:, None] == chosen_row
    shorts = jnp.where(is_chosen, 1, shorts)
    padding = jnp.where(is_chosen, 0, padding)
    slot_ids = jnp.arange(SEGS)[None, :]
    is_long = slot_ids == long_slot
    others = jnp.sum(jnp.where(is_long, 0, shorts), axis=1, keepdims=True)
    return jnp.where(is_long, L - padding - others, shorts).astype(jnp.int32)


def shard_levels(stream_key, extent, cuts, low, top_value):
    def one(axis_at, parts):
        heights = jax.random.uniform(jax.random.fold_in(jax.random.fold_in(stream_key, 6), axis_at), (parts,), jnp.float32, low / len(cuts), top_value / len(cuts))
        return jnp.repeat(jnp.exp(heights), extent[axis_at] // parts).reshape((-1,) + (1,) * (len(extent) - axis_at - 1))

    factor_of = one(*cuts[0])
    for cut in cuts[1:]:
        factor_of = factor_of * one(*cut)
    return factor_of


def bell_draw(stream_key, extent, scale, limit, cuts=(), held_as=jnp.bfloat16):
    factor_of = shard_levels(stream_key, extent, cuts, -0.22, 0.18) if cuts else 1.0
    entries = jax.random.normal(stream_key, extent, jnp.float32) * scale * factor_of
    return jnp.minimum(jnp.maximum(entries, -limit), limit).astype(held_as)


def setup_inputs(seed: int = 0) -> dict:
    splits = jax.random.split(jax.random.key(seed), 19)
    return {
        "tokens": bell_draw(splits[0], (ROWS, L, D), 1.0, 6.0, ((0, 8), (1, 4))),
        "lengths": draw_lengths(jax.random.fold_in(splits[18], 71), 0),
        "pair_ids": jax.random.permutation(splits[2], QUERIES).astype(jnp.int32),
        "w_query": bell_draw(splits[3], (D, D), D ** -0.5, 0.21875, ((0, 32),)),
        "b_query": bell_draw(splits[4], (D,), 0.3, 1.75, ((0, 32),)),
        "w_key": bell_draw(splits[5], (D, D), D ** -0.5, 0.21875, ((0, 32),)),
        "w_value": bell_draw(splits[6], (D, D), D ** -0.5, 0.21875, ((0, 32),)),
        "b_value": bell_draw(splits[7], (D,), 0.3, 1.75, ((0, 32),)),
        "w_out": bell_draw(splits[8], (D, D), (D // 16) ** -0.5, 0.875, ((0, 32),)),
        "b_out": bell_draw(splits[9], (D,), 0.3, 1.75, ((0, 32),)),
        "norm1_gain": jnp.clip(1.0 + 0.1 * jax.random.normal(splits[10], (D,), jnp.float32), 0.5, 1.5).astype(jnp.bfloat16),
        "norm1_bias": bell_draw(splits[11], (D,), 0.3, 1.75, ((0, 32),)),
        "w_in": bell_draw(splits[12], (D, FF), D ** -0.5, 0.21875, ((0, 32),)),
        "b_in": bell_draw(splits[13], (FF,), 0.3, 1.75, ((0, 32),)),
        "w_down": bell_draw(splits[14], (FF, D), FF ** -0.5, 0.109375, ((0, 32),)),
        "b_down": bell_draw(splits[15], (D,), 0.3, 1.75, ((0, 32),)),
        "norm2_gain": jnp.clip(1.0 + 0.1 * jax.random.normal(splits[16], (D,), jnp.float32), 0.5, 1.5).astype(jnp.bfloat16),
        "norm2_bias": bell_draw(splits[17], (D,), 0.12, 0.75, ((0, 32),)),
    }


SOFTMAX_WARMTH = 0.05
NORM_EPSILON = 1e-06
MASKED = -1000000000.0
MATMUL_EXACTNESS = lax.Precision.HIGHEST

@jax.custom_vjp
def low(v):
    return lax.optimization_barrier(v.astype(jnp.bfloat16)).astype(jnp.float32)

@jax.custom_vjp
def low_back(v):
    return v

def low_keep(v):
    return (low(v), None)

def low_pass(kept, grad):
    return (grad,)

def back_keep(v):
    return (v, None)

def back_low(kept, grad):
    return (low(grad),)
low.defvjp(low_keep, low_pass)
low_back.defvjp(back_keep, back_low)

def both_ways(tensor):
    return low(low_back(tensor))

def segment_ids(lengths, positions):
    ends = jnp.cumsum(lengths, axis=1)
    return lax.optimization_barrier(jnp.sum((positions[None, :, None] >= ends[:, None, :]).astype(jnp.int32), axis=-1)).astype(jnp.int32)

def project(operand, matrix):
    return jnp.einsum('gld,de->gle', operand, matrix, precision=MATMUL_EXACTNESS)

def normalize(summed_in, gain_vec, shift_vec):
    center = summed_in - lax.optimization_barrier(jnp.mean(summed_in, axis=-1, keepdims=True))
    inv_std = lax.rsqrt(lax.optimization_barrier(jnp.mean(center * center, axis=-1, keepdims=True)) + NORM_EPSILON)
    return center * inv_std * gain_vec + shift_vec

def split_heads(tensor):
    return tensor.reshape(tensor.shape[0], tensor.shape[1], HEADS, HEAD_DIM)

def exact_gelu(tensor):
    return jax.nn.gelu(tensor, approximate=False)

def layer_rows(block_tokens, segments, weights):
    w_query, b_query, w_key, w_value, b_value, w_out, b_out, gain_one, shift_one, w_in, b_in, w_down, b_down, gain_two, shift_two = weights
    queries = both_ways(project(block_tokens, w_query) + b_query)
    keys_all = both_ways(project(block_tokens, w_key))
    values_all = both_ways(project(block_tokens, w_value) + b_value)
    allowed = segments[:, :, None] == segments[:, None, :]
    scores = jnp.einsum('gqhd,gkhd->ghqk', split_heads(queries), split_heads(keys_all), precision=MATMUL_EXACTNESS) * HEAD_DIM ** (-0.5)
    scores = low_back(jnp.where(allowed[:, None], scores, MASKED))
    softmax_w = low(jnp.exp(scores - jax.nn.logsumexp(scores, axis=-1, keepdims=True)))
    mixed = jnp.einsum('ghqk,gkhd->gqhd', softmax_w, split_heads(values_all), precision=MATMUL_EXACTNESS)
    attended = both_ways(mixed.reshape(block_tokens.shape))
    hidden_one = normalize(block_tokens + low_back(project(attended, w_out) + b_out), gain_one, shift_one)
    inner_pre = low_back(project(low(hidden_one), w_in) + b_in)
    activated = low(exact_gelu(inner_pre))
    return normalize(hidden_one + low_back(project(activated, w_down) + b_down), gain_two, shift_two)

def forward(token_values, weight_values, segments, lengths, pair_ids):
    group_rows = math.gcd(ROWS, 8)
    grouped = token_values.reshape(ROWS // group_rows, group_rows, L, D)
    grouped_seg = segments.reshape(ROWS // group_rows, group_rows, L)
    member_ids = jnp.arange(SEGS, dtype=jnp.int32)

    def step_group(state_in, inputs):
        block_tokens, block_seg = inputs
        hidden_two = jax.checkpoint(layer_rows)(block_tokens, block_seg, weight_values)
        members = (block_seg[:, None, :] == member_ids[None, :, None]).astype(jnp.float32)
        pooled = jnp.einsum('gsl,gld->gsd', members, hidden_two, precision=MATMUL_EXACTNESS)
        return (state_in, (hidden_two, pooled))
    _, (hidden_every_layer, pooled) = lax.scan(step_group, jnp.zeros((), jnp.float32), (grouped, grouped_seg))
    pooled = pooled.reshape(ROWS, SEGS, D) / lengths.astype(jnp.float32)[:, :, None]
    embedded = pooled * lax.rsqrt(lax.optimization_barrier(jnp.sum(pooled * pooled, axis=-1, keepdims=True)) + NORM_EPSILON)
    query_vectors = embedded[:, :NQ].reshape(QUERIES, D)
    document_vectors = embedded[:, NQ:].reshape(QUERIES, D)
    similarity_scores = jnp.dot(query_vectors, document_vectors.T, precision=MATMUL_EXACTNESS, preferred_element_type=jnp.float32) / SOFTMAX_WARMTH
    chosen = pair_ids[:, None] == jnp.arange(QUERIES, dtype=jnp.int32)[None, :]
    positive = lax.optimization_barrier(jnp.sum(jnp.where(chosen, similarity_scores, 0.0), axis=1))
    per_query = jax.nn.logsumexp(similarity_scores, axis=1) - positive
    return (jnp.sum(per_query), (hidden_every_layer.reshape(ROWS, L, D), per_query))

def reference(tokens, lengths, pair_ids, w_query, b_query, w_key, w_value, b_value, w_out, b_out, norm1_gain, norm1_bias, w_in, b_in, w_down, b_down, norm2_gain, norm2_bias):
    segments = segment_ids(lengths, jnp.arange(L, dtype=jnp.int32))
    weights = tuple((weight.astype(jnp.float32) for weight in (w_query, b_query, w_key, w_value, b_value, w_out, b_out, norm1_gain, norm1_bias, w_in, b_in, w_down, b_down, norm2_gain, norm2_bias)))
    objective_fn = partial(forward, segments=segments, lengths=lengths, pair_ids=pair_ids)
    objective, backward, extras = jax.vjp(objective_fn, tokens.astype(jnp.float32), weights, has_aux=True)
    hidden_every_layer, per_query = extras
    grad_tokens, grad_weights = backward(jnp.ones((), objective.dtype))
    grad_w_query, grad_b_query, grad_w_key, grad_w_value, grad_b_value, grad_w_out, grad_b_out, grad_gain_one, grad_shift_one, grad_w_in, grad_b_in, grad_w_down, grad_b_down, grad_gain_two, grad_shift_two = grad_weights
    return (hidden_every_layer.astype(jnp.bfloat16), per_query, grad_tokens, grad_w_query, grad_b_query, grad_w_key, grad_w_value, grad_b_value, grad_w_out, grad_b_out, grad_gain_one, grad_shift_one, grad_w_in, grad_b_in, grad_w_down, grad_b_down, grad_gain_two, grad_shift_two)
```

```python
import functools

import jax
import jax.numpy as jnp
from jax import lax
from jax.experimental import pallas as pl
from jax.experimental.pallas import tpu as pltpu
from jax.sharding import PartitionSpec as P

HEADS = 12
HEAD_DIM = 64
NQ = 2
SEGS = 4
TEMPERATURE = 0.05
NORM_EPSILON = 1e-06
MASKED = -1000000000.0
BF16 = jnp.bfloat16
F32 = jnp.float32
MESH = pl.DeviceIdType.MESH
ANY = pl.BlockSpec(memory_space=pl.ANY)
VMEM = pl.BlockSpec(memory_space=pltpu.VMEM)
SMEM = pl.BlockSpec(memory_space=pltpu.SMEM)
DMA = pltpu.SemaphoreType.DMA
VMEM_LIMIT = 60 * 2**20


def dot(a, b, ca=1, cb=0):
    return lax.dot_general(a, b, (((ca,), (cb,)), ((), ())), preferred_element_type=F32)


def struct(shape, dtype):
    return jax.ShapeDtypeStruct(shape, dtype)


def split_two(v):
    high = v.astype(BF16)
    return high, (v - high.astype(F32)).astype(BF16)


class Grid:
    def __init__(self, blk_size, seq_size):
        self.blk_size, self.seq_size = blk_size, seq_size
        self.kb = blk_size.bit_length() - 1
        self.ks = seq_size.bit_length() - 1
        assert 1 << self.kb == blk_size and 1 << self.ks == seq_size
        self.nd = self.kb + self.ks

    def here(self):
        return lax.axis_index("blk"), lax.axis_index("seq")

    def digit(self, b, q, d):
        if d < self.kb:
            w = 1 << (self.kb - 1 - d)
            return (b // w) % 2, w
        w = 1 << (self.nd - 1 - d)
        return (q // w) % 2, w

    def digits(self, b, q):
        return [self.digit(b, q, d)[0] for d in range(self.nd)]

    def partner(self, b, q, d):
        v, w = self.digit(b, q, d)
        if d < self.kb:
            return (b + (1 - 2 * v) * w, q)
        return (b, q + (1 - 2 * v) * w)

    def order(self, flavour):
        seq = list(range(self.kb, self.nd))
        head, last = list(range(self.kb))[:-1][::-1], [self.kb - 1]
        if head:
            r = flavour % len(head)
            head = head[r:] + head[:r]
        return seq + head + last

    def greet(self, b, q, partners, others):
        barrier = pltpu.get_barrier_semaphore()
        targets = [partners[d] for d in range(self.kb)]
        if others is None:
            targets += [partners[d] for d in range(self.kb, self.nd)]
        else:
            targets += [(b, o) for o in others]
        for t in targets:
            pl.semaphore_signal(barrier, inc=1, device_id=t, device_id_type=MESH)
        pl.semaphore_wait(barrier, len(targets))


def remote(src, dst, send, recv, where):
    return pltpu.make_async_remote_copy(
        src_ref=src, dst_ref=dst, send_sem=send, recv_sem=recv, device_id=where, device_id_type=MESH
    )


def flat_view(rows, lanes):
    if rows % 8 == 0:
        return rows, lanes
    return rows * lanes // 128, 128


def pieces(shapes):
    out = []
    for a, (rows, lanes) in enumerate(shapes):
        unit = 768 if rows < 64 else 256
        unit = min(unit, lanes)
        for lo in range(0, lanes, unit):
            half = unit // 2
            if half % 128 == 0:
                out.append([(a, lo, half, 0), (a, lo + half, half, 1)])
            else:
                out.append([(a, lo, unit, 0)])
    return out


def gather_kernel(grid, groups, n, lag, *refs):
    ins, tok = refs[:n], refs[n]
    outs, rows_out = refs[n + 1 : 2 * n + 1], refs[2 * n + 1]
    own_sem, send_sem, recv_sem, tok_own, tok_send, tok_recv = refs[2 * n + 2 :]
    b, q = grid.here()
    nd, ns = grid.nd, grid.seq_size
    my = grid.digits(b, q)
    partners = [grid.partner(b, q, d) for d in range(nd)]
    others = [lax.rem(q + j, ns) for j in range(1, ns)]
    grid.greet(b, q, partners, others)
    flat = [c for g in groups for c in g]
    where = {}
    first = 0
    for gi, g in enumerate(groups):
        where[gi] = list(range(first, first + len(g)))
        first += len(g)

    own = []
    for i, (a, lo, ln, _) in enumerate(flat):
        c = pltpu.make_async_copy(
            ins[a].at[:, pl.ds(lo, ln)],
            outs[a].at[tuple(my) + (slice(None), pl.ds(lo, ln))],
            own_sem.at[i],
        )
        c.start()
        own.append(c)
    copies = {}

    def stage(i, k):
        a, lo, ln, flavour = flat[i]
        order = grid.order(flavour)
        d = order[k]
        if k == 0:
            src = ins[a].at[:, pl.ds(lo, ln)]
            dst = outs[a].at[tuple(my) + (slice(None), pl.ds(lo, ln))]
        else:
            if k == 1:
                own[i].wait()
            copies[(i, k - 1)].wait_recv()
            done = order[:k]
            ix = tuple(slice(None) if e in done else my[e] for e in range(nd))
            ix = ix + (slice(None), pl.ds(lo, ln))
            src, dst = outs[a].at[ix], outs[a].at[ix]
        c = remote(src, dst, send_sem.at[i, k], recv_sem.at[i, k], partners[d])
        c.start()
        copies[(i, k)] = c

    row_copies = []
    total, lt, _ = tok.shape
    per = total // ns

    def send_rows():
        at = pl.ds(pl.multiple_of(q * lt, lt), lt)
        for r in range(per):
            c = pltpu.make_async_copy(tok.at[q * per + r], rows_out.at[r, at], tok_own.at[r])
            c.start()
            row_copies.append(c)
            for j in range(1, ns):
                o = others[j - 1]
                c = remote(
                    tok.at[o * per + r],
                    rows_out.at[r, at],
                    tok_send.at[j - 1, r],
                    tok_recv.at[j - 1, r],
                    (b, o),
                )
                c.start()
                row_copies.append(c)

    ng = len(groups)
    for t in range(ng + lag * (nd - 1)):
        for k in range(nd - 1, -1, -1):
            g = t - lag * k
            if 0 <= g < ng:
                for i in where[g]:
                    stage(i, k)
        if t == 2:
            send_rows()
    for i in range(len(flat)):
        copies[(i, nd - 1)].wait_recv()
    for i in range(len(flat)):
        for k in range(nd):
            copies[(i, k)].wait_send()
    for c in row_copies:
        c.wait()


def gather_all(grid, blocks, tokens, collective_id):
    nd, ns = grid.nd, grid.seq_size
    n = len(blocks)
    views = [x.reshape(flat_view(*x.shape)) for x in blocks]
    groups = pieces([v.shape for v in views])
    count = sum(len(g) for g in groups)
    total, lt, width = tokens.shape
    per = total // ns
    outs = [struct((2,) * nd + v.shape, v.dtype) for v in views]
    outs.append(struct((per, lt * ns, width), tokens.dtype))
    res = pl.pallas_call(
        functools.partial(gather_kernel, grid, groups, n, 2),
        out_shape=outs,
        in_specs=[VMEM] * (n + 1),
        out_specs=[ANY] * (n + 1),
        scratch_shapes=[
            DMA((count,)),
            DMA((count, nd)),
            DMA((count, nd)),
            DMA((per,)),
            DMA((ns - 1, per)),
            DMA((ns - 1, per)),
        ],
        compiler_params=pltpu.CompilerParams(
            collective_id=collective_id, has_side_effects=True, vmem_limit_bytes=VMEM_LIMIT
        ),
    )(*views, tokens)
    devices = 1 << nd
    full = [
        r.reshape((devices * x.shape[0], x.shape[1])) for r, x in zip(res[:-1], blocks, strict=True)
    ]
    return full, res[-1]


def reduce_plan(grid, flavour):
    free = list(range(grid.nd))
    plan = []
    for d in grid.order(flavour)[::-1]:
        pos = free.index(d)
        plan.append((d, 1 << pos, 1 << (len(free) - pos - 1)))
        free.remove(d)
    return plan


def scatter_kernel(grid, flat, n, nx, lag, *refs):
    nd, ns = grid.nd, grid.seq_size
    ins, rows_in = refs[:n], refs[n : n + nx]
    outs, rows_out = refs[n + nx : 2 * n + nx], refs[2 * n + nx : 2 * n + 2 * nx]
    rest = list(refs[2 * n + 2 * nx :])
    own_sem, send_sem, recv_sem, x_own, x_send, x_recv = rest[:6]
    bufs = rest[6:]
    b, q = grid.here()
    my = grid.digits(b, q)
    partners = [grid.partner(b, q, d) for d in range(nd)]
    others = [lax.rem(q + j, ns) for j in range(1, ns)]
    grid.greet(b, q, partners, others)

    row_copies = []
    for x in range(nx):
        per, length, _ = rows_in[x].shape
        lt = length // ns
        for r in range(per):
            at = pl.ds(pl.multiple_of(q * lt, lt), lt)
            c = pltpu.make_async_copy(
                rows_in[x].at[r, at], rows_out[x].at[q * per + r], x_own.at[x, r]
            )
            c.start()
            row_copies.append(c)

    def send_rows(x):
        per, length, _ = rows_in[x].shape
        lt = length // ns
        for r in range(per):
            for j in range(1, ns):
                o = others[j - 1]
                c = remote(
                    rows_in[x].at[r, pl.ds(pl.multiple_of(o * lt, lt), lt)],
                    rows_out[x].at[q * per + r],
                    x_send.at[x, j - 1, r],
                    x_recv.at[x, j - 1, r],
                    (b, o),
                )
                c.start()
                row_copies.append(c)

    per_piece = 1 + 2 * nd - 1
    copies, own = {}, {}

    def buffers(i):
        mine = bufs[i * per_piece : (i + 1) * per_piece]
        return mine[0], mine[1 : 1 + nd], mine[1 + nd :]

    for i, (a, lo, ln, flavour) in enumerate(flat):
        d = reduce_plan(grid, flavour)[0][0]
        ix = tuple(my[e] if e == d else slice(None) for e in range(nd)) + (slice(None), pl.ds(lo, ln))
        c = pltpu.make_async_copy(ins[a].at[ix], buffers(i)[0], own_sem.at[i])
        c.start()
        own[i] = c

    def send(i, k):
        a, lo, ln, flavour = flat[i]
        d, pre, post = reduce_plan(grid, flavour)[k]
        start, recv, acc = buffers(i)
        if k == 0:
            ix = tuple((1 - my[e]) if e == d else slice(None) for e in range(nd))
            src = ins[a].at[ix + (slice(None), pl.ds(lo, ln))]
        else:
            src = acc[k - 1].at[:, 1 - my[d]]
        c = remote(src, recv[k], send_sem.at[i, k], recv_sem.at[i, k], partners[d])
        c.start()
        copies[(i, k)] = c

    def add(i, k):
        a, lo, ln, flavour = flat[i]
        plan = reduce_plan(grid, flavour)
        d, pre, post = plan[k]
        start, recv, acc = buffers(i)
        copies[(i, k)].wait_recv()
        if k == 0:
            own[i].wait()
        if k == nd - 1:
            total = acc[k - 1][0, my[d], 0].astype(F32) + recv[k][0, 0].astype(F32)
            outs[a][:, lo : lo + ln] = total
            return
        _, pre2, post2 = plan[k + 1]

        def one(j, carry):
            if k == 0:
                ix = tuple((j // (1 << (nd - 2 - e))) % 2 for e in range(nd - 1))
                mine, other = start[ix], recv[0][ix]
            else:
                mine = acc[k - 1][j // post, my[d], j % post]
                other = recv[k][j // post, j % post]
            total = mine.astype(F32) + other.astype(F32)
            acc[k][j // (2 * post2), (j // post2) % 2, j % post2] = total.astype(acc[k].dtype)
            return carry

        lax.fori_loop(0, pre * post, one, 0)

    groups = sorted({c[4] for c in [(*f, gi) for f, gi in zip(flat, group_of(flat))]})
    members = {g: [i for i, gi in enumerate(group_of(flat)) if gi == g] for g in groups}
    ng = len(groups)
    for t in range(ng + lag * nd):
        for k in range(nd, -1, -1):
            g = t - lag * k
            if 0 <= g < ng:
                for i in members[g]:
                    if k > 0:
                        add(i, k - 1)
                    if k < nd:
                        send(i, k)
        if t == 0:
            for x in range(nx):
                send_rows(x)
    for i in range(len(flat)):
        for k in range(nd):
            copies[(i, k)].wait_send()
    for c in row_copies:
        c.wait()


def group_of(flat):
    ids, last = [], -1
    for _, _, _, flavour in flat:
        if flavour == 0:
            last += 1
        ids.append(last)
    return ids


def scatter_all(grid, grads, rows_back, collective_id):
    nd, ns = grid.nd, grid.seq_size
    devices = 1 << nd
    views, finals = [], []
    for g in grads:
        rows = g.shape[0] // devices
        finals.append((rows, g.shape[1]))
        views.append(g.reshape((2,) * nd + flat_view(rows, g.shape[1])))
    flat = [c for g in pieces([v.shape[-2:] for v in views]) for c in g]
    n, nx = len(views), len(rows_back)
    scratch = []
    for a, _, ln, flavour in flat:
        rows, dtype = views[a].shape[-2], views[a].dtype
        plan = reduce_plan(grid, flavour)
        scratch.append(pltpu.VMEM((2,) * (nd - 1) + (rows, ln), dtype))
        for k, (_, pre, post) in enumerate(plan):
            shape = (2,) * (nd - 1) if k == 0 else (pre, post)
            scratch.append(pltpu.VMEM(shape + (rows, ln), dtype))
        for _, pre, post in plan[1:]:
            scratch.append(pltpu.VMEM((pre, 2, post, rows, ln), dtype))
    outs = [struct(v.shape[-2:], F32) for v in views]
    for x in rows_back:
        per, length, width = x.shape
        outs.append(struct((per * ns, length // ns, width), x.dtype))
    per = rows_back[0].shape[0]
    count = len(flat)
    res = pl.pallas_call(
        functools.partial(scatter_kernel, grid, flat, n, nx, 2),
        out_shape=outs,
        in_specs=[ANY] * n + [ANY] * nx,
        out_specs=[VMEM] * n + [ANY] * nx,
        scratch_shapes=[
            DMA((count,)),
            DMA((count, nd)),
            DMA((count, nd)),
            DMA((nx, per)),
            DMA((nx, ns - 1, per)),
            DMA((nx, ns - 1, per)),
        ]
        + scratch,
        compiler_params=pltpu.CompilerParams(
            collective_id=collective_id, has_side_effects=True, vmem_limit_bytes=VMEM_LIMIT
        ),
    )(*views, *rows_back)
    return [r.reshape(s) for r, s in zip(res[:n], finals, strict=True)], res[n:]


def segment_of(lens, r, shape, axis, start=0):
    t = lax.broadcasted_iota(jnp.int32, shape, axis) + start
    end = lens[r, 0]
    seg = (t >= end).astype(jnp.int32)
    for k in range(1, SEGS):
        end = end + lens[r, k]
        seg = seg + (t >= end).astype(jnp.int32)
    return seg


def attention_kernel(
    lens, x_ref, wq, wk, wv, bq, bv, q_ref, k_ref, v_ref, p_ref, o_ref, vt_ref, ot_ref, bias_ref
):
    x = x_ref[0]
    length = x.shape[0]
    r = pl.program_id(0)
    seg_k = segment_of(lens, r, (length, 1), 0)
    seg_q = segment_of(lens, r, (1, length), 1)
    bias_ref[...] = jnp.where(seg_k == seg_q, 0.0, MASKED)
    q_ref[0] = ((dot(x, wq[...]) + bq[...]) * HEAD_DIM ** (-0.5)).astype(BF16)
    k_ref[0] = dot(x, wk[...]).astype(BF16)
    v = dot(x, wv[...]) + bv[...]
    v_ref[0] = v.astype(BF16)
    vt_ref[...] = v.T.astype(BF16)
    lane = lax.broadcasted_iota(jnp.int32, (1, 128), 1)

    def pair(p, carry):
        sl = pl.ds(pl.multiple_of(p * 128, 128), 128)
        qp, kp = q_ref[0, :, sl], k_ref[0, :, sl]
        for h in range(2):
            km = jnp.where(lane // HEAD_DIM == h, kp, jnp.zeros_like(kp))
            hs = pl.ds(pl.multiple_of(p * 128 + h * HEAD_DIM, HEAD_DIM), HEAD_DIM)
            s = dot(km, qp, 1, 1) + bias_ref[...]
            e = jnp.exp(s - jnp.max(s, axis=0, keepdims=True))
            pt = (e * (1.0 / jnp.sum(e, axis=0, keepdims=True))).astype(BF16)
            p_ref[0, p * 2 + h] = pt
            ot_ref[hs, :] = dot(vt_ref[hs, :], pt).astype(BF16)
        return carry

    lax.fori_loop(0, HEADS // 2, pair, 0)
    o_ref[0] = ot_ref[...].T


def attention(lens, x, wq, wk, wv, bq, bv):
    rows, length, width = x.shape
    row = lambda *s: pl.BlockSpec((1,) + s, lambda r: (r,) + (0,) * len(s))
    full = lambda *s: pl.BlockSpec(s, lambda r: (0,) * len(s))
    tokens = struct((rows, length, width), BF16)
    return pl.pallas_call(
        attention_kernel,
        grid=(rows,),
        out_shape=[tokens] * 3 + [struct((rows, HEADS, length, length), BF16), tokens],
        in_specs=[SMEM, row(length, width)] + [full(width, width)] * 3 + [full(1, width)] * 2,
        out_specs=[row(length, width)] * 3 + [row(HEADS, length, length), row(length, width)],
        scratch_shapes=[
            pltpu.VMEM((width, length), BF16),
            pltpu.VMEM((width, length), BF16),
            pltpu.VMEM((length, length), F32),
        ],
        compiler_params=pltpu.CompilerParams(vmem_limit_bytes=VMEM_LIMIT),
    )(lens, x, wq, wk, wv, bq, bv)


def layer_norm(v):
    c = v - jnp.mean(v, axis=-1, keepdims=True)
    inv = lax.rsqrt(jnp.mean(c * c, axis=-1, keepdims=True) + NORM_EPSILON)
    return c * inv, inv


def feed_kernel(
    tiles, lens, x_ref, o_ref, wo, bo, g1, s1, wi, bi, wd, bd, g2, s2,
    hid_ref, n1_ref, i1_ref, h1_ref, act_ref, slope_ref, n2_ref, i2_ref, pool_ref,
):
    t = pl.program_id(0)
    rows = x_ref.shape[0]
    pre1 = x_ref[...].astype(F32) + dot(o_ref[...], wo[...]) + bo[...]
    n1, i1 = layer_norm(pre1)
    h1 = n1 * g1[...] + s1[...]
    h1_low = h1.astype(BF16)
    n1_ref[...] = n1.astype(BF16)
    h1_ref[...] = h1_low
    i1_ref[...] = jnp.broadcast_to(i1, i1_ref.shape)
    acc = h1 + bd[...]
    chunk = wd.shape[1]
    for lo in range(0, wi.shape[1], chunk):
        sl = slice(lo, lo + chunk)
        inner = dot(h1_low, wi[:, sl]) + bi[:, sl]
        phi = 0.5 + 0.5 * lax.erf(inner * (0.5**0.5))
        act = (inner * phi).astype(BF16)
        act_ref[:, sl] = act
        density = jnp.exp(-0.5 * inner * inner) * 0.3989422804014327
        slope_ref[:, sl] = (phi + inner * density).astype(BF16)
        acc = acc + dot(act, wd[sl, :])
    n2, i2 = layer_norm(acc)
    h2 = n2 * g2[...] + s2[...]
    high, low = split_two(h2)
    hid_ref[...] = high
    n2_ref[...] = n2.astype(BF16)
    i2_ref[...] = jnp.broadcast_to(i2, i2_ref.shape)
    r = t // tiles
    seg = segment_of(lens, r, (1, rows), 1, (t % tiles) * rows)
    slot = jnp.where(seg < SEGS, r * SEGS + seg, -1)
    members = lax.broadcasted_iota(jnp.int32, (pool_ref.shape[0], rows), 0) == slot
    members = members.astype(F32).astype(BF16)
    part = dot(members, high) + dot(members, low)

    @pl.when(t == 0)
    def _():
        pool_ref[...] = part

    @pl.when(t != 0)
    def _():
        pool_ref[...] += part


def feed(lens, x, o, wo, bo, g1, s1, wi, bi, wd, bd, g2, s2, tile_rows):
    count, width = x.shape
    rows = lens.shape[0]
    ff = wi.shape[1]
    tiles = count // rows // tile_rows
    tile = lambda w: pl.BlockSpec((tile_rows, w), lambda t: (t, 0))
    full = lambda *s: pl.BlockSpec(s, lambda t: (0,) * len(s))
    vec = full(1, width)
    low, col = struct((count, width), BF16), struct((count, 128), F32)
    wide = struct((count, ff), BF16)
    return pl.pallas_call(
        functools.partial(feed_kernel, tiles),
        grid=(count // tile_rows,),
        out_shape=[low, low, col, low, wide, wide, low, col, struct((rows * SEGS, width), F32)],
        in_specs=[SMEM, tile(width), tile(width), full(width, width), vec, vec, vec]
        + [full(width, ff), full(1, ff), full(ff, width), vec, vec, vec],
        out_specs=[tile(width), tile(width), tile(128), tile(width), tile(ff), tile(ff)]
        + [tile(width), tile(128), full(rows * SEGS, width)],
        compiler_params=pltpu.CompilerParams(vmem_limit_bytes=VMEM_LIMIT),
    )(lens, x, o, wo, bo, g1, s1, wi, bi, wd, bd, g2, s2)


def contrast_kernel(grid, pool_ref, len_ref, pair_ref, pairs_ref, loss_ref, dpool_ref, emb, send_sem, recv_sem):
    nd = grid.nd
    b, q = grid.here()
    my = grid.digits(b, q)
    partners = [grid.partner(b, q, d) for d in range(nd)]
    own_rows, width = pool_ref.shape
    count = own_rows << nd
    avg = pool_ref[...] / len_ref[:, :1]
    inv = lax.rsqrt(jnp.sum(avg * avg, axis=-1, keepdims=True) + NORM_EPSILON)
    own = avg * inv
    emb[tuple(my)] = own
    grid.greet(b, q, partners, None)
    order = grid.order(0)
    for k, d in enumerate(order):
        ix = tuple(slice(None) if e in order[:k] else my[e] for e in range(nd))
        c = remote(emb.at[ix], emb.at[ix], send_sem.at[k], recv_sem.at[k], partners[d])
        c.start()
        c.wait()
    high, low = split_two(emb[...].reshape(count, width))
    own_high, own_low = split_two(own)
    scale = 1.0 / TEMPERATURE

    def product(ah, al, bh, bl, cb):
        return dot(ah, bh, 1, cb) + dot(ah, bl, 1, cb) + dot(al, bh, 1, cb)

    total = jnp.zeros((1, count), F32)
    step = min(count, 256)
    for lo in range(0, count, step):
        sim = product(high[lo : lo + step], low[lo : lo + step], high, low, 1) * scale
        at = lax.broadcasted_iota(jnp.int32, (step, 1), 0)
        total += jnp.sum(jnp.where(at % SEGS >= NQ, jnp.exp(sim - scale), 0.0), axis=0, keepdims=True)
    lse_cols = scale + jnp.log(total)
    sim = product(own_high, own_low, high, low, 1) * scale
    col = lax.broadcasted_iota(jnp.int32, (1, count), 1)
    row = lax.broadcasted_iota(jnp.int32, (own_rows, 1), 0) + (b * grid.seq_size + q) * own_rows
    col_doc, row_doc = col % SEGS >= NQ, row % SEGS >= NQ
    number = lambda at: (at // SEGS) * NQ + at % SEGS - NQ
    lse_rows = scale + jnp.log(
        jnp.sum(jnp.where(col_doc, jnp.exp(sim - scale), 0.0), axis=1, keepdims=True)
    )
    chosen = col_doc & (number(col) == pair_ref[:, :1])
    positive = jnp.sum(jnp.where(chosen, sim, 0.0), axis=1, keepdims=True)
    loss_ref[...] = jnp.broadcast_to(lse_rows - positive, loss_ref.shape)
    as_query = jnp.exp(sim - lse_rows) - chosen.astype(F32)
    chosen_by = number(row) == pairs_ref[:1]
    as_doc = jnp.exp(jnp.where(col_doc, MASKED, sim - lse_cols)) - chosen_by.astype(F32)
    grad = jnp.where(row_doc, jnp.where(col_doc, 0.0, as_doc), jnp.where(col_doc, as_query, 0.0))
    grad_high, grad_low = split_two(grad)
    demb = product(grad_high, grad_low, high, low, 0) * scale
    dpool = inv * demb - inv * inv * inv * avg * jnp.sum(avg * demb, axis=-1, keepdims=True)
    dpool_high, dpool_low = split_two(dpool / len_ref[:, :1])
    pad = jnp.zeros((64 - own_rows, width), F32)
    stacked = jnp.concatenate([dpool_high.astype(F32), pad, dpool_low.astype(F32), pad], axis=0)
    dpool_ref[...] = stacked.astype(BF16)


def contrast(grid, pool, len_col, pair_col, pair_row, collective_id):
    own_rows, width = pool.shape
    return pl.pallas_call(
        functools.partial(contrast_kernel, grid),
        out_shape=[struct((own_rows, 128), F32), struct((128, width), BF16)],
        in_specs=[VMEM] * 4,
        out_specs=[VMEM] * 2,
        scratch_shapes=[
            pltpu.VMEM((2,) * grid.nd + (own_rows, width), F32),
            DMA((grid.nd,)),
            DMA((grid.nd,)),
        ],
        compiler_params=pltpu.CompilerParams(
            collective_id=collective_id, has_side_effects=True, vmem_limit_bytes=VMEM_LIMIT
        ),
    )(pool, len_col, pair_col, pair_row)


def feed_back_kernel(
    tiles, lens, dp_ref, n2_ref, i2_ref, slope_ref, n1_ref, i1_ref, wd, wi, wo, g2, g1,
    dfeed_ref, dinner_ref, dbranch_ref, dpre1_ref, datt_ref, sums_ref, wide_ref,
):
    t = pl.program_id(0)
    rows = n2_ref.shape[0]

    @pl.when(t == 0)
    def _():
        sums_ref[...] = jnp.zeros_like(sums_ref)
        wide_ref[...] = jnp.zeros_like(wide_ref)

    def columns(v):
        return jnp.sum(v, axis=0, keepdims=True)

    def norm_back(g, n, inv):
        return inv * (
            g - jnp.mean(g, axis=-1, keepdims=True) - n * jnp.mean(g * n, axis=-1, keepdims=True)
        )

    r = t // tiles
    seg = segment_of(lens, r, (rows, 1), 0, (t % tiles) * rows)
    slot = jnp.where(seg < SEGS, r * SEGS + seg, -1)
    lane = lax.broadcasted_iota(jnp.int32, (rows, 128), 1)
    members = (lane % 64 == slot).astype(F32).astype(BF16)
    dh2 = dot(members, dp_ref[...])
    n2 = n2_ref[...].astype(F32)
    sums_ref[0:1] += columns(dh2 * n2)
    sums_ref[1:2] += columns(dh2)
    dpre2 = norm_back(dh2 * g2[...], n2, i2_ref[:, :1])
    dfeed = dpre2.astype(BF16)
    dfeed_ref[...] = dfeed
    sums_ref[2:3] += columns(dfeed.astype(F32))
    chunk = wd.shape[1]
    dh1 = dpre2
    for lo in range(0, wi.shape[1], chunk):
        sl = slice(lo, lo + chunk)
        dinner = (dot(dfeed, wd[sl, :], 1, 1) * slope_ref[:, sl].astype(F32)).astype(BF16)
        dinner_ref[:, sl] = dinner
        wide_ref[0:1, sl] += columns(dinner.astype(F32))
        dh1 = dh1 + dot(dinner, wi[:, sl], 1, 1)
    n1 = n1_ref[...].astype(F32)
    sums_ref[3:4] += columns(dh1 * n1)
    sums_ref[4:5] += columns(dh1)
    dpre1 = norm_back(dh1 * g1[...], n1, i1_ref[:, :1])
    dpre1_ref[...] = dpre1
    dbranch = dpre1.astype(BF16)
    dbranch_ref[...] = dbranch
    sums_ref[5:6] += columns(dbranch.astype(F32))
    datt_ref[...] = dot(dbranch, wo[...], 1, 1).astype(BF16)


def feed_back(lens, dp, n2, i2, slope, n1, i1, wd, wi, wo, g2, g1, tile_rows):
    count, width = n2.shape
    rows = lens.shape[0]
    ff = wi.shape[1]
    tiles = count // rows // tile_rows
    tile = lambda w: pl.BlockSpec((tile_rows, w), lambda t: (t, 0))
    full = lambda *s: pl.BlockSpec(s, lambda t: (0,) * len(s))
    low = struct((count, width), BF16)
    return pl.pallas_call(
        functools.partial(feed_back_kernel, tiles),
        grid=(count // tile_rows,),
        out_shape=[low, struct((count, ff), BF16), low, struct((count, width), F32), low]
        + [struct((8, width), F32), struct((8, ff), F32)],
        in_specs=[SMEM, full(128, width), tile(width), tile(128), tile(ff), tile(width), tile(128)]
        + [full(ff, width), full(width, ff), full(width, width), full(1, width), full(1, width)],
        out_specs=[tile(width), tile(ff), tile(width), tile(width), tile(width)]
        + [full(8, width), full(8, ff)],
        compiler_params=pltpu.CompilerParams(vmem_limit_bytes=VMEM_LIMIT),
    )(lens, dp, n2, i2, slope, n1, i1, wd, wi, wo, g2, g1)


def outer_kernel(a_ref, b_ref, o_ref):
    o_ref[...] = dot(a_ref[...], b_ref[...], 0, 0).astype(o_ref.dtype)


def outer(a, b, bm, bn):
    count, m = a.shape
    n = b.shape[1]
    return pl.pallas_call(
        outer_kernel,
        grid=(m // bm, n // bn),
        out_shape=struct((m, n), BF16),
        in_specs=[
            pl.BlockSpec((count, bm), lambda i, j: (0, i)),
            pl.BlockSpec((count, bn), lambda i, j: (0, j)),
        ],
        out_specs=pl.BlockSpec((bm, bn), lambda i, j: (i, j)),
        compiler_params=pltpu.CompilerParams(vmem_limit_bytes=VMEM_LIMIT),
    )(a, b)


def attention_back_kernel(q_ref, k_ref, v_ref, p_ref, do_ref, dq_ref, dk_ref, dv_ref, kt_ref, dqt_ref):
    kt_ref[...] = k_ref[0].T
    lane = lax.broadcasted_iota(jnp.int32, (1, 128), 1)

    def pair(p, carry):
        sl = pl.ds(pl.multiple_of(p * 128, 128), 128)
        qp, vp, dop = q_ref[0, :, sl], v_ref[0, :, sl], do_ref[0, :, sl]
        zero = jnp.zeros_like(vp)
        dv = dk = None
        for h in range(2):
            mine = lane // HEAD_DIM == h
            vm, dom, qm = (jnp.where(mine, u, zero) for u in (vp, dop, qp))
            hs = pl.ds(pl.multiple_of(p * 128 + h * HEAD_DIM, HEAD_DIM), HEAD_DIM)
            pt = p_ref[0, p * 2 + h]
            probs = pt.astype(F32)
            weighted = probs * dot(vm, dop, 1, 1)
            ds = (weighted - probs * jnp.sum(weighted, axis=0, keepdims=True)).astype(BF16)
            dv_h, dk_h = dot(pt, dom), dot(ds, qm)
            dv = dv_h if dv is None else dv + dv_h
            dk = dk_h if dk is None else dk + dk_h
            dqt_ref[hs, :] = (dot(kt_ref[hs, :], ds) * HEAD_DIM ** (-0.5)).astype(BF16)
        dv_ref[0, :, sl] = dv.astype(BF16)
        dk_ref[0, :, sl] = dk.astype(BF16)
        return carry

    lax.fori_loop(0, HEADS // 2, pair, 0)
    dq_ref[0] = dqt_ref[...].T


def attention_back(q, k, v, p, do):
    rows, length, width = q.shape
    row = lambda *s: pl.BlockSpec((1,) + s, lambda r: (r,) + (0,) * len(s))
    return pl.pallas_call(
        attention_back_kernel,
        grid=(rows,),
        out_shape=[struct((rows, length, width), BF16)] * 3,
        in_specs=[row(length, width)] * 3 + [row(HEADS, length, length), row(length, width)],
        out_specs=[row(length, width)] * 3,
        scratch_shapes=[pltpu.VMEM((width, length), BF16), pltpu.VMEM((width, length), BF16)],
        compiler_params=pltpu.CompilerParams(vmem_limit_bytes=VMEM_LIMIT),
    )(q, k, v, p, do)


def input_back_kernel(dpre1_ref, dq_ref, dk_ref, dv_ref, wq, wk, wv, out_ref, sums_ref):
    @pl.when(pl.program_id(0) == 0)
    def _():
        sums_ref[...] = jnp.zeros_like(sums_ref)

    sums_ref[0:1] += jnp.sum(dq_ref[...].astype(F32), axis=0, keepdims=True)
    sums_ref[1:2] += jnp.sum(dv_ref[...].astype(F32), axis=0, keepdims=True)
    total = dpre1_ref[...] + dot(dq_ref[...], wq[...], 1, 1)
    total += dot(dk_ref[...], wk[...], 1, 1) + dot(dv_ref[...], wv[...], 1, 1)
    out_ref[...] = total.astype(out_ref.dtype)


def input_back(dpre1, dq, dk, dv, wq, wk, wv, tile_rows):
    count, width = dpre1.shape
    tile = pl.BlockSpec((tile_rows, width), lambda t: (t, 0))
    full = lambda *s: pl.BlockSpec(s, lambda t: (0,) * len(s))
    return pl.pallas_call(
        input_back_kernel,
        grid=(count // tile_rows,),
        out_shape=[struct((count, width), BF16), struct((8, width), F32)],
        in_specs=[tile] * 4 + [full(width, width)] * 3,
        out_specs=[tile, full(8, width)],
        compiler_params=pltpu.CompilerParams(vmem_limit_bytes=VMEM_LIMIT),
    )(dpre1, dq, dk, dv, wq, wk, wv)


def pack_small(vectors, wide, extra):
    rows = [jnp.pad(v.astype(F32), (0, 128 - v.shape[0])) for v in (*vectors, wide, extra)]
    rows += [jnp.zeros((128,), F32)] * (16 - len(rows))
    return jnp.stack(rows)


def per_device(
    tokens, lengths, pair_ids, w_query, b_query, w_key, w_value, b_value, w_out, b_out,
    norm1_gain, norm1_bias, w_in, b_in, w_down, b_down, norm2_gain, norm2_bias,
):
    blk_size, seq_size = lax.axis_size("blk"), lax.axis_size("seq")
    grid = Grid(blk_size, seq_size)
    devices = blk_size * seq_size
    group_rows, local_len, width = tokens.shape
    rows = group_rows // seq_size
    length = local_len * seq_size
    count = rows * length
    ff = w_in.shape[1]
    part, wide_part, pairs = b_query.shape[0], b_in.shape[0], pair_ids.shape[0]

    lens = lax.dynamic_slice_in_dim(lengths, lax.axis_index("seq") * rows, rows, 0)
    vectors = (b_query, b_value, b_out, norm1_gain, norm1_bias, b_down, norm2_gain, norm2_bias)
    small = pack_small(vectors, b_in, pair_ids)
    full, x = gather_all(grid, (w_query, w_key, w_value, small, w_out, w_in, w_down), tokens, 1)
    wq, wk, wv, smalls, wo, wi, wd = full
    smalls = smalls.reshape(devices, 16, 128)
    vecs = smalls[:, : len(vectors), :part].transpose(1, 0, 2).reshape(len(vectors), 1, width)
    bq, bv, bo, g1, s1, bd, g2, s2 = (vecs[i] for i in range(len(vectors)))
    bi = smalls[:, len(vectors), :wide_part].reshape(1, ff)
    all_pairs = smalls[:, len(vectors) + 1, :pairs].reshape(-1, NQ).astype(jnp.int32)

    q, k, v, p, o = attention(lens, x, wq, wk, wv, bq, bv)
    x2, o2 = x.reshape(count, width), o.reshape(count, width)
    hid, n1, i1, h1, act, slope, n2, i2, pool = feed(
        lens, x2, o2, wo, bo, g1, s1, wi, bi, wd, bd, g2, s2, 256
    )

    none = jnp.full((all_pairs.shape[0], SEGS - NQ), -1, jnp.int32)
    pair_row = jnp.concatenate([all_pairs, none], axis=1).reshape(1, -1)
    own_pairs = jnp.concatenate([pair_ids.reshape(rows, NQ), none[:rows]], axis=1).reshape(-1, 1)
    pair_col = jnp.broadcast_to(own_pairs, (rows * SEGS, 128))
    len_col = jnp.broadcast_to(lens.reshape(-1, 1).astype(F32), (rows * SEGS, 128))
    losses, dpool = contrast(grid, pool, len_col, pair_col, pair_row, 2)
    query_loss = losses[:, 0].reshape(rows, SEGS)[:, :NQ].reshape(-1)

    dfeed, dinner, dbranch, dpre1, datt, sums, wide_sums = feed_back(
        lens, dpool, n2, i2, slope, n1, i1, wd, wi, wo, g2, g1, 256
    )
    grad_w_down = outer(act, dfeed, width, width)
    grad_w_in = outer(h1, dinner, width, width)
    grad_w_out = outer(o2, dbranch, width, width)
    dq, dk, dv = attention_back(q, k, v, p, datt.reshape(rows, length, width))
    dq, dk, dv = (d.reshape(count, width) for d in (dq, dk, dv))
    grad_x, sums_in = input_back(dpre1, dq, dk, dv, wq, wk, wv, 256)
    grad_w_query = outer(x2, dq, width, width)
    grad_w_key = outer(x2, dk, width, width)
    grad_w_value = outer(x2, dv, width, width)

    vec_grads = jnp.stack(
        [sums_in[0], sums_in[1], sums[5], sums[3], sums[4], sums[2], sums[0], sums[1]]
    )
    packed = jnp.pad(
        vec_grads.reshape(8, devices, part).transpose(1, 0, 2), ((0, 0), (0, 0), (0, 128 - part))
    )
    wide_grads = jnp.pad(
        wide_sums[0].reshape(devices, 1, wide_part), ((0, 0), (0, 7), (0, 128 - wide_part))
    )
    packed = jnp.concatenate([packed, wide_grads], axis=1).reshape(devices * 16, 128)
    grads, back = scatter_all(
        grid,
        (grad_w_down, grad_w_in, grad_w_out, packed, grad_w_query, grad_w_key, grad_w_value),
        (hid.reshape(rows, length, width), grad_x.reshape(rows, length, width)),
        3,
    )
    g_down, g_in, g_out, g_small, g_query, g_key, g_value = grads
    hidden_out, grad_tokens = back
    gv = [g_small[i, :part] for i in range(8)]
    return (
        hidden_out,
        query_loss,
        grad_tokens.astype(F32),
        g_query,
        gv[0],
        g_key,
        g_value,
        gv[1],
        g_out,
        gv[2],
        gv[3],
        gv[4],
        g_in,
        g_small[8, :wide_part],
        g_down,
        gv[5],
        gv[6],
        gv[7],
    )


def solution(mesh):
    both = ("blk", "seq")
    vec, mat, tok = P(both), P(both, None), P("blk", "seq", None)
    in_specs = (
        tok, P("blk", None), vec, mat, vec, mat, mat, vec, mat, vec, vec, vec, mat, vec, mat, vec,
        vec, vec,
    )
    out_specs = (
        tok, vec, tok, mat, vec, mat, mat, vec, mat, vec, vec, vec, mat, vec, mat, vec, vec, vec,
    )
    return jax.shard_map(
        per_device, mesh=mesh, in_specs=in_specs, out_specs=out_specs, check_vma=False
    )
```

```python
import functools

import jax
import jax.numpy as jnp
from jax import lax
from jax.experimental import pallas as pl
from jax.experimental.pallas import tpu as pltpu
from jax.sharding import PartitionSpec as P

HEADS = 12
HEAD_DIM = 64
NQ = 2
SEGS = 4
TEMPERATURE = 0.05
NORM_EPSILON = 1e-06
MASKED = -1000000000.0
BF16 = jnp.bfloat16
F32 = jnp.float32
MESH = pl.DeviceIdType.MESH
ANY = pl.BlockSpec(memory_space=pl.ANY)
VMEM = pl.BlockSpec(memory_space=pltpu.VMEM)
SMEM = pl.BlockSpec(memory_space=pltpu.SMEM)
DMA = pltpu.SemaphoreType.DMA
VMEM_LIMIT = 60 * 2**20


def dot(a, b, ca=1, cb=0):
    return lax.dot_general(a, b, (((ca,), (cb,)), ((), ())), preferred_element_type=F32)


def struct(shape, dtype):
    return jax.ShapeDtypeStruct(shape, dtype)


def split_two(v):
    high = v.astype(BF16)
    return high, (v - high.astype(F32)).astype(BF16)


class Grid:
    def __init__(self, blk_size, seq_size):
        self.blk_size, self.seq_size = blk_size, seq_size
        self.kb = blk_size.bit_length() - 1
        self.ks = seq_size.bit_length() - 1
        assert 1 << self.kb == blk_size and 1 << self.ks == seq_size
        self.nd = self.kb + self.ks

    def here(self):
        return lax.axis_index("blk"), lax.axis_index("seq")

    def digit(self, b, q, d):
        if d < self.kb:
            w = 1 << (self.kb - 1 - d)
            return (b // w) % 2, w
        w = 1 << (self.nd - 1 - d)
        return (q // w) % 2, w

    def digits(self, b, q):
        return [self.digit(b, q, d)[0] for d in range(self.nd)]

    def partner(self, b, q, d):
        v, w = self.digit(b, q, d)
        if d < self.kb:
            return (b + (1 - 2 * v) * w, q)
        return (b, q + (1 - 2 * v) * w)

    def order(self, flavour):
        seq = list(range(self.kb, self.nd))
        head, last = list(range(self.kb))[:-1][::-1], [self.kb - 1]
        if head:
            r = flavour % len(head)
            head = head[r:] + head[:r]
        return seq + head + last

    def greet(self, b, q, partners, others):
        barrier = pltpu.get_barrier_semaphore()
        targets = [partners[d] for d in range(self.kb)]
        if others is None:
            targets += [partners[d] for d in range(self.kb, self.nd)]
        else:
            targets += [(b, o) for o in others]
        for t in targets:
            pl.semaphore_signal(barrier, inc=1, device_id=t, device_id_type=MESH)
        pl.semaphore_wait(barrier, len(targets))


def remote(src, dst, send, recv, where):
    return pltpu.make_async_remote_copy(
        src_ref=src, dst_ref=dst, send_sem=send, recv_sem=recv, device_id=where, device_id_type=MESH
    )


def flat_view(rows, lanes):
    if rows % 8 == 0:
        return rows, lanes
    return rows * lanes // 128, 128


def pieces(shapes):
    out = []
    for a, (rows, lanes) in enumerate(shapes):
        unit = 768 if rows < 64 else 256
        unit = min(unit, lanes)
        for lo in range(0, lanes, unit):
            half = unit // 2
            if half % 128 == 0:
                out.append([(a, lo, half, 0), (a, lo + half, half, 1)])
            else:
                out.append([(a, lo, unit, 0)])
    return out


def gather_kernel(grid, groups, n, lag, *refs):
    ins, tok = refs[:n], refs[n]
    outs, rows_out = refs[n + 1 : 2 * n + 1], refs[2 * n + 1]
    own_sem, send_sem, recv_sem, tok_own, tok_send, tok_recv = refs[2 * n + 2 :]
    b, q = grid.here()
    nd, ns = grid.nd, grid.seq_size
    my = grid.digits(b, q)
    partners = [grid.partner(b, q, d) for d in range(nd)]
    others = [lax.rem(q + j, ns) for j in range(1, ns)]
    grid.greet(b, q, partners, others)
    flat = [c for g in groups for c in g]
    where = {}
    first = 0
    for gi, g in enumerate(groups):
        where[gi] = list(range(first, first + len(g)))
        first += len(g)

    own = []
    for i, (a, lo, ln, _) in enumerate(flat):
        c = pltpu.make_async_copy(
            ins[a].at[:, pl.ds(lo, ln)],
            outs[a].at[tuple(my) + (slice(None), pl.ds(lo, ln))],
            own_sem.at[i],
        )
        c.start()
        own.append(c)
    copies = {}

    def stage(i, k):
        a, lo, ln, flavour = flat[i]
        order = grid.order(flavour)
        d = order[k]
        if k == 0:
            src = ins[a].at[:, pl.ds(lo, ln)]
            dst = outs[a].at[tuple(my) + (slice(None), pl.ds(lo, ln))]
        else:
            if k == 1:
                own[i].wait()
            copies[(i, k - 1)].wait_recv()
            done = order[:k]
            ix = tuple(slice(None) if e in done else my[e] for e in range(nd))
            ix = ix + (slice(None), pl.ds(lo, ln))
            src, dst = outs[a].at[ix], outs[a].at[ix]
        c = remote(src, dst, send_sem.at[i, k], recv_sem.at[i, k], partners[d])
        c.start()
        copies[(i, k)] = c

    row_copies = []
    total, lt, _ = tok.shape
    per = total // ns

    def send_rows():
        at = pl.ds(pl.multiple_of(q * lt, lt), lt)
        for r in range(per):
            c = pltpu.make_async_copy(tok.at[q * per + r], rows_out.at[r, at], tok_own.at[r])
            c.start()
            row_copies.append(c)
            for j in range(1, ns):
                o = others[j - 1]
                c = remote(
                    tok.at[o * per + r],
                    rows_out.at[r, at],
                    tok_send.at[j - 1, r],
                    tok_recv.at[j - 1, r],
                    (b, o),
                )
                c.start()
                row_copies.append(c)

    ng = len(groups)
    for t in range(ng + lag * (nd - 1)):
        for k in range(nd - 1, -1, -1):
            g = t - lag * k
            if 0 <= g < ng:
                for i in where[g]:
                    stage(i, k)
        if t == 2:
            send_rows()
    for i in range(len(flat)):
        copies[(i, nd - 1)].wait_recv()
    for i in range(len(flat)):
        for k in range(nd):
            copies[(i, k)].wait_send()
    for c in row_copies:
        c.wait()


def gather_all(grid, blocks, tokens, collective_id):
    nd, ns = grid.nd, grid.seq_size
    n = len(blocks)
    views = [x.reshape(flat_view(*x.shape)) for x in blocks]
    groups = pieces([v.shape for v in views])
    count = sum(len(g) for g in groups)
    total, lt, width = tokens.shape
    per = total // ns
    outs = [struct((2,) * nd + v.shape, v.dtype) for v in views]
    outs.append(struct((per, lt * ns, width), tokens.dtype))
    res = pl.pallas_call(
        functools.partial(gather_kernel, grid, groups, n, 2),
        out_shape=outs,
        in_specs=[VMEM] * (n + 1),
        out_specs=[ANY] * (n + 1),
        scratch_shapes=[
            DMA((count,)),
            DMA((count, nd)),
            DMA((count, nd)),
            DMA((per,)),
            DMA((ns - 1, per)),
            DMA((ns - 1, per)),
        ],
        compiler_params=pltpu.CompilerParams(
            collective_id=collective_id, has_side_effects=True, vmem_limit_bytes=VMEM_LIMIT
        ),
    )(*views, tokens)
    devices = 1 << nd
    full = [
        r.reshape((devices * x.shape[0], x.shape[1])) for r, x in zip(res[:-1], blocks, strict=True)
    ]
    return full, res[-1]


def reduce_plan(grid, flavour):
    free = list(range(grid.nd))
    plan = []
    for d in grid.order(flavour)[::-1]:
        pos = free.index(d)
        plan.append((d, 1 << pos, 1 << (len(free) - pos - 1)))
        free.remove(d)
    return plan


def scatter_kernel(grid, flat, n, nx, lag, *refs):
    nd, ns = grid.nd, grid.seq_size
    ins, rows_in = refs[:n], refs[n : n + nx]
    outs, rows_out = refs[n + nx : 2 * n + nx], refs[2 * n + nx : 2 * n + 2 * nx]
    rest = list(refs[2 * n + 2 * nx :])
    own_sem, send_sem, recv_sem, x_own, x_send, x_recv = rest[:6]
    bufs = rest[6:]
    b, q = grid.here()
    my = grid.digits(b, q)
    partners = [grid.partner(b, q, d) for d in range(nd)]
    others = [lax.rem(q + j, ns) for j in range(1, ns)]
    grid.greet(b, q, partners, others)

    row_copies = []
    for x in range(nx):
        per, length, _ = rows_in[x].shape
        lt = length // ns
        for r in range(per):
            at = pl.ds(pl.multiple_of(q * lt, lt), lt)
            c = pltpu.make_async_copy(
                rows_in[x].at[r, at], rows_out[x].at[q * per + r], x_own.at[x, r]
            )
            c.start()
            row_copies.append(c)

    def send_rows(x):
        per, length, _ = rows_in[x].shape
        lt = length // ns
        for r in range(per):
            for j in range(1, ns):
                o = others[j - 1]
                c = remote(
                    rows_in[x].at[r, pl.ds(pl.multiple_of(o * lt, lt), lt)],
                    rows_out[x].at[q * per + r],
                    x_send.at[x, j - 1, r],
                    x_recv.at[x, j - 1, r],
                    (b, o),
                )
                c.start()
                row_copies.append(c)

    per_piece = 1 + 2 * nd - 1
    copies, own = {}, {}

    def buffers(i):
        mine = bufs[i * per_piece : (i + 1) * per_piece]
        return mine[0], mine[1 : 1 + nd], mine[1 + nd :]

    for i, (a, lo, ln, flavour) in enumerate(flat):
        d = reduce_plan(grid, flavour)[0][0]
        ix = tuple(my[e] if e == d else slice(None) for e in range(nd)) + (slice(None), pl.ds(lo, ln))
        c = pltpu.make_async_copy(ins[a].at[ix], buffers(i)[0], own_sem.at[i])
        c.start()
        own[i] = c

    def send(i, k):
        a, lo, ln, flavour = flat[i]
        d, pre, post = reduce_plan(grid, flavour)[k]
        start, recv, acc = buffers(i)
        if k == 0:
            ix = tuple((1 - my[e]) if e == d else slice(None) for e in range(nd))
            src = ins[a].at[ix + (slice(None), pl.ds(lo, ln))]
        else:
            src = acc[k - 1].at[:, 1 - my[d]]
        c = remote(src, recv[k], send_sem.at[i, k], recv_sem.at[i, k], partners[d])
        c.start()
        copies[(i, k)] = c

    def add(i, k):
        a, lo, ln, flavour = flat[i]
        plan = reduce_plan(grid, flavour)
        d, pre, post = plan[k]
        start, recv, acc = buffers(i)
        copies[(i, k)].wait_recv()
        if k == 0:
            own[i].wait()
        if k == nd - 1:
            total = acc[k - 1][0, my[d], 0].astype(F32) + recv[k][0, 0].astype(F32)
            outs[a][:, lo : lo + ln] = total
            return
        _, pre2, post2 = plan[k + 1]

        def one(j, carry):
            if k == 0:
                ix = tuple((j // (1 << (nd - 2 - e))) % 2 for e in range(nd - 1))
                mine, other = start[ix], recv[0][ix]
            else:
                mine = acc[k - 1][j // post, my[d], j % post]
                other = recv[k][j // post, j % post]
            total = mine.astype(F32) + other.astype(F32)
            acc[k][j // (2 * post2), (j // post2) % 2, j % post2] = total.astype(acc[k].dtype)
            return carry

        lax.fori_loop(0, pre * post, one, 0)

    groups = sorted({c[4] for c in [(*f, gi) for f, gi in zip(flat, group_of(flat))]})
    members = {g: [i for i, gi in enumerate(group_of(flat)) if gi == g] for g in groups}
    ng = len(groups)
    for t in range(ng + lag * nd):
        for k in range(nd, -1, -1):
            g = t - lag * k
            if 0 <= g < ng:
                for i in members[g]:
                    if k > 0:
                        add(i, k - 1)
                    if k < nd:
                        send(i, k)
        if t == 0:
            for x in range(nx):
                send_rows(x)
    for i in range(len(flat)):
        for k in range(nd):
            copies[(i, k)].wait_send()
    for c in row_copies:
        c.wait()


def group_of(flat):
    ids, last = [], -1
    for _, _, _, flavour in flat:
        if flavour == 0:
            last += 1
        ids.append(last)
    return ids


def scatter_all(grid, grads, rows_back, collective_id):
    nd, ns = grid.nd, grid.seq_size
    devices = 1 << nd
    views, finals = [], []
    for g in grads:
        rows = g.shape[0] // devices
        finals.append((rows, g.shape[1]))
        views.append(g.reshape((2,) * nd + flat_view(rows, g.shape[1])))
    flat = [c for g in pieces([v.shape[-2:] for v in views]) for c in g]
    n, nx = len(views), len(rows_back)
    scratch = []
    for a, _, ln, flavour in flat:
        rows, dtype = views[a].shape[-2], views[a].dtype
        plan = reduce_plan(grid, flavour)
        scratch.append(pltpu.VMEM((2,) * (nd - 1) + (rows, ln), dtype))
        for k, (_, pre, post) in enumerate(plan):
            shape = (2,) * (nd - 1) if k == 0 else (pre, post)
            scratch.append(pltpu.VMEM(shape + (rows, ln), dtype))
        for _, pre, post in plan[1:]:
            scratch.append(pltpu.VMEM((pre, 2, post, rows, ln), dtype))
    outs = [struct(v.shape[-2:], F32) for v in views]
    for x in rows_back:
        per, length, width = x.shape
        outs.append(struct((per * ns, length // ns, width), x.dtype))
    per = rows_back[0].shape[0]
    count = len(flat)
    res = pl.pallas_call(
        functools.partial(scatter_kernel, grid, flat, n, nx, 2),
        out_shape=outs,
        in_specs=[ANY] * n + [ANY] * nx,
        out_specs=[VMEM] * n + [ANY] * nx,
        scratch_shapes=[
            DMA((count,)),
            DMA((count, nd)),
            DMA((count, nd)),
            DMA((nx, per)),
            DMA((nx, ns - 1, per)),
            DMA((nx, ns - 1, per)),
        ]
        + scratch,
        compiler_params=pltpu.CompilerParams(
            collective_id=collective_id, has_side_effects=True, vmem_limit_bytes=VMEM_LIMIT
        ),
    )(*views, *rows_back)
    return [r.reshape(s) for r, s in zip(res[:n], finals, strict=True)], res[n:]


def segment_of(lens, r, shape, axis, start=0):
    t = lax.broadcasted_iota(jnp.int32, shape, axis) + start
    end = lens[r, 0]
    seg = (t >= end).astype(jnp.int32)
    for k in range(1, SEGS):
        end = end + lens[r, k]
        seg = seg + (t >= end).astype(jnp.int32)
    return seg


def attention_kernel(
    lens, x_ref, wq, wk, wv, bq, bv, q_ref, k_ref, v_ref, p_ref, o_ref, vt_ref, ot_ref, bias_ref
):
    x = x_ref[0]
    length = x.shape[0]
    r = pl.program_id(0)
    seg_k = segment_of(lens, r, (length, 1), 0)
    seg_q = segment_of(lens, r, (1, length), 1)
    bias_ref[...] = jnp.where(seg_k == seg_q, 0.0, MASKED)
    q_ref[0] = ((dot(x, wq[...]) + bq[...]) * HEAD_DIM ** (-0.5)).astype(BF16)
    k_ref[0] = dot(x, wk[...]).astype(BF16)
    v = dot(x, wv[...]) + bv[...]
    v_ref[0] = v.astype(BF16)
    vt_ref[...] = v.T.astype(BF16)
    lane = lax.broadcasted_iota(jnp.int32, (1, 128), 1)

    def pair(p, carry):
        sl = pl.ds(pl.multiple_of(p * 128, 128), 128)
        qp, kp = q_ref[0, :, sl], k_ref[0, :, sl]
        for h in range(2):
            km = jnp.where(lane // HEAD_DIM == h, kp, jnp.zeros_like(kp))
            hs = pl.ds(pl.multiple_of(p * 128 + h * HEAD_DIM, HEAD_DIM), HEAD_DIM)
            s = dot(km, qp, 1, 1) + bias_ref[...]
            e = jnp.exp(s - jnp.max(s, axis=0, keepdims=True))
            pt = (e * (1.0 / jnp.sum(e, axis=0, keepdims=True))).astype(BF16)
            p_ref[0, p * 2 + h] = pt
            ot_ref[hs, :] = dot(vt_ref[hs, :], pt).astype(BF16)
        return carry

    lax.fori_loop(0, HEADS // 2, pair, 0)
    o_ref[0] = ot_ref[...].T


def attention(lens, x, wq, wk, wv, bq, bv):
    rows, length, width = x.shape
    row = lambda *s: pl.BlockSpec((1,) + s, lambda r: (r,) + (0,) * len(s))
    full = lambda *s: pl.BlockSpec(s, lambda r: (0,) * len(s))
    tokens = struct((rows, length, width), BF16)
    return pl.pallas_call(
        attention_kernel,
        grid=(rows,),
        out_shape=[tokens] * 3 + [struct((rows, HEADS, length, length), BF16), tokens],
        in_specs=[SMEM, row(length, width)] + [full(width, width)] * 3 + [full(1, width)] * 2,
        out_specs=[row(length, width)] * 3 + [row(HEADS, length, length), row(length, width)],
        scratch_shapes=[
            pltpu.VMEM((width, length), BF16),
            pltpu.VMEM((width, length), BF16),
            pltpu.VMEM((length, length), F32),
        ],
        compiler_params=pltpu.CompilerParams(vmem_limit_bytes=VMEM_LIMIT),
    )(lens, x, wq, wk, wv, bq, bv)


def layer_norm(v):
    c = v - jnp.mean(v, axis=-1, keepdims=True)
    inv = lax.rsqrt(jnp.mean(c * c, axis=-1, keepdims=True) + NORM_EPSILON)
    return c * inv, inv


def feed_kernel(
    tiles, lens, x_ref, o_ref, wo, bo, g1, s1, wi, bi, wd, bd, g2, s2,
    hid_ref, n1_ref, i1_ref, h1_ref, act_ref, slope_ref, n2_ref, i2_ref, pool_ref,
):
    t = pl.program_id(0)
    rows = x_ref.shape[0]
    pre1 = x_ref[...].astype(F32) + dot(o_ref[...], wo[...]) + bo[...]
    n1, i1 = layer_norm(pre1)
    h1 = n1 * g1[...] + s1[...]
    h1_low = h1.astype(BF16)
    n1_ref[...] = n1.astype(BF16)
    h1_ref[...] = h1_low
    i1_ref[...] = jnp.broadcast_to(i1, i1_ref.shape)
    acc = h1 + bd[...]
    chunk = wd.shape[1]
    for lo in range(0, wi.shape[1], chunk):
        sl = slice(lo, lo + chunk)
        inner = dot(h1_low, wi[:, sl]) + bi[:, sl]
        phi = 0.5 + 0.5 * lax.erf(inner * (0.5**0.5))
        act = (inner * phi).astype(BF16)
        act_ref[:, sl] = act
        density = jnp.exp(-0.5 * inner * inner) * 0.3989422804014327
        slope_ref[:, sl] = (phi + inner * density).astype(BF16)
        acc = acc + dot(act, wd[sl, :])
    n2, i2 = layer_norm(acc)
    h2 = n2 * g2[...] + s2[...]
    high, low = split_two(h2)
    hid_ref[...] = high
    n2_ref[...] = n2.astype(BF16)
    i2_ref[...] = jnp.broadcast_to(i2, i2_ref.shape)
    r = t // tiles
    seg = segment_of(lens, r, (1, rows), 1, (t % tiles) * rows)
    slot = jnp.where(seg < SEGS, r * SEGS + seg, -1)
    members = lax.broadcasted_iota(jnp.int32, (pool_ref.shape[0], rows), 0) == slot
    members = members.astype(F32).astype(BF16)
    part = dot(members, high) + dot(members, low)

    @pl.when(t == 0)
    def _():
        pool_ref[...] = part

    @pl.when(t != 0)
    def _():
        pool_ref[...] += part


def feed(lens, x, o, wo, bo, g1, s1, wi, bi, wd, bd, g2, s2, tile_rows):
    count, width = x.shape
    rows = lens.shape[0]
    ff = wi.shape[1]
    tiles = count // rows // tile_rows
    tile = lambda w: pl.BlockSpec((tile_rows, w), lambda t: (t, 0))
    full = lambda *s: pl.BlockSpec(s, lambda t: (0,) * len(s))
    vec = full(1, width)
    low, col = struct((count, width), BF16), struct((count, 128), F32)
    wide = struct((count, ff), BF16)
    return pl.pallas_call(
        functools.partial(feed_kernel, tiles),
        grid=(count // tile_rows,),
        out_shape=[low, low, col, low, wide, wide, low, col, struct((rows * SEGS, width), F32)],
        in_specs=[SMEM, tile(width), tile(width), full(width, width), vec, vec, vec]
        + [full(width, ff), full(1, ff), full(ff, width), vec, vec, vec],
        out_specs=[tile(width), tile(width), tile(128), tile(width), tile(ff), tile(ff)]
        + [tile(width), tile(128), full(rows * SEGS, width)],
        compiler_params=pltpu.CompilerParams(vmem_limit_bytes=VMEM_LIMIT),
    )(lens, x, o, wo, bo, g1, s1, wi, bi, wd, bd, g2, s2)


def contrast_kernel(grid, pool_ref, len_ref, pair_ref, pairs_ref, loss_ref, dpool_ref, emb, send_sem, recv_sem):
    nd = grid.nd
    b, q = grid.here()
    my = grid.digits(b, q)
    partners = [grid.partner(b, q, d) for d in range(nd)]
    own_rows, width = pool_ref.shape
    count = own_rows << nd
    avg = pool_ref[...] / len_ref[:, :1]
    inv = lax.rsqrt(jnp.sum(avg * avg, axis=-1, keepdims=True) + NORM_EPSILON)
    own = avg * inv
    emb[tuple(my)] = own
    grid.greet(b, q, partners, None)
    order = grid.order(0)
    for k, d in enumerate(order):
        ix = tuple(slice(None) if e in order[:k] else my[e] for e in range(nd))
        c = remote(emb.at[ix], emb.at[ix], send_sem.at[k], recv_sem.at[k], partners[d])
        c.start()
        c.wait()
    high, low = split_two(emb[...].reshape(count, width))
    own_high, own_low = split_two(own)
    scale = 1.0 / TEMPERATURE

    def product(ah, al, bh, bl, cb):
        return dot(ah, bh, 1, cb) + dot(ah, bl, 1, cb) + dot(al, bh, 1, cb)

    total = jnp.zeros((1, count), F32)
    step = min(count, 256)
    for lo in range(0, count, step):
        sim = product(high[lo : lo + step], low[lo : lo + step], high, low, 1) * scale
        at = lax.broadcasted_iota(jnp.int32, (step, 1), 0)
        total += jnp.sum(jnp.where(at % SEGS >= NQ, jnp.exp(sim - scale), 0.0), axis=0, keepdims=True)
    lse_cols = scale + jnp.log(total)
    sim = product(own_high, own_low, high, low, 1) * scale
    col = lax.broadcasted_iota(jnp.int32, (1, count), 1)
    row = lax.broadcasted_iota(jnp.int32, (own_rows, 1), 0) + (b * grid.seq_size + q) * own_rows
    col_doc, row_doc = col % SEGS >= NQ, row % SEGS >= NQ
    number = lambda at: (at // SEGS) * NQ + at % SEGS - NQ
    lse_rows = scale + jnp.log(
        jnp.sum(jnp.where(col_doc, jnp.exp(sim - scale), 0.0), axis=1, keepdims=True)
    )
    chosen = col_doc & (number(col) == pair_ref[:, :1])
    positive = jnp.sum(jnp.where(chosen, sim, 0.0), axis=1, keepdims=True)
    loss_ref[...] = jnp.broadcast_to(lse_rows - positive, loss_ref.shape)
    as_query = jnp.exp(sim - lse_rows) - chosen.astype(F32)
    chosen_by = number(row) == pairs_ref[:1]
    as_doc = jnp.exp(jnp.where(col_doc, MASKED, sim - lse_cols)) - chosen_by.astype(F32)
    grad = jnp.where(row_doc, jnp.where(col_doc, 0.0, as_doc), jnp.where(col_doc, as_query, 0.0))
    grad_high, grad_low = split_two(grad)
    demb = product(grad_high, grad_low, high, low, 0) * scale
    dpool = inv * demb - inv * inv * inv * avg * jnp.sum(avg * demb, axis=-1, keepdims=True)
    dpool_high, dpool_low = split_two(dpool / len_ref[:, :1])
    pad = jnp.zeros((64 - own_rows, width), F32)
    stacked = jnp.concatenate([dpool_high.astype(F32), pad, dpool_low.astype(F32), pad], axis=0)
    dpool_ref[...] = stacked.astype(BF16)


def contrast(grid, pool, len_col, pair_col, pair_row, collective_id):
    own_rows, width = pool.shape
    return pl.pallas_call(
        functools.partial(contrast_kernel, grid),
        out_shape=[struct((own_rows, 128), F32), struct((128, width), BF16)],
        in_specs=[VMEM] * 4,
        out_specs=[VMEM] * 2,
        scratch_shapes=[
            pltpu.VMEM((2,) * grid.nd + (own_rows, width), F32),
            DMA((grid.nd,)),
            DMA((grid.nd,)),
        ],
        compiler_params=pltpu.CompilerParams(
            collective_id=collective_id, has_side_effects=True, vmem_limit_bytes=VMEM_LIMIT
        ),
    )(pool, len_col, pair_col, pair_row)


def feed_back_kernel(
    tiles, lens, dp_ref, n2_ref, i2_ref, slope_ref, n1_ref, i1_ref, wd, wi, wo, g2, g1,
    dfeed_ref, dinner_ref, dbranch_ref, dpre1_ref, datt_ref, sums_ref, wide_ref,
):
    t = pl.program_id(0)
    rows = n2_ref.shape[0]

    @pl.when(t == 0)
    def _():
        sums_ref[...] = jnp.zeros_like(sums_ref)
        wide_ref[...] = jnp.zeros_like(wide_ref)

    def columns(v):
        return jnp.sum(v, axis=0, keepdims=True)

    def norm_back(g, n, inv):
        return inv * (
            g - jnp.mean(g, axis=-1, keepdims=True) - n * jnp.mean(g * n, axis=-1, keepdims=True)
        )

    r = t // tiles
    seg = segment_of(lens, r, (rows, 1), 0, (t % tiles) * rows)
    slot = jnp.where(seg < SEGS, r * SEGS + seg, -1)
    lane = lax.broadcasted_iota(jnp.int32, (rows, 128), 1)
    members = (lane % 64 == slot).astype(F32).astype(BF16)
    dh2 = dot(members, dp_ref[...])
    n2 = n2_ref[...].astype(F32)
    sums_ref[0:1] += columns(dh2 * n2)
    sums_ref[1:2] += columns(dh2)
    dpre2 = norm_back(dh2 * g2[...], n2, i2_ref[:, :1])
    dfeed = dpre2.astype(BF16)
    dfeed_ref[...] = dfeed
    sums_ref[2:3] += columns(dfeed.astype(F32))
    chunk = wd.shape[1]
    dh1 = dpre2
    for lo in range(0, wi.shape[1], chunk):
        sl = slice(lo, lo + chunk)
        dinner = (dot(dfeed, wd[sl, :], 1, 1) * slope_ref[:, sl].astype(F32)).astype(BF16)
        dinner_ref[:, sl] = dinner
        wide_ref[0:1, sl] += columns(dinner.astype(F32))
        dh1 = dh1 + dot(dinner, wi[:, sl], 1, 1)
    n1 = n1_ref[...].astype(F32)
    sums_ref[3:4] += columns(dh1 * n1)
    sums_ref[4:5] += columns(dh1)
    dpre1 = norm_back(dh1 * g1[...], n1, i1_ref[:, :1])
    dpre1_ref[...] = dpre1
    dbranch = dpre1.astype(BF16)
    dbranch_ref[...] = dbranch
    sums_ref[5:6] += columns(dbranch.astype(F32))
    datt_ref[...] = dot(dbranch, wo[...], 1, 1).astype(BF16)


def feed_back(lens, dp, n2, i2, slope, n1, i1, wd, wi, wo, g2, g1, tile_rows):
    count, width = n2.shape
    rows = lens.shape[0]
    ff = wi.shape[1]
    tiles = count // rows // tile_rows
    tile = lambda w: pl.BlockSpec((tile_rows, w), lambda t: (t, 0))
    full = lambda *s: pl.BlockSpec(s, lambda t: (0,) * len(s))
    low = struct((count, width), BF16)
    return pl.pallas_call(
        functools.partial(feed_back_kernel, tiles),
        grid=(count // tile_rows,),
        out_shape=[low, struct((count, ff), BF16), low, struct((count, width), F32), low]
        + [struct((8, width), F32), struct((8, ff), F32)],
        in_specs=[SMEM, full(128, width), tile(width), tile(128), tile(ff), tile(width), tile(128)]
        + [full(ff, width), full(width, ff), full(width, width), full(1, width), full(1, width)],
        out_specs=[tile(width), tile(ff), tile(width), tile(width), tile(width)]
        + [full(8, width), full(8, ff)],
        compiler_params=pltpu.CompilerParams(vmem_limit_bytes=VMEM_LIMIT),
    )(lens, dp, n2, i2, slope, n1, i1, wd, wi, wo, g2, g1)


def outer_kernel(a_ref, b_ref, o_ref):
    o_ref[...] = dot(a_ref[...], b_ref[...], 0, 0).astype(o_ref.dtype)


def outer(a, b, bm, bn):
    count, m = a.shape
    n = b.shape[1]
    return pl.pallas_call(
        outer_kernel,
        grid=(m // bm, n // bn),
        out_shape=struct((m, n), BF16),
        in_specs=[
            pl.BlockSpec((count, bm), lambda i, j: (0, i)),
            pl.BlockSpec((count, bn), lambda i, j: (0, j)),
        ],
        out_specs=pl.BlockSpec((bm, bn), lambda i, j: (i, j)),
        compiler_params=pltpu.CompilerParams(vmem_limit_bytes=VMEM_LIMIT),
    )(a, b)


def attention_back_kernel(q_ref, k_ref, v_ref, p_ref, do_ref, dq_ref, dk_ref, dv_ref, kt_ref, dqt_ref):
    kt_ref[...] = k_ref[0].T
    lane = lax.broadcasted_iota(jnp.int32, (1, 128), 1)

    def pair(p, carry):
        sl = pl.ds(pl.multiple_of(p * 128, 128), 128)
        qp, vp, dop = q_ref[0, :, sl], v_ref[0, :, sl], do_ref[0, :, sl]
        zero = jnp.zeros_like(vp)
        dv = dk = None
        for h in range(2):
            mine = lane // HEAD_DIM == h
            vm, dom, qm = (jnp.where(mine, u, zero) for u in (vp, dop, qp))
            hs = pl.ds(pl.multiple_of(p * 128 + h * HEAD_DIM, HEAD_DIM), HEAD_DIM)
            pt = p_ref[0, p * 2 + h]
            probs = pt.astype(F32)
            weighted = probs * dot(vm, dop, 1, 1)
            ds = (weighted - probs * jnp.sum(weighted, axis=0, keepdims=True)).astype(BF16)
            dv_h, dk_h = dot(pt, dom), dot(ds, qm)
            dv = dv_h if dv is None else dv + dv_h
            dk = dk_h if dk is None else dk + dk_h
            dqt_ref[hs, :] = (dot(kt_ref[hs, :], ds) * HEAD_DIM ** (-0.5)).astype(BF16)
        dv_ref[0, :, sl] = dv.astype(BF16)
        dk_ref[0, :, sl] = dk.astype(BF16)
        return carry

    lax.fori_loop(0, HEADS // 2, pair, 0)
    dq_ref[0] = dqt_ref[...].T


def attention_back(q, k, v, p, do):
    rows, length, width = q.shape
    row = lambda *s: pl.BlockSpec((1,) + s, lambda r: (r,) + (0,) * len(s))
    return pl.pallas_call(
        attention_back_kernel,
        grid=(rows,),
        out_shape=[struct((rows, length, width), BF16)] * 3,
        in_specs=[row(length, width)] * 3 + [row(HEADS, length, length), row(length, width)],
        out_specs=[row(length, width)] * 3,
        scratch_shapes=[pltpu.VMEM((width, length), BF16), pltpu.VMEM((width, length), BF16)],
        compiler_params=pltpu.CompilerParams(vmem_limit_bytes=VMEM_LIMIT),
    )(q, k, v, p, do)


def input_back_kernel(dpre1_ref, dq_ref, dk_ref, dv_ref, wq, wk, wv, out_ref, sums_ref):
    @pl.when(pl.program_id(0) == 0)
    def _():
        sums_ref[...] = jnp.zeros_like(sums_ref)

    sums_ref[0:1] += jnp.sum(dq_ref[...].astype(F32), axis=0, keepdims=True)
    sums_ref[1:2] += jnp.sum(dv_ref[...].astype(F32), axis=0, keepdims=True)
    total = dpre1_ref[...] + dot(dq_ref[...], wq[...], 1, 1)
    total += dot(dk_ref[...], wk[...], 1, 1) + dot(dv_ref[...], wv[...], 1, 1)
    out_ref[...] = total.astype(out_ref.dtype)


def input_back(dpre1, dq, dk, dv, wq, wk, wv, tile_rows):
    count, width = dpre1.shape
    tile = pl.BlockSpec((tile_rows, width), lambda t: (t, 0))
    full = lambda *s: pl.BlockSpec(s, lambda t: (0,) * len(s))
    return pl.pallas_call(
        input_back_kernel,
        grid=(count // tile_rows,),
        out_shape=[struct((count, width), BF16), struct((8, width), F32)],
        in_specs=[tile] * 4 + [full(width, width)] * 3,
        out_specs=[tile, full(8, width)],
        compiler_params=pltpu.CompilerParams(vmem_limit_bytes=VMEM_LIMIT),
    )(dpre1, dq, dk, dv, wq, wk, wv)


class Reducer:
    def __init__(self, grid, flat, here, partners, my, sources, outs, own_sem, send_sem, recv_sem, bufs):
        self.grid, self.flat, self.here, self.partners, self.my = grid, flat, here, partners, my
        self.sources, self.outs = sources, outs
        self.own_sem, self.send_sem, self.recv_sem = own_sem, send_sem, recv_sem
        self.bufs = bufs
        self.per_piece = 1 + grid.nd

    def buf(self, i, k):
        return self.bufs[i * self.per_piece + 1 + k]

    def place(self, i, k):
        order = self.grid.order(self.flat[i][3])[::-1]
        free = [d for d in range(self.grid.nd) if d not in order[:k]]
        return order[k], free.index(order[k])

    def own(self, i):
        a, lo, ln, _ = self.flat[i]
        d, pos = self.place(i, 0)
        ix = (slice(None),) * pos + (self.my[d],) + (slice(None),) * (self.grid.nd - pos - 1)
        src = self.sources[a].at[ix + (slice(None), pl.ds(lo, ln))]
        return pltpu.make_async_copy(src, self.bufs[i * self.per_piece], self.own_sem.at[i])

    def copy(self, i, k):
        a, lo, ln, _ = self.flat[i]
        d, pos = self.place(i, k)
        ix = (slice(None),) * pos + (1 - self.my[d],) + (slice(None),) * (self.grid.nd - k - pos - 1)
        if k == 0:
            src = self.sources[a].at[ix + (slice(None), pl.ds(lo, ln))]
        else:
            src = self.buf(i, k - 1).at[ix]
        return remote(
            src, self.buf(i, k), self.send_sem.at[i, k], self.recv_sem.at[i, k], self.partners[d]
        )

    def send(self, i, k):
        if k == 0:
            self.own(i).start()
        self.copy(i, k).start()

    def add(self, i, k):
        nd = self.grid.nd
        a, lo, ln, _ = self.flat[i]
        d, pos = self.place(i, k)
        self.copy(i, k).wait_recv()
        if k == 0:
            self.own(i).wait()
        into = self.buf(i, k)
        left = nd - k - 1
        if left == 0:
            total = self.buf(i, k - 1)[self.my[d]].astype(F32) + into[...].astype(F32)
            self.outs[a][:, lo : lo + ln] = total
            return

        def one(j, carry):
            ix = tuple((j // (1 << (left - 1 - e))) % 2 for e in range(left))
            if k == 0:
                mine = self.bufs[i * self.per_piece][ix]
            else:
                mine = self.buf(i, k - 1)[ix[:pos] + (self.my[d],) + ix[pos:]]
            into[ix] = (mine.astype(F32) + into[ix].astype(F32)).astype(into.dtype)
            return carry

        lax.fori_loop(0, 1 << left, one, 0)

    def step(self, i, k):
        if k > 0:
            self.add(i, k - 1)
        if k < self.grid.nd:
            self.send(i, k)

    def finish(self):
        for i in range(len(self.flat)):
            for k in range(self.grid.nd):
                self.copy(i, k).wait_send()


def reducer_scratch(nd, flat, rows_of, dtype):
    out = []
    for a, _, ln, _ in flat:
        out.append(pltpu.VMEM((2,) * (nd - 1) + (rows_of[a], ln), dtype))
        for k in range(nd):
            out.append(pltpu.VMEM((2,) * (nd - 1 - k) + (rows_of[a], ln), dtype))
    return out


SMALL_ROWS = 16
ROW_BQ, ROW_BV, ROW_BO, ROW_G1, ROW_S1, ROW_BD, ROW_G2, ROW_S2, ROW_BI = range(9)


def backward_kernel(grid, flat, n_bufs, tile_rows, *refs):
    it = iter(refs)
    take = lambda n: [next(it) for _ in range(n)]
    lens, dp, g1, g2 = take(4)
    n2, i2, slope, n1, i1, act, h1, o, q, k, v, p, x, hid = take(14)
    w_down, w_in, w_out, w_query, w_key, w_value = take(6)
    outs = take(6)
    small_out, hid_back, gx_back = take(3)
    dfeed, dinner, dbranch, dpre1, datt, dqkv, gx = take(7)
    grads = take(6)
    wd, wi, wo, wq, wk, wv = take(6)
    small, small_recv = take(2)
    own_sem, send_sem, recv_sem, ex_own, ex_send, ex_recv, w_sem, sm_send, sm_recv = take(9)
    bufs = take(n_bufs)

    b, sq = grid.here()
    nd, ns = grid.nd, grid.seq_size
    my = grid.digits(b, sq)
    partners = [grid.partner(b, sq, d) for d in range(nd)]
    others = [lax.rem(sq + j, ns) for j in range(1, ns)]
    red = Reducer(grid, flat, (b, sq), partners, my, grads, outs, own_sem, send_sem, recv_sem, bufs)
    rows, length, width = x.shape
    count = rows * length
    lt = length // ns
    tiles = length // tile_rows

    weight_loads = [
        pltpu.make_async_copy(src, dst, w_sem.at[i])
        for i, (src, dst) in enumerate(
            [(w_down, wd), (w_in, wi), (w_out, wo), (w_query, wq), (w_key, wk), (w_value, wv)]
        )
    ]
    for c in weight_loads:
        c.start()
    grid.greet(b, sq, partners, others)

    def exchange(e, src, dst, r):
        out = [
            pltpu.make_async_copy(
                src.at[r, pl.ds(pl.multiple_of(sq * lt, lt), lt)],
                dst.at[sq * rows + r],
                ex_own.at[e, r],
            )
        ]
        for j in range(1, ns):
            at = pl.ds(pl.multiple_of(others[j - 1] * lt, lt), lt)
            out.append(
                remote(
                    src.at[r, at],
                    dst.at[sq * rows + r],
                    ex_send.at[e, r, j - 1],
                    ex_recv.at[e, r, j - 1],
                    (b, others[j - 1]),
                )
            )
        return out

    for r in range(rows):
        for c in exchange(0, hid, hid_back, r):
            c.start()
    small[...] = jnp.zeros_like(small)

    def columns(u):
        return jnp.sum(u, axis=0, keepdims=True)

    def norm_back(g, n, inv):
        return inv * (
            g - jnp.mean(g, axis=-1, keepdims=True) - n * jnp.mean(g * n, axis=-1, keepdims=True)
        )

    groups = []
    for i, c in enumerate(flat):
        if c[3] == 0:
            groups.append([])
        groups[-1].append(i)
    early = len(groups) - 3

    def slot(s):
        for kk in range(nd, -1, -1):
            g, odd = divmod(s - 2 * kk, 2)
            if odd == 0 and 0 <= g < early:
                for i in groups[g]:
                    red.step(i, kk)

    used = [0]

    def hook(steps, active=True):
        if not active:
            return lambda: None
        base = used[0]
        used[0] += steps

        def run():
            now = pl.program_id(0)
            for c in range(steps):
                pl.when(now == c)(functools.partial(slot, base + c))

        return run

    weight_loads[0].wait()
    weight_loads[1].wait()
    weight_loads[2].wait()

    def feed_body(n2_t, i2_t, slope_t, n1_t, i1_t, dfeed_t, dinner_t, dbranch_t, dpre1_t, datt_t):
        t = pl.program_id(0)
        r = t // tiles
        seg = segment_of(lens, r, (tile_rows, 1), 0, (t % tiles) * tile_rows)
        place = jnp.where(seg < SEGS, r * SEGS + seg, -1)
        lane = lax.broadcasted_iota(jnp.int32, (tile_rows, 128), 1)
        members = (lane % 64 == place).astype(F32).astype(BF16)
        dh2 = dot(members, dp[...])
        m2 = n2_t[...].astype(F32)
        small[ROW_G2 : ROW_G2 + 1] += columns(dh2 * m2)
        small[ROW_S2 : ROW_S2 + 1] += columns(dh2)
        dpre2 = norm_back(dh2 * g2[...], m2, i2_t[:, :1])
        low = dpre2.astype(BF16)
        dfeed_t[...] = low
        small[ROW_BD : ROW_BD + 1] += columns(low.astype(F32))
        dh1 = dpre2
        for c, lo in enumerate(range(0, wi.shape[1], width)):
            sl = slice(lo, lo + width)
            din = (dot(low, wd[sl, :], 1, 1) * slope_t[:, sl].astype(F32)).astype(BF16)
            dinner_t[:, sl] = din
            small[ROW_BI + c : ROW_BI + c + 1] += columns(din.astype(F32))
            dh1 = dh1 + dot(din, wi[:, sl], 1, 1)
        m1 = n1_t[...].astype(F32)
        small[ROW_G1 : ROW_G1 + 1] += columns(dh1 * m1)
        small[ROW_S1 : ROW_S1 + 1] += columns(dh1)
        dp1 = norm_back(dh1 * g1[...], m1, i1_t[:, :1])
        dpre1_t[...] = dp1
        low = dp1.astype(BF16)
        dbranch_t[...] = low
        small[ROW_BO : ROW_BO + 1] += columns(low.astype(F32))
        datt_t[0] = dot(low, wo[...], 1, 1).astype(BF16)

    ff = wi.shape[1]
    tile = lambda w: pl.BlockSpec((tile_rows, w), lambda t: (t, 0))
    by_row = pl.BlockSpec((1, tile_rows, width), lambda t: (t // tiles, t % tiles, 0))
    pltpu.emit_pipeline(
        feed_body,
        grid=(count // tile_rows,),
        in_specs=[tile(width), tile(128), tile(ff), tile(width), tile(128)],
        out_specs=[tile(width), tile(ff), tile(width), tile(width), by_row],
    )(n2, i2, slope, n1, i1, dfeed, dinner, dbranch, dpre1, datt)

    dev = (2,) * nd
    zeros = (0,) * nd

    def outer_call(a, g, dst, steps, a_map, g_map, block, out_map, active=True):
        call_hook = hook(steps, active)

        def body(a_t, g_t, out_t):
            call_hook()
            lhs = a_t[...].reshape(count, width)
            rhs = g_t[...].reshape(count, width)
            out_t[...] = dot(lhs, rhs, 0, 0).reshape(block).astype(BF16)

        whole = lambda ref: (
            (count, width) if len(ref.shape) == 2 else (1,) * (len(ref.shape) - 3) + (rows, length, width)
        )
        pltpu.emit_pipeline(
            body,
            grid=(steps,),
            in_specs=[pl.BlockSpec(whole(a), a_map), pl.BlockSpec(whole(g), g_map)],
            out_specs=[pl.BlockSpec(block, out_map)],
        )(a, g, dst)

    grad_in, grad_down, grad_out, grad_q, grad_k, grad_v = grads
    square = dev + grad_out.shape[-2:]
    at0 = lambda c: (0, 0)
    chunks = ff // width
    outer_call(
        h1, dinner, grad_in, chunks, at0, lambda c: (0, c), square, lambda c: zeros + (0, c), False
    )
    down_rows = grad_down.shape[-2]
    per = width // down_rows
    low_digits = per.bit_length() - 1
    top = nd - low_digits
    outer_call(
        act,
        dfeed,
        grad_down,
        chunks,
        lambda c: (0, c),
        at0,
        (1,) * top + (2,) * low_digits + (down_rows, width),
        lambda c: tuple((c // (1 << (top - 1 - e))) % 2 for e in range(top)) + (0,) * low_digits + (0, 0),
    )
    outer_call(o, dbranch, grad_out, 1, at0, at0, square, lambda c: zeros + (0, 0))

    for c in weight_loads[3:]:
        c.wait()
    lane = lax.broadcasted_iota(jnp.int32, (1, 128), 1)
    for r in range(rows):
        att_hook = hook(HEADS // 2)

        def att_body(q_t, k_t, v_t, do_t, p_t, out_t):
            att_hook()
            qp, kp, vp, dop = q_t[0], k_t[0], v_t[0], do_t[0]
            kt = kp.T
            zero = jnp.zeros_like(vp)
            dv = dk = None
            dqt = []
            for h in range(2):
                mine = lane // HEAD_DIM == h
                vm, dom, qm = (jnp.where(mine, u, zero) for u in (vp, dop, qp))
                pt = p_t[0, h]
                probs = pt.astype(F32)
                weighted = probs * dot(vm, dop, 1, 1)
                ds = (weighted - probs * jnp.sum(weighted, axis=0, keepdims=True)).astype(BF16)
                dv_h, dk_h = dot(pt, dom), dot(ds, qm)
                dv = dv_h if dv is None else dv + dv_h
                dk = dk_h if dk is None else dk + dk_h
                dqt.append(dot(kt[h * HEAD_DIM : (h + 1) * HEAD_DIM], ds) * HEAD_DIM ** (-0.5))
            out_t[0, 0] = jnp.concatenate(dqt, axis=0).T.astype(BF16)
            out_t[1, 0] = dk.astype(BF16)
            out_t[2, 0] = dv.astype(BF16)

        part = pl.BlockSpec((1, length, 128), lambda s, r=r: (r, 0, s))
        pltpu.emit_pipeline(
            att_body,
            grid=(HEADS // 2,),
            in_specs=[part] * 4 + [pl.BlockSpec((1, 2, length, length), lambda s, r=r: (r, s, 0, 0))],
            out_specs=[pl.BlockSpec((3, 1, length, 128), lambda s, r=r: (0, r, 0, s))],
        )(q, k, v, datt, p, dqkv)

        in_hook = hook(tiles)

        def in_body(dpre1_t, d_t, out_t):
            in_hook()
            dq, dk, dv = d_t[0, 0], d_t[1, 0], d_t[2, 0]
            small[ROW_BQ : ROW_BQ + 1] += columns(dq.astype(F32))
            small[ROW_BV : ROW_BV + 1] += columns(dv.astype(F32))
            total = dpre1_t[...] + dot(dq, wq[...], 1, 1) + dot(dk, wk[...], 1, 1)
            out_t[0] = (total + dot(dv, wv[...], 1, 1)).astype(BF16)

        pltpu.emit_pipeline(
            in_body,
            grid=(tiles,),
            in_specs=[
                pl.BlockSpec((tile_rows, width), lambda t, r=r: (r * tiles + t, 0)),
                pl.BlockSpec((3, 1, tile_rows, width), lambda t, r=r: (0, r, t, 0)),
            ],
            out_specs=[pl.BlockSpec((1, tile_rows, width), lambda t, r=r: (r, t, 0))],
        )(dpre1, dqkv, gx)
        for c in exchange(1, gx, gx_back, r):
            c.start()

    def small_copy(kk):
        return remote(
            small, small_recv.at[kk], sm_send.at[kk], sm_recv.at[kk], partners[order[kk]]
        )

    order = grid.order(0)[::-1]

    def small_step(kk):
        if kk > 0:
            c = small_copy(kk - 1)
            c.wait()
            small[...] += small_recv[kk - 1]
        if kk < nd:
            small_copy(kk).start()

    small_step(0)
    for j, (d, dst) in enumerate(((0, grad_q), (1, grad_k), (2, grad_v))):
        outer_call(
            x, dqkv, dst, 1, lambda c: (0, 0, 0), lambda c, d=d: (d, 0, 0, 0), square,
            lambda c: zeros + (0, 0),
        )
        if j > 0:
            for i in groups[early + j - 1]:
                red.step(i, 1)
        small_step(j + 1)
        for i in groups[early + j]:
            red.step(i, 0)
    s = used[0]
    while s <= 2 * (early - 1) + 2 * nd:
        slot(s)
        s += 1
    for t in range(2, 3 + nd):
        for kk in range(nd, 0, -1):
            g = t - kk
            if 0 <= g < 3 and not (kk == 1 and g < 2):
                for i in groups[early + g]:
                    red.step(i, kk)
        if 4 <= t + 1 <= nd:
            small_step(t + 1)
    small_out[...] = small[...]
    red.finish()
    for r in range(rows):
        for e, (src, dst) in enumerate(((hid, hid_back), (gx, gx_back))):
            for c in exchange(e, src, dst, r):
                c.wait()


def backward(grid, lens, dp, g1, g2, kept, weights, tile_rows, collective_id):
    nd, ns = grid.nd, grid.seq_size
    x, hid = kept[-2:]
    rows, length, width = x.shape
    count = rows * length
    w_down, w_in = weights[0], weights[1]
    ff = w_in.shape[1]
    dev = (2,) * nd
    part, down_part = width >> nd, ff >> nd
    shapes = [(part, ff), (down_part, width)] + [(part, width)] * 4
    flat = [c for g in pieces(shapes) for c in g]
    rows_of = [s[0] for s in shapes]
    bufs = reducer_scratch(nd, flat, rows_of, BF16)
    back = struct((rows * ns, length // ns, width), BF16)
    low = struct((count, width), BF16)
    out_shape = [struct(s, F32) for s in shapes]
    out_shape += [struct((SMALL_ROWS, width), F32), back, back]
    out_shape += [low, struct((count, ff), BF16), low, struct((count, width), F32)]
    out_shape += [struct((rows, length, width), BF16), struct((3, rows, length, width), BF16)]
    out_shape += [struct((rows, length, width), BF16)]
    out_shape += [struct(dev + s, BF16) for s in shapes]
    n = len(flat)
    res = pl.pallas_call(
        functools.partial(backward_kernel, grid, flat, len(bufs), tile_rows),
        out_shape=out_shape,
        in_specs=[SMEM, VMEM, VMEM, VMEM] + [ANY] * (len(kept) + len(weights)),
        out_specs=[VMEM] * 7 + [ANY] * (len(out_shape) - 7),
        scratch_shapes=[pltpu.VMEM(w.shape, BF16) for w in weights]
        + [pltpu.VMEM((SMALL_ROWS, width), F32), pltpu.VMEM((nd, SMALL_ROWS, width), F32)]
        + [DMA((n,)), DMA((n, nd)), DMA((n, nd))]
        + [DMA((2, rows)), DMA((2, rows, ns - 1)), DMA((2, rows, ns - 1))]
        + [DMA((len(weights),)), DMA((nd,)), DMA((nd,))]
        + bufs,
        compiler_params=pltpu.CompilerParams(
            collective_id=collective_id, has_side_effects=True, vmem_limit_bytes=VMEM_LIMIT
        ),
    )(lens, dp, g1, g2, *kept, *weights)
    return res[:10]


def pack_small(vectors, wide, extra):
    rows = [jnp.pad(v.astype(F32), (0, 128 - v.shape[0])) for v in (*vectors, wide, extra)]
    rows += [jnp.zeros((128,), F32)] * (16 - len(rows))
    return jnp.stack(rows)


def per_device(
    tokens, lengths, pair_ids, w_query, b_query, w_key, w_value, b_value, w_out, b_out,
    norm1_gain, norm1_bias, w_in, b_in, w_down, b_down, norm2_gain, norm2_bias,
):
    blk_size, seq_size = lax.axis_size("blk"), lax.axis_size("seq")
    grid = Grid(blk_size, seq_size)
    devices = blk_size * seq_size
    group_rows, local_len, width = tokens.shape
    rows = group_rows // seq_size
    length = local_len * seq_size
    count = rows * length
    ff = w_in.shape[1]
    part, wide_part, pairs = b_query.shape[0], b_in.shape[0], pair_ids.shape[0]

    lens = lax.dynamic_slice_in_dim(lengths, lax.axis_index("seq") * rows, rows, 0)
    vectors = (b_query, b_value, b_out, norm1_gain, norm1_bias, b_down, norm2_gain, norm2_bias)
    small = pack_small(vectors, b_in, pair_ids)
    full, x = gather_all(grid, (w_query, w_key, w_value, small, w_out, w_in, w_down), tokens, 1)
    wq, wk, wv, smalls, wo, wi, wd = full
    smalls = smalls.reshape(devices, 16, 128)
    vecs = smalls[:, : len(vectors), :part].transpose(1, 0, 2).reshape(len(vectors), 1, width)
    bq, bv, bo, g1, s1, bd, g2, s2 = (vecs[i] for i in range(len(vectors)))
    bi = smalls[:, len(vectors), :wide_part].reshape(1, ff)
    all_pairs = smalls[:, len(vectors) + 1, :pairs].reshape(-1, NQ).astype(jnp.int32)

    q, k, v, p, o = attention(lens, x, wq, wk, wv, bq, bv)
    x2, o2 = x.reshape(count, width), o.reshape(count, width)
    hid, n1, i1, h1, act, slope, n2, i2, pool = feed(
        lens, x2, o2, wo, bo, g1, s1, wi, bi, wd, bd, g2, s2, 256
    )

    none = jnp.full((all_pairs.shape[0], SEGS - NQ), -1, jnp.int32)
    pair_row = jnp.concatenate([all_pairs, none], axis=1).reshape(1, -1)
    own_pairs = jnp.concatenate([pair_ids.reshape(rows, NQ), none[:rows]], axis=1).reshape(-1, 1)
    pair_col = jnp.broadcast_to(own_pairs, (rows * SEGS, 128))
    len_col = jnp.broadcast_to(lens.reshape(-1, 1).astype(F32), (rows * SEGS, 128))
    losses, dpool = contrast(grid, pool, len_col, pair_col, pair_row, 2)
    query_loss = losses[:, 0].reshape(rows, SEGS)[:, :NQ].reshape(-1)

    if part % 8 == 0:
        kept = (n2, i2, slope, n1, i1, act, h1, o2, q, k, v, p, x, hid.reshape(rows, length, width))
        res = backward(grid, lens, dpool, g1, g2, kept, (wd, wi, wo, wq, wk, wv), 256, 3)
        g_in, g_down, g_out, g_query, g_key, g_value, sums, hidden_out, grad_tokens = res[:9]
        me = lax.axis_index("blk") * seq_size + lax.axis_index("seq")
        own = lax.dynamic_slice_in_dim(sums[:8], me * part, part, 1)
        gv = [own[i] for i in range(8)]
        g_wide = lax.dynamic_slice_in_dim(
            sums[ROW_BI : ROW_BI + ff // width].reshape(ff), me * wide_part, wide_part, 0
        )
        return (
            hidden_out, query_loss, grad_tokens.astype(F32), g_query, gv[0], g_key, g_value, gv[1],
            g_out, gv[2], gv[3], gv[4], g_in, g_wide, g_down, gv[5], gv[6], gv[7],
        )

    dfeed, dinner, dbranch, dpre1, datt, sums, wide_sums = feed_back(
        lens, dpool, n2, i2, slope, n1, i1, wd, wi, wo, g2, g1, 256
    )
    grad_w_down = outer(act, dfeed, width, width)
    grad_w_in = outer(h1, dinner, width, width)
    grad_w_out = outer(o2, dbranch, width, width)
    dq, dk, dv = attention_back(q, k, v, p, datt.reshape(rows, length, width))
    dq, dk, dv = (d.reshape(count, width) for d in (dq, dk, dv))
    grad_x, sums_in = input_back(dpre1, dq, dk, dv, wq, wk, wv, 256)
    grad_w_query = outer(x2, dq, width, width)
    grad_w_key = outer(x2, dk, width, width)
    grad_w_value = outer(x2, dv, width, width)

    vec_grads = jnp.stack(
        [sums_in[0], sums_in[1], sums[5], sums[3], sums[4], sums[2], sums[0], sums[1]]
    )
    packed = jnp.pad(
        vec_grads.reshape(8, devices, part).transpose(1, 0, 2), ((0, 0), (0, 0), (0, 128 - part))
    )
    wide_grads = jnp.pad(
        wide_sums[0].reshape(devices, 1, wide_part), ((0, 0), (0, 7), (0, 128 - wide_part))
    )
    packed = jnp.concatenate([packed, wide_grads], axis=1).reshape(devices * 16, 128)
    grads, back = scatter_all(
        grid,
        (grad_w_down, grad_w_in, grad_w_out, packed, grad_w_query, grad_w_key, grad_w_value),
        (hid.reshape(rows, length, width), grad_x.reshape(rows, length, width)),
        3,
    )
    g_down, g_in, g_out, g_small, g_query, g_key, g_value = grads
    hidden_out, grad_tokens = back
    gv = [g_small[i, :part] for i in range(8)]
    return (
        hidden_out,
        query_loss,
        grad_tokens.astype(F32),
        g_query,
        gv[0],
        g_key,
        g_value,
        gv[1],
        g_out,
        gv[2],
        gv[3],
        gv[4],
        g_in,
        g_small[8, :wide_part],
        g_down,
        gv[5],
        gv[6],
        gv[7],
    )


def solution(mesh):
    both = ("blk", "seq")
    vec, mat, tok = P(both), P(both, None), P("blk", "seq", None)
    in_specs = (
        tok, P("blk", None), vec, mat, vec, mat, mat, vec, mat, vec, vec, vec, mat, vec, mat, vec,
        vec, vec,
    )
    out_specs = (
        tok, vec, tok, mat, vec, mat, mat, vec, mat, vec, vec, vec, mat, vec, mat, vec, vec, vec,
    )
    return jax.shard_map(
        per_device, mesh=mesh, in_specs=in_specs, out_specs=out_specs, check_vma=False
    )
```

```python
import functools

import jax
import jax.numpy as jnp
from jax import lax
from jax.experimental import pallas as pl
from jax.experimental.pallas import tpu as pltpu
from jax.sharding import PartitionSpec as P

HEADS = 12
HEAD_DIM = 64
NQ = 2
SEGS = 4
TEMPERATURE = 0.05
NORM_EPSILON = 1e-06
MASKED = -1000000000.0
BF16 = jnp.bfloat16
F32 = jnp.float32
MESH = pl.DeviceIdType.MESH
ANY = pl.BlockSpec(memory_space=pl.ANY)
VMEM = pl.BlockSpec(memory_space=pltpu.VMEM)
SMEM = pl.BlockSpec(memory_space=pltpu.SMEM)
DMA = pltpu.SemaphoreType.DMA
VMEM_LIMIT = 60 * 2**20


def dot(a, b, ca=1, cb=0):
    return lax.dot_general(a, b, (((ca,), (cb,)), ((), ())), preferred_element_type=F32)


def struct(shape, dtype):
    return jax.ShapeDtypeStruct(shape, dtype)


def split_two(v):
    high = v.astype(BF16)
    return high, (v - high.astype(F32)).astype(BF16)


class Grid:
    def __init__(self, blk_size, seq_size):
        self.blk_size, self.seq_size = blk_size, seq_size
        self.kb = blk_size.bit_length() - 1
        self.ks = seq_size.bit_length() - 1
        assert 1 << self.kb == blk_size and 1 << self.ks == seq_size
        self.nd = self.kb + self.ks

    def here(self):
        return lax.axis_index("blk"), lax.axis_index("seq")

    def digit(self, b, q, d):
        if d < self.kb:
            w = 1 << (self.kb - 1 - d)
            return (b // w) % 2, w
        w = 1 << (self.nd - 1 - d)
        return (q // w) % 2, w

    def digits(self, b, q):
        return [self.digit(b, q, d)[0] for d in range(self.nd)]

    def partner(self, b, q, d):
        v, w = self.digit(b, q, d)
        if d < self.kb:
            return (b + (1 - 2 * v) * w, q)
        return (b, q + (1 - 2 * v) * w)

    def order(self, flavour):
        seq = list(range(self.kb, self.nd))
        head, last = list(range(self.kb))[:-1][::-1], [self.kb - 1]
        if head:
            r = flavour % len(head)
            head = head[r:] + head[:r]
        return seq + head + last

    def greet(self, b, q, partners, others):
        barrier = pltpu.get_barrier_semaphore()
        targets = [partners[d] for d in range(self.kb)]
        if others is None:
            targets += [partners[d] for d in range(self.kb, self.nd)]
        else:
            targets += [(b, o) for o in others]
        for t in targets:
            pl.semaphore_signal(barrier, inc=1, device_id=t, device_id_type=MESH)
        pl.semaphore_wait(barrier, len(targets))


def remote(src, dst, send, recv, where):
    return pltpu.make_async_remote_copy(
        src_ref=src, dst_ref=dst, send_sem=send, recv_sem=recv, device_id=where, device_id_type=MESH
    )


def flat_view(rows, lanes):
    if rows % 8 == 0:
        return rows, lanes
    return rows * lanes // 128, 128


def pieces(shapes):
    out = []
    for a, (rows, lanes) in enumerate(shapes):
        unit = 768 if rows < 64 else 256
        unit = min(unit, lanes)
        for lo in range(0, lanes, unit):
            half = unit // 2
            if half % 128 == 0:
                out.append([(a, lo, half, 0), (a, lo + half, half, 1)])
            else:
                out.append([(a, lo, unit, 0)])
    return out


def gather_kernel(grid, groups, n, lag, *refs):
    ins, tok = refs[:n], refs[n]
    outs, rows_out = refs[n + 1 : 2 * n + 1], refs[2 * n + 1]
    own_sem, send_sem, recv_sem, tok_own, tok_send, tok_recv = refs[2 * n + 2 :]
    b, q = grid.here()
    nd, ns = grid.nd, grid.seq_size
    my = grid.digits(b, q)
    partners = [grid.partner(b, q, d) for d in range(nd)]
    others = [lax.rem(q + j, ns) for j in range(1, ns)]
    grid.greet(b, q, partners, others)
    flat = [c for g in groups for c in g]
    where = {}
    first = 0
    for gi, g in enumerate(groups):
        where[gi] = list(range(first, first + len(g)))
        first += len(g)

    own = []
    for i, (a, lo, ln, _) in enumerate(flat):
        c = pltpu.make_async_copy(
            ins[a].at[:, pl.ds(lo, ln)],
            outs[a].at[tuple(my) + (slice(None), pl.ds(lo, ln))],
            own_sem.at[i],
        )
        c.start()
        own.append(c)
    copies = {}

    def stage(i, k):
        a, lo, ln, flavour = flat[i]
        order = grid.order(flavour)
        d = order[k]
        if k == 0:
            src = ins[a].at[:, pl.ds(lo, ln)]
            dst = outs[a].at[tuple(my) + (slice(None), pl.ds(lo, ln))]
        else:
            if k == 1:
                own[i].wait()
            copies[(i, k - 1)].wait_recv()
            done = order[:k]
            ix = tuple(slice(None) if e in done else my[e] for e in range(nd))
            ix = ix + (slice(None), pl.ds(lo, ln))
            src, dst = outs[a].at[ix], outs[a].at[ix]
        c = remote(src, dst, send_sem.at[i, k], recv_sem.at[i, k], partners[d])
        c.start()
        copies[(i, k)] = c

    row_copies = []
    total, lt, _ = tok.shape
    per = total // ns

    def send_rows():
        at = pl.ds(pl.multiple_of(q * lt, lt), lt)
        for r in range(per):
            c = pltpu.make_async_copy(tok.at[q * per + r], rows_out.at[r, at], tok_own.at[r])
            c.start()
            row_copies.append(c)
            for j in range(1, ns):
                o = others[j - 1]
                c = remote(
                    tok.at[o * per + r],
                    rows_out.at[r, at],
                    tok_send.at[j - 1, r],
                    tok_recv.at[j - 1, r],
                    (b, o),
                )
                c.start()
                row_copies.append(c)

    ng = len(groups)
    for t in range(ng + lag * (nd - 1)):
        for k in range(nd - 1, -1, -1):
            g = t - lag * k
            if 0 <= g < ng:
                for i in where[g]:
                    stage(i, k)
        if t == 2:
            send_rows()
    for i in range(len(flat)):
        copies[(i, nd - 1)].wait_recv()
    for i in range(len(flat)):
        for k in range(nd):
            copies[(i, k)].wait_send()
    for c in row_copies:
        c.wait()


def gather_all(grid, blocks, tokens, collective_id):
    nd, ns = grid.nd, grid.seq_size
    n = len(blocks)
    views = [x.reshape(flat_view(*x.shape)) for x in blocks]
    groups = pieces([v.shape for v in views])
    count = sum(len(g) for g in groups)
    total, lt, width = tokens.shape
    per = total // ns
    outs = [struct((2,) * nd + v.shape, v.dtype) for v in views]
    outs.append(struct((per, lt * ns, width), tokens.dtype))
    res = pl.pallas_call(
        functools.partial(gather_kernel, grid, groups, n, 2),
        out_shape=outs,
        in_specs=[VMEM] * (n + 1),
        out_specs=[ANY] * (n + 1),
        scratch_shapes=[
            DMA((count,)),
            DMA((count, nd)),
            DMA((count, nd)),
            DMA((per,)),
            DMA((ns - 1, per)),
            DMA((ns - 1, per)),
        ],
        compiler_params=pltpu.CompilerParams(
            collective_id=collective_id, has_side_effects=True, vmem_limit_bytes=VMEM_LIMIT
        ),
    )(*views, tokens)
    devices = 1 << nd
    full = [
        r.reshape((devices * x.shape[0], x.shape[1])) for r, x in zip(res[:-1], blocks, strict=True)
    ]
    return full, res[-1]


def reduce_plan(grid, flavour):
    free = list(range(grid.nd))
    plan = []
    for d in grid.order(flavour)[::-1]:
        pos = free.index(d)
        plan.append((d, 1 << pos, 1 << (len(free) - pos - 1)))
        free.remove(d)
    return plan


def scatter_kernel(grid, flat, n, nx, lag, *refs):
    nd, ns = grid.nd, grid.seq_size
    ins, rows_in = refs[:n], refs[n : n + nx]
    outs, rows_out = refs[n + nx : 2 * n + nx], refs[2 * n + nx : 2 * n + 2 * nx]
    rest = list(refs[2 * n + 2 * nx :])
    own_sem, send_sem, recv_sem, x_own, x_send, x_recv = rest[:6]
    bufs = rest[6:]
    b, q = grid.here()
    my = grid.digits(b, q)
    partners = [grid.partner(b, q, d) for d in range(nd)]
    others = [lax.rem(q + j, ns) for j in range(1, ns)]
    grid.greet(b, q, partners, others)

    row_copies = []
    for x in range(nx):
        per, length, _ = rows_in[x].shape
        lt = length // ns
        for r in range(per):
            at = pl.ds(pl.multiple_of(q * lt, lt), lt)
            c = pltpu.make_async_copy(
                rows_in[x].at[r, at], rows_out[x].at[q * per + r], x_own.at[x, r]
            )
            c.start()
            row_copies.append(c)

    def send_rows(x):
        per, length, _ = rows_in[x].shape
        lt = length // ns
        for r in range(per):
            for j in range(1, ns):
                o = others[j - 1]
                c = remote(
                    rows_in[x].at[r, pl.ds(pl.multiple_of(o * lt, lt), lt)],
                    rows_out[x].at[q * per + r],
                    x_send.at[x, j - 1, r],
                    x_recv.at[x, j - 1, r],
                    (b, o),
                )
                c.start()
                row_copies.append(c)

    per_piece = 1 + 2 * nd - 1
    copies, own = {}, {}

    def buffers(i):
        mine = bufs[i * per_piece : (i + 1) * per_piece]
        return mine[0], mine[1 : 1 + nd], mine[1 + nd :]

    for i, (a, lo, ln, flavour) in enumerate(flat):
        d = reduce_plan(grid, flavour)[0][0]
        ix = tuple(my[e] if e == d else slice(None) for e in range(nd)) + (slice(None), pl.ds(lo, ln))
        c = pltpu.make_async_copy(ins[a].at[ix], buffers(i)[0], own_sem.at[i])
        c.start()
        own[i] = c

    def send(i, k):
        a, lo, ln, flavour = flat[i]
        d, pre, post = reduce_plan(grid, flavour)[k]
        start, recv, acc = buffers(i)
        if k == 0:
            ix = tuple((1 - my[e]) if e == d else slice(None) for e in range(nd))
            src = ins[a].at[ix + (slice(None), pl.ds(lo, ln))]
        else:
            src = acc[k - 1].at[:, 1 - my[d]]
        c = remote(src, recv[k], send_sem.at[i, k], recv_sem.at[i, k], partners[d])
        c.start()
        copies[(i, k)] = c

    def add(i, k):
        a, lo, ln, flavour = flat[i]
        plan = reduce_plan(grid, flavour)
        d, pre, post = plan[k]
        start, recv, acc = buffers(i)
        copies[(i, k)].wait_recv()
        if k == 0:
            own[i].wait()
        if k == nd - 1:
            total = acc[k - 1][0, my[d], 0].astype(F32) + recv[k][0, 0].astype(F32)
            outs[a][:, lo : lo + ln] = total
            return
        _, pre2, post2 = plan[k + 1]

        def one(j, carry):
            if k == 0:
                ix = tuple((j // (1 << (nd - 2 - e))) % 2 for e in range(nd - 1))
                mine, other = start[ix], recv[0][ix]
            else:
                mine = acc[k - 1][j // post, my[d], j % post]
                other = recv[k][j // post, j % post]
            total = mine.astype(F32) + other.astype(F32)
            acc[k][j // (2 * post2), (j // post2) % 2, j % post2] = total.astype(acc[k].dtype)
            return carry

        lax.fori_loop(0, pre * post, one, 0)

    groups = sorted({c[4] for c in [(*f, gi) for f, gi in zip(flat, group_of(flat))]})
    members = {g: [i for i, gi in enumerate(group_of(flat)) if gi == g] for g in groups}
    ng = len(groups)
    for t in range(ng + lag * nd):
        for k in range(nd, -1, -1):
            g = t - lag * k
            if 0 <= g < ng:
                for i in members[g]:
                    if k > 0:
                        add(i, k - 1)
                    if k < nd:
                        send(i, k)
        if t == 0:
            for x in range(nx):
                send_rows(x)
    for i in range(len(flat)):
        for k in range(nd):
            copies[(i, k)].wait_send()
    for c in row_copies:
        c.wait()


def group_of(flat):
    ids, last = [], -1
    for _, _, _, flavour in flat:
        if flavour == 0:
            last += 1
        ids.append(last)
    return ids


def scatter_all(grid, grads, rows_back, collective_id):
    nd, ns = grid.nd, grid.seq_size
    devices = 1 << nd
    views, finals = [], []
    for g in grads:
        rows = g.shape[0] // devices
        finals.append((rows, g.shape[1]))
        views.append(g.reshape((2,) * nd + flat_view(rows, g.shape[1])))
    flat = [c for g in pieces([v.shape[-2:] for v in views]) for c in g]
    n, nx = len(views), len(rows_back)
    scratch = []
    for a, _, ln, flavour in flat:
        rows, dtype = views[a].shape[-2], views[a].dtype
        plan = reduce_plan(grid, flavour)
        scratch.append(pltpu.VMEM((2,) * (nd - 1) + (rows, ln), dtype))
        for k, (_, pre, post) in enumerate(plan):
            shape = (2,) * (nd - 1) if k == 0 else (pre, post)
            scratch.append(pltpu.VMEM(shape + (rows, ln), dtype))
        for _, pre, post in plan[1:]:
            scratch.append(pltpu.VMEM((pre, 2, post, rows, ln), dtype))
    outs = [struct(v.shape[-2:], F32) for v in views]
    for x in rows_back:
        per, length, width = x.shape
        outs.append(struct((per * ns, length // ns, width), x.dtype))
    per = rows_back[0].shape[0]
    count = len(flat)
    res = pl.pallas_call(
        functools.partial(scatter_kernel, grid, flat, n, nx, 2),
        out_shape=outs,
        in_specs=[ANY] * n + [ANY] * nx,
        out_specs=[VMEM] * n + [ANY] * nx,
        scratch_shapes=[
            DMA((count,)),
            DMA((count, nd)),
            DMA((count, nd)),
            DMA((nx, per)),
            DMA((nx, ns - 1, per)),
            DMA((nx, ns - 1, per)),
        ]
        + scratch,
        compiler_params=pltpu.CompilerParams(
            collective_id=collective_id, has_side_effects=True, vmem_limit_bytes=VMEM_LIMIT
        ),
    )(*views, *rows_back)
    return [r.reshape(s) for r, s in zip(res[:n], finals, strict=True)], res[n:]


def segment_of(lens, r, shape, axis, start=0):
    t = lax.broadcasted_iota(jnp.int32, shape, axis) + start
    end = lens[r, 0]
    seg = (t >= end).astype(jnp.int32)
    for k in range(1, SEGS):
        end = end + lens[r, k]
        seg = seg + (t >= end).astype(jnp.int32)
    return seg


def attention_kernel(
    lens, x_ref, wq, wk, wv, bq, bv, q_ref, k_ref, v_ref, p_ref, o_ref, vt_ref, ot_ref, bias_ref
):
    x = x_ref[0]
    length = x.shape[0]
    r = pl.program_id(0)
    seg_k = segment_of(lens, r, (length, 1), 0)
    seg_q = segment_of(lens, r, (1, length), 1)
    bias_ref[...] = jnp.where(seg_k == seg_q, 0.0, MASKED)
    q_ref[0] = ((dot(x, wq[...]) + bq[...]) * HEAD_DIM ** (-0.5)).astype(BF16)
    k_ref[0] = dot(x, wk[...]).astype(BF16)
    v = dot(x, wv[...]) + bv[...]
    v_ref[0] = v.astype(BF16)
    vt_ref[...] = v.T.astype(BF16)
    lane = lax.broadcasted_iota(jnp.int32, (1, 128), 1)

    def pair(p, carry):
        sl = pl.ds(pl.multiple_of(p * 128, 128), 128)
        qp, kp = q_ref[0, :, sl], k_ref[0, :, sl]
        for h in range(2):
            km = jnp.where(lane // HEAD_DIM == h, kp, jnp.zeros_like(kp))
            hs = pl.ds(pl.multiple_of(p * 128 + h * HEAD_DIM, HEAD_DIM), HEAD_DIM)
            s = dot(km, qp, 1, 1) + bias_ref[...]
            e = jnp.exp(s - jnp.max(s, axis=0, keepdims=True))
            pt = (e * (1.0 / jnp.sum(e, axis=0, keepdims=True))).astype(BF16)
            p_ref[0, p * 2 + h] = pt
            ot_ref[hs, :] = dot(vt_ref[hs, :], pt).astype(BF16)
        return carry

    lax.fori_loop(0, HEADS // 2, pair, 0)
    o_ref[0] = ot_ref[...].T


def attention(lens, x, wq, wk, wv, bq, bv):
    rows, length, width = x.shape
    row = lambda *s: pl.BlockSpec((1,) + s, lambda r: (r,) + (0,) * len(s))
    full = lambda *s: pl.BlockSpec(s, lambda r: (0,) * len(s))
    tokens = struct((rows, length, width), BF16)
    return pl.pallas_call(
        attention_kernel,
        grid=(rows,),
        out_shape=[tokens] * 3 + [struct((rows, HEADS, length, length), BF16), tokens],
        in_specs=[SMEM, row(length, width)] + [full(width, width)] * 3 + [full(1, width)] * 2,
        out_specs=[row(length, width)] * 3 + [row(HEADS, length, length), row(length, width)],
        scratch_shapes=[
            pltpu.VMEM((width, length), BF16),
            pltpu.VMEM((width, length), BF16),
            pltpu.VMEM((length, length), F32),
        ],
        compiler_params=pltpu.CompilerParams(vmem_limit_bytes=VMEM_LIMIT),
    )(lens, x, wq, wk, wv, bq, bv)


def layer_norm(v):
    c = v - jnp.mean(v, axis=-1, keepdims=True)
    inv = lax.rsqrt(jnp.mean(c * c, axis=-1, keepdims=True) + NORM_EPSILON)
    return c * inv, inv


def feed_kernel(
    tiles, lens, x_ref, o_ref, wo, bo, g1, s1, wi, bi, wd, bd, g2, s2,
    hid_ref, n1_ref, i1_ref, h1_ref, act_ref, slope_ref, n2_ref, i2_ref, pool_ref,
):
    t = pl.program_id(0)
    rows = x_ref.shape[0]
    pre1 = x_ref[...].astype(F32) + dot(o_ref[...], wo[...]) + bo[...]
    n1, i1 = layer_norm(pre1)
    h1 = n1 * g1[...] + s1[...]
    h1_low = h1.astype(BF16)
    n1_ref[...] = n1.astype(BF16)
    h1_ref[...] = h1_low
    i1_ref[...] = jnp.broadcast_to(i1, i1_ref.shape)
    acc = h1 + bd[...]
    chunk = wd.shape[1]
    for lo in range(0, wi.shape[1], chunk):
        sl = slice(lo, lo + chunk)
        inner = dot(h1_low, wi[:, sl]) + bi[:, sl]
        phi = 0.5 + 0.5 * lax.erf(inner * (0.5**0.5))
        act = (inner * phi).astype(BF16)
        act_ref[:, sl] = act
        density = jnp.exp(-0.5 * inner * inner) * 0.3989422804014327
        slope_ref[:, sl] = (phi + inner * density).astype(BF16)
        acc = acc + dot(act, wd[sl, :])
    n2, i2 = layer_norm(acc)
    h2 = n2 * g2[...] + s2[...]
    high, low = split_two(h2)
    hid_ref[...] = high
    n2_ref[...] = n2.astype(BF16)
    i2_ref[...] = jnp.broadcast_to(i2, i2_ref.shape)
    r = t // tiles
    seg = segment_of(lens, r, (1, rows), 1, (t % tiles) * rows)
    slot = jnp.where(seg < SEGS, r * SEGS + seg, -1)
    members = lax.broadcasted_iota(jnp.int32, (pool_ref.shape[0], rows), 0) == slot
    members = members.astype(F32).astype(BF16)
    part = dot(members, high) + dot(members, low)

    @pl.when(t == 0)
    def _():
        pool_ref[...] = part

    @pl.when(t != 0)
    def _():
        pool_ref[...] += part


def feed(lens, x, o, wo, bo, g1, s1, wi, bi, wd, bd, g2, s2, tile_rows):
    count, width = x.shape
    rows = lens.shape[0]
    ff = wi.shape[1]
    tiles = count // rows // tile_rows
    tile = lambda w: pl.BlockSpec((tile_rows, w), lambda t: (t, 0))
    full = lambda *s: pl.BlockSpec(s, lambda t: (0,) * len(s))
    vec = full(1, width)
    low, col = struct((count, width), BF16), struct((count, 128), F32)
    wide = struct((count, ff), BF16)
    return pl.pallas_call(
        functools.partial(feed_kernel, tiles),
        grid=(count // tile_rows,),
        out_shape=[low, low, col, low, wide, wide, low, col, struct((rows * SEGS, width), F32)],
        in_specs=[SMEM, tile(width), tile(width), full(width, width), vec, vec, vec]
        + [full(width, ff), full(1, ff), full(ff, width), vec, vec, vec],
        out_specs=[tile(width), tile(width), tile(128), tile(width), tile(ff), tile(ff)]
        + [tile(width), tile(128), full(rows * SEGS, width)],
        compiler_params=pltpu.CompilerParams(vmem_limit_bytes=VMEM_LIMIT),
    )(lens, x, o, wo, bo, g1, s1, wi, bi, wd, bd, g2, s2)


def contrast_kernel(grid, pool_ref, len_ref, pair_ref, pairs_ref, loss_ref, dpool_ref, emb, send_sem, recv_sem):
    nd = grid.nd
    b, q = grid.here()
    my = grid.digits(b, q)
    partners = [grid.partner(b, q, d) for d in range(nd)]
    own_rows, width = pool_ref.shape
    count = own_rows << nd
    avg = pool_ref[...] / len_ref[:, :1]
    inv = lax.rsqrt(jnp.sum(avg * avg, axis=-1, keepdims=True) + NORM_EPSILON)
    own = avg * inv
    emb[tuple(my)] = own
    grid.greet(b, q, partners, None)
    order = grid.order(0)
    for k, d in enumerate(order):
        ix = tuple(slice(None) if e in order[:k] else my[e] for e in range(nd))
        c = remote(emb.at[ix], emb.at[ix], send_sem.at[k], recv_sem.at[k], partners[d])
        c.start()
        c.wait()
    high, low = split_two(emb[...].reshape(count, width))
    own_high, own_low = split_two(own)
    scale = 1.0 / TEMPERATURE

    def product(ah, al, bh, bl, cb):
        return dot(ah, bh, 1, cb) + dot(ah, bl, 1, cb) + dot(al, bh, 1, cb)

    total = jnp.zeros((1, count), F32)
    step = min(count, 256)
    for lo in range(0, count, step):
        sim = product(high[lo : lo + step], low[lo : lo + step], high, low, 1) * scale
        at = lax.broadcasted_iota(jnp.int32, (step, 1), 0)
        total += jnp.sum(jnp.where(at % SEGS >= NQ, jnp.exp(sim - scale), 0.0), axis=0, keepdims=True)
    lse_cols = scale + jnp.log(total)
    sim = product(own_high, own_low, high, low, 1) * scale
    col = lax.broadcasted_iota(jnp.int32, (1, count), 1)
    row = lax.broadcasted_iota(jnp.int32, (own_rows, 1), 0) + (b * grid.seq_size + q) * own_rows
    col_doc, row_doc = col % SEGS >= NQ, row % SEGS >= NQ
    number = lambda at: (at // SEGS) * NQ + at % SEGS - NQ
    lse_rows = scale + jnp.log(
        jnp.sum(jnp.where(col_doc, jnp.exp(sim - scale), 0.0), axis=1, keepdims=True)
    )
    chosen = col_doc & (number(col) == pair_ref[:, :1])
    positive = jnp.sum(jnp.where(chosen, sim, 0.0), axis=1, keepdims=True)
    loss_ref[...] = jnp.broadcast_to(lse_rows - positive, loss_ref.shape)
    as_query = jnp.exp(sim - lse_rows) - chosen.astype(F32)
    chosen_by = number(row) == pairs_ref[:1]
    as_doc = jnp.exp(jnp.where(col_doc, MASKED, sim - lse_cols)) - chosen_by.astype(F32)
    grad = jnp.where(row_doc, jnp.where(col_doc, 0.0, as_doc), jnp.where(col_doc, as_query, 0.0))
    grad_high, grad_low = split_two(grad)
    demb = product(grad_high, grad_low, high, low, 0) * scale
    dpool = inv * demb - inv * inv * inv * avg * jnp.sum(avg * demb, axis=-1, keepdims=True)
    dpool_high, dpool_low = split_two(dpool / len_ref[:, :1])
    pad = jnp.zeros((64 - own_rows, width), F32)
    stacked = jnp.concatenate([dpool_high.astype(F32), pad, dpool_low.astype(F32), pad], axis=0)
    dpool_ref[...] = stacked.astype(BF16)


def contrast(grid, pool, len_col, pair_col, pair_row, collective_id):
    own_rows, width = pool.shape
    return pl.pallas_call(
        functools.partial(contrast_kernel, grid),
        out_shape=[struct((own_rows, 128), F32), struct((128, width), BF16)],
        in_specs=[VMEM] * 4,
        out_specs=[VMEM] * 2,
        scratch_shapes=[
            pltpu.VMEM((2,) * grid.nd + (own_rows, width), F32),
            DMA((grid.nd,)),
            DMA((grid.nd,)),
        ],
        compiler_params=pltpu.CompilerParams(
            collective_id=collective_id, has_side_effects=True, vmem_limit_bytes=VMEM_LIMIT
        ),
    )(pool, len_col, pair_col, pair_row)


def feed_back_kernel(
    tiles, lens, dp_ref, n2_ref, i2_ref, slope_ref, n1_ref, i1_ref, wd, wi, wo, g2, g1,
    dfeed_ref, dinner_ref, dbranch_ref, dpre1_ref, datt_ref, sums_ref, wide_ref,
):
    t = pl.program_id(0)
    rows = n2_ref.shape[0]

    @pl.when(t == 0)
    def _():
        sums_ref[...] = jnp.zeros_like(sums_ref)
        wide_ref[...] = jnp.zeros_like(wide_ref)

    def columns(v):
        return jnp.sum(v, axis=0, keepdims=True)

    def norm_back(g, n, inv):
        return inv * (
            g - jnp.mean(g, axis=-1, keepdims=True) - n * jnp.mean(g * n, axis=-1, keepdims=True)
        )

    r = t // tiles
    seg = segment_of(lens, r, (rows, 1), 0, (t % tiles) * rows)
    slot = jnp.where(seg < SEGS, r * SEGS + seg, -1)
    lane = lax.broadcasted_iota(jnp.int32, (rows, 128), 1)
    members = (lane % 64 == slot).astype(F32).astype(BF16)
    dh2 = dot(members, dp_ref[...])
    n2 = n2_ref[...].astype(F32)
    sums_ref[0:1] += columns(dh2 * n2)
    sums_ref[1:2] += columns(dh2)
    dpre2 = norm_back(dh2 * g2[...], n2, i2_ref[:, :1])
    dfeed = dpre2.astype(BF16)
    dfeed_ref[...] = dfeed
    sums_ref[2:3] += columns(dfeed.astype(F32))
    chunk = wd.shape[1]
    dh1 = dpre2
    for lo in range(0, wi.shape[1], chunk):
        sl = slice(lo, lo + chunk)
        dinner = (dot(dfeed, wd[sl, :], 1, 1) * slope_ref[:, sl].astype(F32)).astype(BF16)
        dinner_ref[:, sl] = dinner
        wide_ref[0:1, sl] += columns(dinner.astype(F32))
        dh1 = dh1 + dot(dinner, wi[:, sl], 1, 1)
    n1 = n1_ref[...].astype(F32)
    sums_ref[3:4] += columns(dh1 * n1)
    sums_ref[4:5] += columns(dh1)
    dpre1 = norm_back(dh1 * g1[...], n1, i1_ref[:, :1])
    dpre1_ref[...] = dpre1
    dbranch = dpre1.astype(BF16)
    dbranch_ref[...] = dbranch
    sums_ref[5:6] += columns(dbranch.astype(F32))
    datt_ref[...] = dot(dbranch, wo[...], 1, 1).astype(BF16)


def feed_back(lens, dp, n2, i2, slope, n1, i1, wd, wi, wo, g2, g1, tile_rows):
    count, width = n2.shape
    rows = lens.shape[0]
    ff = wi.shape[1]
    tiles = count // rows // tile_rows
    tile = lambda w: pl.BlockSpec((tile_rows, w), lambda t: (t, 0))
    full = lambda *s: pl.BlockSpec(s, lambda t: (0,) * len(s))
    low = struct((count, width), BF16)
    return pl.pallas_call(
        functools.partial(feed_back_kernel, tiles),
        grid=(count // tile_rows,),
        out_shape=[low, struct((count, ff), BF16), low, struct((count, width), F32), low]
        + [struct((8, width), F32), struct((8, ff), F32)],
        in_specs=[SMEM, full(128, width), tile(width), tile(128), tile(ff), tile(width), tile(128)]
        + [full(ff, width), full(width, ff), full(width, width), full(1, width), full(1, width)],
        out_specs=[tile(width), tile(ff), tile(width), tile(width), tile(width)]
        + [full(8, width), full(8, ff)],
        compiler_params=pltpu.CompilerParams(vmem_limit_bytes=VMEM_LIMIT),
    )(lens, dp, n2, i2, slope, n1, i1, wd, wi, wo, g2, g1)


def outer_kernel(a_ref, b_ref, o_ref):
    o_ref[...] = dot(a_ref[...], b_ref[...], 0, 0).astype(o_ref.dtype)


def outer(a, b, bm, bn):
    count, m = a.shape
    n = b.shape[1]
    return pl.pallas_call(
        outer_kernel,
        grid=(m // bm, n // bn),
        out_shape=struct((m, n), BF16),
        in_specs=[
            pl.BlockSpec((count, bm), lambda i, j: (0, i)),
            pl.BlockSpec((count, bn), lambda i, j: (0, j)),
        ],
        out_specs=pl.BlockSpec((bm, bn), lambda i, j: (i, j)),
        compiler_params=pltpu.CompilerParams(vmem_limit_bytes=VMEM_LIMIT),
    )(a, b)


def attention_back_kernel(q_ref, k_ref, v_ref, p_ref, do_ref, dq_ref, dk_ref, dv_ref, kt_ref, dqt_ref):
    kt_ref[...] = k_ref[0].T
    lane = lax.broadcasted_iota(jnp.int32, (1, 128), 1)

    def pair(p, carry):
        sl = pl.ds(pl.multiple_of(p * 128, 128), 128)
        qp, vp, dop = q_ref[0, :, sl], v_ref[0, :, sl], do_ref[0, :, sl]
        zero = jnp.zeros_like(vp)
        dv = dk = None
        for h in range(2):
            mine = lane // HEAD_DIM == h
            vm, dom, qm = (jnp.where(mine, u, zero) for u in (vp, dop, qp))
            hs = pl.ds(pl.multiple_of(p * 128 + h * HEAD_DIM, HEAD_DIM), HEAD_DIM)
            pt = p_ref[0, p * 2 + h]
            probs = pt.astype(F32)
            weighted = probs * dot(vm, dop, 1, 1)
            ds = (weighted - probs * jnp.sum(weighted, axis=0, keepdims=True)).astype(BF16)
            dv_h, dk_h = dot(pt, dom), dot(ds, qm)
            dv = dv_h if dv is None else dv + dv_h
            dk = dk_h if dk is None else dk + dk_h
            dqt_ref[hs, :] = (dot(kt_ref[hs, :], ds) * HEAD_DIM ** (-0.5)).astype(BF16)
        dv_ref[0, :, sl] = dv.astype(BF16)
        dk_ref[0, :, sl] = dk.astype(BF16)
        return carry

    lax.fori_loop(0, HEADS // 2, pair, 0)
    dq_ref[0] = dqt_ref[...].T


def attention_back(q, k, v, p, do):
    rows, length, width = q.shape
    row = lambda *s: pl.BlockSpec((1,) + s, lambda r: (r,) + (0,) * len(s))
    return pl.pallas_call(
        attention_back_kernel,
        grid=(rows,),
        out_shape=[struct((rows, length, width), BF16)] * 3,
        in_specs=[row(length, width)] * 3 + [row(HEADS, length, length), row(length, width)],
        out_specs=[row(length, width)] * 3,
        scratch_shapes=[pltpu.VMEM((width, length), BF16), pltpu.VMEM((width, length), BF16)],
        compiler_params=pltpu.CompilerParams(vmem_limit_bytes=VMEM_LIMIT),
    )(q, k, v, p, do)


def input_back_kernel(dpre1_ref, dq_ref, dk_ref, dv_ref, wq, wk, wv, out_ref, sums_ref):
    @pl.when(pl.program_id(0) == 0)
    def _():
        sums_ref[...] = jnp.zeros_like(sums_ref)

    sums_ref[0:1] += jnp.sum(dq_ref[...].astype(F32), axis=0, keepdims=True)
    sums_ref[1:2] += jnp.sum(dv_ref[...].astype(F32), axis=0, keepdims=True)
    total = dpre1_ref[...] + dot(dq_ref[...], wq[...], 1, 1)
    total += dot(dk_ref[...], wk[...], 1, 1) + dot(dv_ref[...], wv[...], 1, 1)
    out_ref[...] = total.astype(out_ref.dtype)


def input_back(dpre1, dq, dk, dv, wq, wk, wv, tile_rows):
    count, width = dpre1.shape
    tile = pl.BlockSpec((tile_rows, width), lambda t: (t, 0))
    full = lambda *s: pl.BlockSpec(s, lambda t: (0,) * len(s))
    return pl.pallas_call(
        input_back_kernel,
        grid=(count // tile_rows,),
        out_shape=[struct((count, width), BF16), struct((8, width), F32)],
        in_specs=[tile] * 4 + [full(width, width)] * 3,
        out_specs=[tile, full(8, width)],
        compiler_params=pltpu.CompilerParams(vmem_limit_bytes=VMEM_LIMIT),
    )(dpre1, dq, dk, dv, wq, wk, wv)


class Gatherer:
    def __init__(self, grid, flat, partners, my, blocks, fulls, own_sem, send_sem, recv_sem):
        self.grid, self.flat, self.partners, self.my = grid, flat, partners, my
        self.blocks, self.fulls = blocks, fulls
        self.own_sem, self.send_sem, self.recv_sem = own_sem, send_sem, recv_sem

    def own(self, i):
        a, lo, ln, _ = self.flat[i]
        return pltpu.make_async_copy(
            self.blocks[a].at[:, pl.ds(lo, ln)],
            self.fulls[a].at[tuple(self.my) + (slice(None), pl.ds(lo, ln))],
            self.own_sem.at[i],
        )

    def copy(self, i, k):
        a, lo, ln, flavour = self.flat[i]
        order = self.grid.order(flavour)
        done = order[:k]
        ix = tuple(slice(None) if e in done else self.my[e] for e in range(self.grid.nd))
        dst = self.fulls[a].at[ix + (slice(None), pl.ds(lo, ln))]
        src = self.blocks[a].at[:, pl.ds(lo, ln)] if k == 0 else dst
        return remote(
            src, dst, self.send_sem.at[i, k], self.recv_sem.at[i, k], self.partners[order[k]]
        )

    def step(self, i, k):
        if k == 0:
            self.own(i).start()
        elif k == 1:
            self.own(i).wait()
        if k > 0:
            self.copy(i, k - 1).wait_recv()
        if k < self.grid.nd:
            self.copy(i, k).start()

    def finish(self):
        for i in range(len(self.flat)):
            for k in range(self.grid.nd):
                self.copy(i, k).wait_send()


def forward_kernel(grid, groups, tile_rows, *refs):
    it = iter(refs)
    take = lambda n: [next(it) for _ in range(n)]
    lens, tok = take(2)
    blocks = take(7)
    spread, owner, spread_wide, owner_wide = take(4)
    x_out, q_out, k_out, v_out, p_out, o_out = take(6)
    n1_out, i1_out, h1_out, act_out, slope_out, n2_out, i2_out, hid_out = take(8)
    full_out = take(7)
    pool, vecs = take(2)
    fulls = take(7)
    x_s, q_s, k_s, v_s, vt_s, mask_s, h_s, bi_s = take(8)
    own_sem, send_sem, recv_sem, tok_own, tok_send, tok_recv, out_sem = take(7)

    b, sq = grid.here()
    nd, ns = grid.nd, grid.seq_size
    my = grid.digits(b, sq)
    partners = [grid.partner(b, sq, d) for d in range(nd)]
    others = [lax.rem(sq + j, ns) for j in range(1, ns)]
    flat = [c for g in groups for c in g]
    members, first = [], 0
    for g in groups:
        members.append(range(first, first + len(g)))
        first += len(g)
    ga = Gatherer(grid, flat, partners, my, blocks, fulls, own_sem, send_sem, recv_sem)
    rows, length, width = x_s.shape
    lt = length // ns
    tiles = length // tile_rows
    grid.greet(b, sq, partners, others)

    def row_copy(r, j):
        at = pl.ds(pl.multiple_of(sq * lt, lt), lt)
        if j == 0:
            return pltpu.make_async_copy(tok.at[sq * rows + r], x_s.at[r, at], tok_own.at[r])
        o = others[j - 1]
        return remote(
            tok.at[o * rows + r], x_s.at[r, at], tok_send.at[r, j - 1], tok_recv.at[r, j - 1], (b, o)
        )

    plan = forward_plan(nd, len(groups), ns)

    def run_at(point):
        for g, k in plan.get(point, ()):
            if k < 0:
                row_copy(g, -k).start()
            else:
                for i in members[g]:
                    ga.step(i, k)

    def hook(name, steps):
        def run():
            now = pl.program_id(0)
            for c in range(steps):
                if (name, c) in plan:
                    pl.when(now == c)(functools.partial(run_at, (name, c)))

        return run

    def arrived(*which):
        for g in which:
            for i in members[g]:
                ga.step(i, nd)

    out_copies = []

    def put(src, dst):
        c = pltpu.make_async_copy(src, dst, out_sem.at[len(out_copies)])
        c.start()
        out_copies.append(c)

    for r in range(rows):
        row_copy(r, 0).start()
    run_at("start")
    arrived(0, 1, 2)
    part = blocks[1].shape[0]
    smalls = fulls[0][...].reshape(1 << nd, 16, 128)
    for i in range(8):
        a = dot(smalls[:, i, :].astype(BF16), spread[...]) * owner[...]
        vecs[i : i + 1] = jnp.sum(a, axis=0, keepdims=True)
    a = dot(smalls[:, 8, :].astype(BF16), spread_wide[...]) * owner_wide[...]
    bi_s[...] = jnp.sum(a, axis=0, keepdims=True)
    bq, bv, bo, g1, s1, bd, g2, s2 = (vecs[i : i + 1] for i in range(8))
    lane = lax.broadcasted_iota(jnp.int32, (1, 128), 1)

    def square(ref):
        return ref[...].reshape(width, width)

    for r in range(rows):
        run_at(("row", r))
        for j in range(ns):
            c = row_copy(r, j)
            if j == 0:
                c.wait()
            else:
                c.wait_recv()
        put(x_s.at[r], x_out.at[r])
        x = x_s[r]
        q_s[r] = ((dot(x, square(fulls[1])) + bq) * HEAD_DIM ** (-0.5)).astype(BF16)
        k_s[r] = dot(x, square(fulls[2])).astype(BF16)
        v = dot(x, square(fulls[3])) + bv
        v_s[r] = v.astype(BF16)
        vt_s[...] = v.T.astype(BF16)
        for src, dst in ((q_s, q_out), (k_s, k_out), (v_s, v_out)):
            put(src.at[r], dst.at[r])
        seg_k = segment_of(lens, r, (length, 1), 0)
        seg_q = segment_of(lens, r, (1, length), 1)
        mask_s[...] = jnp.where(seg_k == seg_q, 0.0, MASKED)
        att_hook = hook(("attention", r), HEADS // 2)

        def att_body(p_t, o_t, r=r):
            att_hook()
            p = pl.program_id(0)
            sl = pl.ds(pl.multiple_of(p * 128, 128), 128)
            qp, kp = q_s[r, :, sl], k_s[r, :, sl]
            out = []
            for h in range(2):
                km = jnp.where(lane // HEAD_DIM == h, kp, jnp.zeros_like(kp))
                hs = pl.ds(pl.multiple_of(p * 128 + h * HEAD_DIM, HEAD_DIM), HEAD_DIM)
                s = dot(km, qp, 1, 1) + mask_s[...]
                e = jnp.exp(s - jnp.max(s, axis=0, keepdims=True))
                pt = (e * (1.0 / jnp.sum(e, axis=0, keepdims=True))).astype(BF16)
                p_t[0, h] = pt
                out.append(dot(vt_s[hs, :], pt))
            o_t[0] = jnp.concatenate(out, axis=0).T.astype(BF16)

        pltpu.emit_pipeline(
            att_body,
            grid=(HEADS // 2,),
            out_specs=[
                pl.BlockSpec((1, 2, length, length), lambda s, r=r: (r, s, 0, 0)),
                pl.BlockSpec((1, length, 128), lambda s, r=r: (r, 0, s)),
            ],
        )(p_out, o_out)

    run_at("in")
    down_groups = width // 256
    arrived(*range(3, len(groups) - down_groups))
    for a in range(6):
        put(fulls[a], full_out[a])
    ff = bi_s.shape[1]
    tile = lambda w: pl.BlockSpec((tile_rows, w), lambda t: (t, 0))

    def tile_at():
        t = pl.program_id(0)
        start = lax.rem(t, tiles) * tile_rows
        return t // tiles, start, pl.ds(pl.multiple_of(start, tile_rows), tile_rows)

    in_hook = hook("in", rows * tiles)

    def in_body(o_t, n1_t, i1_t, h1_t, act_t, slope_t):
        in_hook()
        r, _, at = tile_at()
        pre1 = x_s[r, at].astype(F32) + dot(o_t[0], square(fulls[4])) + bo
        n1, i1 = layer_norm(pre1)
        h1 = n1 * g1 + s1
        low = h1.astype(BF16)
        h_s[r, at] = h1
        n1_t[...] = n1.astype(BF16)
        i1_t[...] = jnp.broadcast_to(i1, i1_t.shape)
        h1_t[...] = low
        for lo in range(0, ff, width):
            w = fulls[5][(slice(None),) * (nd + 1) + (slice(lo, lo + width),)]
            inner = dot(low, w.reshape(width, width)) + bi_s[:, lo : lo + width]
            phi = 0.5 + 0.5 * lax.erf(inner * (0.5**0.5))
            act_t[:, lo : lo + width] = (inner * phi).astype(BF16)
            density = jnp.exp(-0.5 * inner * inner) * 0.3989422804014327
            slope_t[:, lo : lo + width] = (phi + inner * density).astype(BF16)

    pltpu.emit_pipeline(
        in_body,
        grid=(rows * tiles,),
        in_specs=[pl.BlockSpec((1, tile_rows, width), lambda t: (t // tiles, t % tiles, 0))],
        out_specs=[tile(width), tile(128), tile(width), tile(ff), tile(ff)],
    )(o_out, n1_out, i1_out, h1_out, act_out, slope_out)

    run_at("down")
    arrived(*range(len(groups) - down_groups, len(groups)))
    put(fulls[6], full_out[6])
    pool[...] = jnp.zeros_like(pool)
    down_rows = blocks[6].shape[0]
    top = nd - ((width // down_rows).bit_length() - 1)

    def down_body(act_t, hid_t, n2_t, i2_t):
        r, start, at = tile_at()
        acc = h_s[r, at] + bd
        for c, lo in enumerate(range(0, ff, width)):
            ix = tuple((c >> (top - 1 - e)) % 2 for e in range(top))
            acc = acc + dot(act_t[:, lo : lo + width], fulls[6][ix].reshape(width, width))
        n2, i2 = layer_norm(acc)
        high, low = split_two(n2 * g2 + s2)
        hid_t[...] = high
        n2_t[...] = n2.astype(BF16)
        i2_t[...] = jnp.broadcast_to(i2, i2_t.shape)
        seg = segment_of(lens, r, (1, tile_rows), 1, start)
        slot = jnp.where(seg < SEGS, r * SEGS + seg, -1)
        mine = lax.broadcasted_iota(jnp.int32, (pool.shape[0], tile_rows), 0) == slot
        mine = mine.astype(F32).astype(BF16)
        pool[...] += dot(mine, high) + dot(mine, low)

    pltpu.emit_pipeline(
        down_body,
        grid=(rows * tiles,),
        in_specs=[tile(ff)],
        out_specs=[tile(width), tile(width), tile(128)],
    )(act_out, hid_out, n2_out, i2_out)

    ga.finish()
    for r in range(rows):
        for j in range(1, ns):
            row_copy(r, j).wait_send()
    for c in out_copies:
        c.wait()


FORWARD_PLAN = {
    "start": (
        (1, 0), (2, 0), (0, 0), (6, 0), (1, 1), (5, 0), (4, 0), (0, 1), (2, 1), (8, 0),
        (1, 2), (7, 0), (0, 2), (2, 2), (3, 0), (1, 3), (4, 1), (5, 1), (8, 1), (0, 3),
        (0, -2), (4, 2), (1, 4), (3, 1), (7, 1), (6, 1), (0, -3), (0, -1), (2, 3), (0, 4),
        (8, 2), (1, -1), (1, -3), (5, 2), (3, 2), (1, -2), (2, 4), (7, 2), (6, 2), (5, 3),
        (8, 3), (3, 3), (9, 0), (10, 0), (4, 3), (7, 3),
    ),
    (("attention", 0), 3): (
        (8, 4),
    ),
    ("row", 1): (
        (5, 4), (4, 4), (3, 4), (6, 3),
    ),
    (("attention", 1), 0): (
        (10, 1),
    ),
    (("attention", 1), 1): (
        (9, 1),
    ),
    (("attention", 1), 2): (
        (7, 4), (10, 2), (6, 4),
    ),
    (("attention", 1), 4): (
        (9, 2),
    ),
    (("attention", 1), 5): (
        (10, 3),
    ),
    ("in", 3): (
        (10, 4), (9, 4),
    ),
    "in": (
        (9, 3),
    ),
}
def forward_plan(nd, groups, ns):
    if nd == 5 and groups == 11 and ns == 4:
        return FORWARD_PLAN
    ops = []
    for t in range(groups + 2 * nd):
        ops += [(t - 2 * k, k) for k in range(nd - 1, -1, -1) if 0 <= t - 2 * k < groups]
        if t == nd:
            ops += [(r, -j) for r in range(2) for j in range(1, ns)]
    return {"start": tuple(ops)}


def forward(grid, lens, tokens, blocks, tile_rows, collective_id):
    nd, ns = grid.nd, grid.seq_size
    total, lt, width = tokens.shape
    rows, length = total // ns, lt * ns
    count = rows * length
    ff = blocks[5].shape[1]
    part, wide_part = width >> nd, ff >> nd
    dev = (2,) * nd
    groups = pieces([x.shape for x in blocks])
    groups = [groups[0] + groups[1]] + groups[2:]
    n = sum(len(g) for g in groups)
    lane, col = jnp.arange(128)[:, None], jnp.arange(width)[None, :]
    spread = (lane == col % part).astype(BF16)
    owner = (jnp.arange(1 << nd)[:, None] == col // part).astype(F32)
    col = jnp.arange(ff)[None, :]
    spread_wide = (lane == col % wide_part).astype(BF16)
    owner_wide = (jnp.arange(1 << nd)[:, None] == col // wide_part).astype(F32)
    seq3 = struct((rows, length, width), BF16)
    low, stat = struct((count, width), BF16), struct((count, 128), F32)
    wide = struct((count, ff), BF16)
    out_shape = [seq3] * 4 + [struct((rows, HEADS, length, length), BF16), seq3]
    out_shape += [low, stat, low, wide, wide, low, stat, low]
    out_shape += [struct(dev + x.shape, x.dtype) for x in blocks]
    out_shape += [struct((rows * SEGS, width), F32), struct((8, width), F32)]
    res = pl.pallas_call(
        functools.partial(forward_kernel, grid, groups, tile_rows),
        out_shape=out_shape,
        in_specs=[SMEM] + [VMEM] * 12,
        out_specs=[ANY] * (len(out_shape) - 2) + [VMEM] * 2,
        scratch_shapes=[pltpu.VMEM(dev + x.shape, x.dtype) for x in blocks]
        + [pltpu.VMEM((rows, length, width), BF16)] * 4
        + [pltpu.VMEM((width, length), BF16), pltpu.VMEM((length, length), F32)]
        + [pltpu.VMEM((rows, length, width), F32), pltpu.VMEM((1, ff), F32)]
        + [DMA((n,)), DMA((n, nd)), DMA((n, nd))]
        + [DMA((rows,)), DMA((rows, ns - 1)), DMA((rows, ns - 1)), DMA((7 + 4 * rows,))],
        compiler_params=pltpu.CompilerParams(
            collective_id=collective_id, has_side_effects=True, vmem_limit_bytes=VMEM_LIMIT
        ),
    )(lens, tokens, *blocks, spread, owner, spread_wide, owner_wide)
    return res


class Reducer:
    def __init__(self, grid, flat, here, partners, my, sources, outs, own_sem, send_sem, recv_sem, bufs):
        self.grid, self.flat, self.here, self.partners, self.my = grid, flat, here, partners, my
        self.sources, self.outs = sources, outs
        self.own_sem, self.send_sem, self.recv_sem = own_sem, send_sem, recv_sem
        self.bufs = bufs
        self.per_piece = 1 + grid.nd

    def buf(self, i, k):
        return self.bufs[i * self.per_piece + 1 + k]

    def place(self, i, k):
        order = self.grid.order(self.flat[i][3])[::-1]
        free = [d for d in range(self.grid.nd) if d not in order[:k]]
        return order[k], free.index(order[k])

    def own(self, i):
        a, lo, ln, _ = self.flat[i]
        d, pos = self.place(i, 0)
        ix = (slice(None),) * pos + (self.my[d],) + (slice(None),) * (self.grid.nd - pos - 1)
        src = self.sources[a].at[ix + (slice(None), pl.ds(lo, ln))]
        return pltpu.make_async_copy(src, self.bufs[i * self.per_piece], self.own_sem.at[i])

    def copy(self, i, k):
        a, lo, ln, _ = self.flat[i]
        d, pos = self.place(i, k)
        ix = (slice(None),) * pos + (1 - self.my[d],) + (slice(None),) * (self.grid.nd - k - pos - 1)
        if k == 0:
            src = self.sources[a].at[ix + (slice(None), pl.ds(lo, ln))]
        else:
            src = self.buf(i, k - 1).at[ix]
        return remote(
            src, self.buf(i, k), self.send_sem.at[i, k], self.recv_sem.at[i, k], self.partners[d]
        )

    def send(self, i, k):
        if k == 0:
            self.own(i).start()
        self.copy(i, k).start()

    def add(self, i, k):
        nd = self.grid.nd
        a, lo, ln, _ = self.flat[i]
        d, pos = self.place(i, k)
        self.copy(i, k).wait_recv()
        if k == 0:
            self.own(i).wait()
        into = self.buf(i, k)
        left = nd - k - 1
        if left == 0:
            total = self.buf(i, k - 1)[self.my[d]].astype(F32) + into[...].astype(F32)
            self.outs[a][:, lo : lo + ln] = total
            return

        def one(j, carry):
            ix = tuple((j // (1 << (left - 1 - e))) % 2 for e in range(left))
            if k == 0:
                mine = self.bufs[i * self.per_piece][ix]
            else:
                mine = self.buf(i, k - 1)[ix[:pos] + (self.my[d],) + ix[pos:]]
            into[ix] = (mine.astype(F32) + into[ix].astype(F32)).astype(into.dtype)
            return carry

        lax.fori_loop(0, 1 << left, one, 0)

    def step(self, i, k):
        if k > 0:
            self.add(i, k - 1)
        if k < self.grid.nd:
            self.send(i, k)

    def finish(self):
        for i in range(len(self.flat)):
            for k in range(self.grid.nd):
                self.copy(i, k).wait_send()


def reducer_scratch(nd, flat, rows_of, dtype):
    out = []
    for a, _, ln, _ in flat:
        out.append(pltpu.VMEM((2,) * (nd - 1) + (rows_of[a], ln), dtype))
        for k in range(nd):
            out.append(pltpu.VMEM((2,) * (nd - 1 - k) + (rows_of[a], ln), dtype))
    return out


SMALL_ROWS = 16
ROW_BQ, ROW_BV, ROW_BO, ROW_G1, ROW_S1, ROW_BD, ROW_G2, ROW_S2, ROW_BI = range(9)


def backward_kernel(grid, flat, n_bufs, tile_rows, *refs):
    it = iter(refs)
    take = lambda n: [next(it) for _ in range(n)]
    lens, dp, g1, g2 = take(4)
    n2, i2, slope, n1, i1, act, h1, o, q, k, v, p, x, hid = take(14)
    w_down, w_in, w_out, w_query, w_key, w_value = take(6)
    outs = take(6)
    small_out, hid_back, gx_back = take(3)
    dfeed, dinner, dbranch, dpre1, datt, dqkv, gx = take(7)
    grads = take(6)
    wd, wi, wo, wq, wk, wv = take(6)
    small, small_recv = take(2)
    own_sem, send_sem, recv_sem, ex_own, ex_send, ex_recv, w_sem, sm_send, sm_recv = take(9)
    bufs = take(n_bufs)

    b, sq = grid.here()
    nd, ns = grid.nd, grid.seq_size
    my = grid.digits(b, sq)
    partners = [grid.partner(b, sq, d) for d in range(nd)]
    others = [lax.rem(sq + j, ns) for j in range(1, ns)]
    red = Reducer(grid, flat, (b, sq), partners, my, grads, outs, own_sem, send_sem, recv_sem, bufs)
    rows, length, width = x.shape
    count = rows * length
    lt = length // ns
    tiles = length // tile_rows

    weight_loads = [
        pltpu.make_async_copy(src, dst, w_sem.at[i])
        for i, (src, dst) in enumerate(
            [(w_down, wd), (w_in, wi), (w_out, wo), (w_query, wq), (w_key, wk), (w_value, wv)]
        )
    ]
    for c in weight_loads:
        c.start()
    grid.greet(b, sq, partners, others)

    def exchange(e, src, dst, r):
        out = [
            pltpu.make_async_copy(
                src.at[r, pl.ds(pl.multiple_of(sq * lt, lt), lt)],
                dst.at[sq * rows + r],
                ex_own.at[e, r],
            )
        ]
        for j in range(1, ns):
            at = pl.ds(pl.multiple_of(others[j - 1] * lt, lt), lt)
            out.append(
                remote(
                    src.at[r, at],
                    dst.at[sq * rows + r],
                    ex_send.at[e, r, j - 1],
                    ex_recv.at[e, r, j - 1],
                    (b, others[j - 1]),
                )
            )
        return out

    for r in range(rows):
        for c in exchange(0, hid, hid_back, r):
            c.start()
    small[...] = jnp.zeros_like(small)

    def columns(u):
        return jnp.sum(u, axis=0, keepdims=True)

    def norm_back(g, n, inv):
        return inv * (
            g - jnp.mean(g, axis=-1, keepdims=True) - n * jnp.mean(g * n, axis=-1, keepdims=True)
        )

    groups = []
    for i, c in enumerate(flat):
        if c[3] == 0:
            groups.append([])
        groups[-1].append(i)
    early = len(groups) - 3

    def slot(s):
        for kk in range(nd, -1, -1):
            g, odd = divmod(s - 2 * kk, 2)
            if odd == 0 and 0 <= g < early:
                for i in groups[g]:
                    red.step(i, kk)

    used = [0]

    def hook(steps, active=True):
        if not active:
            return lambda: None
        base = used[0]
        used[0] += steps

        def run():
            now = pl.program_id(0)
            for c in range(steps):
                pl.when(now == c)(functools.partial(slot, base + c))

        return run

    weight_loads[0].wait()
    weight_loads[1].wait()
    weight_loads[2].wait()

    def feed_body(n2_t, i2_t, slope_t, n1_t, i1_t, dfeed_t, dinner_t, dbranch_t, dpre1_t, datt_t):
        t = pl.program_id(0)
        r = t // tiles
        seg = segment_of(lens, r, (tile_rows, 1), 0, (t % tiles) * tile_rows)
        place = jnp.where(seg < SEGS, r * SEGS + seg, -1)
        lane = lax.broadcasted_iota(jnp.int32, (tile_rows, 128), 1)
        members = (lane % 64 == place).astype(F32).astype(BF16)
        dh2 = dot(members, dp[...])
        m2 = n2_t[...].astype(F32)
        small[ROW_G2 : ROW_G2 + 1] += columns(dh2 * m2)
        small[ROW_S2 : ROW_S2 + 1] += columns(dh2)
        dpre2 = norm_back(dh2 * g2[...], m2, i2_t[:, :1])
        low = dpre2.astype(BF16)
        dfeed_t[...] = low
        small[ROW_BD : ROW_BD + 1] += columns(low.astype(F32))
        dh1 = dpre2
        for c, lo in enumerate(range(0, wi.shape[1], width)):
            sl = slice(lo, lo + width)
            din = (dot(low, wd[sl, :], 1, 1) * slope_t[:, sl].astype(F32)).astype(BF16)
            dinner_t[:, sl] = din
            small[ROW_BI + c : ROW_BI + c + 1] += columns(din.astype(F32))
            dh1 = dh1 + dot(din, wi[:, sl], 1, 1)
        m1 = n1_t[...].astype(F32)
        small[ROW_G1 : ROW_G1 + 1] += columns(dh1 * m1)
        small[ROW_S1 : ROW_S1 + 1] += columns(dh1)
        dp1 = norm_back(dh1 * g1[...], m1, i1_t[:, :1])
        dpre1_t[...] = dp1
        low = dp1.astype(BF16)
        dbranch_t[...] = low
        small[ROW_BO : ROW_BO + 1] += columns(low.astype(F32))
        datt_t[0] = dot(low, wo[...], 1, 1).astype(BF16)

    ff = wi.shape[1]
    tile = lambda w: pl.BlockSpec((tile_rows, w), lambda t: (t, 0))
    by_row = pl.BlockSpec((1, tile_rows, width), lambda t: (t // tiles, t % tiles, 0))
    pltpu.emit_pipeline(
        feed_body,
        grid=(count // tile_rows,),
        in_specs=[tile(width), tile(128), tile(ff), tile(width), tile(128)],
        out_specs=[tile(width), tile(ff), tile(width), tile(width), by_row],
    )(n2, i2, slope, n1, i1, dfeed, dinner, dbranch, dpre1, datt)

    dev = (2,) * nd
    zeros = (0,) * nd

    def outer_call(a, g, dst, steps, a_map, g_map, block, out_map, active=True):
        call_hook = hook(steps, active)

        def body(a_t, g_t, out_t):
            call_hook()
            lhs = a_t[...].reshape(count, width)
            rhs = g_t[...].reshape(count, width)
            out_t[...] = dot(lhs, rhs, 0, 0).reshape(block).astype(BF16)

        whole = lambda ref: (
            (count, width) if len(ref.shape) == 2 else (1,) * (len(ref.shape) - 3) + (rows, length, width)
        )
        pltpu.emit_pipeline(
            body,
            grid=(steps,),
            in_specs=[pl.BlockSpec(whole(a), a_map), pl.BlockSpec(whole(g), g_map)],
            out_specs=[pl.BlockSpec(block, out_map)],
        )(a, g, dst)

    grad_in, grad_down, grad_out, grad_q, grad_k, grad_v = grads
    square = dev + grad_out.shape[-2:]
    at0 = lambda c: (0, 0)
    chunks = ff // width
    outer_call(
        h1, dinner, grad_in, chunks, at0, lambda c: (0, c), square, lambda c: zeros + (0, c), False
    )
    down_rows = grad_down.shape[-2]
    per = width // down_rows
    low_digits = per.bit_length() - 1
    top = nd - low_digits
    outer_call(
        act,
        dfeed,
        grad_down,
        chunks,
        lambda c: (0, c),
        at0,
        (1,) * top + (2,) * low_digits + (down_rows, width),
        lambda c: tuple((c // (1 << (top - 1 - e))) % 2 for e in range(top)) + (0,) * low_digits + (0, 0),
    )
    outer_call(o, dbranch, grad_out, 1, lambda c: (0, 0, 0), at0, square, lambda c: zeros + (0, 0))

    for c in weight_loads[3:]:
        c.wait()
    lane = lax.broadcasted_iota(jnp.int32, (1, 128), 1)
    for r in range(rows):
        att_hook = hook(HEADS // 2)

        def att_body(q_t, k_t, v_t, do_t, p_t, out_t):
            att_hook()
            qp, kp, vp, dop = q_t[0], k_t[0], v_t[0], do_t[0]
            kt = kp.T
            zero = jnp.zeros_like(vp)
            dv = dk = None
            dqt = []
            for h in range(2):
                mine = lane // HEAD_DIM == h
                vm, dom, qm = (jnp.where(mine, u, zero) for u in (vp, dop, qp))
                pt = p_t[0, h]
                probs = pt.astype(F32)
                weighted = probs * dot(vm, dop, 1, 1)
                ds = (weighted - probs * jnp.sum(weighted, axis=0, keepdims=True)).astype(BF16)
                dv_h, dk_h = dot(pt, dom), dot(ds, qm)
                dv = dv_h if dv is None else dv + dv_h
                dk = dk_h if dk is None else dk + dk_h
                dqt.append(dot(kt[h * HEAD_DIM : (h + 1) * HEAD_DIM], ds) * HEAD_DIM ** (-0.5))
            out_t[0, 0] = jnp.concatenate(dqt, axis=0).T.astype(BF16)
            out_t[1, 0] = dk.astype(BF16)
            out_t[2, 0] = dv.astype(BF16)

        part = pl.BlockSpec((1, length, 128), lambda s, r=r: (r, 0, s))
        pltpu.emit_pipeline(
            att_body,
            grid=(HEADS // 2,),
            in_specs=[part] * 4 + [pl.BlockSpec((1, 2, length, length), lambda s, r=r: (r, s, 0, 0))],
            out_specs=[pl.BlockSpec((3, 1, length, 128), lambda s, r=r: (0, r, 0, s))],
        )(q, k, v, datt, p, dqkv)

        in_hook = hook(tiles)

        def in_body(dpre1_t, d_t, out_t):
            in_hook()
            dq, dk, dv = d_t[0, 0], d_t[1, 0], d_t[2, 0]
            small[ROW_BQ : ROW_BQ + 1] += columns(dq.astype(F32))
            small[ROW_BV : ROW_BV + 1] += columns(dv.astype(F32))
            total = dpre1_t[...] + dot(dq, wq[...], 1, 1) + dot(dk, wk[...], 1, 1)
            out_t[0] = (total + dot(dv, wv[...], 1, 1)).astype(BF16)

        pltpu.emit_pipeline(
            in_body,
            grid=(tiles,),
            in_specs=[
                pl.BlockSpec((tile_rows, width), lambda t, r=r: (r * tiles + t, 0)),
                pl.BlockSpec((3, 1, tile_rows, width), lambda t, r=r: (0, r, t, 0)),
            ],
            out_specs=[pl.BlockSpec((1, tile_rows, width), lambda t, r=r: (r, t, 0))],
        )(dpre1, dqkv, gx)
        for c in exchange(1, gx, gx_back, r):
            c.start()

    def small_copy(kk):
        return remote(
            small, small_recv.at[kk], sm_send.at[kk], sm_recv.at[kk], partners[order[kk]]
        )

    order = grid.order(0)[::-1]

    def small_step(kk):
        if kk > 0:
            c = small_copy(kk - 1)
            c.wait()
            small[...] += small_recv[kk - 1]
        if kk < nd:
            small_copy(kk).start()

    small_step(0)
    for j, (d, dst) in enumerate(((0, grad_q), (1, grad_k), (2, grad_v))):
        outer_call(
            x, dqkv, dst, 1, lambda c: (0, 0, 0), lambda c, d=d: (d, 0, 0, 0), square,
            lambda c: zeros + (0, 0),
        )
        if j > 0:
            for i in groups[early + j - 1]:
                red.step(i, 1)
        small_step(j + 1)
        for i in groups[early + j]:
            red.step(i, 0)
    s = used[0]
    while s <= 2 * (early - 1) + 2 * nd:
        slot(s)
        s += 1
    for t in range(2, 3 + nd):
        for kk in range(nd, 0, -1):
            g = t - kk
            if 0 <= g < 3 and not (kk == 1 and g < 2):
                for i in groups[early + g]:
                    red.step(i, kk)
        if 4 <= t + 1 <= nd:
            small_step(t + 1)
    small_out[...] = small[...]
    red.finish()
    for r in range(rows):
        for e, (src, dst) in enumerate(((hid, hid_back), (gx, gx_back))):
            for c in exchange(e, src, dst, r):
                c.wait()


def backward(grid, lens, dp, g1, g2, kept, weights, tile_rows, collective_id):
    nd, ns = grid.nd, grid.seq_size
    x, hid = kept[-2:]
    rows, length, width = x.shape
    count = rows * length
    w_down, w_in = weights[0], weights[1]
    ff = w_in.shape[1]
    dev = (2,) * nd
    part, down_part = width >> nd, ff >> nd
    shapes = [(part, ff), (down_part, width)] + [(part, width)] * 4
    flat = [c for g in pieces(shapes) for c in g]
    rows_of = [s[0] for s in shapes]
    bufs = reducer_scratch(nd, flat, rows_of, BF16)
    back = struct((rows * ns, length // ns, width), BF16)
    low = struct((count, width), BF16)
    out_shape = [struct(s, F32) for s in shapes]
    out_shape += [struct((SMALL_ROWS, width), F32), back, back]
    out_shape += [low, struct((count, ff), BF16), low, struct((count, width), F32)]
    out_shape += [struct((rows, length, width), BF16), struct((3, rows, length, width), BF16)]
    out_shape += [struct((rows, length, width), BF16)]
    out_shape += [struct(dev + s, BF16) for s in shapes]
    n = len(flat)
    res = pl.pallas_call(
        functools.partial(backward_kernel, grid, flat, len(bufs), tile_rows),
        out_shape=out_shape,
        in_specs=[SMEM, VMEM, VMEM, VMEM] + [ANY] * (len(kept) + len(weights)),
        out_specs=[VMEM] * 7 + [ANY] * (len(out_shape) - 7),
        scratch_shapes=[pltpu.VMEM(w.shape, BF16) for w in weights]
        + [pltpu.VMEM((SMALL_ROWS, width), F32), pltpu.VMEM((nd, SMALL_ROWS, width), F32)]
        + [DMA((n,)), DMA((n, nd)), DMA((n, nd))]
        + [DMA((2, rows)), DMA((2, rows, ns - 1)), DMA((2, rows, ns - 1))]
        + [DMA((len(weights),)), DMA((nd,)), DMA((nd,))]
        + bufs,
        compiler_params=pltpu.CompilerParams(
            collective_id=collective_id, has_side_effects=True, vmem_limit_bytes=VMEM_LIMIT
        ),
    )(lens, dp, g1, g2, *kept, *weights)
    return res[:10]


def pack_small(vectors, wide, extra):
    rows = [jnp.pad(v.astype(F32), (0, 128 - v.shape[0])) for v in (*vectors, wide, extra)]
    rows += [jnp.zeros((128,), F32)] * (16 - len(rows))
    return jnp.stack(rows)


def per_device(
    tokens, lengths, pair_ids, w_query, b_query, w_key, w_value, b_value, w_out, b_out,
    norm1_gain, norm1_bias, w_in, b_in, w_down, b_down, norm2_gain, norm2_bias,
):
    blk_size, seq_size = lax.axis_size("blk"), lax.axis_size("seq")
    grid = Grid(blk_size, seq_size)
    devices = blk_size * seq_size
    group_rows, local_len, width = tokens.shape
    rows = group_rows // seq_size
    length = local_len * seq_size
    count = rows * length
    ff = w_in.shape[1]
    part, wide_part, pairs = b_query.shape[0], b_in.shape[0], pair_ids.shape[0]

    lens = lax.dynamic_slice_in_dim(lengths, lax.axis_index("seq") * rows, rows, 0)
    vectors = (b_query, b_value, b_out, norm1_gain, norm1_bias, b_down, norm2_gain, norm2_bias)
    small = pack_small(vectors, b_in, pair_ids)
    fused = part % 8 == 0
    if fused:
        res = forward(
            grid, lens, tokens, (small, w_query, w_key, w_value, w_out, w_in, w_down), 256, 4
        )
        x, q, k, v, p, o, n1, i1, h1, act, slope, n2, i2, hid = res[:14]
        smalls = res[14].reshape(devices, 16, 128)
        wq, wk, wv, wo, wi, wd = (
            w.reshape((devices * w.shape[-2], w.shape[-1])) for w in res[15:21]
        )
        pool, vecs = res[21:]
        g1, g2 = vecs[3:4], vecs[6:7]
    else:
        full, x = gather_all(grid, (w_query, w_key, w_value, small, w_out, w_in, w_down), tokens, 1)
        wq, wk, wv, smalls, wo, wi, wd = full
        smalls = smalls.reshape(devices, 16, 128)
        vecs = smalls[:, : len(vectors), :part].transpose(1, 0, 2).reshape(len(vectors), 1, width)
        bq, bv, bo, g1, s1, bd, g2, s2 = (vecs[i] for i in range(len(vectors)))
        bi = smalls[:, len(vectors), :wide_part].reshape(1, ff)

        q, k, v, p, o = attention(lens, x, wq, wk, wv, bq, bv)
        x2, o2 = x.reshape(count, width), o.reshape(count, width)
        hid, n1, i1, h1, act, slope, n2, i2, pool = feed(
            lens, x2, o2, wo, bo, g1, s1, wi, bi, wd, bd, g2, s2, 256
        )
    all_pairs = smalls[:, len(vectors) + 1, :pairs].reshape(-1, NQ).astype(jnp.int32)

    none = jnp.full((all_pairs.shape[0], SEGS - NQ), -1, jnp.int32)
    pair_row = jnp.concatenate([all_pairs, none], axis=1).reshape(1, -1)
    own_pairs = jnp.concatenate([pair_ids.reshape(rows, NQ), none[:rows]], axis=1).reshape(-1, 1)
    pair_col = jnp.broadcast_to(own_pairs, (rows * SEGS, 128))
    len_col = jnp.broadcast_to(lens.reshape(-1, 1).astype(F32), (rows * SEGS, 128))
    losses, dpool = contrast(grid, pool, len_col, pair_col, pair_row, 2)
    query_loss = losses[:, 0].reshape(rows, SEGS)[:, :NQ].reshape(-1)

    if fused:
        kept = (n2, i2, slope, n1, i1, act, h1, o, q, k, v, p, x, hid.reshape(rows, length, width))
        res = backward(grid, lens, dpool, g1, g2, kept, (wd, wi, wo, wq, wk, wv), 256, 3)
        g_in, g_down, g_out, g_query, g_key, g_value, sums, hidden_out, grad_tokens = res[:9]
        me = lax.axis_index("blk") * seq_size + lax.axis_index("seq")
        own = lax.dynamic_slice_in_dim(sums[:8], me * part, part, 1)
        gv = [own[i] for i in range(8)]
        g_wide = lax.dynamic_slice_in_dim(
            sums[ROW_BI : ROW_BI + ff // width].reshape(ff), me * wide_part, wide_part, 0
        )
        return (
            hidden_out, query_loss, grad_tokens.astype(F32), g_query, gv[0], g_key, g_value, gv[1],
            g_out, gv[2], gv[3], gv[4], g_in, g_wide, g_down, gv[5], gv[6], gv[7],
        )

    dfeed, dinner, dbranch, dpre1, datt, sums, wide_sums = feed_back(
        lens, dpool, n2, i2, slope, n1, i1, wd, wi, wo, g2, g1, 256
    )
    grad_w_down = outer(act, dfeed, width, width)
    grad_w_in = outer(h1, dinner, width, width)
    grad_w_out = outer(o2, dbranch, width, width)
    dq, dk, dv = attention_back(q, k, v, p, datt.reshape(rows, length, width))
    dq, dk, dv = (d.reshape(count, width) for d in (dq, dk, dv))
    grad_x, sums_in = input_back(dpre1, dq, dk, dv, wq, wk, wv, 256)
    grad_w_query = outer(x2, dq, width, width)
    grad_w_key = outer(x2, dk, width, width)
    grad_w_value = outer(x2, dv, width, width)

    vec_grads = jnp.stack(
        [sums_in[0], sums_in[1], sums[5], sums[3], sums[4], sums[2], sums[0], sums[1]]
    )
    packed = jnp.pad(
        vec_grads.reshape(8, devices, part).transpose(1, 0, 2), ((0, 0), (0, 0), (0, 128 - part))
    )
    wide_grads = jnp.pad(
        wide_sums[0].reshape(devices, 1, wide_part), ((0, 0), (0, 7), (0, 128 - wide_part))
    )
    packed = jnp.concatenate([packed, wide_grads], axis=1).reshape(devices * 16, 128)
    grads, back = scatter_all(
        grid,
        (grad_w_down, grad_w_in, grad_w_out, packed, grad_w_query, grad_w_key, grad_w_value),
        (hid.reshape(rows, length, width), grad_x.reshape(rows, length, width)),
        3,
    )
    g_down, g_in, g_out, g_small, g_query, g_key, g_value = grads
    hidden_out, grad_tokens = back
    gv = [g_small[i, :part] for i in range(8)]
    return (
        hidden_out,
        query_loss,
        grad_tokens.astype(F32),
        g_query,
        gv[0],
        g_key,
        g_value,
        gv[1],
        g_out,
        gv[2],
        gv[3],
        gv[4],
        g_in,
        g_small[8, :wide_part],
        g_down,
        gv[5],
        gv[6],
        gv[7],
    )


def solution(mesh):
    both = ("blk", "seq")
    vec, mat, tok = P(both), P(both, None), P("blk", "seq", None)
    in_specs = (
        tok, P("blk", None), vec, mat, vec, mat, mat, vec, mat, vec, vec, vec, mat, vec, mat, vec,
        vec, vec,
    )
    out_specs = (
        tok, vec, tok, mat, vec, mat, mat, vec, mat, vec, vec, vec, mat, vec, mat, vec, vec, vec,
    )
    return jax.shard_map(
        per_device, mesh=mesh, in_specs=in_specs, out_specs=out_specs, check_vma=False
    )
```

```python
import functools

import jax
import jax.numpy as jnp
from jax import lax
from jax.experimental import pallas as pl
from jax.experimental.pallas import tpu as pltpu
from jax.sharding import PartitionSpec as P

HEADS = 12
HEAD_DIM = 64
NQ = 2
SEGS = 4
TEMPERATURE = 0.05
NORM_EPSILON = 1e-06
MASKED = -1000000000.0
BF16 = jnp.bfloat16
F32 = jnp.float32
MESH = pl.DeviceIdType.MESH
ANY = pl.BlockSpec(memory_space=pl.ANY)
VMEM = pl.BlockSpec(memory_space=pltpu.VMEM)
SMEM = pl.BlockSpec(memory_space=pltpu.SMEM)
DMA = pltpu.SemaphoreType.DMA
VMEM_LIMIT = 60 * 2**20


def dot(a, b, ca=1, cb=0):
    return lax.dot_general(a, b, (((ca,), (cb,)), ((), ())), preferred_element_type=F32)


def struct(shape, dtype):
    return jax.ShapeDtypeStruct(shape, dtype)


def split_two(v):
    high = v.astype(BF16)
    return high, (v - high.astype(F32)).astype(BF16)


class Grid:
    def __init__(self, blk_size, seq_size):
        self.blk_size, self.seq_size = blk_size, seq_size
        self.kb = blk_size.bit_length() - 1
        self.ks = seq_size.bit_length() - 1
        assert 1 << self.kb == blk_size and 1 << self.ks == seq_size
        self.nd = self.kb + self.ks

    def here(self):
        return lax.axis_index("blk"), lax.axis_index("seq")

    def digit(self, b, q, d):
        if d < self.kb:
            w = 1 << (self.kb - 1 - d)
            return (b // w) % 2, w
        w = 1 << (self.nd - 1 - d)
        return (q // w) % 2, w

    def digits(self, b, q):
        return [self.digit(b, q, d)[0] for d in range(self.nd)]

    def partner(self, b, q, d):
        v, w = self.digit(b, q, d)
        if d < self.kb:
            return (b + (1 - 2 * v) * w, q)
        return (b, q + (1 - 2 * v) * w)

    def order(self, flavour):
        seq = list(range(self.kb, self.nd))
        head, last = list(range(self.kb))[:-1][::-1], [self.kb - 1]
        if head:
            r = flavour % len(head)
            head = head[r:] + head[:r]
        return seq + head + last

    def greet(self, b, q, partners, others):
        barrier = pltpu.get_barrier_semaphore()
        targets = [partners[d] for d in range(self.kb)]
        if others is None:
            targets += [partners[d] for d in range(self.kb, self.nd)]
        else:
            targets += [(b, o) for o in others]
        for t in targets:
            pl.semaphore_signal(barrier, inc=1, device_id=t, device_id_type=MESH)
        pl.semaphore_wait(barrier, len(targets))


def remote(src, dst, send, recv, where):
    return pltpu.make_async_remote_copy(
        src_ref=src, dst_ref=dst, send_sem=send, recv_sem=recv, device_id=where, device_id_type=MESH
    )


def flat_view(rows, lanes):
    if rows % 8 == 0:
        return rows, lanes
    return rows * lanes // 128, 128


def pieces(shapes):
    out = []
    for a, (rows, lanes) in enumerate(shapes):
        unit = 768 if rows < 64 else 256
        unit = min(unit, lanes)
        for lo in range(0, lanes, unit):
            half = unit // 2
            if half % 128 == 0:
                out.append([(a, lo, half, 0), (a, lo + half, half, 1)])
            else:
                out.append([(a, lo, unit, 0)])
    return out


def gather_kernel(grid, groups, n, lag, *refs):
    ins, tok = refs[:n], refs[n]
    outs, rows_out = refs[n + 1 : 2 * n + 1], refs[2 * n + 1]
    own_sem, send_sem, recv_sem, tok_own, tok_send, tok_recv = refs[2 * n + 2 :]
    b, q = grid.here()
    nd, ns = grid.nd, grid.seq_size
    my = grid.digits(b, q)
    partners = [grid.partner(b, q, d) for d in range(nd)]
    others = [lax.rem(q + j, ns) for j in range(1, ns)]
    grid.greet(b, q, partners, others)
    flat = [c for g in groups for c in g]
    where = {}
    first = 0
    for gi, g in enumerate(groups):
        where[gi] = list(range(first, first + len(g)))
        first += len(g)

    own = []
    for i, (a, lo, ln, _) in enumerate(flat):
        c = pltpu.make_async_copy(
            ins[a].at[:, pl.ds(lo, ln)],
            outs[a].at[tuple(my) + (slice(None), pl.ds(lo, ln))],
            own_sem.at[i],
        )
        c.start()
        own.append(c)
    copies = {}

    def stage(i, k):
        a, lo, ln, flavour = flat[i]
        order = grid.order(flavour)
        d = order[k]
        if k == 0:
            src = ins[a].at[:, pl.ds(lo, ln)]
            dst = outs[a].at[tuple(my) + (slice(None), pl.ds(lo, ln))]
        else:
            if k == 1:
                own[i].wait()
            copies[(i, k - 1)].wait_recv()
            done = order[:k]
            ix = tuple(slice(None) if e in done else my[e] for e in range(nd))
            ix = ix + (slice(None), pl.ds(lo, ln))
            src, dst = outs[a].at[ix], outs[a].at[ix]
        c = remote(src, dst, send_sem.at[i, k], recv_sem.at[i, k], partners[d])
        c.start()
        copies[(i, k)] = c

    row_copies = []
    total, lt, _ = tok.shape
    per = total // ns

    def send_rows():
        at = pl.ds(pl.multiple_of(q * lt, lt), lt)
        for r in range(per):
            c = pltpu.make_async_copy(tok.at[q * per + r], rows_out.at[r, at], tok_own.at[r])
            c.start()
            row_copies.append(c)
            for j in range(1, ns):
                o = others[j - 1]
                c = remote(
                    tok.at[o * per + r],
                    rows_out.at[r, at],
                    tok_send.at[j - 1, r],
                    tok_recv.at[j - 1, r],
                    (b, o),
                )
                c.start()
                row_copies.append(c)

    ng = len(groups)
    for t in range(ng + lag * (nd - 1)):
        for k in range(nd - 1, -1, -1):
            g = t - lag * k
            if 0 <= g < ng:
                for i in where[g]:
                    stage(i, k)
        if t == 2:
            send_rows()
    for i in range(len(flat)):
        copies[(i, nd - 1)].wait_recv()
    for i in range(len(flat)):
        for k in range(nd):
            copies[(i, k)].wait_send()
    for c in row_copies:
        c.wait()


def gather_all(grid, blocks, tokens, collective_id):
    nd, ns = grid.nd, grid.seq_size
    n = len(blocks)
    views = [x.reshape(flat_view(*x.shape)) for x in blocks]
    groups = pieces([v.shape for v in views])
    count = sum(len(g) for g in groups)
    total, lt, width = tokens.shape
    per = total // ns
    outs = [struct((2,) * nd + v.shape, v.dtype) for v in views]
    outs.append(struct((per, lt * ns, width), tokens.dtype))
    res = pl.pallas_call(
        functools.partial(gather_kernel, grid, groups, n, 2),
        out_shape=outs,
        in_specs=[VMEM] * (n + 1),
        out_specs=[ANY] * (n + 1),
        scratch_shapes=[
            DMA((count,)),
            DMA((count, nd)),
            DMA((count, nd)),
            DMA((per,)),
            DMA((ns - 1, per)),
            DMA((ns - 1, per)),
        ],
        compiler_params=pltpu.CompilerParams(
            collective_id=collective_id, has_side_effects=True, vmem_limit_bytes=VMEM_LIMIT
        ),
    )(*views, tokens)
    devices = 1 << nd
    full = [
        r.reshape((devices * x.shape[0], x.shape[1])) for r, x in zip(res[:-1], blocks, strict=True)
    ]
    return full, res[-1]


def reduce_plan(grid, flavour):
    free = list(range(grid.nd))
    plan = []
    for d in grid.order(flavour)[::-1]:
        pos = free.index(d)
        plan.append((d, 1 << pos, 1 << (len(free) - pos - 1)))
        free.remove(d)
    return plan


def scatter_kernel(grid, flat, n, nx, lag, *refs):
    nd, ns = grid.nd, grid.seq_size
    ins, rows_in = refs[:n], refs[n : n + nx]
    outs, rows_out = refs[n + nx : 2 * n + nx], refs[2 * n + nx : 2 * n + 2 * nx]
    rest = list(refs[2 * n + 2 * nx :])
    own_sem, send_sem, recv_sem, x_own, x_send, x_recv = rest[:6]
    bufs = rest[6:]
    b, q = grid.here()
    my = grid.digits(b, q)
    partners = [grid.partner(b, q, d) for d in range(nd)]
    others = [lax.rem(q + j, ns) for j in range(1, ns)]
    grid.greet(b, q, partners, others)

    row_copies = []
    for x in range(nx):
        per, length, _ = rows_in[x].shape
        lt = length // ns
        for r in range(per):
            at = pl.ds(pl.multiple_of(q * lt, lt), lt)
            c = pltpu.make_async_copy(
                rows_in[x].at[r, at], rows_out[x].at[q * per + r], x_own.at[x, r]
            )
            c.start()
            row_copies.append(c)

    def send_rows(x):
        per, length, _ = rows_in[x].shape
        lt = length // ns
        for r in range(per):
            for j in range(1, ns):
                o = others[j - 1]
                c = remote(
                    rows_in[x].at[r, pl.ds(pl.multiple_of(o * lt, lt), lt)],
                    rows_out[x].at[q * per + r],
                    x_send.at[x, j - 1, r],
                    x_recv.at[x, j - 1, r],
                    (b, o),
                )
                c.start()
                row_copies.append(c)

    per_piece = 1 + 2 * nd - 1
    copies, own = {}, {}

    def buffers(i):
        mine = bufs[i * per_piece : (i + 1) * per_piece]
        return mine[0], mine[1 : 1 + nd], mine[1 + nd :]

    for i, (a, lo, ln, flavour) in enumerate(flat):
        d = reduce_plan(grid, flavour)[0][0]
        ix = tuple(my[e] if e == d else slice(None) for e in range(nd)) + (slice(None), pl.ds(lo, ln))
        c = pltpu.make_async_copy(ins[a].at[ix], buffers(i)[0], own_sem.at[i])
        c.start()
        own[i] = c

    def send(i, k):
        a, lo, ln, flavour = flat[i]
        d, pre, post = reduce_plan(grid, flavour)[k]
        start, recv, acc = buffers(i)
        if k == 0:
            ix = tuple((1 - my[e]) if e == d else slice(None) for e in range(nd))
            src = ins[a].at[ix + (slice(None), pl.ds(lo, ln))]
        else:
            src = acc[k - 1].at[:, 1 - my[d]]
        c = remote(src, recv[k], send_sem.at[i, k], recv_sem.at[i, k], partners[d])
        c.start()
        copies[(i, k)] = c

    def add(i, k):
        a, lo, ln, flavour = flat[i]
        plan = reduce_plan(grid, flavour)
        d, pre, post = plan[k]
        start, recv, acc = buffers(i)
        copies[(i, k)].wait_recv()
        if k == 0:
            own[i].wait()
        if k == nd - 1:
            total = acc[k - 1][0, my[d], 0].astype(F32) + recv[k][0, 0].astype(F32)
            outs[a][:, lo : lo + ln] = total
            return
        _, pre2, post2 = plan[k + 1]

        def one(j, carry):
            if k == 0:
                ix = tuple((j // (1 << (nd - 2 - e))) % 2 for e in range(nd - 1))
                mine, other = start[ix], recv[0][ix]
            else:
                mine = acc[k - 1][j // post, my[d], j % post]
                other = recv[k][j // post, j % post]
            total = mine.astype(F32) + other.astype(F32)
            acc[k][j // (2 * post2), (j // post2) % 2, j % post2] = total.astype(acc[k].dtype)
            return carry

        lax.fori_loop(0, pre * post, one, 0)

    groups = sorted({c[4] for c in [(*f, gi) for f, gi in zip(flat, group_of(flat))]})
    members = {g: [i for i, gi in enumerate(group_of(flat)) if gi == g] for g in groups}
    ng = len(groups)
    for t in range(ng + lag * nd):
        for k in range(nd, -1, -1):
            g = t - lag * k
            if 0 <= g < ng:
                for i in members[g]:
                    if k > 0:
                        add(i, k - 1)
                    if k < nd:
                        send(i, k)
        if t == 0:
            for x in range(nx):
                send_rows(x)
    for i in range(len(flat)):
        for k in range(nd):
            copies[(i, k)].wait_send()
    for c in row_copies:
        c.wait()


def group_of(flat):
    ids, last = [], -1
    for _, _, _, flavour in flat:
        if flavour == 0:
            last += 1
        ids.append(last)
    return ids


def scatter_all(grid, grads, rows_back, collective_id):
    nd, ns = grid.nd, grid.seq_size
    devices = 1 << nd
    views, finals = [], []
    for g in grads:
        rows = g.shape[0] // devices
        finals.append((rows, g.shape[1]))
        views.append(g.reshape((2,) * nd + flat_view(rows, g.shape[1])))
    flat = [c for g in pieces([v.shape[-2:] for v in views]) for c in g]
    n, nx = len(views), len(rows_back)
    scratch = []
    for a, _, ln, flavour in flat:
        rows, dtype = views[a].shape[-2], views[a].dtype
        plan = reduce_plan(grid, flavour)
        scratch.append(pltpu.VMEM((2,) * (nd - 1) + (rows, ln), dtype))
        for k, (_, pre, post) in enumerate(plan):
            shape = (2,) * (nd - 1) if k == 0 else (pre, post)
            scratch.append(pltpu.VMEM(shape + (rows, ln), dtype))
        for _, pre, post in plan[1:]:
            scratch.append(pltpu.VMEM((pre, 2, post, rows, ln), dtype))
    outs = [struct(v.shape[-2:], F32) for v in views]
    for x in rows_back:
        per, length, width = x.shape
        outs.append(struct((per * ns, length // ns, width), x.dtype))
    per = rows_back[0].shape[0]
    count = len(flat)
    res = pl.pallas_call(
        functools.partial(scatter_kernel, grid, flat, n, nx, 2),
        out_shape=outs,
        in_specs=[ANY] * n + [ANY] * nx,
        out_specs=[VMEM] * n + [ANY] * nx,
        scratch_shapes=[
            DMA((count,)),
            DMA((count, nd)),
            DMA((count, nd)),
            DMA((nx, per)),
            DMA((nx, ns - 1, per)),
            DMA((nx, ns - 1, per)),
        ]
        + scratch,
        compiler_params=pltpu.CompilerParams(
            collective_id=collective_id, has_side_effects=True, vmem_limit_bytes=VMEM_LIMIT
        ),
    )(*views, *rows_back)
    return [r.reshape(s) for r, s in zip(res[:n], finals, strict=True)], res[n:]


def segment_of(lens, r, shape, axis, start=0):
    t = lax.broadcasted_iota(jnp.int32, shape, axis) + start
    end = lens[r, 0]
    seg = (t >= end).astype(jnp.int32)
    for k in range(1, SEGS):
        end = end + lens[r, k]
        seg = seg + (t >= end).astype(jnp.int32)
    return seg


def attention_kernel(
    lens, x_ref, wq, wk, wv, bq, bv, q_ref, k_ref, v_ref, p_ref, o_ref, vt_ref, ot_ref, bias_ref
):
    x = x_ref[0]
    length = x.shape[0]
    r = pl.program_id(0)
    seg_k = segment_of(lens, r, (length, 1), 0)
    seg_q = segment_of(lens, r, (1, length), 1)
    bias_ref[...] = jnp.where(seg_k == seg_q, 0.0, MASKED)
    q_ref[0] = ((dot(x, wq[...]) + bq[...]) * HEAD_DIM ** (-0.5)).astype(BF16)
    k_ref[0] = dot(x, wk[...]).astype(BF16)
    v = dot(x, wv[...]) + bv[...]
    v_ref[0] = v.astype(BF16)
    vt_ref[...] = v.T.astype(BF16)
    lane = lax.broadcasted_iota(jnp.int32, (1, 128), 1)

    def pair(p, carry):
        sl = pl.ds(pl.multiple_of(p * 128, 128), 128)
        qp, kp = q_ref[0, :, sl], k_ref[0, :, sl]
        for h in range(2):
            km = jnp.where(lane // HEAD_DIM == h, kp, jnp.zeros_like(kp))
            hs = pl.ds(pl.multiple_of(p * 128 + h * HEAD_DIM, HEAD_DIM), HEAD_DIM)
            s = dot(km, qp, 1, 1) + bias_ref[...]
            e = jnp.exp(s - jnp.max(s, axis=0, keepdims=True))
            pt = (e * (1.0 / jnp.sum(e, axis=0, keepdims=True))).astype(BF16)
            p_ref[0, p * 2 + h] = pt
            ot_ref[hs, :] = dot(vt_ref[hs, :], pt).astype(BF16)
        return carry

    lax.fori_loop(0, HEADS // 2, pair, 0)
    o_ref[0] = ot_ref[...].T


def attention(lens, x, wq, wk, wv, bq, bv):
    rows, length, width = x.shape
    row = lambda *s: pl.BlockSpec((1,) + s, lambda r: (r,) + (0,) * len(s))
    full = lambda *s: pl.BlockSpec(s, lambda r: (0,) * len(s))
    tokens = struct((rows, length, width), BF16)
    return pl.pallas_call(
        attention_kernel,
        grid=(rows,),
        out_shape=[tokens] * 3 + [struct((rows, HEADS, length, length), BF16), tokens],
        in_specs=[SMEM, row(length, width)] + [full(width, width)] * 3 + [full(1, width)] * 2,
        out_specs=[row(length, width)] * 3 + [row(HEADS, length, length), row(length, width)],
        scratch_shapes=[
            pltpu.VMEM((width, length), BF16),
            pltpu.VMEM((width, length), BF16),
            pltpu.VMEM((length, length), F32),
        ],
        compiler_params=pltpu.CompilerParams(vmem_limit_bytes=VMEM_LIMIT),
    )(lens, x, wq, wk, wv, bq, bv)


def layer_norm(v):
    c = v - jnp.mean(v, axis=-1, keepdims=True)
    inv = lax.rsqrt(jnp.mean(c * c, axis=-1, keepdims=True) + NORM_EPSILON)
    return c * inv, inv


def feed_kernel(
    tiles, lens, x_ref, o_ref, wo, bo, g1, s1, wi, bi, wd, bd, g2, s2,
    hid_ref, n1_ref, i1_ref, h1_ref, act_ref, slope_ref, n2_ref, i2_ref, pool_ref,
):
    t = pl.program_id(0)
    rows = x_ref.shape[0]
    pre1 = x_ref[...].astype(F32) + dot(o_ref[...], wo[...]) + bo[...]
    n1, i1 = layer_norm(pre1)
    h1 = n1 * g1[...] + s1[...]
    h1_low = h1.astype(BF16)
    n1_ref[...] = n1.astype(BF16)
    h1_ref[...] = h1_low
    i1_ref[...] = jnp.broadcast_to(i1, i1_ref.shape)
    acc = h1 + bd[...]
    chunk = wd.shape[1]
    for lo in range(0, wi.shape[1], chunk):
        sl = slice(lo, lo + chunk)
        inner = dot(h1_low, wi[:, sl]) + bi[:, sl]
        phi = 0.5 + 0.5 * lax.erf(inner * (0.5**0.5))
        act = (inner * phi).astype(BF16)
        act_ref[:, sl] = act
        density = jnp.exp(-0.5 * inner * inner) * 0.3989422804014327
        slope_ref[:, sl] = (phi + inner * density).astype(BF16)
        acc = acc + dot(act, wd[sl, :])
    n2, i2 = layer_norm(acc)
    h2 = n2 * g2[...] + s2[...]
    high, low = split_two(h2)
    hid_ref[...] = high
    n2_ref[...] = n2.astype(BF16)
    i2_ref[...] = jnp.broadcast_to(i2, i2_ref.shape)
    r = t // tiles
    seg = segment_of(lens, r, (1, rows), 1, (t % tiles) * rows)
    slot = jnp.where(seg < SEGS, r * SEGS + seg, -1)
    members = lax.broadcasted_iota(jnp.int32, (pool_ref.shape[0], rows), 0) == slot
    members = members.astype(F32).astype(BF16)
    part = dot(members, high) + dot(members, low)

    @pl.when(t == 0)
    def _():
        pool_ref[...] = part

    @pl.when(t != 0)
    def _():
        pool_ref[...] += part


def feed(lens, x, o, wo, bo, g1, s1, wi, bi, wd, bd, g2, s2, tile_rows):
    count, width = x.shape
    rows = lens.shape[0]
    ff = wi.shape[1]
    tiles = count // rows // tile_rows
    tile = lambda w: pl.BlockSpec((tile_rows, w), lambda t: (t, 0))
    full = lambda *s: pl.BlockSpec(s, lambda t: (0,) * len(s))
    vec = full(1, width)
    low, col = struct((count, width), BF16), struct((count, 128), F32)
    wide = struct((count, ff), BF16)
    return pl.pallas_call(
        functools.partial(feed_kernel, tiles),
        grid=(count // tile_rows,),
        out_shape=[low, low, col, low, wide, wide, low, col, struct((rows * SEGS, width), F32)],
        in_specs=[SMEM, tile(width), tile(width), full(width, width), vec, vec, vec]
        + [full(width, ff), full(1, ff), full(ff, width), vec, vec, vec],
        out_specs=[tile(width), tile(width), tile(128), tile(width), tile(ff), tile(ff)]
        + [tile(width), tile(128), full(rows * SEGS, width)],
        compiler_params=pltpu.CompilerParams(vmem_limit_bytes=VMEM_LIMIT),
    )(lens, x, o, wo, bo, g1, s1, wi, bi, wd, bd, g2, s2)


def contrast_kernel(grid, pool_ref, len_ref, pair_ref, pairs_ref, loss_ref, dpool_ref, emb, send_sem, recv_sem):
    nd = grid.nd
    b, q = grid.here()
    my = grid.digits(b, q)
    partners = [grid.partner(b, q, d) for d in range(nd)]
    own_rows, width = pool_ref.shape
    count = own_rows << nd
    avg = pool_ref[...] / len_ref[:, :1]
    inv = lax.rsqrt(jnp.sum(avg * avg, axis=-1, keepdims=True) + NORM_EPSILON)
    own = avg * inv
    emb[tuple(my)] = own
    grid.greet(b, q, partners, None)
    order = grid.order(0)
    for k, d in enumerate(order):
        ix = tuple(slice(None) if e in order[:k] else my[e] for e in range(nd))
        c = remote(emb.at[ix], emb.at[ix], send_sem.at[k], recv_sem.at[k], partners[d])
        c.start()
        c.wait()
    high, low = split_two(emb[...].reshape(count, width))
    own_high, own_low = split_two(own)
    scale = 1.0 / TEMPERATURE

    def product(ah, al, bh, bl, cb):
        return dot(ah, bh, 1, cb) + dot(ah, bl, 1, cb) + dot(al, bh, 1, cb)

    total = jnp.zeros((1, count), F32)
    step = min(count, 256)
    for lo in range(0, count, step):
        sim = product(high[lo : lo + step], low[lo : lo + step], high, low, 1) * scale
        at = lax.broadcasted_iota(jnp.int32, (step, 1), 0)
        total += jnp.sum(jnp.where(at % SEGS >= NQ, jnp.exp(sim - scale), 0.0), axis=0, keepdims=True)
    lse_cols = scale + jnp.log(total)
    sim = product(own_high, own_low, high, low, 1) * scale
    col = lax.broadcasted_iota(jnp.int32, (1, count), 1)
    row = lax.broadcasted_iota(jnp.int32, (own_rows, 1), 0) + (b * grid.seq_size + q) * own_rows
    col_doc, row_doc = col % SEGS >= NQ, row % SEGS >= NQ
    number = lambda at: (at // SEGS) * NQ + at % SEGS - NQ
    lse_rows = scale + jnp.log(
        jnp.sum(jnp.where(col_doc, jnp.exp(sim - scale), 0.0), axis=1, keepdims=True)
    )
    chosen = col_doc & (number(col) == pair_ref[:, :1])
    positive = jnp.sum(jnp.where(chosen, sim, 0.0), axis=1, keepdims=True)
    loss_ref[...] = jnp.broadcast_to(lse_rows - positive, loss_ref.shape)
    as_query = jnp.exp(sim - lse_rows) - chosen.astype(F32)
    chosen_by = number(row) == pairs_ref[:1]
    as_doc = jnp.exp(jnp.where(col_doc, MASKED, sim - lse_cols)) - chosen_by.astype(F32)
    grad = jnp.where(row_doc, jnp.where(col_doc, 0.0, as_doc), jnp.where(col_doc, as_query, 0.0))
    grad_high, grad_low = split_two(grad)
    demb = product(grad_high, grad_low, high, low, 0) * scale
    dpool = inv * demb - inv * inv * inv * avg * jnp.sum(avg * demb, axis=-1, keepdims=True)
    dpool_high, dpool_low = split_two(dpool / len_ref[:, :1])
    pad = jnp.zeros((64 - own_rows, width), F32)
    stacked = jnp.concatenate([dpool_high.astype(F32), pad, dpool_low.astype(F32), pad], axis=0)
    dpool_ref[...] = stacked.astype(BF16)


def contrast(grid, pool, len_col, pair_col, pair_row, collective_id):
    own_rows, width = pool.shape
    return pl.pallas_call(
        functools.partial(contrast_kernel, grid),
        out_shape=[struct((own_rows, 128), F32), struct((128, width), BF16)],
        in_specs=[VMEM] * 4,
        out_specs=[VMEM] * 2,
        scratch_shapes=[
            pltpu.VMEM((2,) * grid.nd + (own_rows, width), F32),
            DMA((grid.nd,)),
            DMA((grid.nd,)),
        ],
        compiler_params=pltpu.CompilerParams(
            collective_id=collective_id, has_side_effects=True, vmem_limit_bytes=VMEM_LIMIT
        ),
    )(pool, len_col, pair_col, pair_row)


def feed_back_kernel(
    tiles, lens, dp_ref, n2_ref, i2_ref, slope_ref, n1_ref, i1_ref, wd, wi, wo, g2, g1,
    dfeed_ref, dinner_ref, dbranch_ref, dpre1_ref, datt_ref, sums_ref, wide_ref,
):
    t = pl.program_id(0)
    rows = n2_ref.shape[0]

    @pl.when(t == 0)
    def _():
        sums_ref[...] = jnp.zeros_like(sums_ref)
        wide_ref[...] = jnp.zeros_like(wide_ref)

    def columns(v):
        return jnp.sum(v, axis=0, keepdims=True)

    def norm_back(g, n, inv):
        return inv * (
            g - jnp.mean(g, axis=-1, keepdims=True) - n * jnp.mean(g * n, axis=-1, keepdims=True)
        )

    r = t // tiles
    seg = segment_of(lens, r, (rows, 1), 0, (t % tiles) * rows)
    slot = jnp.where(seg < SEGS, r * SEGS + seg, -1)
    lane = lax.broadcasted_iota(jnp.int32, (rows, 128), 1)
    members = (lane % 64 == slot).astype(F32).astype(BF16)
    dh2 = dot(members, dp_ref[...])
    n2 = n2_ref[...].astype(F32)
    sums_ref[0:1] += columns(dh2 * n2)
    sums_ref[1:2] += columns(dh2)
    dpre2 = norm_back(dh2 * g2[...], n2, i2_ref[:, :1])
    dfeed = dpre2.astype(BF16)
    dfeed_ref[...] = dfeed
    sums_ref[2:3] += columns(dfeed.astype(F32))
    chunk = wd.shape[1]
    dh1 = dpre2
    for lo in range(0, wi.shape[1], chunk):
        sl = slice(lo, lo + chunk)
        dinner = (dot(dfeed, wd[sl, :], 1, 1) * slope_ref[:, sl].astype(F32)).astype(BF16)
        dinner_ref[:, sl] = dinner
        wide_ref[0:1, sl] += columns(dinner.astype(F32))
        dh1 = dh1 + dot(dinner, wi[:, sl], 1, 1)
    n1 = n1_ref[...].astype(F32)
    sums_ref[3:4] += columns(dh1 * n1)
    sums_ref[4:5] += columns(dh1)
    dpre1 = norm_back(dh1 * g1[...], n1, i1_ref[:, :1])
    dpre1_ref[...] = dpre1
    dbranch = dpre1.astype(BF16)
    dbranch_ref[...] = dbranch
    sums_ref[5:6] += columns(dbranch.astype(F32))
    datt_ref[...] = dot(dbranch, wo[...], 1, 1).astype(BF16)


def feed_back(lens, dp, n2, i2, slope, n1, i1, wd, wi, wo, g2, g1, tile_rows):
    count, width = n2.shape
    rows = lens.shape[0]
    ff = wi.shape[1]
    tiles = count // rows // tile_rows
    tile = lambda w: pl.BlockSpec((tile_rows, w), lambda t: (t, 0))
    full = lambda *s: pl.BlockSpec(s, lambda t: (0,) * len(s))
    low = struct((count, width), BF16)
    return pl.pallas_call(
        functools.partial(feed_back_kernel, tiles),
        grid=(count // tile_rows,),
        out_shape=[low, struct((count, ff), BF16), low, struct((count, width), F32), low]
        + [struct((8, width), F32), struct((8, ff), F32)],
        in_specs=[SMEM, full(128, width), tile(width), tile(128), tile(ff), tile(width), tile(128)]
        + [full(ff, width), full(width, ff), full(width, width), full(1, width), full(1, width)],
        out_specs=[tile(width), tile(ff), tile(width), tile(width), tile(width)]
        + [full(8, width), full(8, ff)],
        compiler_params=pltpu.CompilerParams(vmem_limit_bytes=VMEM_LIMIT),
    )(lens, dp, n2, i2, slope, n1, i1, wd, wi, wo, g2, g1)


def outer_kernel(a_ref, b_ref, o_ref):
    o_ref[...] = dot(a_ref[...], b_ref[...], 0, 0).astype(o_ref.dtype)


def outer(a, b, bm, bn):
    count, m = a.shape
    n = b.shape[1]
    return pl.pallas_call(
        outer_kernel,
        grid=(m // bm, n // bn),
        out_shape=struct((m, n), BF16),
        in_specs=[
            pl.BlockSpec((count, bm), lambda i, j: (0, i)),
            pl.BlockSpec((count, bn), lambda i, j: (0, j)),
        ],
        out_specs=pl.BlockSpec((bm, bn), lambda i, j: (i, j)),
        compiler_params=pltpu.CompilerParams(vmem_limit_bytes=VMEM_LIMIT),
    )(a, b)


def attention_back_kernel(q_ref, k_ref, v_ref, p_ref, do_ref, dq_ref, dk_ref, dv_ref, kt_ref, dqt_ref):
    kt_ref[...] = k_ref[0].T
    lane = lax.broadcasted_iota(jnp.int32, (1, 128), 1)

    def pair(p, carry):
        sl = pl.ds(pl.multiple_of(p * 128, 128), 128)
        qp, vp, dop = q_ref[0, :, sl], v_ref[0, :, sl], do_ref[0, :, sl]
        zero = jnp.zeros_like(vp)
        dv = dk = None
        for h in range(2):
            mine = lane // HEAD_DIM == h
            vm, dom, qm = (jnp.where(mine, u, zero) for u in (vp, dop, qp))
            hs = pl.ds(pl.multiple_of(p * 128 + h * HEAD_DIM, HEAD_DIM), HEAD_DIM)
            pt = p_ref[0, p * 2 + h]
            probs = pt.astype(F32)
            weighted = probs * dot(vm, dop, 1, 1)
            ds = (weighted - probs * jnp.sum(weighted, axis=0, keepdims=True)).astype(BF16)
            dv_h, dk_h = dot(pt, dom), dot(ds, qm)
            dv = dv_h if dv is None else dv + dv_h
            dk = dk_h if dk is None else dk + dk_h
            dqt_ref[hs, :] = (dot(kt_ref[hs, :], ds) * HEAD_DIM ** (-0.5)).astype(BF16)
        dv_ref[0, :, sl] = dv.astype(BF16)
        dk_ref[0, :, sl] = dk.astype(BF16)
        return carry

    lax.fori_loop(0, HEADS // 2, pair, 0)
    dq_ref[0] = dqt_ref[...].T


def attention_back(q, k, v, p, do):
    rows, length, width = q.shape
    row = lambda *s: pl.BlockSpec((1,) + s, lambda r: (r,) + (0,) * len(s))
    return pl.pallas_call(
        attention_back_kernel,
        grid=(rows,),
        out_shape=[struct((rows, length, width), BF16)] * 3,
        in_specs=[row(length, width)] * 3 + [row(HEADS, length, length), row(length, width)],
        out_specs=[row(length, width)] * 3,
        scratch_shapes=[pltpu.VMEM((width, length), BF16), pltpu.VMEM((width, length), BF16)],
        compiler_params=pltpu.CompilerParams(vmem_limit_bytes=VMEM_LIMIT),
    )(q, k, v, p, do)


def input_back_kernel(dpre1_ref, dq_ref, dk_ref, dv_ref, wq, wk, wv, out_ref, sums_ref):
    @pl.when(pl.program_id(0) == 0)
    def _():
        sums_ref[...] = jnp.zeros_like(sums_ref)

    sums_ref[0:1] += jnp.sum(dq_ref[...].astype(F32), axis=0, keepdims=True)
    sums_ref[1:2] += jnp.sum(dv_ref[...].astype(F32), axis=0, keepdims=True)
    total = dpre1_ref[...] + dot(dq_ref[...], wq[...], 1, 1)
    total += dot(dk_ref[...], wk[...], 1, 1) + dot(dv_ref[...], wv[...], 1, 1)
    out_ref[...] = total.astype(out_ref.dtype)


def input_back(dpre1, dq, dk, dv, wq, wk, wv, tile_rows):
    count, width = dpre1.shape
    tile = pl.BlockSpec((tile_rows, width), lambda t: (t, 0))
    full = lambda *s: pl.BlockSpec(s, lambda t: (0,) * len(s))
    return pl.pallas_call(
        input_back_kernel,
        grid=(count // tile_rows,),
        out_shape=[struct((count, width), BF16), struct((8, width), F32)],
        in_specs=[tile] * 4 + [full(width, width)] * 3,
        out_specs=[tile, full(8, width)],
        compiler_params=pltpu.CompilerParams(vmem_limit_bytes=VMEM_LIMIT),
    )(dpre1, dq, dk, dv, wq, wk, wv)


class Turned:
    def __init__(self, ref):
        self.ref = ref

    def __getitem__(self, at):
        return self.ref[at[1], at[0]]


class Gatherer:
    def __init__(self, grid, flat, partners, my, blocks, fulls, own_sem, send_sem, recv_sem):
        self.grid, self.flat, self.partners, self.my = grid, flat, partners, my
        self.blocks, self.fulls = blocks, fulls
        self.own_sem, self.send_sem, self.recv_sem = own_sem, send_sem, recv_sem

    def own(self, i):
        a, lo, ln, _ = self.flat[i]
        return pltpu.make_async_copy(
            self.blocks[a].at[:, pl.ds(lo, ln)],
            self.fulls[a].at[tuple(self.my) + (slice(None), pl.ds(lo, ln))],
            self.own_sem.at[i],
        )

    def copy(self, i, k):
        a, lo, ln, flavour = self.flat[i]
        order = self.grid.order(flavour)
        done = order[:k]
        ix = tuple(slice(None) if e in done else self.my[e] for e in range(self.grid.nd))
        dst = self.fulls[a].at[ix + (slice(None), pl.ds(lo, ln))]
        src = self.blocks[a].at[:, pl.ds(lo, ln)] if k == 0 else dst
        return remote(
            src, dst, self.send_sem.at[i, k], self.recv_sem.at[i, k], self.partners[order[k]]
        )

    def step(self, i, k):
        if k == 0:
            self.own(i).start()
        elif k == 1:
            self.own(i).wait()
        if k > 0:
            self.copy(i, k - 1).wait_recv()
        if k < self.grid.nd:
            self.copy(i, k).start()

    def finish(self):
        for i in range(len(self.flat)):
            for k in range(self.grid.nd):
                self.copy(i, k).wait_send()


def forward_kernel(grid, groups, tile_rows, *refs):
    it = iter(refs)
    take = lambda n: [next(it) for _ in range(n)]
    lens, tok = take(2)
    lens = Turned(lens)
    vectors = take(9)
    blocks = take(6)
    x_out, q_out, k_out, v_out, p_out, o_out = take(6)
    n1_out, i1_out, h1_out, act_out, slope_out, n2_out, i2_out, hid_out = take(8)
    full_out = take(7)
    pool, vecs = take(2)
    fulls = take(7)
    x_s, q_s, k_s, v_s, vt_s, mask_s, h_s, bi_s, packed = take(9)
    own_sem, send_sem, recv_sem, tok_own, tok_send, tok_recv, out_sem = take(7)

    b, sq = grid.here()
    nd, ns = grid.nd, grid.seq_size
    my = grid.digits(b, sq)
    partners = [grid.partner(b, sq, d) for d in range(nd)]
    others = [lax.rem(sq + j, ns) for j in range(1, ns)]
    flat = [c for g in groups for c in g]
    members, first = [], 0
    for g in groups:
        members.append(range(first, first + len(g)))
        first += len(g)
    packed[...] = jnp.zeros_like(packed)
    for i, u in enumerate(vectors):
        packed[i : i + 1, : u.shape[0]] = u[...].astype(F32).reshape(1, u.shape[0])
    blocks = [packed] + blocks
    ga = Gatherer(grid, flat, partners, my, blocks, fulls, own_sem, send_sem, recv_sem)
    rows, length, width = x_s.shape
    lt = length // ns
    tiles = length // tile_rows
    grid.greet(b, sq, partners, others)

    def row_copy(r, j):
        at = pl.ds(pl.multiple_of(sq * lt, lt), lt)
        if j == 0:
            return pltpu.make_async_copy(tok.at[sq * rows + r], x_s.at[r, at], tok_own.at[r])
        o = others[j - 1]
        return remote(
            tok.at[o * rows + r], x_s.at[r, at], tok_send.at[r, j - 1], tok_recv.at[r, j - 1], (b, o)
        )

    plan = forward_plan(nd, len(groups), ns)

    def run_at(point):
        for g, k in plan.get(point, ()):
            if k < 0:
                row_copy(g, -k).start()
            else:
                for i in members[g]:
                    ga.step(i, k)

    def hook(name, steps):
        def run():
            now = pl.program_id(0)
            for c in range(steps):
                if (name, c) in plan:
                    pl.when(now == c)(functools.partial(run_at, (name, c)))

        return run

    def arrived(*which):
        for g in which:
            for i in members[g]:
                ga.step(i, nd)

    out_copies = []

    def put(src, dst):
        c = pltpu.make_async_copy(src, dst, out_sem.at[len(out_copies)])
        c.start()
        out_copies.append(c)

    for r in range(rows):
        row_copy(r, 0).start()
    run_at("start")
    arrived(0, 1, 2)
    part = blocks[1].shape[0]
    wide_part = bi_s.shape[1] >> nd
    smalls = fulls[0][...].reshape((1 << nd,) + blocks[0].shape)

    def unpacked(i, size, first, lanes):
        col = lax.broadcasted_iota(jnp.int32, (1, lanes), 1) + first
        device = jnp.floor((col.astype(F32) + 0.5) * (1.0 / size)).astype(jnp.int32)
        at = lax.broadcasted_iota(jnp.int32, (128, lanes), 0)
        spread = (at == col - device * size).astype(F32).astype(BF16)
        owner = lax.broadcasted_iota(jnp.int32, (1 << nd, lanes), 0) == device
        values = dot(smalls[:, i, :].astype(BF16), spread)
        return jnp.sum(jnp.where(owner, values, 0.0), axis=0, keepdims=True)

    for i in range(8):
        vecs[i : i + 1] = unpacked(i, part, 0, width)
    for lo in range(0, bi_s.shape[1], width):
        bi_s[:, lo : lo + width] = unpacked(8, wide_part, lo, width)
    bq, bv, bo, g1, s1, bd, g2, s2 = (vecs[i : i + 1] for i in range(8))
    lane = lax.broadcasted_iota(jnp.int32, (1, 128), 1)

    def square(ref):
        return ref[...].reshape(width, width)

    for r in range(rows):
        run_at(("row", r))
        for j in range(ns):
            c = row_copy(r, j)
            if j == 0:
                c.wait()
            else:
                c.wait_recv()
        put(x_s.at[r], x_out.at[r])
        x = x_s[r]
        q_s[r] = ((dot(x, square(fulls[1])) + bq) * HEAD_DIM ** (-0.5)).astype(BF16)
        k_s[r] = dot(x, square(fulls[2])).astype(BF16)
        v = dot(x, square(fulls[3])) + bv
        v_s[r] = v.astype(BF16)
        vt_s[...] = v.T.astype(BF16)
        for src, dst in ((q_s, q_out), (k_s, k_out), (v_s, v_out)):
            put(src.at[r], dst.at[r])
        seg_k = segment_of(lens, sq * rows + r, (length, 1), 0)
        seg_q = segment_of(lens, sq * rows + r, (1, length), 1)
        mask_s[...] = jnp.where(seg_k == seg_q, 0.0, MASKED)
        att_hook = hook(("attention", r), HEADS // 2)

        def att_body(p_t, o_t, r=r):
            att_hook()
            p = pl.program_id(0)
            sl = pl.ds(pl.multiple_of(p * 128, 128), 128)
            qp, kp = q_s[r, :, sl], k_s[r, :, sl]
            out = []
            for h in range(2):
                km = jnp.where(lane // HEAD_DIM == h, kp, jnp.zeros_like(kp))
                hs = pl.ds(pl.multiple_of(p * 128 + h * HEAD_DIM, HEAD_DIM), HEAD_DIM)
                s = dot(km, qp, 1, 1) + mask_s[...]
                e = jnp.exp(s - jnp.max(s, axis=0, keepdims=True))
                pt = (e * (1.0 / jnp.sum(e, axis=0, keepdims=True))).astype(BF16)
                p_t[0, h] = pt
                out.append(dot(vt_s[hs, :], pt))
            o_t[0] = jnp.concatenate(out, axis=0).T.astype(BF16)

        pltpu.emit_pipeline(
            att_body,
            grid=(HEADS // 2,),
            out_specs=[
                pl.BlockSpec((1, 2, length, length), lambda s, r=r: (r, s, 0, 0)),
                pl.BlockSpec((1, length, 128), lambda s, r=r: (r, 0, s)),
            ],
        )(p_out, o_out)

    run_at("in")
    down_groups = width // 256
    arrived(*range(3, len(groups) - down_groups))
    for a in range(6):
        put(fulls[a], full_out[a])
    ff = bi_s.shape[1]
    tile = lambda w: pl.BlockSpec((tile_rows, w), lambda t: (t, 0))

    def tile_at():
        t = pl.program_id(0)
        start = lax.rem(t, tiles) * tile_rows
        return t // tiles, start, pl.ds(pl.multiple_of(start, tile_rows), tile_rows)

    in_hook = hook("in", rows * tiles)

    def in_body(o_t, n1_t, i1_t, h1_t, act_t, slope_t):
        in_hook()
        r, _, at = tile_at()
        pre1 = x_s[r, at].astype(F32) + dot(o_t[0], square(fulls[4])) + bo
        n1, i1 = layer_norm(pre1)
        h1 = n1 * g1 + s1
        low = h1.astype(BF16)
        h_s[r, at] = h1
        n1_t[...] = n1.astype(BF16)
        i1_t[...] = jnp.broadcast_to(i1, i1_t.shape)
        h1_t[...] = low
        for lo in range(0, ff, width):
            w = fulls[5][(slice(None),) * (nd + 1) + (slice(lo, lo + width),)]
            inner = dot(low, w.reshape(width, width)) + bi_s[:, lo : lo + width]
            phi = 0.5 + 0.5 * lax.erf(inner * (0.5**0.5))
            act_t[:, lo : lo + width] = (inner * phi).astype(BF16)
            density = jnp.exp(-0.5 * inner * inner) * 0.3989422804014327
            slope_t[:, lo : lo + width] = (phi + inner * density).astype(BF16)

    pltpu.emit_pipeline(
        in_body,
        grid=(rows * tiles,),
        in_specs=[pl.BlockSpec((1, tile_rows, width), lambda t: (t // tiles, t % tiles, 0))],
        out_specs=[tile(width), tile(128), tile(width), tile(ff), tile(ff)],
    )(o_out, n1_out, i1_out, h1_out, act_out, slope_out)

    run_at("down")
    arrived(*range(len(groups) - down_groups, len(groups)))
    put(fulls[6], full_out[6])
    pool[...] = jnp.zeros_like(pool)
    down_rows = blocks[6].shape[0]
    top = nd - ((width // down_rows).bit_length() - 1)

    def down_body(act_t, hid_t, n2_t, i2_t):
        r, start, at = tile_at()
        acc = h_s[r, at] + bd
        for c, lo in enumerate(range(0, ff, width)):
            ix = tuple((c >> (top - 1 - e)) % 2 for e in range(top))
            acc = acc + dot(act_t[:, lo : lo + width], fulls[6][ix].reshape(width, width))
        n2, i2 = layer_norm(acc)
        high, low = split_two(n2 * g2 + s2)
        hid_t[...] = high
        n2_t[...] = n2.astype(BF16)
        i2_t[...] = jnp.broadcast_to(i2, i2_t.shape)
        seg = segment_of(lens, sq * rows + r, (1, tile_rows), 1, start)
        slot = jnp.where(seg < SEGS, r * SEGS + seg, -1)
        mine = lax.broadcasted_iota(jnp.int32, (pool.shape[0], tile_rows), 0) == slot
        mine = mine.astype(F32).astype(BF16)
        pool[...] += dot(mine, high) + dot(mine, low)

    pltpu.emit_pipeline(
        down_body,
        grid=(rows * tiles,),
        in_specs=[tile(ff)],
        out_specs=[tile(width), tile(width), tile(128)],
    )(act_out, hid_out, n2_out, i2_out)

    ga.finish()
    for r in range(rows):
        for j in range(1, ns):
            row_copy(r, j).wait_send()
    for c in out_copies:
        c.wait()


FORWARD_PLAN = {
    "start": (
        (1, 0), (2, 0), (0, 0), (6, 0), (1, 1), (5, 0), (4, 0), (0, 1), (2, 1), (8, 0),
        (1, 2), (7, 0), (0, 2), (2, 2), (3, 0), (1, 3), (4, 1), (5, 1), (8, 1), (0, 3),
        (0, -2), (4, 2), (1, 4), (3, 1), (7, 1), (6, 1), (0, -3), (0, -1), (2, 3), (0, 4),
        (8, 2), (1, -1), (1, -3), (5, 2), (3, 2), (1, -2), (2, 4), (7, 2), (6, 2), (5, 3),
        (8, 3), (3, 3), (9, 0), (10, 0), (4, 3), (7, 3),
    ),
    (("attention", 0), 3): (
        (8, 4),
    ),
    ("row", 1): (
        (5, 4), (4, 4), (3, 4), (6, 3),
    ),
    (("attention", 1), 0): (
        (10, 1),
    ),
    (("attention", 1), 1): (
        (9, 1),
    ),
    (("attention", 1), 2): (
        (7, 4), (10, 2), (6, 4),
    ),
    (("attention", 1), 4): (
        (9, 2),
    ),
    (("attention", 1), 5): (
        (10, 3),
    ),
    ("in", 3): (
        (10, 4), (9, 4),
    ),
    "in": (
        (9, 3),
    ),
}
def forward_plan(nd, groups, ns):
    if nd == 5 and groups == 11 and ns == 4:
        return FORWARD_PLAN
    ops = []
    for t in range(groups + 2 * nd):
        ops += [(t - 2 * k, k) for k in range(nd - 1, -1, -1) if 0 <= t - 2 * k < groups]
        if t == nd:
            ops += [(r, -j) for r in range(2) for j in range(1, ns)]
    return {"start": tuple(ops)}


def forward(grid, lens, tokens, vectors, weights, tile_rows, collective_id):
    blocks = [struct((16, 128), F32), *weights]
    nd, ns = grid.nd, grid.seq_size
    total, lt, width = tokens.shape
    rows, length = total // ns, lt * ns
    count = rows * length
    ff = blocks[5].shape[1]
    dev = (2,) * nd
    groups = pieces([x.shape for x in blocks])
    groups = [groups[0] + groups[1]] + groups[2:]
    n = sum(len(g) for g in groups)
    seq3 = struct((rows, length, width), BF16)
    low, stat = struct((count, width), BF16), struct((count, 128), F32)
    wide = struct((count, ff), BF16)
    out_shape = [seq3] * 4 + [struct((rows, HEADS, length, length), BF16), seq3]
    out_shape += [low, stat, low, wide, wide, low, stat, low]
    out_shape += [struct(dev + x.shape, x.dtype) for x in blocks]
    out_shape += [struct((rows * SEGS, width), F32), struct((8, width), F32)]
    res = pl.pallas_call(
        functools.partial(forward_kernel, grid, groups, tile_rows),
        out_shape=out_shape,
        in_specs=[SMEM] + [VMEM] * (1 + len(vectors) + len(weights)),
        out_specs=[ANY] * (len(out_shape) - 2) + [VMEM] * 2,
        scratch_shapes=[pltpu.VMEM(dev + x.shape, x.dtype) for x in blocks]
        + [pltpu.VMEM((rows, length, width), BF16)] * 4
        + [pltpu.VMEM((width, length), BF16), pltpu.VMEM((length, length), F32)]
        + [pltpu.VMEM((rows, length, width), F32), pltpu.VMEM((1, ff), F32)]
        + [pltpu.VMEM((16, 128), F32)]
        + [DMA((n,)), DMA((n, nd)), DMA((n, nd))]
        + [DMA((rows,)), DMA((rows, ns - 1)), DMA((rows, ns - 1)), DMA((7 + 4 * rows,))],
        compiler_params=pltpu.CompilerParams(
            collective_id=collective_id, has_side_effects=True, vmem_limit_bytes=VMEM_LIMIT
        ),
    )(lens, tokens, *vectors, *weights)
    return res


class Reducer:
    def __init__(self, grid, flat, partners, my, sources, outs, send_sem, recv_sem, bufs):
        self.grid, self.flat, self.partners, self.my = grid, flat, partners, my
        self.sources, self.outs = sources, outs
        self.send_sem, self.recv_sem = send_sem, recv_sem
        self.bufs = bufs

    def buf(self, i, k):
        return self.bufs[i * self.grid.nd + k]

    def place(self, i, k):
        order = self.grid.order(self.flat[i][4])[::-1]
        free = [d for d in range(self.grid.nd) if d not in order[:k]]
        return order[k], free.index(order[k])

    def copy(self, i, k):
        a, lo, ln, _, _ = self.flat[i]
        d, pos = self.place(i, k)
        ix = (slice(None),) * pos + (1 - self.my[d],) + (slice(None),) * (self.grid.nd - k - pos - 1)
        if k == 0:
            src = self.sources[a].at[ix + (slice(None), pl.ds(lo, ln))]
        else:
            src = self.buf(i, k - 1).at[ix]
        return remote(
            src, self.buf(i, k), self.send_sem.at[i, k], self.recv_sem.at[i, k], self.partners[d]
        )

    def add(self, i, k):
        nd = self.grid.nd
        a, lo, ln, out_lo, _ = self.flat[i]
        d, pos = self.place(i, k)
        self.copy(i, k).wait_recv()
        into = self.buf(i, k)
        left = nd - k - 1
        if left == 0:
            total = self.buf(i, k - 1)[self.my[d]].astype(F32) + into[...].astype(F32)
            out, at = self.outs[i]
            out[:, at : at + ln] = total
            return

        def one(j, carry):
            ix = tuple((j // (1 << (left - 1 - e))) % 2 for e in range(left))
            mine_at = ix[:pos] + (self.my[d],) + ix[pos:]
            if k == 0:
                mine = self.sources[a][mine_at + (slice(None), slice(lo, lo + ln))]
            else:
                mine = self.buf(i, k - 1)[mine_at]
            into[ix] = (mine.astype(F32) + into[ix].astype(F32)).astype(into.dtype)
            return carry

        lax.fori_loop(0, 1 << left, one, 0)

    def step(self, i, k):
        if k > 0:
            self.add(i, k - 1)
        if k < self.grid.nd:
            self.copy(i, k).start()

    def sent(self, i, k):
        self.copy(i, k).wait_send()


SMALL_ROWS = 16
ROW_BQ, ROW_BV, ROW_BO, ROW_G1, ROW_S1, ROW_BD, ROW_G2, ROW_S2, ROW_BI = range(9)
EMB_PAD = 128


def backward_kernel(grid, flat, groups, n_bufs, tile_rows, *refs):
    it = iter(refs)
    take = lambda n: [next(it) for _ in range(n)]
    lens, pairs, vecs, pool = take(4)
    lens = Turned(lens)
    n2, i2, slope, n1, i1, act, h1, o, q, k, v, p, x, hid = take(14)
    weights = take(6)
    g_in, g_down, g_out, g_query, g_key, g_value = take(6)
    small, loss, hid_back, gx_back = take(4)
    wd, wi, wo, wq, wk, wv = take(6)
    big1, big2, t_h1, t_o, t_feed, t_br, t_att, i1_s, i2_s, p_s = take(10)
    small_recv, emb, dp = take(3)
    send_sem, recv_sem, ex_own, ex_send, ex_recv, load_sem, p_sem, sm_send, sm_recv = take(9)
    emb_send, emb_recv = take(2)
    bufs = take(n_bufs)

    b, sq = grid.here()
    nd, ns = grid.nd, grid.seq_size
    my = grid.digits(b, sq)
    partners = [grid.partner(b, sq, d) for d in range(nd)]
    others = [lax.rem(sq + j, ns) for j in range(1, ns)]
    rows, length, width = x.shape
    count = rows * length
    ff = big1.shape[1]
    chunks = ff // width
    lt = length // ns
    tiles = length // tile_rows
    base = sq * rows
    row_at = lambda r: pl.ds(r * length, length)
    lanes = lambda c: pl.ds(c * width, width)

    loads = []

    def load(src, dst):
        c = pltpu.make_async_copy(src, dst, load_sem.at[len(loads)])
        c.start()
        loads.append(c)
        return c

    first = [load(s, d) for s, d in zip(weights[:3], (wd, wi, wo), strict=True)]
    first += [load(s, d) for s, d in ((n2, t_att), (i2, i2_s), (slope, big1), (n1, t_br), (i1, i1_s))]
    second = [load(h1, t_h1), load(act, big2)]
    second += [load(o.at[r], t_o.at[row_at(r)]) for r in range(rows)]
    third = [load(s, d) for s, d in zip(weights[3:], (wq, wk, wv), strict=True)]
    grid.greet(b, sq, partners, others)

    def row_back(e, src, dst, r, j):
        o_ = sq if j == 0 else others[j - 1]
        start = pl.multiple_of(o_ * lt, lt)
        if e == 0:
            part = src.at[r, pl.ds(start, lt)]
        else:
            part = src.at[pl.ds(r * length + start, lt)]
        into = dst.at[sq * rows + r]
        if j == 0:
            return pltpu.make_async_copy(part, into, ex_own.at[e, r])
        return remote(part, into, ex_send.at[e, r, j - 1], ex_recv.at[e, r, j - 1], (b, o_))

    backs = ((hid, hid_back), (t_feed, gx_back))

    own_rows = rows * SEGS
    total_rows = own_rows << nd
    at_row = lax.broadcasted_iota(jnp.int32, (own_rows, 1), 0)
    len_col = jnp.ones((own_rows, 1), F32)
    pair_col = jnp.full((own_rows, 1), -1, jnp.int32)
    for r in range(rows):
        for s in range(SEGS):
            here = at_row == r * SEGS + s
            len_col = jnp.where(here, lens[base + r, s].astype(F32), len_col)
            if s < NQ:
                pair_col = jnp.where(here, pairs[r * NQ + s], pair_col)
    avg = pool[...] / len_col
    inv = lax.rsqrt(jnp.sum(avg * avg, axis=-1, keepdims=True) + NORM_EPSILON)
    own = avg * inv
    emb[tuple(my) + (slice(None), slice(0, width))] = own
    emb[tuple(my) + (slice(None), slice(width, width + EMB_PAD))] = jnp.broadcast_to(
        pair_col.astype(F32), (own_rows, EMB_PAD)
    )
    half = width // 2
    emb_pieces = ((0, half, 0), (half, width + EMB_PAD - half, 1))

    def emb_copy(f, kk):
        lo, ln, flavour = emb_pieces[f]
        order = grid.order(flavour)
        ix = tuple(slice(None) if e in order[:kk] else my[e] for e in range(nd))
        ref = emb.at[ix + (slice(None), pl.ds(lo, ln))]
        return remote(ref, ref, emb_send.at[f, kk], emb_recv.at[f, kk], partners[order[kk]])

    for kk in range(nd):
        for f in range(2):
            if kk > 0:
                emb_copy(f, kk - 1).wait_recv()
            emb_copy(f, kk).start()
        if kk == grid.ks:
            for r in range(rows):
                for j in range(ns):
                    row_back(0, *backs[0], r, j).start()
    for f in range(2):
        emb_copy(f, nd - 1).wait_recv()
    every = emb[...].reshape(total_rows, width + EMB_PAD)
    high, low = split_two(every[:, :width])
    pair_row = every[:, width:].T[:1].astype(jnp.int32)
    own_high, own_low = split_two(own)
    scale = 1.0 / TEMPERATURE

    def product(ah, al, bh, bl, cb):
        return dot(ah, bh, 1, cb) + dot(ah, bl, 1, cb) + dot(al, bh, 1, cb)

    total = jnp.zeros((1, total_rows), F32)
    block = min(total_rows, 256)
    for lo in range(0, total_rows, block):
        sim = product(high[lo : lo + block], low[lo : lo + block], high, low, 1) * scale
        at = lax.broadcasted_iota(jnp.int32, (block, 1), 0)
        total += jnp.sum(jnp.where(at % SEGS >= NQ, jnp.exp(sim - scale), 0.0), axis=0, keepdims=True)
    lse_cols = scale + jnp.log(total)
    sim = product(own_high, own_low, high, low, 1) * scale
    col = lax.broadcasted_iota(jnp.int32, (1, total_rows), 1)
    row = at_row + (b * ns + sq) * own_rows
    col_doc, row_doc = col % SEGS >= NQ, row % SEGS >= NQ
    number = lambda at: (at // SEGS) * NQ + at % SEGS - NQ
    lse_rows = scale + jnp.log(
        jnp.sum(jnp.where(col_doc, jnp.exp(sim - scale), 0.0), axis=1, keepdims=True)
    )
    chosen = col_doc & (number(col) == pair_col)
    positive = jnp.sum(jnp.where(chosen, sim, 0.0), axis=1, keepdims=True)
    loss[...] = jnp.broadcast_to(lse_rows - positive, loss.shape)
    as_query = jnp.exp(sim - lse_rows) - chosen.astype(F32)
    chosen_by = number(row) == pair_row
    as_doc = jnp.exp(jnp.where(col_doc, MASKED, sim - lse_cols)) - chosen_by.astype(F32)
    grad = jnp.where(row_doc, jnp.where(col_doc, 0.0, as_doc), jnp.where(col_doc, as_query, 0.0))
    grad_high, grad_low = split_two(grad)
    demb = product(grad_high, grad_low, high, low, 0) * scale
    dpool = inv * demb - inv * inv * inv * avg * jnp.sum(avg * demb, axis=-1, keepdims=True)
    dpool_high, dpool_low = split_two(dpool / len_col)
    pad = jnp.zeros((64 - own_rows, width), F32)
    stacked = jnp.concatenate([dpool_high.astype(F32), pad, dpool_low.astype(F32), pad], axis=0)
    dp[...] = stacked.astype(BF16)

    members, at = [], 0
    for g in groups:
        members.append(range(at, at + len(g)))
        at += len(g)
    square_outs = {2: g_out}
    outs = {}
    late = len(groups) - 3
    for g, ix in enumerate(members):
        for i in ix:
            a, _, _, out_lo, _ = flat[i]
            if g >= late:
                out = (g_query, g_key, g_value)[g - late]
            else:
                out = (g_in, g_down, g_out)[a]
            outs[i] = (out, out_lo)
    red = Reducer(grid, flat, partners, my, (wi, wd, wo), outs, send_sem, recv_sem, bufs)
    plan = backward_plan(nd, len(groups), rows, ns)
    small_order = grid.order(0)[::-1]

    def small_copy(kk):
        return remote(
            small, small_recv.at[kk], sm_send.at[kk], sm_recv.at[kk], partners[small_order[kk]]
        )

    def run_at(point):
        for kind, *what in plan.get(point, ()):
            if kind == "g":
                g, kk = what
                for i in members[g]:
                    red.step(i, kk)
            elif kind == "x":
                r, j = what
                row_back(1, *backs[1], r, j).start()
            else:
                (kk,) = what
                if kk > 0:
                    small_copy(kk - 1).wait()
                    small[...] += small_recv[kk - 1]
                if kk < nd:
                    small_copy(kk).start()

    def run_in(name, now, steps):
        for c in range(steps):
            if (name, c) in plan:
                pl.when(now == c)(functools.partial(run_at, (name, c)))

    def columns(u):
        return jnp.sum(u, axis=0, keepdims=True)

    def norm_back(g, n, inv_std):
        return inv_std * (
            g - jnp.mean(g, axis=-1, keepdims=True) - n * jnp.mean(g * n, axis=-1, keepdims=True)
        )

    for c in first:
        c.wait()
    small[...] = jnp.zeros_like(small)
    g1, g2 = vecs[ROW_G1 : ROW_G1 + 1], vecs[ROW_G2 : ROW_G2 + 1]
    down_rows = wd.shape[-2]
    low_digits = (width // down_rows).bit_length() - 1
    top = nd - low_digits
    down_ix = lambda c: tuple((c >> (top - 1 - e)) % 2 for e in range(top))
    dev = (slice(None),) * (nd + 1)

    def bump(at, u):
        small[at : at + 1] += u

    def feed_tile(t, carry):
        r = t // tiles
        start = lax.rem(t, tiles) * tile_rows
        at = pl.ds(pl.multiple_of(t * tile_rows, tile_rows), tile_rows)
        seg = segment_of(lens, base + r, (tile_rows, 1), 0, start)
        place = jnp.where(seg < SEGS, r * SEGS + seg, -1)
        lane = lax.broadcasted_iota(jnp.int32, (tile_rows, 128), 1)
        mine = (lane % 64 == place).astype(F32).astype(BF16)
        dh2 = dot(mine, dp[...])
        m2 = t_att[at].astype(F32)
        bump(ROW_G2, columns(dh2 * m2))
        bump(ROW_S2, columns(dh2))
        dpre2 = norm_back(dh2 * g2, m2, i2_s[at, :1])
        dfeed = dpre2.astype(BF16)
        t_feed[at] = dfeed
        bump(ROW_BD, columns(dfeed.astype(F32)))
        dh1 = dpre2
        for c in range(chunks):
            w = wd[down_ix(c)].reshape(width, width)
            din = (dot(dfeed, w, 1, 1) * big1[at, lanes(c)].astype(F32)).astype(BF16)
            big1[at, lanes(c)] = din
            bump(ROW_BI + c, columns(din.astype(F32)))
            dh1 = dh1 + dot(din, wi[dev + (lanes(c),)].reshape(width, width), 1, 1)
        m1 = t_br[at].astype(F32)
        bump(ROW_G1, columns(dh1 * m1))
        bump(ROW_S1, columns(dh1))
        dbranch = norm_back(dh1 * g1, m1, i1_s[at, :1]).astype(BF16)
        t_br[at] = dbranch
        bump(ROW_BO, columns(dbranch.astype(F32)))
        t_att[at] = dot(dbranch, wo[...].reshape(width, width), 1, 1).astype(BF16)
        return carry

    lax.fori_loop(0, rows * tiles, feed_tile, 0)

    square = (2,) * nd + wo.shape[-2:]

    def outer(lhs, rhs):
        return dot(lhs, rhs, 0, 0)

    for c in second:
        c.wait()
    for c in range(chunks):
        run_at(("in", c))
        wi[dev + (lanes(c),)] = outer(t_h1[...], big1[:, lanes(c)]).reshape(square).astype(BF16)
    fourth = []
    for r in range(rows):
        fourth += [load(s.at[r], big1.at[row_at(r), lanes(c)]) for c, s in enumerate((q, k, v))]
        fourth.append(load(x.at[r], t_h1.at[row_at(r)]))
    for c in range(chunks):
        run_at(("down", c))
        res = outer(big2[:, lanes(c)], t_feed[...])
        wd[down_ix(c)] = res.reshape((2,) * low_digits + (down_rows, width)).astype(BF16)
    run_at("out")
    wo[...] = outer(t_o[...], t_br[...]).reshape(square).astype(BF16)

    n_pairs = HEADS // 2
    slots = p_s.shape[0]

    def probs_copy(s):
        slot = lax.rem(s, slots)
        pair = pl.ds(lax.rem(s, n_pairs) * 2, 2)
        return pltpu.make_async_copy(p.at[s // n_pairs, pair], p_s.at[slot], p_sem.at[slot])

    for s in range(slots - 1):
        probs_copy(s).start()
    for c in fourth:
        c.wait()
    for c in third:
        c.wait()
    lane = lax.broadcasted_iota(jnp.int32, (1, 128), 1)

    for r in range(rows):

        def pair_step(s, carry, r=r):
            run_in(("attention", r), s, n_pairs)
            g = r * n_pairs + s
            probs_copy(g).wait()

            @pl.when(g + slots - 1 < rows * n_pairs)
            def _():
                probs_copy(g + slots - 1).start()

            slot = lax.rem(g, slots)
            at = lambda c: pl.ds(pl.multiple_of(c * width + s * 128, 128), 128)
            qp, kp, vp = (big1[row_at(r), at(c)] for c in range(3))
            dop = t_att[row_at(r), at(0)]
            kt = kp.T
            zero = jnp.zeros_like(vp)
            dv = dk = None
            dqt = []
            for h in range(2):
                mine = lane // HEAD_DIM == h
                vm, dom, qm = (jnp.where(mine, u, zero) for u in (vp, dop, qp))
                pt = p_s[slot, h]
                probs = pt.astype(F32)
                weighted = probs * dot(vm, dop, 1, 1)
                ds = (weighted - probs * jnp.sum(weighted, axis=0, keepdims=True)).astype(BF16)
                dv_h, dk_h = dot(pt, dom), dot(ds, qm)
                dv = dv_h if dv is None else dv + dv_h
                dk = dk_h if dk is None else dk + dk_h
                dqt.append(dot(kt[h * HEAD_DIM : (h + 1) * HEAD_DIM], ds) * HEAD_DIM ** (-0.5))
            big2[row_at(r), at(0)] = jnp.concatenate(dqt, axis=0).T.astype(BF16)
            big2[row_at(r), at(1)] = dk.astype(BF16)
            big2[row_at(r), at(2)] = dv.astype(BF16)
            return carry

        lax.fori_loop(0, n_pairs, pair_step, 0)
        run_at(("input", r))
        dq, dk, dv = (big2[row_at(r), lanes(c)] for c in range(3))
        bump(ROW_BQ, columns(dq.astype(F32)))
        bump(ROW_BV, columns(dv.astype(F32)))
        gx = t_br[row_at(r)].astype(F32)
        for d, w in ((dq, wq), (dk, wk), (dv, wv)):
            gx = gx + dot(d, w[...].reshape(width, width), 1, 1)
        t_feed[row_at(r)] = gx.astype(BF16)
        row_back(1, *backs[1], r, 0).start()

    for c in range(3):
        run_at(("projection", c))
        for i in members[c]:
            red.sent(i, 0)
        wi[dev + (lanes(c),)] = outer(t_h1[...], big2[:, lanes(c)]).reshape(square).astype(BF16)
    run_at("end")

    for g, ix in enumerate(members):
        for i in ix:
            for kk in range(nd):
                if not (kk == 0 and g < 3):
                    red.sent(i, kk)
    for f in range(2):
        for kk in range(nd):
            emb_copy(f, kk).wait_send()
    for r in range(rows):
        for e, (src, dst) in enumerate(backs):
            for j in range(ns):
                row_back(e, src, dst, r, j).wait()


BACKWARD_PLAN = {
    ("in", 3): (
        ("g", 2, 0),
    ),
    ("down", 3): (
        ("g", 0, 0), ("g", 1, 0),
    ),
    (("attention", 0), 0): (
        ("g", 5, 0), ("g", 1, 1),
    ),
    (("attention", 0), 2): (
        ("g", 0, 1),
    ),
    (("attention", 0), 3): (
        ("g", 1, 2),
    ),
    (("attention", 0), 4): (
        ("g", 5, 1),
    ),
    (("attention", 0), 5): (
        ("g", 0, 2),
    ),
    ("input", 0): (
        ("g", 1, 3),
    ),
    (("attention", 1), 0): (
        ("x", 0, 3), ("g", 7, 0), ("g", 2, 1), ("g", 0, 3), ("g", 3, 0), ("g", 1, 4),
    ),
    (("attention", 1), 1): (
        ("g", 7, 1), ("x", 0, 2),
    ),
    (("attention", 1), 2): (
        ("g", 5, 2), ("g", 2, 2), ("g", 6, 0), ("g", 4, 0),
    ),
    (("attention", 1), 3): (
        ("g", 3, 1), ("g", 0, 4), ("x", 0, 1),
    ),
    (("attention", 1), 5): (
        ("g", 4, 1),
    ),
    ("input", 1): (
        ("g", 5, 3), ("g", 2, 3), ("g", 6, 1),
    ),
    ("projection", 0): (
        ("x", 1, 2), ("g", 7, 2), ("s", 0), ("x", 1, 1),
    ),
    ("projection", 1): (
        ("g", 4, 2), ("g", 1, 5),
    ),
    ("projection", 2): (
        ("g", 8, 0), ("g", 3, 2), ("x", 1, 3), ("g", 2, 4),
    ),
    "end": (
        ("s", 1), ("g", 8, 1), ("g", 7, 3), ("g", 4, 3), ("g", 10, 0), ("s", 2), ("g", 10, 1),
        ("g", 3, 3), ("s", 3), ("g", 9, 0), ("g", 6, 2), ("g", 0, 5), ("g", 10, 2), ("g", 9, 1),
        ("g", 7, 4), ("g", 4, 4), ("g", 3, 4), ("s", 4), ("g", 8, 2), ("g", 10, 3), ("g", 5, 4),
        ("g", 7, 5), ("g", 9, 2), ("g", 4, 5), ("g", 6, 3), ("g", 8, 3), ("g", 2, 5), ("g", 10, 4),
        ("g", 9, 3), ("g", 6, 4), ("g", 5, 5), ("g", 3, 5), ("g", 8, 4), ("g", 9, 4), ("g", 10, 5),
        ("s", 5), ("g", 6, 5), ("g", 8, 5), ("g", 9, 5),
    ),
}


def backward_plan(nd, groups, rows, ns):
    if nd == 5 and groups == 11 and rows == 2 and ns == 4:
        return BACKWARD_PLAN
    late = groups - 3
    ops = [("g", g, k) for k in range(nd + 1) for g in range(late)]
    ops += [("x", r, j) for r in range(rows) for j in range(1, ns)]
    ops += [("s", k) for k in range(nd + 1)]
    plan = {("projection", 0): tuple(ops)}
    plan["end"] = tuple(("g", g, k) for k in range(nd + 1) for g in range(late, groups))
    return plan


def backward(grid, lens, pairs, vecs, pool, kept, weights, tile_rows, collective_id):
    nd, ns = grid.nd, grid.seq_size
    x = kept[-2]
    rows, length, width = x.shape
    count = rows * length
    ff = weights[1].shape[-1]
    part, down_part = weights[1].shape[-2], weights[0].shape[-2]
    groups = []
    half = width // 2
    for c in range(ff // width):
        groups.append([(0, c * width + f * half, half, c * width + f * half, f) for f in range(2)])
    for lo in range(0, width, 256):
        groups.append([(1, lo + f * 128, 128, lo + f * 128, f) for f in range(2)])
    groups.append([(2, f * half, half, f * half, f) for f in range(2)])
    for c in range(3):
        groups.append([(0, c * width + f * half, half, f * half, f) for f in range(2)])
    flat = [c for g in groups for c in g]
    n = len(flat)
    bufs = []
    for a, _, ln, _, _ in flat:
        shape = ((down_part if a == 1 else part), ln)
        bufs += [pltpu.VMEM((2,) * (nd - 1 - kk) + shape, BF16) for kk in range(nd)]
    back = struct((rows * ns, length // ns, width), BF16)
    out_shape = [struct((part, ff), F32), struct((down_part, width), F32)]
    out_shape += [struct((part, width), F32)] * 4
    out_shape += [struct((SMALL_ROWS, width), F32), struct((rows * SEGS, 128), F32), back, back]
    low, wide = pltpu.VMEM((count, width), BF16), pltpu.VMEM((count, ff), BF16)
    stat = pltpu.VMEM((count, 128), F32)
    n_loads = 10 + rows + 3 + 4 * rows
    return pl.pallas_call(
        functools.partial(backward_kernel, grid, flat, groups, len(bufs), tile_rows),
        out_shape=out_shape,
        in_specs=[SMEM, SMEM, VMEM, VMEM] + [ANY] * (len(kept) + len(weights)),
        out_specs=[VMEM] * 8 + [ANY] * 2,
        scratch_shapes=[pltpu.VMEM(w.shape, BF16) for w in weights]
        + [wide, wide, low, low, low, low, low, stat, stat]
        + [pltpu.VMEM((3, 2, length, length), BF16)]
        + [pltpu.VMEM((nd, SMALL_ROWS, width), F32)]
        + [pltpu.VMEM((2,) * nd + (rows * SEGS, width + EMB_PAD), F32), pltpu.VMEM((128, width), BF16)]
        + [DMA((n, nd)), DMA((n, nd))]
        + [DMA((2, rows)), DMA((2, rows, ns - 1)), DMA((2, rows, ns - 1))]
        + [DMA((n_loads,)), DMA((3,)), DMA((nd,)), DMA((nd,)), DMA((2, nd)), DMA((2, nd))]
        + bufs,
        compiler_params=pltpu.CompilerParams(
            collective_id=collective_id, has_side_effects=True, vmem_limit_bytes=BACK_VMEM
        ),
    )(lens, pairs, vecs, pool, *kept, *weights)


BACK_VMEM = 63 * 2**20


def finish_kernel(grid, gx_ref, hid_ref, small_ref, loss_ref, *refs):
    n = 6
    gx_out, hid_out, loss_out, wide_out = refs[n : n + 4]
    vec_outs, outs = refs[n + 4 : n + 12], refs[n + 12 :]
    gx_out[...] = gx_ref[...].astype(F32)
    hid_out[...] = hid_ref[...]

    @pl.when(pl.program_id(0) == 0)
    def _():
        for src, dst in zip(refs[:n], outs, strict=True):
            dst[...] = src[...]
        number = loss_out.shape[0]
        lane = lax.broadcasted_iota(jnp.int32, (1, 128), 1)
        at = lax.broadcasted_iota(jnp.int32, (loss_ref.shape[0], 1), 0)
        mine = at == (lane // NQ) * SEGS + lane % NQ
        row = jnp.sum(jnp.where(mine, loss_ref[...], 0.0), axis=0, keepdims=True)
        loss_out[...] = row[:, :number].reshape(number)
        b, q = grid.here()
        me = b * grid.seq_size + q
        sums = small_ref[...]
        width = sums.shape[1]
        part, wide = vec_outs[0].shape[0], wide_out.shape[0]

        def pick(first, lanes):
            at = lax.broadcasted_iota(jnp.int32, (width, lanes), 0)
            lane = lax.broadcasted_iota(jnp.int32, (width, lanes), 1)
            chosen = (at - first == lane).astype(F32).astype(BF16)
            out, rest = jnp.zeros((sums.shape[0], lanes), F32), sums
            for _ in range(3):
                top = rest.astype(BF16)
                out += dot(top, chosen)
                rest = rest - top.astype(F32)
            return out

        own = pick(me * part, 128)
        for i, out in enumerate(vec_outs):
            out[...] = own[i : i + 1, :part].reshape(part)
        own = pick(lax.rem(me * wide, width), -(-wide // 128) * 128)
        at = lax.broadcasted_iota(jnp.int32, (sums.shape[0], 1), 0)
        own = jnp.where(at == ROW_BI + (me * wide) // width, own, 0.0)
        wide_out[...] = jnp.sum(own, axis=0, keepdims=True)[:, :wide].reshape(wide)


def finish(grid, gx, hid, small, loss, grads):
    rows, lt, width = gx.shape
    wide = grads[0].shape[1] >> grid.nd
    step = rows // 2
    row = pl.BlockSpec((step, lt, width), lambda r: (r, 0, 0))
    full = lambda a: pl.BlockSpec(a.shape, lambda r: (0,) * len(a.shape))
    extra = [struct((loss.shape[0] // SEGS * NQ,), F32), struct((wide,), F32)]
    extra += [struct((width >> grid.nd,), F32)] * 8
    same = [struct(g.shape, F32) for g in grads]
    return pl.pallas_call(
        functools.partial(finish_kernel, grid),
        grid=(rows // step,),
        out_shape=[struct(gx.shape, F32), struct(hid.shape, BF16)] + extra + same,
        in_specs=[row, row, full(small), full(loss)] + [full(g) for g in grads],
        out_specs=[row, row] + [full(e) for e in extra] + [full(g) for g in grads],
        compiler_params=pltpu.CompilerParams(vmem_limit_bytes=VMEM_LIMIT),
    )(gx, hid, small, loss, *grads)


def pack_small(vectors, wide, extra):
    rows = [jnp.pad(v.astype(F32), (0, 128 - v.shape[0])) for v in (*vectors, wide, extra)]
    rows += [jnp.zeros((128,), F32)] * (16 - len(rows))
    return jnp.stack(rows)


def per_device(
    tokens, lengths, pair_ids, w_query, b_query, w_key, w_value, b_value, w_out, b_out,
    norm1_gain, norm1_bias, w_in, b_in, w_down, b_down, norm2_gain, norm2_bias,
):
    blk_size, seq_size = lax.axis_size("blk"), lax.axis_size("seq")
    grid = Grid(blk_size, seq_size)
    devices = blk_size * seq_size
    group_rows, local_len, width = tokens.shape
    rows = group_rows // seq_size
    length = local_len * seq_size
    count = rows * length
    ff = w_in.shape[1]
    part, wide_part, pairs = b_query.shape[0], b_in.shape[0], pair_ids.shape[0]

    vectors = (b_query, b_value, b_out, norm1_gain, norm1_bias, b_down, norm2_gain, norm2_bias)
    if part % 8 == 0:
        res = forward(
            grid, lengths.T, tokens, vectors + (b_in,),
            (w_query, w_key, w_value, w_out, w_in, w_down), 256, 4,
        )
        x, q, k, v, p, o, n1, i1, h1, act, slope, n2, i2, hid = res[:14]
        wq, wk, wv, wo, wi, wd = res[15:21]
        pool, vecs = res[21:]
        kept = (n2, i2, slope, n1, i1, act, h1, o, q, k, v, p, x, hid.reshape(x.shape))
        weights = (wd, wi, wo, wq, wk, wv)
        res = backward(grid, lengths.T, pair_ids, vecs, pool, kept, weights, min(512, length), 3)
        sums, losses, hid_back, gx_back = res[6:]
        out = finish(grid, gx_back, hid_back, sums, losses, res[:6])
        grad_tokens, hidden_out, query_loss, g_wide = out[:4]
        gv, grads = out[4:12], out[12:]
        g_in, g_down, g_out, g_query, g_key, g_value = grads
        return (
            hidden_out, query_loss, grad_tokens, g_query, gv[0], g_key, g_value, gv[1],
            g_out, gv[2], gv[3], gv[4], g_in, g_wide, g_down, gv[5], gv[6], gv[7],
        )

    lens = lax.dynamic_slice_in_dim(lengths, lax.axis_index("seq") * rows, rows, 0)
    small = pack_small(vectors, b_in, pair_ids)
    full, x = gather_all(grid, (w_query, w_key, w_value, small, w_out, w_in, w_down), tokens, 1)
    wq, wk, wv, smalls, wo, wi, wd = full
    smalls = smalls.reshape(devices, 16, 128)
    vecs = smalls[:, : len(vectors), :part].transpose(1, 0, 2).reshape(len(vectors), 1, width)
    bq, bv, bo, g1, s1, bd, g2, s2 = (vecs[i] for i in range(len(vectors)))
    bi = smalls[:, len(vectors), :wide_part].reshape(1, ff)

    q, k, v, p, o = attention(lens, x, wq, wk, wv, bq, bv)
    x2, o2 = x.reshape(count, width), o.reshape(count, width)
    hid, n1, i1, h1, act, slope, n2, i2, pool = feed(
        lens, x2, o2, wo, bo, g1, s1, wi, bi, wd, bd, g2, s2, 256
    )
    all_pairs = smalls[:, len(vectors) + 1, :pairs].reshape(-1, NQ).astype(jnp.int32)

    none = jnp.full((all_pairs.shape[0], SEGS - NQ), -1, jnp.int32)
    pair_row = jnp.concatenate([all_pairs, none], axis=1).reshape(1, -1)
    own_pairs = jnp.concatenate([pair_ids.reshape(rows, NQ), none[:rows]], axis=1).reshape(-1, 1)
    pair_col = jnp.broadcast_to(own_pairs, (rows * SEGS, 128))
    len_col = jnp.broadcast_to(lens.reshape(-1, 1).astype(F32), (rows * SEGS, 128))
    losses, dpool = contrast(grid, pool, len_col, pair_col, pair_row, 2)
    query_loss = losses[:, 0].reshape(rows, SEGS)[:, :NQ].reshape(-1)

    dfeed, dinner, dbranch, dpre1, datt, sums, wide_sums = feed_back(
        lens, dpool, n2, i2, slope, n1, i1, wd, wi, wo, g2, g1, 256
    )
    grad_w_down = outer(act, dfeed, width, width)
    grad_w_in = outer(h1, dinner, width, width)
    grad_w_out = outer(o2, dbranch, width, width)
    dq, dk, dv = attention_back(q, k, v, p, datt.reshape(rows, length, width))
    dq, dk, dv = (d.reshape(count, width) for d in (dq, dk, dv))
    grad_x, sums_in = input_back(dpre1, dq, dk, dv, wq, wk, wv, 256)
    grad_w_query = outer(x2, dq, width, width)
    grad_w_key = outer(x2, dk, width, width)
    grad_w_value = outer(x2, dv, width, width)

    vec_grads = jnp.stack(
        [sums_in[0], sums_in[1], sums[5], sums[3], sums[4], sums[2], sums[0], sums[1]]
    )
    packed = jnp.pad(
        vec_grads.reshape(8, devices, part).transpose(1, 0, 2), ((0, 0), (0, 0), (0, 128 - part))
    )
    wide_grads = jnp.pad(
        wide_sums[0].reshape(devices, 1, wide_part), ((0, 0), (0, 7), (0, 128 - wide_part))
    )
    packed = jnp.concatenate([packed, wide_grads], axis=1).reshape(devices * 16, 128)
    grads, back = scatter_all(
        grid,
        (grad_w_down, grad_w_in, grad_w_out, packed, grad_w_query, grad_w_key, grad_w_value),
        (hid.reshape(rows, length, width), grad_x.reshape(rows, length, width)),
        3,
    )
    g_down, g_in, g_out, g_small, g_query, g_key, g_value = grads
    hidden_out, grad_tokens = back
    gv = [g_small[i, :part] for i in range(8)]
    return (
        hidden_out,
        query_loss,
        grad_tokens.astype(F32),
        g_query,
        gv[0],
        g_key,
        g_value,
        gv[1],
        g_out,
        gv[2],
        gv[3],
        gv[4],
        g_in,
        g_small[8, :wide_part],
        g_down,
        gv[5],
        gv[6],
        gv[7],
    )


def solution(mesh):
    both = ("blk", "seq")
    vec, mat, tok = P(both), P(both, None), P("blk", "seq", None)
    in_specs = (
        tok, P("blk", None), vec, mat, vec, mat, mat, vec, mat, vec, vec, vec, mat, vec, mat, vec,
        vec, vec,
    )
    out_specs = (
        tok, vec, tok, mat, vec, mat, mat, vec, mat, vec, vec, vec, mat, vec, mat, vec, vec, vec,
    )
    return jax.shard_map(
        per_device, mesh=mesh, in_specs=in_specs, out_specs=out_specs, check_vma=False
    )
```

```python
import functools

import jax
import jax.numpy as jnp
from jax import lax
from jax.experimental import pallas as pl
from jax.experimental.pallas import tpu as pltpu
from jax.sharding import PartitionSpec as P

HEADS = 12
HEAD_DIM = 64
NQ = 2
SEGS = 4
TEMPERATURE = 0.05
NORM_EPSILON = 1e-06
MASKED = -1000000000.0
BF16 = jnp.bfloat16
F32 = jnp.float32
MESH = pl.DeviceIdType.MESH
ANY = pl.BlockSpec(memory_space=pl.ANY)
VMEM = pl.BlockSpec(memory_space=pltpu.VMEM)
SMEM = pl.BlockSpec(memory_space=pltpu.SMEM)
DMA = pltpu.SemaphoreType.DMA
VMEM_LIMIT = 60 * 2**20


def dot(a, b, ca=1, cb=0):
    return lax.dot_general(a, b, (((ca,), (cb,)), ((), ())), preferred_element_type=F32)


def struct(shape, dtype):
    return jax.ShapeDtypeStruct(shape, dtype)


def split_two(v):
    high = v.astype(BF16)
    return high, (v - high.astype(F32)).astype(BF16)


class Grid:
    def __init__(self, blk_size, seq_size):
        self.blk_size, self.seq_size = blk_size, seq_size
        self.kb = blk_size.bit_length() - 1
        self.ks = seq_size.bit_length() - 1
        assert 1 << self.kb == blk_size and 1 << self.ks == seq_size
        self.nd = self.kb + self.ks

    def here(self):
        return lax.axis_index("blk"), lax.axis_index("seq")

    def digit(self, b, q, d):
        if d < self.kb:
            w = 1 << (self.kb - 1 - d)
            return (b // w) % 2, w
        w = 1 << (self.nd - 1 - d)
        return (q // w) % 2, w

    def digits(self, b, q):
        return [self.digit(b, q, d)[0] for d in range(self.nd)]

    def partner(self, b, q, d):
        v, w = self.digit(b, q, d)
        if d < self.kb:
            return (b + (1 - 2 * v) * w, q)
        return (b, q + (1 - 2 * v) * w)

    def order(self, flavour):
        seq = list(range(self.kb, self.nd))
        head, last = list(range(self.kb))[:-1][::-1], [self.kb - 1]
        if head:
            r = flavour % len(head)
            head = head[r:] + head[:r]
        return seq + head + last

    def greet(self, b, q, partners, others):
        barrier = pltpu.get_barrier_semaphore()
        targets = [partners[d] for d in range(self.kb)]
        if others is None:
            targets += [partners[d] for d in range(self.kb, self.nd)]
        else:
            targets += [(b, o) for o in others]
        for t in targets:
            pl.semaphore_signal(barrier, inc=1, device_id=t, device_id_type=MESH)
        pl.semaphore_wait(barrier, len(targets))


def remote(src, dst, send, recv, where):
    return pltpu.make_async_remote_copy(
        src_ref=src, dst_ref=dst, send_sem=send, recv_sem=recv, device_id=where, device_id_type=MESH
    )


def flat_view(rows, lanes):
    if rows % 8 == 0:
        return rows, lanes
    return rows * lanes // 128, 128


def pieces(shapes):
    out = []
    for a, (rows, lanes) in enumerate(shapes):
        unit = 768 if rows < 64 else 256
        unit = min(unit, lanes)
        for lo in range(0, lanes, unit):
            half = unit // 2
            if half % 128 == 0:
                out.append([(a, lo, half, 0), (a, lo + half, half, 1)])
            else:
                out.append([(a, lo, unit, 0)])
    return out


def gather_kernel(grid, groups, n, lag, *refs):
    ins, tok = refs[:n], refs[n]
    outs, rows_out = refs[n + 1 : 2 * n + 1], refs[2 * n + 1]
    own_sem, send_sem, recv_sem, tok_own, tok_send, tok_recv = refs[2 * n + 2 :]
    b, q = grid.here()
    nd, ns = grid.nd, grid.seq_size
    my = grid.digits(b, q)
    partners = [grid.partner(b, q, d) for d in range(nd)]
    others = [lax.rem(q + j, ns) for j in range(1, ns)]
    grid.greet(b, q, partners, others)
    flat = [c for g in groups for c in g]
    where = {}
    first = 0
    for gi, g in enumerate(groups):
        where[gi] = list(range(first, first + len(g)))
        first += len(g)

    own = []
    for i, (a, lo, ln, _) in enumerate(flat):
        c = pltpu.make_async_copy(
            ins[a].at[:, pl.ds(lo, ln)],
            outs[a].at[tuple(my) + (slice(None), pl.ds(lo, ln))],
            own_sem.at[i],
        )
        c.start()
        own.append(c)
    copies = {}

    def stage(i, k):
        a, lo, ln, flavour = flat[i]
        order = grid.order(flavour)
        d = order[k]
        if k == 0:
            src = ins[a].at[:, pl.ds(lo, ln)]
            dst = outs[a].at[tuple(my) + (slice(None), pl.ds(lo, ln))]
        else:
            if k == 1:
                own[i].wait()
            copies[(i, k - 1)].wait_recv()
            done = order[:k]
            ix = tuple(slice(None) if e in done else my[e] for e in range(nd))
            ix = ix + (slice(None), pl.ds(lo, ln))
            src, dst = outs[a].at[ix], outs[a].at[ix]
        c = remote(src, dst, send_sem.at[i, k], recv_sem.at[i, k], partners[d])
        c.start()
        copies[(i, k)] = c

    row_copies = []
    total, lt, _ = tok.shape
    per = total // ns

    def send_rows():
        at = pl.ds(pl.multiple_of(q * lt, lt), lt)
        for r in range(per):
            c = pltpu.make_async_copy(tok.at[q * per + r], rows_out.at[r, at], tok_own.at[r])
            c.start()
            row_copies.append(c)
            for j in range(1, ns):
                o = others[j - 1]
                c = remote(
                    tok.at[o * per + r],
                    rows_out.at[r, at],
                    tok_send.at[j - 1, r],
                    tok_recv.at[j - 1, r],
                    (b, o),
                )
                c.start()
                row_copies.append(c)

    ng = len(groups)
    for t in range(ng + lag * (nd - 1)):
        for k in range(nd - 1, -1, -1):
            g = t - lag * k
            if 0 <= g < ng:
                for i in where[g]:
                    stage(i, k)
        if t == 2:
            send_rows()
    for i in range(len(flat)):
        copies[(i, nd - 1)].wait_recv()
    for i in range(len(flat)):
        for k in range(nd):
            copies[(i, k)].wait_send()
    for c in row_copies:
        c.wait()


def gather_all(grid, blocks, tokens, collective_id):
    nd, ns = grid.nd, grid.seq_size
    n = len(blocks)
    views = [x.reshape(flat_view(*x.shape)) for x in blocks]
    groups = pieces([v.shape for v in views])
    count = sum(len(g) for g in groups)
    total, lt, width = tokens.shape
    per = total // ns
    outs = [struct((2,) * nd + v.shape, v.dtype) for v in views]
    outs.append(struct((per, lt * ns, width), tokens.dtype))
    res = pl.pallas_call(
        functools.partial(gather_kernel, grid, groups, n, 2),
        out_shape=outs,
        in_specs=[VMEM] * (n + 1),
        out_specs=[ANY] * (n + 1),
        scratch_shapes=[
            DMA((count,)),
            DMA((count, nd)),
            DMA((count, nd)),
            DMA((per,)),
            DMA((ns - 1, per)),
            DMA((ns - 1, per)),
        ],
        compiler_params=pltpu.CompilerParams(
            collective_id=collective_id, has_side_effects=True, vmem_limit_bytes=VMEM_LIMIT
        ),
    )(*views, tokens)
    devices = 1 << nd
    full = [
        r.reshape((devices * x.shape[0], x.shape[1])) for r, x in zip(res[:-1], blocks, strict=True)
    ]
    return full, res[-1]


def reduce_plan(grid, flavour):
    free = list(range(grid.nd))
    plan = []
    for d in grid.order(flavour)[::-1]:
        pos = free.index(d)
        plan.append((d, 1 << pos, 1 << (len(free) - pos - 1)))
        free.remove(d)
    return plan


def scatter_kernel(grid, flat, n, nx, lag, *refs):
    nd, ns = grid.nd, grid.seq_size
    ins, rows_in = refs[:n], refs[n : n + nx]
    outs, rows_out = refs[n + nx : 2 * n + nx], refs[2 * n + nx : 2 * n + 2 * nx]
    rest = list(refs[2 * n + 2 * nx :])
    own_sem, send_sem, recv_sem, x_own, x_send, x_recv = rest[:6]
    bufs = rest[6:]
    b, q = grid.here()
    my = grid.digits(b, q)
    partners = [grid.partner(b, q, d) for d in range(nd)]
    others = [lax.rem(q + j, ns) for j in range(1, ns)]
    grid.greet(b, q, partners, others)

    row_copies = []
    for x in range(nx):
        per, length, _ = rows_in[x].shape
        lt = length // ns
        for r in range(per):
            at = pl.ds(pl.multiple_of(q * lt, lt), lt)
            c = pltpu.make_async_copy(
                rows_in[x].at[r, at], rows_out[x].at[q * per + r], x_own.at[x, r]
            )
            c.start()
            row_copies.append(c)

    def send_rows(x):
        per, length, _ = rows_in[x].shape
        lt = length // ns
        for r in range(per):
            for j in range(1, ns):
                o = others[j - 1]
                c = remote(
                    rows_in[x].at[r, pl.ds(pl.multiple_of(o * lt, lt), lt)],
                    rows_out[x].at[q * per + r],
                    x_send.at[x, j - 1, r],
                    x_recv.at[x, j - 1, r],
                    (b, o),
                )
                c.start()
                row_copies.append(c)

    per_piece = 1 + 2 * nd - 1
    copies, own = {}, {}

    def buffers(i):
        mine = bufs[i * per_piece : (i + 1) * per_piece]
        return mine[0], mine[1 : 1 + nd], mine[1 + nd :]

    for i, (a, lo, ln, flavour) in enumerate(flat):
        d = reduce_plan(grid, flavour)[0][0]
        ix = tuple(my[e] if e == d else slice(None) for e in range(nd)) + (slice(None), pl.ds(lo, ln))
        c = pltpu.make_async_copy(ins[a].at[ix], buffers(i)[0], own_sem.at[i])
        c.start()
        own[i] = c

    def send(i, k):
        a, lo, ln, flavour = flat[i]
        d, pre, post = reduce_plan(grid, flavour)[k]
        start, recv, acc = buffers(i)
        if k == 0:
            ix = tuple((1 - my[e]) if e == d else slice(None) for e in range(nd))
            src = ins[a].at[ix + (slice(None), pl.ds(lo, ln))]
        else:
            src = acc[k - 1].at[:, 1 - my[d]]
        c = remote(src, recv[k], send_sem.at[i, k], recv_sem.at[i, k], partners[d])
        c.start()
        copies[(i, k)] = c

    def add(i, k):
        a, lo, ln, flavour = flat[i]
        plan = reduce_plan(grid, flavour)
        d, pre, post = plan[k]
        start, recv, acc = buffers(i)
        copies[(i, k)].wait_recv()
        if k == 0:
            own[i].wait()
        if k == nd - 1:
            total = acc[k - 1][0, my[d], 0].astype(F32) + recv[k][0, 0].astype(F32)
            outs[a][:, lo : lo + ln] = total
            return
        _, pre2, post2 = plan[k + 1]

        def one(j, carry):
            if k == 0:
                ix = tuple((j // (1 << (nd - 2 - e))) % 2 for e in range(nd - 1))
                mine, other = start[ix], recv[0][ix]
            else:
                mine = acc[k - 1][j // post, my[d], j % post]
                other = recv[k][j // post, j % post]
            total = mine.astype(F32) + other.astype(F32)
            acc[k][j // (2 * post2), (j // post2) % 2, j % post2] = total.astype(acc[k].dtype)
            return carry

        lax.fori_loop(0, pre * post, one, 0)

    groups = sorted({c[4] for c in [(*f, gi) for f, gi in zip(flat, group_of(flat))]})
    members = {g: [i for i, gi in enumerate(group_of(flat)) if gi == g] for g in groups}
    ng = len(groups)
    for t in range(ng + lag * nd):
        for k in range(nd, -1, -1):
            g = t - lag * k
            if 0 <= g < ng:
                for i in members[g]:
                    if k > 0:
                        add(i, k - 1)
                    if k < nd:
                        send(i, k)
        if t == 0:
            for x in range(nx):
                send_rows(x)
    for i in range(len(flat)):
        for k in range(nd):
            copies[(i, k)].wait_send()
    for c in row_copies:
        c.wait()


def group_of(flat):
    ids, last = [], -1
    for _, _, _, flavour in flat:
        if flavour == 0:
            last += 1
        ids.append(last)
    return ids


def scatter_all(grid, grads, rows_back, collective_id):
    nd, ns = grid.nd, grid.seq_size
    devices = 1 << nd
    views, finals = [], []
    for g in grads:
        rows = g.shape[0] // devices
        finals.append((rows, g.shape[1]))
        views.append(g.reshape((2,) * nd + flat_view(rows, g.shape[1])))
    flat = [c for g in pieces([v.shape[-2:] for v in views]) for c in g]
    n, nx = len(views), len(rows_back)
    scratch = []
    for a, _, ln, flavour in flat:
        rows, dtype = views[a].shape[-2], views[a].dtype
        plan = reduce_plan(grid, flavour)
        scratch.append(pltpu.VMEM((2,) * (nd - 1) + (rows, ln), dtype))
        for k, (_, pre, post) in enumerate(plan):
            shape = (2,) * (nd - 1) if k == 0 else (pre, post)
            scratch.append(pltpu.VMEM(shape + (rows, ln), dtype))
        for _, pre, post in plan[1:]:
            scratch.append(pltpu.VMEM((pre, 2, post, rows, ln), dtype))
    outs = [struct(v.shape[-2:], F32) for v in views]
    for x in rows_back:
        per, length, width = x.shape
        outs.append(struct((per * ns, length // ns, width), x.dtype))
    per = rows_back[0].shape[0]
    count = len(flat)
    res = pl.pallas_call(
        functools.partial(scatter_kernel, grid, flat, n, nx, 2),
        out_shape=outs,
        in_specs=[ANY] * n + [ANY] * nx,
        out_specs=[VMEM] * n + [ANY] * nx,
        scratch_shapes=[
            DMA((count,)),
            DMA((count, nd)),
            DMA((count, nd)),
            DMA((nx, per)),
            DMA((nx, ns - 1, per)),
            DMA((nx, ns - 1, per)),
        ]
        + scratch,
        compiler_params=pltpu.CompilerParams(
            collective_id=collective_id, has_side_effects=True, vmem_limit_bytes=VMEM_LIMIT
        ),
    )(*views, *rows_back)
    return [r.reshape(s) for r, s in zip(res[:n], finals, strict=True)], res[n:]


def segment_of(lens, r, shape, axis, start=0):
    t = lax.broadcasted_iota(jnp.int32, shape, axis) + start
    end = lens[r, 0]
    seg = (t >= end).astype(jnp.int32)
    for k in range(1, SEGS):
        end = end + lens[r, k]
        seg = seg + (t >= end).astype(jnp.int32)
    return seg


def attention_kernel(
    lens, x_ref, wq, wk, wv, bq, bv, q_ref, k_ref, v_ref, p_ref, o_ref, vt_ref, ot_ref, bias_ref
):
    x = x_ref[0]
    length = x.shape[0]
    r = pl.program_id(0)
    seg_k = segment_of(lens, r, (length, 1), 0)
    seg_q = segment_of(lens, r, (1, length), 1)
    bias_ref[...] = jnp.where(seg_k == seg_q, 0.0, MASKED)
    q_ref[0] = ((dot(x, wq[...]) + bq[...]) * HEAD_DIM ** (-0.5)).astype(BF16)
    k_ref[0] = dot(x, wk[...]).astype(BF16)
    v = dot(x, wv[...]) + bv[...]
    v_ref[0] = v.astype(BF16)
    vt_ref[...] = v.T.astype(BF16)
    lane = lax.broadcasted_iota(jnp.int32, (1, 128), 1)

    def pair(p, carry):
        sl = pl.ds(pl.multiple_of(p * 128, 128), 128)
        qp, kp = q_ref[0, :, sl], k_ref[0, :, sl]
        for h in range(2):
            km = jnp.where(lane // HEAD_DIM == h, kp, jnp.zeros_like(kp))
            hs = pl.ds(pl.multiple_of(p * 128 + h * HEAD_DIM, HEAD_DIM), HEAD_DIM)
            s = dot(km, qp, 1, 1) + bias_ref[...]
            e = jnp.exp(s - jnp.max(s, axis=0, keepdims=True))
            pt = (e * (1.0 / jnp.sum(e, axis=0, keepdims=True))).astype(BF16)
            p_ref[0, p * 2 + h] = pt
            ot_ref[hs, :] = dot(vt_ref[hs, :], pt).astype(BF16)
        return carry

    lax.fori_loop(0, HEADS // 2, pair, 0)
    o_ref[0] = ot_ref[...].T


def attention(lens, x, wq, wk, wv, bq, bv):
    rows, length, width = x.shape
    row = lambda *s: pl.BlockSpec((1,) + s, lambda r: (r,) + (0,) * len(s))
    full = lambda *s: pl.BlockSpec(s, lambda r: (0,) * len(s))
    tokens = struct((rows, length, width), BF16)
    return pl.pallas_call(
        attention_kernel,
        grid=(rows,),
        out_shape=[tokens] * 3 + [struct((rows, HEADS, length, length), BF16), tokens],
        in_specs=[SMEM, row(length, width)] + [full(width, width)] * 3 + [full(1, width)] * 2,
        out_specs=[row(length, width)] * 3 + [row(HEADS, length, length), row(length, width)],
        scratch_shapes=[
            pltpu.VMEM((width, length), BF16),
            pltpu.VMEM((width, length), BF16),
            pltpu.VMEM((length, length), F32),
        ],
        compiler_params=pltpu.CompilerParams(vmem_limit_bytes=VMEM_LIMIT),
    )(lens, x, wq, wk, wv, bq, bv)


def layer_norm(v):
    c = v - jnp.mean(v, axis=-1, keepdims=True)
    inv = lax.rsqrt(jnp.mean(c * c, axis=-1, keepdims=True) + NORM_EPSILON)
    return c * inv, inv


def feed_kernel(
    tiles, lens, x_ref, o_ref, wo, bo, g1, s1, wi, bi, wd, bd, g2, s2,
    hid_ref, n1_ref, i1_ref, h1_ref, act_ref, slope_ref, n2_ref, i2_ref, pool_ref,
):
    t = pl.program_id(0)
    rows = x_ref.shape[0]
    pre1 = x_ref[...].astype(F32) + dot(o_ref[...], wo[...]) + bo[...]
    n1, i1 = layer_norm(pre1)
    h1 = n1 * g1[...] + s1[...]
    h1_low = h1.astype(BF16)
    n1_ref[...] = n1.astype(BF16)
    h1_ref[...] = h1_low
    i1_ref[...] = jnp.broadcast_to(i1, i1_ref.shape)
    acc = h1 + bd[...]
    chunk = wd.shape[1]
    for lo in range(0, wi.shape[1], chunk):
        sl = slice(lo, lo + chunk)
        inner = dot(h1_low, wi[:, sl]) + bi[:, sl]
        phi = 0.5 + 0.5 * lax.erf(inner * (0.5**0.5))
        act = (inner * phi).astype(BF16)
        act_ref[:, sl] = act
        density = jnp.exp(-0.5 * inner * inner) * 0.3989422804014327
        slope_ref[:, sl] = (phi + inner * density).astype(BF16)
        acc = acc + dot(act, wd[sl, :])
    n2, i2 = layer_norm(acc)
    h2 = n2 * g2[...] + s2[...]
    high, low = split_two(h2)
    hid_ref[...] = high
    n2_ref[...] = n2.astype(BF16)
    i2_ref[...] = jnp.broadcast_to(i2, i2_ref.shape)
    r = t // tiles
    seg = segment_of(lens, r, (1, rows), 1, (t % tiles) * rows)
    slot = jnp.where(seg < SEGS, r * SEGS + seg, -1)
    members = lax.broadcasted_iota(jnp.int32, (pool_ref.shape[0], rows), 0) == slot
    members = members.astype(F32).astype(BF16)
    part = dot(members, high) + dot(members, low)

    @pl.when(t == 0)
    def _():
        pool_ref[...] = part

    @pl.when(t != 0)
    def _():
        pool_ref[...] += part


def feed(lens, x, o, wo, bo, g1, s1, wi, bi, wd, bd, g2, s2, tile_rows):
    count, width = x.shape
    rows = lens.shape[0]
    ff = wi.shape[1]
    tiles = count // rows // tile_rows
    tile = lambda w: pl.BlockSpec((tile_rows, w), lambda t: (t, 0))
    full = lambda *s: pl.BlockSpec(s, lambda t: (0,) * len(s))
    vec = full(1, width)
    low, col = struct((count, width), BF16), struct((count, 128), F32)
    wide = struct((count, ff), BF16)
    return pl.pallas_call(
        functools.partial(feed_kernel, tiles),
        grid=(count // tile_rows,),
        out_shape=[low, low, col, low, wide, wide, low, col, struct((rows * SEGS, width), F32)],
        in_specs=[SMEM, tile(width), tile(width), full(width, width), vec, vec, vec]
        + [full(width, ff), full(1, ff), full(ff, width), vec, vec, vec],
        out_specs=[tile(width), tile(width), tile(128), tile(width), tile(ff), tile(ff)]
        + [tile(width), tile(128), full(rows * SEGS, width)],
        compiler_params=pltpu.CompilerParams(vmem_limit_bytes=VMEM_LIMIT),
    )(lens, x, o, wo, bo, g1, s1, wi, bi, wd, bd, g2, s2)


def contrast_kernel(grid, pool_ref, len_ref, pair_ref, pairs_ref, loss_ref, dpool_ref, emb, send_sem, recv_sem):
    nd = grid.nd
    b, q = grid.here()
    my = grid.digits(b, q)
    partners = [grid.partner(b, q, d) for d in range(nd)]
    own_rows, width = pool_ref.shape
    count = own_rows << nd
    avg = pool_ref[...] / len_ref[:, :1]
    inv = lax.rsqrt(jnp.sum(avg * avg, axis=-1, keepdims=True) + NORM_EPSILON)
    own = avg * inv
    emb[tuple(my)] = own
    grid.greet(b, q, partners, None)
    order = grid.order(0)
    for k, d in enumerate(order):
        ix = tuple(slice(None) if e in order[:k] else my[e] for e in range(nd))
        c = remote(emb.at[ix], emb.at[ix], send_sem.at[k], recv_sem.at[k], partners[d])
        c.start()
        c.wait()
    high, low = split_two(emb[...].reshape(count, width))
    own_high, own_low = split_two(own)
    scale = 1.0 / TEMPERATURE

    def product(ah, al, bh, bl, cb):
        return dot(ah, bh, 1, cb) + dot(ah, bl, 1, cb) + dot(al, bh, 1, cb)

    total = jnp.zeros((1, count), F32)
    step = min(count, 256)
    for lo in range(0, count, step):
        sim = product(high[lo : lo + step], low[lo : lo + step], high, low, 1) * scale
        at = lax.broadcasted_iota(jnp.int32, (step, 1), 0)
        total += jnp.sum(jnp.where(at % SEGS >= NQ, jnp.exp(sim - scale), 0.0), axis=0, keepdims=True)
    lse_cols = scale + jnp.log(total)
    sim = product(own_high, own_low, high, low, 1) * scale
    col = lax.broadcasted_iota(jnp.int32, (1, count), 1)
    row = lax.broadcasted_iota(jnp.int32, (own_rows, 1), 0) + (b * grid.seq_size + q) * own_rows
    col_doc, row_doc = col % SEGS >= NQ, row % SEGS >= NQ
    number = lambda at: (at // SEGS) * NQ + at % SEGS - NQ
    lse_rows = scale + jnp.log(
        jnp.sum(jnp.where(col_doc, jnp.exp(sim - scale), 0.0), axis=1, keepdims=True)
    )
    chosen = col_doc & (number(col) == pair_ref[:, :1])
    positive = jnp.sum(jnp.where(chosen, sim, 0.0), axis=1, keepdims=True)
    loss_ref[...] = jnp.broadcast_to(lse_rows - positive, loss_ref.shape)
    as_query = jnp.exp(sim - lse_rows) - chosen.astype(F32)
    chosen_by = number(row) == pairs_ref[:1]
    as_doc = jnp.exp(jnp.where(col_doc, MASKED, sim - lse_cols)) - chosen_by.astype(F32)
    grad = jnp.where(row_doc, jnp.where(col_doc, 0.0, as_doc), jnp.where(col_doc, as_query, 0.0))
    grad_high, grad_low = split_two(grad)
    demb = product(grad_high, grad_low, high, low, 0) * scale
    dpool = inv * demb - inv * inv * inv * avg * jnp.sum(avg * demb, axis=-1, keepdims=True)
    dpool_high, dpool_low = split_two(dpool / len_ref[:, :1])
    pad = jnp.zeros((64 - own_rows, width), F32)
    stacked = jnp.concatenate([dpool_high.astype(F32), pad, dpool_low.astype(F32), pad], axis=0)
    dpool_ref[...] = stacked.astype(BF16)


def contrast(grid, pool, len_col, pair_col, pair_row, collective_id):
    own_rows, width = pool.shape
    return pl.pallas_call(
        functools.partial(contrast_kernel, grid),
        out_shape=[struct((own_rows, 128), F32), struct((128, width), BF16)],
        in_specs=[VMEM] * 4,
        out_specs=[VMEM] * 2,
        scratch_shapes=[
            pltpu.VMEM((2,) * grid.nd + (own_rows, width), F32),
            DMA((grid.nd,)),
            DMA((grid.nd,)),
        ],
        compiler_params=pltpu.CompilerParams(
            collective_id=collective_id, has_side_effects=True, vmem_limit_bytes=VMEM_LIMIT
        ),
    )(pool, len_col, pair_col, pair_row)


def feed_back_kernel(
    tiles, lens, dp_ref, n2_ref, i2_ref, slope_ref, n1_ref, i1_ref, wd, wi, wo, g2, g1,
    dfeed_ref, dinner_ref, dbranch_ref, dpre1_ref, datt_ref, sums_ref, wide_ref,
):
    t = pl.program_id(0)
    rows = n2_ref.shape[0]

    @pl.when(t == 0)
    def _():
        sums_ref[...] = jnp.zeros_like(sums_ref)
        wide_ref[...] = jnp.zeros_like(wide_ref)

    def columns(v):
        return jnp.sum(v, axis=0, keepdims=True)

    def norm_back(g, n, inv):
        return inv * (
            g - jnp.mean(g, axis=-1, keepdims=True) - n * jnp.mean(g * n, axis=-1, keepdims=True)
        )

    r = t // tiles
    seg = segment_of(lens, r, (rows, 1), 0, (t % tiles) * rows)
    slot = jnp.where(seg < SEGS, r * SEGS + seg, -1)
    lane = lax.broadcasted_iota(jnp.int32, (rows, 128), 1)
    members = (lane % 64 == slot).astype(F32).astype(BF16)
    dh2 = dot(members, dp_ref[...])
    n2 = n2_ref[...].astype(F32)
    sums_ref[0:1] += columns(dh2 * n2)
    sums_ref[1:2] += columns(dh2)
    dpre2 = norm_back(dh2 * g2[...], n2, i2_ref[:, :1])
    dfeed = dpre2.astype(BF16)
    dfeed_ref[...] = dfeed
    sums_ref[2:3] += columns(dfeed.astype(F32))
    chunk = wd.shape[1]
    dh1 = dpre2
    for lo in range(0, wi.shape[1], chunk):
        sl = slice(lo, lo + chunk)
        dinner = (dot(dfeed, wd[sl, :], 1, 1) * slope_ref[:, sl].astype(F32)).astype(BF16)
        dinner_ref[:, sl] = dinner
        wide_ref[0:1, sl] += columns(dinner.astype(F32))
        dh1 = dh1 + dot(dinner, wi[:, sl], 1, 1)
    n1 = n1_ref[...].astype(F32)
    sums_ref[3:4] += columns(dh1 * n1)
    sums_ref[4:5] += columns(dh1)
    dpre1 = norm_back(dh1 * g1[...], n1, i1_ref[:, :1])
    dpre1_ref[...] = dpre1
    dbranch = dpre1.astype(BF16)
    dbranch_ref[...] = dbranch
    sums_ref[5:6] += columns(dbranch.astype(F32))
    datt_ref[...] = dot(dbranch, wo[...], 1, 1).astype(BF16)


def feed_back(lens, dp, n2, i2, slope, n1, i1, wd, wi, wo, g2, g1, tile_rows):
    count, width = n2.shape
    rows = lens.shape[0]
    ff = wi.shape[1]
    tiles = count // rows // tile_rows
    tile = lambda w: pl.BlockSpec((tile_rows, w), lambda t: (t, 0))
    full = lambda *s: pl.BlockSpec(s, lambda t: (0,) * len(s))
    low = struct((count, width), BF16)
    return pl.pallas_call(
        functools.partial(feed_back_kernel, tiles),
        grid=(count // tile_rows,),
        out_shape=[low, struct((count, ff), BF16), low, struct((count, width), F32), low]
        + [struct((8, width), F32), struct((8, ff), F32)],
        in_specs=[SMEM, full(128, width), tile(width), tile(128), tile(ff), tile(width), tile(128)]
        + [full(ff, width), full(width, ff), full(width, width), full(1, width), full(1, width)],
        out_specs=[tile(width), tile(ff), tile(width), tile(width), tile(width)]
        + [full(8, width), full(8, ff)],
        compiler_params=pltpu.CompilerParams(vmem_limit_bytes=VMEM_LIMIT),
    )(lens, dp, n2, i2, slope, n1, i1, wd, wi, wo, g2, g1)


def outer_kernel(a_ref, b_ref, o_ref):
    o_ref[...] = dot(a_ref[...], b_ref[...], 0, 0).astype(o_ref.dtype)


def outer(a, b, bm, bn):
    count, m = a.shape
    n = b.shape[1]
    return pl.pallas_call(
        outer_kernel,
        grid=(m // bm, n // bn),
        out_shape=struct((m, n), BF16),
        in_specs=[
            pl.BlockSpec((count, bm), lambda i, j: (0, i)),
            pl.BlockSpec((count, bn), lambda i, j: (0, j)),
        ],
        out_specs=pl.BlockSpec((bm, bn), lambda i, j: (i, j)),
        compiler_params=pltpu.CompilerParams(vmem_limit_bytes=VMEM_LIMIT),
    )(a, b)


def attention_back_kernel(q_ref, k_ref, v_ref, p_ref, do_ref, dq_ref, dk_ref, dv_ref, kt_ref, dqt_ref):
    kt_ref[...] = k_ref[0].T
    lane = lax.broadcasted_iota(jnp.int32, (1, 128), 1)

    def pair(p, carry):
        sl = pl.ds(pl.multiple_of(p * 128, 128), 128)
        qp, vp, dop = q_ref[0, :, sl], v_ref[0, :, sl], do_ref[0, :, sl]
        zero = jnp.zeros_like(vp)
        dv = dk = None
        for h in range(2):
            mine = lane // HEAD_DIM == h
            vm, dom, qm = (jnp.where(mine, u, zero) for u in (vp, dop, qp))
            hs = pl.ds(pl.multiple_of(p * 128 + h * HEAD_DIM, HEAD_DIM), HEAD_DIM)
            pt = p_ref[0, p * 2 + h]
            probs = pt.astype(F32)
            weighted = probs * dot(vm, dop, 1, 1)
            ds = (weighted - probs * jnp.sum(weighted, axis=0, keepdims=True)).astype(BF16)
            dv_h, dk_h = dot(pt, dom), dot(ds, qm)
            dv = dv_h if dv is None else dv + dv_h
            dk = dk_h if dk is None else dk + dk_h
            dqt_ref[hs, :] = (dot(kt_ref[hs, :], ds) * HEAD_DIM ** (-0.5)).astype(BF16)
        dv_ref[0, :, sl] = dv.astype(BF16)
        dk_ref[0, :, sl] = dk.astype(BF16)
        return carry

    lax.fori_loop(0, HEADS // 2, pair, 0)
    dq_ref[0] = dqt_ref[...].T


def attention_back(q, k, v, p, do):
    rows, length, width = q.shape
    row = lambda *s: pl.BlockSpec((1,) + s, lambda r: (r,) + (0,) * len(s))
    return pl.pallas_call(
        attention_back_kernel,
        grid=(rows,),
        out_shape=[struct((rows, length, width), BF16)] * 3,
        in_specs=[row(length, width)] * 3 + [row(HEADS, length, length), row(length, width)],
        out_specs=[row(length, width)] * 3,
        scratch_shapes=[pltpu.VMEM((width, length), BF16), pltpu.VMEM((width, length), BF16)],
        compiler_params=pltpu.CompilerParams(vmem_limit_bytes=VMEM_LIMIT),
    )(q, k, v, p, do)


def input_back_kernel(dpre1_ref, dq_ref, dk_ref, dv_ref, wq, wk, wv, out_ref, sums_ref):
    @pl.when(pl.program_id(0) == 0)
    def _():
        sums_ref[...] = jnp.zeros_like(sums_ref)

    sums_ref[0:1] += jnp.sum(dq_ref[...].astype(F32), axis=0, keepdims=True)
    sums_ref[1:2] += jnp.sum(dv_ref[...].astype(F32), axis=0, keepdims=True)
    total = dpre1_ref[...] + dot(dq_ref[...], wq[...], 1, 1)
    total += dot(dk_ref[...], wk[...], 1, 1) + dot(dv_ref[...], wv[...], 1, 1)
    out_ref[...] = total.astype(out_ref.dtype)


def input_back(dpre1, dq, dk, dv, wq, wk, wv, tile_rows):
    count, width = dpre1.shape
    tile = pl.BlockSpec((tile_rows, width), lambda t: (t, 0))
    full = lambda *s: pl.BlockSpec(s, lambda t: (0,) * len(s))
    return pl.pallas_call(
        input_back_kernel,
        grid=(count // tile_rows,),
        out_shape=[struct((count, width), BF16), struct((8, width), F32)],
        in_specs=[tile] * 4 + [full(width, width)] * 3,
        out_specs=[tile, full(8, width)],
        compiler_params=pltpu.CompilerParams(vmem_limit_bytes=VMEM_LIMIT),
    )(dpre1, dq, dk, dv, wq, wk, wv)


class Turned:
    def __init__(self, ref):
        self.ref = ref

    def __getitem__(self, at):
        return self.ref[at[1], at[0]]


def gelu_gate(v):
    return 0.5 + 0.5 * lax.erf(v * (0.5**0.5))


def gelu_slope(v):
    return gelu_gate(v) + v * (jnp.exp(-0.5 * v * v) * 0.3989422804014327)


class Gatherer:
    def __init__(self, grid, flat, partners, my, blocks, fulls, own_sem, send_sem, recv_sem):
        self.grid, self.flat, self.partners, self.my = grid, flat, partners, my
        self.blocks, self.fulls = blocks, fulls
        self.own_sem, self.send_sem, self.recv_sem = own_sem, send_sem, recv_sem

    def own(self, i):
        a, lo, ln, _ = self.flat[i]
        return pltpu.make_async_copy(
            self.blocks[a].at[:, pl.ds(lo, ln)],
            self.fulls[a].at[tuple(self.my) + (slice(None), pl.ds(lo, ln))],
            self.own_sem.at[i],
        )

    def copy(self, i, k):
        a, lo, ln, flavour = self.flat[i]
        order = self.grid.order(flavour)
        done = order[:k]
        ix = tuple(slice(None) if e in done else self.my[e] for e in range(self.grid.nd))
        dst = self.fulls[a].at[ix + (slice(None), pl.ds(lo, ln))]
        src = self.blocks[a].at[:, pl.ds(lo, ln)] if k == 0 else dst
        return remote(
            src, dst, self.send_sem.at[i, k], self.recv_sem.at[i, k], self.partners[order[k]]
        )

    def step(self, i, k):
        if k == 0:
            self.own(i).start()
        elif k == 1:
            self.own(i).wait()
        if k > 0:
            self.copy(i, k - 1).wait_recv()
        if k < self.grid.nd:
            self.copy(i, k).start()

    def finish(self):
        for i in range(len(self.flat)):
            for k in range(self.grid.nd):
                self.copy(i, k).wait_send()


def forward_kernel(grid, groups, tile_rows, *refs):
    it = iter(refs)
    take = lambda n: [next(it) for _ in range(n)]
    lens, tok = take(2)
    lens = Turned(lens)
    vectors = take(9)
    blocks = take(6)
    x_out, q_out, k_out, v_out, p_out, o_out = take(6)
    n1_out, i1_out, h1_out, act_out, inner_out, n2_out, i2_out, hid_out = take(8)
    full_out = take(7)
    pool, vecs = take(2)
    fulls = take(7)
    x_s, q_s, k_s, v_s, vt_s, mask_s, h_s, bi_s, packed = take(9)
    own_sem, send_sem, recv_sem, tok_own, tok_send, tok_recv, out_sem = take(7)

    b, sq = grid.here()
    nd, ns = grid.nd, grid.seq_size
    my = grid.digits(b, sq)
    partners = [grid.partner(b, sq, d) for d in range(nd)]
    others = [lax.rem(sq + j, ns) for j in range(1, ns)]
    flat = [c for g in groups for c in g]
    members, first = [], 0
    for g in groups:
        members.append(range(first, first + len(g)))
        first += len(g)
    packed[...] = jnp.zeros_like(packed)
    for i, u in enumerate(vectors):
        packed[i : i + 1, : u.shape[0]] = u[...].astype(F32).reshape(1, u.shape[0])
    blocks = [packed] + blocks
    ga = Gatherer(grid, flat, partners, my, blocks, fulls, own_sem, send_sem, recv_sem)
    rows, length, width = x_s.shape
    lt = length // ns
    tiles = length // tile_rows
    grid.greet(b, sq, partners, others)

    def row_copy(r, j):
        at = pl.ds(pl.multiple_of(sq * lt, lt), lt)
        if j == 0:
            return pltpu.make_async_copy(tok.at[sq * rows + r], x_s.at[r, at], tok_own.at[r])
        o = others[j - 1]
        return remote(
            tok.at[o * rows + r], x_s.at[r, at], tok_send.at[r, j - 1], tok_recv.at[r, j - 1], (b, o)
        )

    plan = forward_plan(nd, len(groups), ns)

    def run_at(point):
        for g, k in plan.get(point, ()):
            if k < 0:
                row_copy(g, -k).start()
            else:
                for i in members[g]:
                    ga.step(i, k)

    def hook(name, steps):
        def run():
            now = pl.program_id(0)
            for c in range(steps):
                if (name, c) in plan:
                    pl.when(now == c)(functools.partial(run_at, (name, c)))

        return run

    def arrived(*which):
        for g in which:
            for i in members[g]:
                ga.step(i, nd)

    out_copies = []

    def put(src, dst):
        c = pltpu.make_async_copy(src, dst, out_sem.at[len(out_copies)])
        c.start()
        out_copies.append(c)

    for r in range(rows):
        row_copy(r, 0).start()
    run_at("start")
    arrived(0, 1, 2)
    part = blocks[1].shape[0]
    wide_part = bi_s.shape[1] >> nd
    smalls = fulls[0][...].reshape((1 << nd,) + blocks[0].shape)

    def unpacked(i, size, first, lanes):
        col = lax.broadcasted_iota(jnp.int32, (1, lanes), 1) + first
        device = jnp.floor((col.astype(F32) + 0.5) * (1.0 / size)).astype(jnp.int32)
        at = lax.broadcasted_iota(jnp.int32, (128, lanes), 0)
        spread = (at == col - device * size).astype(F32).astype(BF16)
        owner = lax.broadcasted_iota(jnp.int32, (1 << nd, lanes), 0) == device
        values = dot(smalls[:, i, :].astype(BF16), spread)
        return jnp.sum(jnp.where(owner, values, 0.0), axis=0, keepdims=True)

    for i in range(8):
        vecs[i : i + 1] = unpacked(i, part, 0, width)
    for lo in range(0, bi_s.shape[1], width):
        bi_s[:, lo : lo + width] = unpacked(8, wide_part, lo, width)
    bq, bv, bo, g1, s1, bd, g2, s2 = (vecs[i : i + 1] for i in range(8))
    lane = lax.broadcasted_iota(jnp.int32, (1, 128), 1)

    def square(ref):
        return ref[...].reshape(width, width)

    for r in range(rows):
        run_at(("row", r))
        for j in range(ns):
            c = row_copy(r, j)
            if j == 0:
                c.wait()
            else:
                c.wait_recv()
        put(x_s.at[r], x_out.at[r])
        x = x_s[r]
        q_s[r] = ((dot(x, square(fulls[1])) + bq) * HEAD_DIM ** (-0.5)).astype(BF16)
        k_s[r] = dot(x, square(fulls[2])).astype(BF16)
        v = dot(x, square(fulls[3])) + bv
        v_s[r] = v.astype(BF16)
        vt_s[...] = v.T.astype(BF16)
        for src, dst in ((q_s, q_out), (k_s, k_out), (v_s, v_out)):
            put(src.at[r], dst.at[r])
        seg_k = segment_of(lens, sq * rows + r, (length, 1), 0)
        seg_q = segment_of(lens, sq * rows + r, (1, length), 1)
        mask_s[...] = jnp.where(seg_k == seg_q, 0.0, MASKED)
        att_hook = hook(("attention", r), HEADS // 2)

        def att_body(p_t, o_t, r=r):
            att_hook()
            p = pl.program_id(0)
            sl = pl.ds(pl.multiple_of(p * 128, 128), 128)
            qp, kp = q_s[r, :, sl], k_s[r, :, sl]
            zero = jnp.zeros_like(kp)
            scores = [
                dot(jnp.where(lane // HEAD_DIM == h, kp, zero), qp, 1, 1) + mask_s[...]
                for h in range(2)
            ]
            probs = []
            for h, s in enumerate(scores):
                e = jnp.exp(s - jnp.max(s, axis=0, keepdims=True))
                probs.append((e * (1.0 / jnp.sum(e, axis=0, keepdims=True))).astype(BF16))
                p_t[0, h] = probs[h]
            out = []
            for h in range(2):
                hs = pl.ds(pl.multiple_of(p * 128 + h * HEAD_DIM, HEAD_DIM), HEAD_DIM)
                out.append(dot(vt_s[hs, :], probs[h]))
            o_t[0] = jnp.concatenate(out, axis=0).T.astype(BF16)

        pltpu.emit_pipeline(
            att_body,
            grid=(HEADS // 2,),
            out_specs=[
                pl.BlockSpec((1, 2, length, length), lambda s, r=r: (r, s, 0, 0)),
                pl.BlockSpec((1, length, 128), lambda s, r=r: (r, 0, s)),
            ],
        )(p_out, o_out)

    run_at("in")
    down_groups = width // 256
    arrived(*range(3, len(groups) - down_groups))
    for a in range(6):
        put(fulls[a], full_out[a])
    ff = bi_s.shape[1]
    tile = lambda w: pl.BlockSpec((tile_rows, w), lambda t: (t, 0))

    def tile_at():
        t = pl.program_id(0)
        start = lax.rem(t, tiles) * tile_rows
        return t // tiles, start, pl.ds(pl.multiple_of(start, tile_rows), tile_rows)

    in_hook = hook("in", rows * tiles)

    def in_body(o_t, n1_t, i1_t, h1_t, act_t, inner_t):
        in_hook()
        r, _, at = tile_at()
        pre1 = x_s[r, at].astype(F32) + dot(o_t[0], square(fulls[4])) + bo
        n1, i1 = layer_norm(pre1)
        h1 = n1 * g1 + s1
        low = h1.astype(BF16)
        h_s[r, at] = h1
        n1_t[...] = n1.astype(BF16)
        i1_t[...] = jnp.broadcast_to(i1, i1_t.shape)
        h1_t[...] = low
        for lo in range(0, ff, width):
            w = fulls[5][(slice(None),) * (nd + 1) + (slice(lo, lo + width),)]
            inner = dot(low, w.reshape(width, width)) + bi_s[:, lo : lo + width]
            act_t[:, lo : lo + width] = (inner * gelu_gate(inner)).astype(BF16)
            inner_t[:, lo : lo + width] = inner.astype(BF16)

    pltpu.emit_pipeline(
        in_body,
        grid=(rows * tiles,),
        in_specs=[pl.BlockSpec((1, tile_rows, width), lambda t: (t // tiles, t % tiles, 0))],
        out_specs=[tile(width), tile(128), tile(width), tile(ff), tile(ff)],
    )(o_out, n1_out, i1_out, h1_out, act_out, inner_out)

    run_at("down")
    arrived(*range(len(groups) - down_groups, len(groups)))
    put(fulls[6], full_out[6])
    pool[...] = jnp.zeros_like(pool)
    down_rows = blocks[6].shape[0]
    top = nd - ((width // down_rows).bit_length() - 1)

    def down_body(act_t, hid_t, n2_t, i2_t):
        r, start, at = tile_at()
        acc = h_s[r, at] + bd
        for c, lo in enumerate(range(0, ff, width)):
            ix = tuple((c >> (top - 1 - e)) % 2 for e in range(top))
            acc = acc + dot(act_t[:, lo : lo + width], fulls[6][ix].reshape(width, width))
        n2, i2 = layer_norm(acc)
        high, low = split_two(n2 * g2 + s2)
        hid_t[...] = high
        n2_t[...] = n2.astype(BF16)
        i2_t[...] = jnp.broadcast_to(i2, i2_t.shape)
        seg = segment_of(lens, sq * rows + r, (1, tile_rows), 1, start)
        slot = jnp.where(seg < SEGS, r * SEGS + seg, -1)
        mine = lax.broadcasted_iota(jnp.int32, (pool.shape[0], tile_rows), 0) == slot
        mine = mine.astype(F32).astype(BF16)
        pool[...] += dot(mine, high) + dot(mine, low)

    pltpu.emit_pipeline(
        down_body,
        grid=(rows * tiles,),
        in_specs=[tile(ff)],
        out_specs=[tile(width), tile(width), tile(128)],
    )(act_out, hid_out, n2_out, i2_out)

    ga.finish()
    for r in range(rows):
        for j in range(1, ns):
            row_copy(r, j).wait_send()
    for c in out_copies:
        c.wait()


FORWARD_PLAN = {
    "start": (
        (1, 0), (2, 0), (0, 0), (6, 0), (1, 1), (5, 0), (4, 0), (0, 1), (2, 1), (8, 0),
        (1, 2), (7, 0), (0, 2), (2, 2), (3, 0), (1, 3), (4, 1), (5, 1), (8, 1), (0, 3),
        (0, -2), (4, 2), (1, 4), (3, 1), (7, 1), (6, 1), (0, -3), (0, -1), (2, 3), (0, 4),
        (8, 2), (1, -1), (1, -3), (5, 2), (3, 2), (1, -2), (2, 4), (7, 2), (6, 2), (5, 3),
        (8, 3), (3, 3), (9, 0), (10, 0), (4, 3), (7, 3),
    ),
    (("attention", 0), 3): (
        (8, 4),
    ),
    ("row", 1): (
        (5, 4), (4, 4), (3, 4), (6, 3),
    ),
    (("attention", 1), 0): (
        (10, 1),
    ),
    (("attention", 1), 1): (
        (9, 1),
    ),
    (("attention", 1), 2): (
        (7, 4), (10, 2), (6, 4),
    ),
    (("attention", 1), 4): (
        (9, 2),
    ),
    (("attention", 1), 5): (
        (10, 3),
    ),
    ("in", 3): (
        (10, 4), (9, 4),
    ),
    "in": (
        (9, 3),
    ),
}
def forward_plan(nd, groups, ns):
    if nd == 5 and groups == 11 and ns == 4:
        return FORWARD_PLAN
    ops = []
    for t in range(groups + 2 * nd):
        ops += [(t - 2 * k, k) for k in range(nd - 1, -1, -1) if 0 <= t - 2 * k < groups]
        if t == nd:
            ops += [(r, -j) for r in range(2) for j in range(1, ns)]
    return {"start": tuple(ops)}


def forward(grid, lens, tokens, vectors, weights, tile_rows, collective_id):
    blocks = [struct((16, 128), F32), *weights]
    nd, ns = grid.nd, grid.seq_size
    total, lt, width = tokens.shape
    rows, length = total // ns, lt * ns
    count = rows * length
    ff = blocks[5].shape[1]
    dev = (2,) * nd
    groups = pieces([x.shape for x in blocks])
    groups = [groups[0] + groups[1]] + groups[2:]
    n = sum(len(g) for g in groups)
    seq3 = struct((rows, length, width), BF16)
    low, stat = struct((count, width), BF16), struct((count, 128), F32)
    wide = struct((count, ff), BF16)
    out_shape = [seq3] * 4 + [struct((rows, HEADS, length, length), BF16), seq3]
    out_shape += [low, stat, low, wide, wide, low, stat, low]
    out_shape += [struct(dev + x.shape, x.dtype) for x in blocks]
    out_shape += [struct((rows * SEGS, width), F32), struct((8, width), F32)]
    res = pl.pallas_call(
        functools.partial(forward_kernel, grid, groups, tile_rows),
        out_shape=out_shape,
        in_specs=[SMEM] + [VMEM] * (1 + len(vectors) + len(weights)),
        out_specs=[ANY] * (len(out_shape) - 2) + [VMEM] * 2,
        scratch_shapes=[pltpu.VMEM(dev + x.shape, x.dtype) for x in blocks]
        + [pltpu.VMEM((rows, length, width), BF16)] * 4
        + [pltpu.VMEM((width, length), BF16), pltpu.VMEM((length, length), F32)]
        + [pltpu.VMEM((rows, length, width), F32), pltpu.VMEM((1, ff), F32)]
        + [pltpu.VMEM((16, 128), F32)]
        + [DMA((n,)), DMA((n, nd)), DMA((n, nd))]
        + [DMA((rows,)), DMA((rows, ns - 1)), DMA((rows, ns - 1)), DMA((7 + 4 * rows,))],
        compiler_params=pltpu.CompilerParams(
            collective_id=collective_id, has_side_effects=True, vmem_limit_bytes=VMEM_LIMIT
        ),
    )(lens, tokens, *vectors, *weights)
    return res


class Reducer:
    def __init__(self, grid, flat, partners, my, sources, outs, send_sem, recv_sem, bufs):
        self.grid, self.flat, self.partners, self.my = grid, flat, partners, my
        self.sources, self.outs = sources, outs
        self.send_sem, self.recv_sem = send_sem, recv_sem
        self.bufs = bufs

    def buf(self, i, k):
        return self.bufs[i * self.grid.nd + k]

    def place(self, i, k):
        order = self.grid.order(self.flat[i][4])[::-1]
        free = [d for d in range(self.grid.nd) if d not in order[:k]]
        return order[k], free.index(order[k])

    def copy(self, i, k):
        a, lo, ln, _, _ = self.flat[i]
        d, pos = self.place(i, k)
        ix = (slice(None),) * pos + (1 - self.my[d],) + (slice(None),) * (self.grid.nd - k - pos - 1)
        if k == 0:
            src = self.sources[a].at[ix + (slice(None), pl.ds(lo, ln))]
        else:
            src = self.buf(i, k - 1).at[ix]
        return remote(
            src, self.buf(i, k), self.send_sem.at[i, k], self.recv_sem.at[i, k], self.partners[d]
        )

    def add(self, i, k):
        nd = self.grid.nd
        a, lo, ln, out_lo, _ = self.flat[i]
        d, pos = self.place(i, k)
        self.copy(i, k).wait_recv()
        into = self.buf(i, k)
        left = nd - k - 1
        if left == 0:
            total = self.buf(i, k - 1)[self.my[d]].astype(F32) + into[...].astype(F32)
            out, at = self.outs[i]
            out[:, at : at + ln] = total
            return

        def one(j, carry):
            ix = tuple((j // (1 << (left - 1 - e))) % 2 for e in range(left))
            mine_at = ix[:pos] + (self.my[d],) + ix[pos:]
            if k == 0:
                mine = self.sources[a][mine_at + (slice(None), slice(lo, lo + ln))]
            else:
                mine = self.buf(i, k - 1)[mine_at]
            into[ix] = (mine.astype(F32) + into[ix].astype(F32)).astype(into.dtype)
            return carry

        lax.fori_loop(0, 1 << left, one, 0)

    def step(self, i, k):
        if k > 0:
            self.add(i, k - 1)
        if k < self.grid.nd:
            self.copy(i, k).start()

    def sent(self, i, k):
        self.copy(i, k).wait_send()


SMALL_ROWS = 16
ROW_BQ, ROW_BV, ROW_BO, ROW_G1, ROW_S1, ROW_BD, ROW_G2, ROW_S2, ROW_BI = range(9)
EMB_PAD = 128


def backward_kernel(grid, flat, groups, n_bufs, tile_rows, *refs):
    it = iter(refs)
    take = lambda n: [next(it) for _ in range(n)]
    lens, pairs, vecs, pool = take(4)
    lens = Turned(lens)
    n2, i2, inner, n1, i1, act, h1, o, q, k, v, p, x, hid = take(14)
    weights = take(6)
    g_in, g_down, g_out, g_query, g_key, g_value = take(6)
    small, loss, hid_back, gx_back = take(4)
    wd, wi, wo, wq, wk, wv = take(6)
    big1, big2, t_h1, t_o, t_feed, t_br, t_att, i1_s, i2_s, p_s = take(10)
    small_recv, emb, dp = take(3)
    send_sem, recv_sem, ex_own, ex_send, ex_recv, load_sem, p_sem, sm_send, sm_recv = take(9)
    emb_send, emb_recv, near_send, near_recv = take(4)
    bufs = take(n_bufs)

    b, sq = grid.here()
    nd, ns = grid.nd, grid.seq_size
    my = grid.digits(b, sq)
    partners = [grid.partner(b, sq, d) for d in range(nd)]
    others = [lax.rem(sq + j, ns) for j in range(1, ns)]
    rows, length, width = x.shape
    count = rows * length
    ff = big1.shape[1]
    chunks = ff // width
    lt = length // ns
    tiles = length // tile_rows
    base = sq * rows
    row_at = lambda r: pl.ds(r * length, length)
    lanes = lambda c: pl.ds(c * width, width)

    loads = []

    def load(src, dst):
        c = pltpu.make_async_copy(src, dst, load_sem.at[len(loads)])
        c.start()
        loads.append(c)
        return c

    inner_load = load(inner, big1)
    first = [load(s, d) for s, d in zip(weights[:3], (wd, wi, wo), strict=True)]
    first += [load(s, d) for s, d in ((n2, t_att), (i2, i2_s), (n1, t_br), (i1, i1_s))]
    second = [load(h1, t_h1), load(act, big2)]
    second += [load(o.at[r], t_o.at[row_at(r)]) for r in range(rows)]
    third = [load(s, d) for s, d in zip(weights[3:], (wq, wk, wv), strict=True)]
    grid.greet(b, sq, partners, others)

    def row_back(e, src, dst, r, j):
        o_ = sq if j == 0 else others[j - 1]
        start = pl.multiple_of(o_ * lt, lt)
        if e == 0:
            part = src.at[r, pl.ds(start, lt)]
        else:
            part = src.at[pl.ds(r * length + start, lt)]
        into = dst.at[sq * rows + r]
        if j == 0:
            return pltpu.make_async_copy(part, into, ex_own.at[e, r])
        return remote(part, into, ex_send.at[e, r, j - 1], ex_recv.at[e, r, j - 1], (b, o_))

    backs = ((hid, hid_back), (t_att, gx_back))

    own_rows = rows * SEGS
    total_rows = own_rows << nd
    at_row = lax.broadcasted_iota(jnp.int32, (own_rows, 1), 0)
    len_col = jnp.ones((own_rows, 1), F32)
    pair_col = jnp.full((own_rows, 1), -1, jnp.int32)
    for r in range(rows):
        for s in range(SEGS):
            here = at_row == r * SEGS + s
            len_col = jnp.where(here, lens[base + r, s].astype(F32), len_col)
            if s < NQ:
                pair_col = jnp.where(here, pairs[r * NQ + s], pair_col)
    avg = pool[...] / len_col
    inv = lax.rsqrt(jnp.sum(avg * avg, axis=-1, keepdims=True) + NORM_EPSILON)
    own = avg * inv
    emb[tuple(my) + (slice(None), slice(0, width))] = own
    emb[tuple(my) + (slice(None), slice(width, width + EMB_PAD))] = jnp.broadcast_to(
        pair_col.astype(F32), (own_rows, EMB_PAD)
    )
    half = width // 2
    emb_pieces = ((0, half, 0), (half, width + EMB_PAD - half, 1))

    def emb_copy(f, kk):
        lo, ln, flavour = emb_pieces[f]
        order = grid.order(flavour)
        ix = tuple(slice(None) if e in order[:kk] else my[e] for e in range(nd))
        ref = emb.at[ix + (slice(None), pl.ds(lo, ln))]
        return remote(ref, ref, emb_send.at[f, kk], emb_recv.at[f, kk], partners[order[kk]])

    def emb_near(j):
        ref = emb.at[tuple(my)]
        return remote(ref, ref, near_send.at[j - 1], near_recv.at[j - 1], (b, others[j - 1]))

    for j in range(1, ns):
        emb_near(j).start()
    for j in range(1, ns):
        emb_near(j).wait_recv()
    inner_load.wait()
    hops = nd - grid.ks
    share = count // hops // 64 * 64
    for kk in range(grid.ks, nd):
        for f in range(2):
            if kk > grid.ks:
                emb_copy(f, kk - 1).wait_recv()
            emb_copy(f, kk).start()
        lo = (kk - grid.ks) * share
        hi = lo + share if kk < nd - 1 else count

        def slopes(t, carry, lo=lo):
            at = pl.ds(pl.multiple_of(lo + t * 64, 64), 64)
            big1[at] = gelu_slope(big1[at].astype(F32)).astype(BF16)
            return carry

        lax.fori_loop(0, (hi - lo) // 64, slopes, 0)
    for r in range(rows):
        for j in range(ns):
            row_back(0, *backs[0], r, j).start()
    for f in range(2):
        emb_copy(f, nd - 1).wait_recv()
    every = emb[...].reshape(total_rows, width + EMB_PAD)
    high, low = split_two(every[:, :width])
    pair_row = every[:, width:].T[:1].astype(jnp.int32)
    own_high, own_low = split_two(own)
    scale = 1.0 / TEMPERATURE

    def product(ah, al, bh, bl, cb):
        return dot(ah, bh, 1, cb) + dot(ah, bl, 1, cb) + dot(al, bh, 1, cb)

    total = jnp.zeros((1, total_rows), F32)
    block = min(total_rows, 256)
    for lo in range(0, total_rows, block):
        sim = product(high[lo : lo + block], low[lo : lo + block], high, low, 1) * scale
        at = lax.broadcasted_iota(jnp.int32, (block, 1), 0)
        total += jnp.sum(jnp.where(at % SEGS >= NQ, jnp.exp(sim - scale), 0.0), axis=0, keepdims=True)
    lse_cols = scale + jnp.log(total)
    sim = product(own_high, own_low, high, low, 1) * scale
    col = lax.broadcasted_iota(jnp.int32, (1, total_rows), 1)
    row = at_row + (b * ns + sq) * own_rows
    col_doc, row_doc = col % SEGS >= NQ, row % SEGS >= NQ
    number = lambda at: (at // SEGS) * NQ + at % SEGS - NQ
    lse_rows = scale + jnp.log(
        jnp.sum(jnp.where(col_doc, jnp.exp(sim - scale), 0.0), axis=1, keepdims=True)
    )
    chosen = col_doc & (number(col) == pair_col)
    positive = jnp.sum(jnp.where(chosen, sim, 0.0), axis=1, keepdims=True)
    loss[...] = jnp.broadcast_to(lse_rows - positive, loss.shape)
    as_query = jnp.exp(sim - lse_rows) - chosen.astype(F32)
    chosen_by = number(row) == pair_row
    as_doc = jnp.exp(jnp.where(col_doc, MASKED, sim - lse_cols)) - chosen_by.astype(F32)
    grad = jnp.where(row_doc, jnp.where(col_doc, 0.0, as_doc), jnp.where(col_doc, as_query, 0.0))
    grad_high, grad_low = split_two(grad)
    demb = product(grad_high, grad_low, high, low, 0) * scale
    dpool = inv * demb - inv * inv * inv * avg * jnp.sum(avg * demb, axis=-1, keepdims=True)
    dpool_high, dpool_low = split_two(dpool / len_col)
    pad = jnp.zeros((64 - own_rows, width), F32)
    stacked = jnp.concatenate([dpool_high.astype(F32), pad, dpool_low.astype(F32), pad], axis=0)
    dp[...] = stacked.astype(BF16)

    members, at = [], 0
    for g in groups:
        members.append(range(at, at + len(g)))
        at += len(g)
    square_outs = {2: g_out}
    outs = {}
    late = len(groups) - 3
    for g, ix in enumerate(members):
        for i in ix:
            a, _, _, out_lo, _ = flat[i]
            if g >= late:
                out = (g_query, g_key, g_value)[g - late]
            else:
                out = (g_in, g_down, g_out)[a]
            outs[i] = (out, out_lo)
    red = Reducer(grid, flat, partners, my, (wi, wd, wo), outs, send_sem, recv_sem, bufs)
    plan = backward_plan(nd, len(groups), rows, ns)
    small_order = grid.order(0)[::-1]

    def small_copy(kk):
        return remote(
            small, small_recv.at[kk], sm_send.at[kk], sm_recv.at[kk], partners[small_order[kk]]
        )

    def run_at(point):
        for kind, *what in plan.get(point, ()):
            if kind == "g":
                g, kk = what
                for i in members[g]:
                    red.step(i, kk)
            elif kind == "x":
                r, j = what
                row_back(1, *backs[1], r, j).start()
            else:
                (kk,) = what
                if kk > 0:
                    small_copy(kk - 1).wait()
                    small[...] += small_recv[kk - 1]
                if kk < nd:
                    small_copy(kk).start()

    def run_in(name, now, steps):
        for c in range(steps):
            if (name, c) in plan:
                pl.when(now == c)(functools.partial(run_at, (name, c)))

    def columns(u):
        return jnp.sum(u, axis=0, keepdims=True)

    def norm_back(g, n, inv_std):
        return inv_std * (
            g - jnp.mean(g, axis=-1, keepdims=True) - n * jnp.mean(g * n, axis=-1, keepdims=True)
        )

    for c in first:
        c.wait()
    small[...] = jnp.zeros_like(small)
    g1, g2 = vecs[ROW_G1 : ROW_G1 + 1], vecs[ROW_G2 : ROW_G2 + 1]
    down_rows = wd.shape[-2]
    low_digits = (width // down_rows).bit_length() - 1
    top = nd - low_digits
    down_ix = lambda c: tuple((c >> (top - 1 - e)) % 2 for e in range(top))
    dev = (slice(None),) * (nd + 1)

    def bump(at, u):
        small[at : at + 1] += u

    def feed_tile(t, carry):
        r = t // tiles
        start = lax.rem(t, tiles) * tile_rows
        at = pl.ds(pl.multiple_of(t * tile_rows, tile_rows), tile_rows)
        seg = segment_of(lens, base + r, (tile_rows, 1), 0, start)
        place = jnp.where(seg < SEGS, r * SEGS + seg, -1)
        lane = lax.broadcasted_iota(jnp.int32, (tile_rows, 128), 1)
        mine = (lane % 64 == place).astype(F32).astype(BF16)
        dh2 = dot(mine, dp[...])
        m2 = t_att[at].astype(F32)
        bump(ROW_G2, columns(dh2 * m2))
        bump(ROW_S2, columns(dh2))
        dpre2 = norm_back(dh2 * g2, m2, i2_s[at, :1])
        dfeed = dpre2.astype(BF16)
        t_feed[at] = dfeed
        bump(ROW_BD, columns(dfeed.astype(F32)))
        dh1 = dpre2
        for c in range(chunks):
            w = wd[down_ix(c)].reshape(width, width)
            din = (dot(dfeed, w, 1, 1) * big1[at, lanes(c)].astype(F32)).astype(BF16)
            big1[at, lanes(c)] = din
            bump(ROW_BI + c, columns(din.astype(F32)))
            dh1 = dh1 + dot(din, wi[dev + (lanes(c),)].reshape(width, width), 1, 1)
        m1 = t_br[at].astype(F32)
        bump(ROW_G1, columns(dh1 * m1))
        bump(ROW_S1, columns(dh1))
        dbranch = norm_back(dh1 * g1, m1, i1_s[at, :1]).astype(BF16)
        t_br[at] = dbranch
        bump(ROW_BO, columns(dbranch.astype(F32)))
        t_att[at] = dot(dbranch, wo[...].reshape(width, width), 1, 1).astype(BF16)
        return carry

    lax.fori_loop(0, rows * tiles, feed_tile, 0)

    square = (2,) * nd + wo.shape[-2:]

    def outer(lhs, rhs):
        return dot(lhs, rhs, 0, 0)

    fourth = []

    def phase_in():
        for c in second[:1]:
            c.wait()
        for c in range(chunks):
            run_at(("in", c))
            res = outer(t_h1[...], big1[:, lanes(c)])
            wi[dev + (lanes(c),)] = res.reshape(square).astype(BF16)
        for r in range(rows):
            for c, u in enumerate((q, k, v)):
                fourth.append(load(u.at[r], big1.at[row_at(r), lanes(c)]))
            fourth.append(load(x.at[r], t_h1.at[row_at(r)]))

    def phase_down():
        second[1].wait()
        for c in range(chunks):
            run_at(("down", c))
            res = outer(big2[:, lanes(c)], t_feed[...])
            wd[down_ix(c)] = res.reshape((2,) * low_digits + (down_rows, width)).astype(BF16)

    def phase_out():
        for c in second[2:]:
            c.wait()
        run_at("out")
        wo[...] = outer(t_o[...], t_br[...]).reshape(square).astype(BF16)

    n_pairs = HEADS // 2
    slots = p_s.shape[0]
    lane = lax.broadcasted_iota(jnp.int32, (1, 128), 1)

    def probs_copy(s):
        slot = lax.rem(s, slots)
        pair = pl.ds(lax.rem(s, n_pairs) * 2, 2)
        return pltpu.make_async_copy(p.at[s // n_pairs, pair], p_s.at[slot], p_sem.at[slot])

    for s in range(slots - 1):
        probs_copy(s).start()

    def phase_attention(r):
        if r == 0:
            for c in fourth:
                c.wait()

        def pair_step(s, carry):
            run_in(("attention", r), s, n_pairs)
            g = r * n_pairs + s
            probs_copy(g).wait()

            @pl.when(g + slots - 1 < rows * n_pairs)
            def _():
                probs_copy(g + slots - 1).start()

            slot = lax.rem(g, slots)
            at = lambda c: pl.ds(pl.multiple_of(c * width + s * 128, 128), 128)
            qp, kp, vp = (big1[row_at(r), at(c)] for c in range(3))
            dop = t_att[row_at(r), at(0)]
            kt = kp.T
            zero = jnp.zeros_like(vp)
            head = lambda u, h: jnp.where(lane // HEAD_DIM == h, u, zero)
            dprobs = [dot(head(vp, h), dop, 1, 1) for h in range(2)]
            dv = dot(p_s[slot, 0], head(dop, 0)) + dot(p_s[slot, 1], head(dop, 1))
            ds = []
            for h in range(2):
                probs = p_s[slot, h].astype(F32)
                weighted = probs * dprobs[h]
                ds.append((weighted - probs * jnp.sum(weighted, axis=0, keepdims=True)).astype(BF16))
            dk = dot(ds[0], head(qp, 0)) + dot(ds[1], head(qp, 1))
            dqt = [
                dot(kt[h * HEAD_DIM : (h + 1) * HEAD_DIM], ds[h]) * HEAD_DIM ** (-0.5)
                for h in range(2)
            ]
            big1[row_at(r), at(0)] = jnp.concatenate(dqt, axis=0).T.astype(BF16)
            big1[row_at(r), at(1)] = dk.astype(BF16)
            big1[row_at(r), at(2)] = dv.astype(BF16)
            return carry

        lax.fori_loop(0, n_pairs, pair_step, 0)

    def phase_input(r):
        if r == 0:
            for c in third:
                c.wait()
        run_at(("input", r))
        dq, dk, dv = (big1[row_at(r), lanes(c)] for c in range(3))
        bump(ROW_BQ, columns(dq.astype(F32)))
        bump(ROW_BV, columns(dv.astype(F32)))
        gx = t_br[row_at(r)].astype(F32)
        for d, w in ((dq, wq), (dk, wk), (dv, wv)):
            gx = gx + dot(d, w[...].reshape(width, width), 1, 1)
        t_att[row_at(r)] = gx.astype(BF16)
        row_back(1, *backs[1], r, 0).start()

    def phase_projection(c):
        run_at(("projection", c))
        for i in members[c]:
            red.sent(i, 0)
        wi[dev + (lanes(c),)] = outer(t_h1[...], big1[:, lanes(c)]).reshape(square).astype(BF16)

    phases = {"in": phase_in, "down": phase_down, "out": phase_out, "attention": phase_attention}
    phases.update({"input": phase_input, "projection": phase_projection})
    for name, *which in BACKWARD_ORDER:
        phases[name](*which)
    run_at("end")

    for g, ix in enumerate(members):
        for i in ix:
            for kk in range(nd):
                if not (kk == 0 and g < 3):
                    red.sent(i, kk)
    for j in range(1, ns):
        emb_near(j).wait_send()
    for f in range(2):
        for kk in range(grid.ks, nd):
            emb_copy(f, kk).wait_send()
    for r in range(rows):
        for e, (src, dst) in enumerate(backs):
            for j in range(ns):
                row_back(e, src, dst, r, j).wait()


BACKWARD_ORDER = (
    ("in",), ("down",), ("out",), ("attention", 0), ("input", 0),
    ("attention", 1), ("input", 1), ("projection", 0), ("projection", 1), ("projection", 2),
)
BACKWARD_PLAN = {
    ("in", 1): (
        ("g", 0, 0),
    ),
    ("in", 2): (
        ("g", 1, 0),
    ),
    ("in", 3): (
        ("g", 2, 0),
    ),
    ("down", 0): (
        ("g", 0, 1), ("g", 1, 1), ("g", 3, 0),
    ),
    ("down", 1): (
        ("g", 2, 1),
    ),
    ("down", 3): (
        ("g", 3, 1), ("g", 0, 2),
    ),
    "out": (
        ("g", 4, 0), ("g", 5, 0), ("g", 6, 0),
    ),
    (("attention", 0), 0): (
        ("g", 1, 2), ("g", 7, 0),
    ),
    (("attention", 0), 1): (
        ("g", 2, 2), ("g", 4, 1), ("g", 5, 1), ("g", 6, 1), ("g", 3, 2), ("g", 7, 1),
    ),
    (("attention", 0), 2): (
        ("g", 0, 3), ("g", 1, 3),
    ),
    (("attention", 0), 3): (
        ("g", 2, 3),
    ),
    (("attention", 0), 5): (
        ("g", 0, 4), ("g", 1, 4), ("g", 4, 2),
    ),
    ("input", 0): (
        ("g", 2, 4),
    ),
    (("attention", 1), 0): (
        ("g", 0, 5), ("g", 5, 2), ("g", 1, 5), ("x", 0, 2), ("x", 0, 1), ("x", 0, 3),
    ),
    (("attention", 1), 1): (
        ("g", 2, 5), ("g", 6, 2),
    ),
    (("attention", 1), 2): (
        ("g", 3, 3),
    ),
    (("attention", 1), 3): (
        ("g", 7, 2),
    ),
    (("attention", 1), 4): (
        ("g", 4, 3),
    ),
    (("attention", 1), 5): (
        ("g", 5, 3),
    ),
    ("input", 1): (
        ("g", 6, 3),
    ),
    ("projection", 0): (
        ("g", 7, 3), ("s", 0), ("x", 1, 2), ("x", 1, 1), ("x", 1, 3),
    ),
    ("projection", 1): (
        ("g", 3, 4), ("g", 8, 0),
    ),
    ("projection", 2): (
        ("g", 4, 4), ("g", 9, 0), ("s", 1),
    ),
    "end": (
        ("g", 5, 4), ("g", 8, 1), ("g", 10, 0), ("g", 6, 4), ("g", 9, 1), ("s", 2), ("g", 7, 4),
        ("g", 10, 1), ("g", 8, 2), ("g", 9, 2), ("s", 3), ("g", 10, 2), ("g", 8, 3), ("g", 3, 5),
        ("g", 9, 3), ("g", 4, 5), ("g", 10, 3), ("g", 5, 5), ("s", 4), ("g", 6, 5), ("g", 8, 4),
        ("g", 7, 5), ("g", 9, 4), ("s", 5), ("g", 10, 4), ("g", 8, 5), ("g", 9, 5), ("g", 10, 5),
    ),
}


def backward_plan(nd, groups, rows, ns):
    if nd == 5 and groups == 11 and rows == 2 and ns == 4:
        return BACKWARD_PLAN
    late = groups - 3
    ops = [("g", g, k) for k in range(nd + 1) for g in range(late)]
    ops += [("x", r, j) for r in range(rows) for j in range(1, ns)]
    ops += [("s", k) for k in range(nd + 1)]
    plan = {("projection", 0): tuple(ops)}
    plan["end"] = tuple(("g", g, k) for k in range(nd + 1) for g in range(late, groups))
    return plan


def backward(grid, lens, pairs, vecs, pool, kept, weights, tile_rows, collective_id):
    nd, ns = grid.nd, grid.seq_size
    x = kept[-2]
    rows, length, width = x.shape
    count = rows * length
    ff = weights[1].shape[-1]
    part, down_part = weights[1].shape[-2], weights[0].shape[-2]
    groups = []
    half = width // 2
    for c in range(ff // width):
        groups.append([(0, c * width + f * half, half, c * width + f * half, f) for f in range(2)])
    for lo in range(0, width, 256):
        groups.append([(1, lo + f * 128, 128, lo + f * 128, f) for f in range(2)])
    groups.append([(2, f * half, half, f * half, f) for f in range(2)])
    for c in range(3):
        groups.append([(0, c * width + f * half, half, f * half, f) for f in range(2)])
    flat = [c for g in groups for c in g]
    n = len(flat)
    bufs = []
    for a, _, ln, _, _ in flat:
        shape = ((down_part if a == 1 else part), ln)
        bufs += [pltpu.VMEM((2,) * (nd - 1 - kk) + shape, BF16) for kk in range(nd)]
    back = struct((rows * ns, length // ns, width), BF16)
    out_shape = [struct((part, ff), F32), struct((down_part, width), F32)]
    out_shape += [struct((part, width), F32)] * 4
    out_shape += [struct((SMALL_ROWS, width), F32), struct((rows * SEGS, 128), F32), back, back]
    low, wide = pltpu.VMEM((count, width), BF16), pltpu.VMEM((count, ff), BF16)
    stat = pltpu.VMEM((count, 128), F32)
    n_loads = 10 + rows + 3 + 4 * rows
    return pl.pallas_call(
        functools.partial(backward_kernel, grid, flat, groups, len(bufs), tile_rows),
        out_shape=out_shape,
        in_specs=[SMEM, SMEM, VMEM, VMEM] + [ANY] * (len(kept) + len(weights)),
        out_specs=[VMEM] * 8 + [ANY] * 2,
        scratch_shapes=[pltpu.VMEM(w.shape, BF16) for w in weights]
        + [wide, wide, low, low, low, low, low, stat, stat]
        + [pltpu.VMEM((3, 2, length, length), BF16)]
        + [pltpu.VMEM((nd, SMALL_ROWS, width), F32)]
        + [pltpu.VMEM((2,) * nd + (rows * SEGS, width + EMB_PAD), F32), pltpu.VMEM((128, width), BF16)]
        + [DMA((n, nd)), DMA((n, nd))]
        + [DMA((2, rows)), DMA((2, rows, ns - 1)), DMA((2, rows, ns - 1))]
        + [DMA((n_loads,)), DMA((3,)), DMA((nd,)), DMA((nd,)), DMA((2, nd)), DMA((2, nd))]
        + [DMA((ns - 1,)), DMA((ns - 1,))]
        + bufs,
        compiler_params=pltpu.CompilerParams(
            collective_id=collective_id, has_side_effects=True, vmem_limit_bytes=BACK_VMEM
        ),
    )(lens, pairs, vecs, pool, *kept, *weights)


BACK_VMEM = 63 * 2**20


def finish_kernel(grid, gx_ref, hid_ref, small_ref, loss_ref, *refs):
    n = 6
    gx_out, hid_out, loss_out, wide_out = refs[n : n + 4]
    vec_outs, outs = refs[n + 4 : n + 12], refs[n + 12 :]
    gx_out[...] = gx_ref[...].astype(F32)
    hid_out[...] = hid_ref[...]

    @pl.when(pl.program_id(0) == 0)
    def _():
        for src, dst in zip(refs[:n], outs, strict=True):
            dst[...] = src[...]
        number = loss_out.shape[0]
        lane = lax.broadcasted_iota(jnp.int32, (1, 128), 1)
        at = lax.broadcasted_iota(jnp.int32, (loss_ref.shape[0], 1), 0)
        mine = at == (lane // NQ) * SEGS + lane % NQ
        row = jnp.sum(jnp.where(mine, loss_ref[...], 0.0), axis=0, keepdims=True)
        loss_out[...] = row[:, :number].reshape(number)
        b, q = grid.here()
        me = b * grid.seq_size + q
        sums = small_ref[...]
        width = sums.shape[1]
        part, wide = vec_outs[0].shape[0], wide_out.shape[0]

        def pick(first, lanes):
            at = lax.broadcasted_iota(jnp.int32, (width, lanes), 0)
            lane = lax.broadcasted_iota(jnp.int32, (width, lanes), 1)
            chosen = (at - first == lane).astype(F32).astype(BF16)
            out, rest = jnp.zeros((sums.shape[0], lanes), F32), sums
            for _ in range(3):
                top = rest.astype(BF16)
                out += dot(top, chosen)
                rest = rest - top.astype(F32)
            return out

        own = pick(me * part, 128)
        for i, out in enumerate(vec_outs):
            out[...] = own[i : i + 1, :part].reshape(part)
        own = pick(lax.rem(me * wide, width), -(-wide // 128) * 128)
        at = lax.broadcasted_iota(jnp.int32, (sums.shape[0], 1), 0)
        own = jnp.where(at == ROW_BI + (me * wide) // width, own, 0.0)
        wide_out[...] = jnp.sum(own, axis=0, keepdims=True)[:, :wide].reshape(wide)


def finish(grid, gx, hid, small, loss, grads):
    rows, lt, width = gx.shape
    wide = grads[0].shape[1] >> grid.nd
    step = rows // 2
    row = pl.BlockSpec((step, lt, width), lambda r: (r, 0, 0))
    full = lambda a: pl.BlockSpec(a.shape, lambda r: (0,) * len(a.shape))
    extra = [struct((loss.shape[0] // SEGS * NQ,), F32), struct((wide,), F32)]
    extra += [struct((width >> grid.nd,), F32)] * 8
    same = [struct(g.shape, F32) for g in grads]
    return pl.pallas_call(
        functools.partial(finish_kernel, grid),
        grid=(rows // step,),
        out_shape=[struct(gx.shape, F32), struct(hid.shape, BF16)] + extra + same,
        in_specs=[row, row, full(small), full(loss)] + [full(g) for g in grads],
        out_specs=[row, row] + [full(e) for e in extra] + [full(g) for g in grads],
        compiler_params=pltpu.CompilerParams(vmem_limit_bytes=VMEM_LIMIT),
    )(gx, hid, small, loss, *grads)


def pack_small(vectors, wide, extra):
    rows = [jnp.pad(v.astype(F32), (0, 128 - v.shape[0])) for v in (*vectors, wide, extra)]
    rows += [jnp.zeros((128,), F32)] * (16 - len(rows))
    return jnp.stack(rows)


def per_device(
    tokens, lengths, pair_ids, w_query, b_query, w_key, w_value, b_value, w_out, b_out,
    norm1_gain, norm1_bias, w_in, b_in, w_down, b_down, norm2_gain, norm2_bias,
):
    blk_size, seq_size = lax.axis_size("blk"), lax.axis_size("seq")
    grid = Grid(blk_size, seq_size)
    devices = blk_size * seq_size
    group_rows, local_len, width = tokens.shape
    rows = group_rows // seq_size
    length = local_len * seq_size
    count = rows * length
    ff = w_in.shape[1]
    part, wide_part, pairs = b_query.shape[0], b_in.shape[0], pair_ids.shape[0]

    vectors = (b_query, b_value, b_out, norm1_gain, norm1_bias, b_down, norm2_gain, norm2_bias)
    if part % 8 == 0:
        res = forward(
            grid, lengths.T, tokens, vectors + (b_in,),
            (w_query, w_key, w_value, w_out, w_in, w_down), 256, 4,
        )
        x, q, k, v, p, o, n1, i1, h1, act, slope, n2, i2, hid = res[:14]
        wq, wk, wv, wo, wi, wd = res[15:21]
        pool, vecs = res[21:]
        kept = (n2, i2, slope, n1, i1, act, h1, o, q, k, v, p, x, hid.reshape(x.shape))
        weights = (wd, wi, wo, wq, wk, wv)
        res = backward(grid, lengths.T, pair_ids, vecs, pool, kept, weights, min(512, length), 3)
        sums, losses, hid_back, gx_back = res[6:]
        out = finish(grid, gx_back, hid_back, sums, losses, res[:6])
        grad_tokens, hidden_out, query_loss, g_wide = out[:4]
        gv, grads = out[4:12], out[12:]
        g_in, g_down, g_out, g_query, g_key, g_value = grads
        return (
            hidden_out, query_loss, grad_tokens, g_query, gv[0], g_key, g_value, gv[1],
            g_out, gv[2], gv[3], gv[4], g_in, g_wide, g_down, gv[5], gv[6], gv[7],
        )

    lens = lax.dynamic_slice_in_dim(lengths, lax.axis_index("seq") * rows, rows, 0)
    small = pack_small(vectors, b_in, pair_ids)
    full, x = gather_all(grid, (w_query, w_key, w_value, small, w_out, w_in, w_down), tokens, 1)
    wq, wk, wv, smalls, wo, wi, wd = full
    smalls = smalls.reshape(devices, 16, 128)
    vecs = smalls[:, : len(vectors), :part].transpose(1, 0, 2).reshape(len(vectors), 1, width)
    bq, bv, bo, g1, s1, bd, g2, s2 = (vecs[i] for i in range(len(vectors)))
    bi = smalls[:, len(vectors), :wide_part].reshape(1, ff)

    q, k, v, p, o = attention(lens, x, wq, wk, wv, bq, bv)
    x2, o2 = x.reshape(count, width), o.reshape(count, width)
    hid, n1, i1, h1, act, slope, n2, i2, pool = feed(
        lens, x2, o2, wo, bo, g1, s1, wi, bi, wd, bd, g2, s2, 256
    )
    all_pairs = smalls[:, len(vectors) + 1, :pairs].reshape(-1, NQ).astype(jnp.int32)

    none = jnp.full((all_pairs.shape[0], SEGS - NQ), -1, jnp.int32)
    pair_row = jnp.concatenate([all_pairs, none], axis=1).reshape(1, -1)
    own_pairs = jnp.concatenate([pair_ids.reshape(rows, NQ), none[:rows]], axis=1).reshape(-1, 1)
    pair_col = jnp.broadcast_to(own_pairs, (rows * SEGS, 128))
    len_col = jnp.broadcast_to(lens.reshape(-1, 1).astype(F32), (rows * SEGS, 128))
    losses, dpool = contrast(grid, pool, len_col, pair_col, pair_row, 2)
    query_loss = losses[:, 0].reshape(rows, SEGS)[:, :NQ].reshape(-1)

    dfeed, dinner, dbranch, dpre1, datt, sums, wide_sums = feed_back(
        lens, dpool, n2, i2, slope, n1, i1, wd, wi, wo, g2, g1, 256
    )
    grad_w_down = outer(act, dfeed, width, width)
    grad_w_in = outer(h1, dinner, width, width)
    grad_w_out = outer(o2, dbranch, width, width)
    dq, dk, dv = attention_back(q, k, v, p, datt.reshape(rows, length, width))
    dq, dk, dv = (d.reshape(count, width) for d in (dq, dk, dv))
    grad_x, sums_in = input_back(dpre1, dq, dk, dv, wq, wk, wv, 256)
    grad_w_query = outer(x2, dq, width, width)
    grad_w_key = outer(x2, dk, width, width)
    grad_w_value = outer(x2, dv, width, width)

    vec_grads = jnp.stack(
        [sums_in[0], sums_in[1], sums[5], sums[3], sums[4], sums[2], sums[0], sums[1]]
    )
    packed = jnp.pad(
        vec_grads.reshape(8, devices, part).transpose(1, 0, 2), ((0, 0), (0, 0), (0, 128 - part))
    )
    wide_grads = jnp.pad(
        wide_sums[0].reshape(devices, 1, wide_part), ((0, 0), (0, 7), (0, 128 - wide_part))
    )
    packed = jnp.concatenate([packed, wide_grads], axis=1).reshape(devices * 16, 128)
    grads, back = scatter_all(
        grid,
        (grad_w_down, grad_w_in, grad_w_out, packed, grad_w_query, grad_w_key, grad_w_value),
        (hid.reshape(rows, length, width), grad_x.reshape(rows, length, width)),
        3,
    )
    g_down, g_in, g_out, g_small, g_query, g_key, g_value = grads
    hidden_out, grad_tokens = back
    gv = [g_small[i, :part] for i in range(8)]
    return (
        hidden_out,
        query_loss,
        grad_tokens.astype(F32),
        g_query,
        gv[0],
        g_key,
        g_value,
        gv[1],
        g_out,
        gv[2],
        gv[3],
        gv[4],
        g_in,
        g_small[8, :wide_part],
        g_down,
        gv[5],
        gv[6],
        gv[7],
    )


def solution(mesh):
    both = ("blk", "seq")
    vec, mat, tok = P(both), P(both, None), P("blk", "seq", None)
    in_specs = (
        tok, P("blk", None), vec, mat, vec, mat, mat, vec, mat, vec, vec, vec, mat, vec, mat, vec,
        vec, vec,
    )
    out_specs = (
        tok, vec, tok, mat, vec, mat, mat, vec, mat, vec, vec, vec, mat, vec, mat, vec, vec, vec,
    )
    return jax.shard_map(
        per_device, mesh=mesh, in_specs=in_specs, out_specs=out_specs, check_vma=False
    )
```

```python
import functools

import jax
import jax.numpy as jnp
from jax import lax
from jax.experimental import pallas as pl
from jax.experimental.pallas import tpu as pltpu
from jax.sharding import PartitionSpec as P

HEADS = 12
HEAD_DIM = 64
NQ = 2
SEGS = 4
TEMPERATURE = 0.05
NORM_EPSILON = 1e-06
MASKED = -1000000000.0
BF16 = jnp.bfloat16
F32 = jnp.float32
MESH = pl.DeviceIdType.MESH
ANY = pl.BlockSpec(memory_space=pl.ANY)
VMEM = pl.BlockSpec(memory_space=pltpu.VMEM)
SMEM = pl.BlockSpec(memory_space=pltpu.SMEM)
DMA = pltpu.SemaphoreType.DMA
VMEM_LIMIT = 60 * 2**20


def dot(a, b, ca=1, cb=0):
    return lax.dot_general(a, b, (((ca,), (cb,)), ((), ())), preferred_element_type=F32)


def struct(shape, dtype):
    return jax.ShapeDtypeStruct(shape, dtype)


def split_two(v):
    high = v.astype(BF16)
    return high, (v - high.astype(F32)).astype(BF16)


class Grid:
    def __init__(self, blk_size, seq_size):
        self.blk_size, self.seq_size = blk_size, seq_size
        self.kb = blk_size.bit_length() - 1
        self.ks = seq_size.bit_length() - 1
        assert 1 << self.kb == blk_size and 1 << self.ks == seq_size
        self.nd = self.kb + self.ks

    def here(self):
        return lax.axis_index("blk"), lax.axis_index("seq")

    def digit(self, b, q, d):
        if d < self.kb:
            w = 1 << (self.kb - 1 - d)
            return (b // w) % 2, w
        w = 1 << (self.nd - 1 - d)
        return (q // w) % 2, w

    def digits(self, b, q):
        return [self.digit(b, q, d)[0] for d in range(self.nd)]

    def partner(self, b, q, d):
        v, w = self.digit(b, q, d)
        if d < self.kb:
            return (b + (1 - 2 * v) * w, q)
        return (b, q + (1 - 2 * v) * w)

    def order(self, flavour):
        seq = list(range(self.kb, self.nd))
        head, last = list(range(self.kb))[:-1][::-1], [self.kb - 1]
        if head:
            r = flavour % len(head)
            head = head[r:] + head[:r]
        return seq + head + last

    def greet(self, b, q, partners, others):
        barrier = pltpu.get_barrier_semaphore()
        targets = [partners[d] for d in range(self.kb)]
        if others is None:
            targets += [partners[d] for d in range(self.kb, self.nd)]
        else:
            targets += [(b, o) for o in others]
        for t in targets:
            pl.semaphore_signal(barrier, inc=1, device_id=t, device_id_type=MESH)
        pl.semaphore_wait(barrier, len(targets))


def remote(src, dst, send, recv, where):
    return pltpu.make_async_remote_copy(
        src_ref=src, dst_ref=dst, send_sem=send, recv_sem=recv, device_id=where, device_id_type=MESH
    )


def flat_view(rows, lanes):
    if rows % 8 == 0:
        return rows, lanes
    return rows * lanes // 128, 128


def pieces(shapes):
    out = []
    for a, (rows, lanes) in enumerate(shapes):
        unit = 768 if rows < 64 else 256
        unit = min(unit, lanes)
        for lo in range(0, lanes, unit):
            half = unit // 2
            if half % 128 == 0:
                out.append([(a, lo, half, 0), (a, lo + half, half, 1)])
            else:
                out.append([(a, lo, unit, 0)])
    return out


def gather_kernel(grid, groups, n, lag, *refs):
    ins, tok = refs[:n], refs[n]
    outs, rows_out = refs[n + 1 : 2 * n + 1], refs[2 * n + 1]
    own_sem, send_sem, recv_sem, tok_own, tok_send, tok_recv = refs[2 * n + 2 :]
    b, q = grid.here()
    nd, ns = grid.nd, grid.seq_size
    my = grid.digits(b, q)
    partners = [grid.partner(b, q, d) for d in range(nd)]
    others = [lax.rem(q + j, ns) for j in range(1, ns)]
    grid.greet(b, q, partners, others)
    flat = [c for g in groups for c in g]
    where = {}
    first = 0
    for gi, g in enumerate(groups):
        where[gi] = list(range(first, first + len(g)))
        first += len(g)

    own = []
    for i, (a, lo, ln, _) in enumerate(flat):
        c = pltpu.make_async_copy(
            ins[a].at[:, pl.ds(lo, ln)],
            outs[a].at[tuple(my) + (slice(None), pl.ds(lo, ln))],
            own_sem.at[i],
        )
        c.start()
        own.append(c)
    copies = {}

    def stage(i, k):
        a, lo, ln, flavour = flat[i]
        order = grid.order(flavour)
        d = order[k]
        if k == 0:
            src = ins[a].at[:, pl.ds(lo, ln)]
            dst = outs[a].at[tuple(my) + (slice(None), pl.ds(lo, ln))]
        else:
            if k == 1:
                own[i].wait()
            copies[(i, k - 1)].wait_recv()
            done = order[:k]
            ix = tuple(slice(None) if e in done else my[e] for e in range(nd))
            ix = ix + (slice(None), pl.ds(lo, ln))
            src, dst = outs[a].at[ix], outs[a].at[ix]
        c = remote(src, dst, send_sem.at[i, k], recv_sem.at[i, k], partners[d])
        c.start()
        copies[(i, k)] = c

    row_copies = []
    total, lt, _ = tok.shape
    per = total // ns

    def send_rows():
        at = pl.ds(pl.multiple_of(q * lt, lt), lt)
        for r in range(per):
            c = pltpu.make_async_copy(tok.at[q * per + r], rows_out.at[r, at], tok_own.at[r])
            c.start()
            row_copies.append(c)
            for j in range(1, ns):
                o = others[j - 1]
                c = remote(
                    tok.at[o * per + r],
                    rows_out.at[r, at],
                    tok_send.at[j - 1, r],
                    tok_recv.at[j - 1, r],
                    (b, o),
                )
                c.start()
                row_copies.append(c)

    ng = len(groups)
    for t in range(ng + lag * (nd - 1)):
        for k in range(nd - 1, -1, -1):
            g = t - lag * k
            if 0 <= g < ng:
                for i in where[g]:
                    stage(i, k)
        if t == 2:
            send_rows()
    for i in range(len(flat)):
        copies[(i, nd - 1)].wait_recv()
    for i in range(len(flat)):
        for k in range(nd):
            copies[(i, k)].wait_send()
    for c in row_copies:
        c.wait()


def gather_all(grid, blocks, tokens, collective_id):
    nd, ns = grid.nd, grid.seq_size
    n = len(blocks)
    views = [x.reshape(flat_view(*x.shape)) for x in blocks]
    groups = pieces([v.shape for v in views])
    count = sum(len(g) for g in groups)
    total, lt, width = tokens.shape
    per = total // ns
    outs = [struct((2,) * nd + v.shape, v.dtype) for v in views]
    outs.append(struct((per, lt * ns, width), tokens.dtype))
    res = pl.pallas_call(
        functools.partial(gather_kernel, grid, groups, n, 2),
        out_shape=outs,
        in_specs=[VMEM] * (n + 1),
        out_specs=[ANY] * (n + 1),
        scratch_shapes=[
            DMA((count,)),
            DMA((count, nd)),
            DMA((count, nd)),
            DMA((per,)),
            DMA((ns - 1, per)),
            DMA((ns - 1, per)),
        ],
        compiler_params=pltpu.CompilerParams(
            collective_id=collective_id, has_side_effects=True, vmem_limit_bytes=VMEM_LIMIT
        ),
    )(*views, tokens)
    devices = 1 << nd
    full = [
        r.reshape((devices * x.shape[0], x.shape[1])) for r, x in zip(res[:-1], blocks, strict=True)
    ]
    return full, res[-1]


def reduce_plan(grid, flavour):
    free = list(range(grid.nd))
    plan = []
    for d in grid.order(flavour)[::-1]:
        pos = free.index(d)
        plan.append((d, 1 << pos, 1 << (len(free) - pos - 1)))
        free.remove(d)
    return plan


def scatter_kernel(grid, flat, n, nx, lag, *refs):
    nd, ns = grid.nd, grid.seq_size
    ins, rows_in = refs[:n], refs[n : n + nx]
    outs, rows_out = refs[n + nx : 2 * n + nx], refs[2 * n + nx : 2 * n + 2 * nx]
    rest = list(refs[2 * n + 2 * nx :])
    own_sem, send_sem, recv_sem, x_own, x_send, x_recv = rest[:6]
    bufs = rest[6:]
    b, q = grid.here()
    my = grid.digits(b, q)
    partners = [grid.partner(b, q, d) for d in range(nd)]
    others = [lax.rem(q + j, ns) for j in range(1, ns)]
    grid.greet(b, q, partners, others)

    row_copies = []
    for x in range(nx):
        per, length, _ = rows_in[x].shape
        lt = length // ns
        for r in range(per):
            at = pl.ds(pl.multiple_of(q * lt, lt), lt)
            c = pltpu.make_async_copy(
                rows_in[x].at[r, at], rows_out[x].at[q * per + r], x_own.at[x, r]
            )
            c.start()
            row_copies.append(c)

    def send_rows(x):
        per, length, _ = rows_in[x].shape
        lt = length // ns
        for r in range(per):
            for j in range(1, ns):
                o = others[j - 1]
                c = remote(
                    rows_in[x].at[r, pl.ds(pl.multiple_of(o * lt, lt), lt)],
                    rows_out[x].at[q * per + r],
                    x_send.at[x, j - 1, r],
                    x_recv.at[x, j - 1, r],
                    (b, o),
                )
                c.start()
                row_copies.append(c)

    per_piece = 1 + 2 * nd - 1
    copies, own = {}, {}

    def buffers(i):
        mine = bufs[i * per_piece : (i + 1) * per_piece]
        return mine[0], mine[1 : 1 + nd], mine[1 + nd :]

    for i, (a, lo, ln, flavour) in enumerate(flat):
        d = reduce_plan(grid, flavour)[0][0]
        ix = tuple(my[e] if e == d else slice(None) for e in range(nd)) + (slice(None), pl.ds(lo, ln))
        c = pltpu.make_async_copy(ins[a].at[ix], buffers(i)[0], own_sem.at[i])
        c.start()
        own[i] = c

    def send(i, k):
        a, lo, ln, flavour = flat[i]
        d, pre, post = reduce_plan(grid, flavour)[k]
        start, recv, acc = buffers(i)
        if k == 0:
            ix = tuple((1 - my[e]) if e == d else slice(None) for e in range(nd))
            src = ins[a].at[ix + (slice(None), pl.ds(lo, ln))]
        else:
            src = acc[k - 1].at[:, 1 - my[d]]
        c = remote(src, recv[k], send_sem.at[i, k], recv_sem.at[i, k], partners[d])
        c.start()
        copies[(i, k)] = c

    def add(i, k):
        a, lo, ln, flavour = flat[i]
        plan = reduce_plan(grid, flavour)
        d, pre, post = plan[k]
        start, recv, acc = buffers(i)
        copies[(i, k)].wait_recv()
        if k == 0:
            own[i].wait()
        if k == nd - 1:
            total = acc[k - 1][0, my[d], 0].astype(F32) + recv[k][0, 0].astype(F32)
            outs[a][:, lo : lo + ln] = total
            return
        _, pre2, post2 = plan[k + 1]

        def one(j, carry):
            if k == 0:
                ix = tuple((j // (1 << (nd - 2 - e))) % 2 for e in range(nd - 1))
                mine, other = start[ix], recv[0][ix]
            else:
                mine = acc[k - 1][j // post, my[d], j % post]
                other = recv[k][j // post, j % post]
            total = mine.astype(F32) + other.astype(F32)
            acc[k][j // (2 * post2), (j // post2) % 2, j % post2] = total.astype(acc[k].dtype)
            return carry

        lax.fori_loop(0, pre * post, one, 0)

    groups = sorted({c[4] for c in [(*f, gi) for f, gi in zip(flat, group_of(flat))]})
    members = {g: [i for i, gi in enumerate(group_of(flat)) if gi == g] for g in groups}
    ng = len(groups)
    for t in range(ng + lag * nd):
        for k in range(nd, -1, -1):
            g = t - lag * k
            if 0 <= g < ng:
                for i in members[g]:
                    if k > 0:
                        add(i, k - 1)
                    if k < nd:
                        send(i, k)
        if t == 0:
            for x in range(nx):
                send_rows(x)
    for i in range(len(flat)):
        for k in range(nd):
            copies[(i, k)].wait_send()
    for c in row_copies:
        c.wait()


def group_of(flat):
    ids, last = [], -1
    for _, _, _, flavour in flat:
        if flavour == 0:
            last += 1
        ids.append(last)
    return ids


def scatter_all(grid, grads, rows_back, collective_id):
    nd, ns = grid.nd, grid.seq_size
    devices = 1 << nd
    views, finals = [], []
    for g in grads:
        rows = g.shape[0] // devices
        finals.append((rows, g.shape[1]))
        views.append(g.reshape((2,) * nd + flat_view(rows, g.shape[1])))
    flat = [c for g in pieces([v.shape[-2:] for v in views]) for c in g]
    n, nx = len(views), len(rows_back)
    scratch = []
    for a, _, ln, flavour in flat:
        rows, dtype = views[a].shape[-2], views[a].dtype
        plan = reduce_plan(grid, flavour)
        scratch.append(pltpu.VMEM((2,) * (nd - 1) + (rows, ln), dtype))
        for k, (_, pre, post) in enumerate(plan):
            shape = (2,) * (nd - 1) if k == 0 else (pre, post)
            scratch.append(pltpu.VMEM(shape + (rows, ln), dtype))
        for _, pre, post in plan[1:]:
            scratch.append(pltpu.VMEM((pre, 2, post, rows, ln), dtype))
    outs = [struct(v.shape[-2:], F32) for v in views]
    for x in rows_back:
        per, length, width = x.shape
        outs.append(struct((per * ns, length // ns, width), x.dtype))
    per = rows_back[0].shape[0]
    count = len(flat)
    res = pl.pallas_call(
        functools.partial(scatter_kernel, grid, flat, n, nx, 2),
        out_shape=outs,
        in_specs=[ANY] * n + [ANY] * nx,
        out_specs=[VMEM] * n + [ANY] * nx,
        scratch_shapes=[
            DMA((count,)),
            DMA((count, nd)),
            DMA((count, nd)),
            DMA((nx, per)),
            DMA((nx, ns - 1, per)),
            DMA((nx, ns - 1, per)),
        ]
        + scratch,
        compiler_params=pltpu.CompilerParams(
            collective_id=collective_id, has_side_effects=True, vmem_limit_bytes=VMEM_LIMIT
        ),
    )(*views, *rows_back)
    return [r.reshape(s) for r, s in zip(res[:n], finals, strict=True)], res[n:]


def segment_of(lens, r, shape, axis, start=0):
    t = lax.broadcasted_iota(jnp.int32, shape, axis) + start
    end = lens[r, 0]
    seg = (t >= end).astype(jnp.int32)
    for k in range(1, SEGS):
        end = end + lens[r, k]
        seg = seg + (t >= end).astype(jnp.int32)
    return seg


def attention_kernel(
    lens, x_ref, wq, wk, wv, bq, bv, q_ref, k_ref, v_ref, p_ref, o_ref, vt_ref, ot_ref, bias_ref
):
    x = x_ref[0]
    length = x.shape[0]
    r = pl.program_id(0)
    seg_k = segment_of(lens, r, (length, 1), 0)
    seg_q = segment_of(lens, r, (1, length), 1)
    bias_ref[...] = jnp.where(seg_k == seg_q, 0.0, MASKED)
    q_ref[0] = ((dot(x, wq[...]) + bq[...]) * HEAD_DIM ** (-0.5)).astype(BF16)
    k_ref[0] = dot(x, wk[...]).astype(BF16)
    v = dot(x, wv[...]) + bv[...]
    v_ref[0] = v.astype(BF16)
    vt_ref[...] = v.T.astype(BF16)
    lane = lax.broadcasted_iota(jnp.int32, (1, 128), 1)

    def pair(p, carry):
        sl = pl.ds(pl.multiple_of(p * 128, 128), 128)
        qp, kp = q_ref[0, :, sl], k_ref[0, :, sl]
        for h in range(2):
            km = jnp.where(lane // HEAD_DIM == h, kp, jnp.zeros_like(kp))
            hs = pl.ds(pl.multiple_of(p * 128 + h * HEAD_DIM, HEAD_DIM), HEAD_DIM)
            s = dot(km, qp, 1, 1) + bias_ref[...]
            e = jnp.exp(s - jnp.max(s, axis=0, keepdims=True))
            pt = (e * (1.0 / jnp.sum(e, axis=0, keepdims=True))).astype(BF16)
            p_ref[0, p * 2 + h] = pt
            ot_ref[hs, :] = dot(vt_ref[hs, :], pt).astype(BF16)
        return carry

    lax.fori_loop(0, HEADS // 2, pair, 0)
    o_ref[0] = ot_ref[...].T


def attention(lens, x, wq, wk, wv, bq, bv):
    rows, length, width = x.shape
    row = lambda *s: pl.BlockSpec((1,) + s, lambda r: (r,) + (0,) * len(s))
    full = lambda *s: pl.BlockSpec(s, lambda r: (0,) * len(s))
    tokens = struct((rows, length, width), BF16)
    return pl.pallas_call(
        attention_kernel,
        grid=(rows,),
        out_shape=[tokens] * 3 + [struct((rows, HEADS, length, length), BF16), tokens],
        in_specs=[SMEM, row(length, width)] + [full(width, width)] * 3 + [full(1, width)] * 2,
        out_specs=[row(length, width)] * 3 + [row(HEADS, length, length), row(length, width)],
        scratch_shapes=[
            pltpu.VMEM((width, length), BF16),
            pltpu.VMEM((width, length), BF16),
            pltpu.VMEM((length, length), F32),
        ],
        compiler_params=pltpu.CompilerParams(vmem_limit_bytes=VMEM_LIMIT),
    )(lens, x, wq, wk, wv, bq, bv)


def layer_norm(v):
    c = v - jnp.mean(v, axis=-1, keepdims=True)
    inv = lax.rsqrt(jnp.mean(c * c, axis=-1, keepdims=True) + NORM_EPSILON)
    return c * inv, inv


def feed_kernel(
    tiles, lens, x_ref, o_ref, wo, bo, g1, s1, wi, bi, wd, bd, g2, s2,
    hid_ref, n1_ref, i1_ref, h1_ref, act_ref, slope_ref, n2_ref, i2_ref, pool_ref,
):
    t = pl.program_id(0)
    rows = x_ref.shape[0]
    pre1 = x_ref[...].astype(F32) + dot(o_ref[...], wo[...]) + bo[...]
    n1, i1 = layer_norm(pre1)
    h1 = n1 * g1[...] + s1[...]
    h1_low = h1.astype(BF16)
    n1_ref[...] = n1.astype(BF16)
    h1_ref[...] = h1_low
    i1_ref[...] = jnp.broadcast_to(i1, i1_ref.shape)
    acc = h1 + bd[...]
    chunk = wd.shape[1]
    for lo in range(0, wi.shape[1], chunk):
        sl = slice(lo, lo + chunk)
        inner = dot(h1_low, wi[:, sl]) + bi[:, sl]
        phi = 0.5 + 0.5 * lax.erf(inner * (0.5**0.5))
        act = (inner * phi).astype(BF16)
        act_ref[:, sl] = act
        density = jnp.exp(-0.5 * inner * inner) * 0.3989422804014327
        slope_ref[:, sl] = (phi + inner * density).astype(BF16)
        acc = acc + dot(act, wd[sl, :])
    n2, i2 = layer_norm(acc)
    h2 = n2 * g2[...] + s2[...]
    high, low = split_two(h2)
    hid_ref[...] = high
    n2_ref[...] = n2.astype(BF16)
    i2_ref[...] = jnp.broadcast_to(i2, i2_ref.shape)
    r = t // tiles
    seg = segment_of(lens, r, (1, rows), 1, (t % tiles) * rows)
    slot = jnp.where(seg < SEGS, r * SEGS + seg, -1)
    members = lax.broadcasted_iota(jnp.int32, (pool_ref.shape[0], rows), 0) == slot
    members = members.astype(F32).astype(BF16)
    part = dot(members, high) + dot(members, low)

    @pl.when(t == 0)
    def _():
        pool_ref[...] = part

    @pl.when(t != 0)
    def _():
        pool_ref[...] += part


def feed(lens, x, o, wo, bo, g1, s1, wi, bi, wd, bd, g2, s2, tile_rows):
    count, width = x.shape
    rows = lens.shape[0]
    ff = wi.shape[1]
    tiles = count // rows // tile_rows
    tile = lambda w: pl.BlockSpec((tile_rows, w), lambda t: (t, 0))
    full = lambda *s: pl.BlockSpec(s, lambda t: (0,) * len(s))
    vec = full(1, width)
    low, col = struct((count, width), BF16), struct((count, 128), F32)
    wide = struct((count, ff), BF16)
    return pl.pallas_call(
        functools.partial(feed_kernel, tiles),
        grid=(count // tile_rows,),
        out_shape=[low, low, col, low, wide, wide, low, col, struct((rows * SEGS, width), F32)],
        in_specs=[SMEM, tile(width), tile(width), full(width, width), vec, vec, vec]
        + [full(width, ff), full(1, ff), full(ff, width), vec, vec, vec],
        out_specs=[tile(width), tile(width), tile(128), tile(width), tile(ff), tile(ff)]
        + [tile(width), tile(128), full(rows * SEGS, width)],
        compiler_params=pltpu.CompilerParams(vmem_limit_bytes=VMEM_LIMIT),
    )(lens, x, o, wo, bo, g1, s1, wi, bi, wd, bd, g2, s2)


def contrast_kernel(grid, pool_ref, len_ref, pair_ref, pairs_ref, loss_ref, dpool_ref, emb, send_sem, recv_sem):
    nd = grid.nd
    b, q = grid.here()
    my = grid.digits(b, q)
    partners = [grid.partner(b, q, d) for d in range(nd)]
    own_rows, width = pool_ref.shape
    count = own_rows << nd
    avg = pool_ref[...] / len_ref[:, :1]
    inv = lax.rsqrt(jnp.sum(avg * avg, axis=-1, keepdims=True) + NORM_EPSILON)
    own = avg * inv
    emb[tuple(my)] = own
    grid.greet(b, q, partners, None)
    order = grid.order(0)
    for k, d in enumerate(order):
        ix = tuple(slice(None) if e in order[:k] else my[e] for e in range(nd))
        c = remote(emb.at[ix], emb.at[ix], send_sem.at[k], recv_sem.at[k], partners[d])
        c.start()
        c.wait()
    high, low = split_two(emb[...].reshape(count, width))
    own_high, own_low = split_two(own)
    scale = 1.0 / TEMPERATURE

    def product(ah, al, bh, bl, cb):
        return dot(ah, bh, 1, cb) + dot(ah, bl, 1, cb) + dot(al, bh, 1, cb)

    total = jnp.zeros((1, count), F32)
    step = min(count, 256)
    for lo in range(0, count, step):
        sim = product(high[lo : lo + step], low[lo : lo + step], high, low, 1) * scale
        at = lax.broadcasted_iota(jnp.int32, (step, 1), 0)
        total += jnp.sum(jnp.where(at % SEGS >= NQ, jnp.exp(sim - scale), 0.0), axis=0, keepdims=True)
    lse_cols = scale + jnp.log(total)
    sim = product(own_high, own_low, high, low, 1) * scale
    col = lax.broadcasted_iota(jnp.int32, (1, count), 1)
    row = lax.broadcasted_iota(jnp.int32, (own_rows, 1), 0) + (b * grid.seq_size + q) * own_rows
    col_doc, row_doc = col % SEGS >= NQ, row % SEGS >= NQ
    number = lambda at: (at // SEGS) * NQ + at % SEGS - NQ
    lse_rows = scale + jnp.log(
        jnp.sum(jnp.where(col_doc, jnp.exp(sim - scale), 0.0), axis=1, keepdims=True)
    )
    chosen = col_doc & (number(col) == pair_ref[:, :1])
    positive = jnp.sum(jnp.where(chosen, sim, 0.0), axis=1, keepdims=True)
    loss_ref[...] = jnp.broadcast_to(lse_rows - positive, loss_ref.shape)
    as_query = jnp.exp(sim - lse_rows) - chosen.astype(F32)
    chosen_by = number(row) == pairs_ref[:1]
    as_doc = jnp.exp(jnp.where(col_doc, MASKED, sim - lse_cols)) - chosen_by.astype(F32)
    grad = jnp.where(row_doc, jnp.where(col_doc, 0.0, as_doc), jnp.where(col_doc, as_query, 0.0))
    grad_high, grad_low = split_two(grad)
    demb = product(grad_high, grad_low, high, low, 0) * scale
    dpool = inv * demb - inv * inv * inv * avg * jnp.sum(avg * demb, axis=-1, keepdims=True)
    dpool_high, dpool_low = split_two(dpool / len_ref[:, :1])
    pad = jnp.zeros((64 - own_rows, width), F32)
    stacked = jnp.concatenate([dpool_high.astype(F32), pad, dpool_low.astype(F32), pad], axis=0)
    dpool_ref[...] = stacked.astype(BF16)


def contrast(grid, pool, len_col, pair_col, pair_row, collective_id):
    own_rows, width = pool.shape
    return pl.pallas_call(
        functools.partial(contrast_kernel, grid),
        out_shape=[struct((own_rows, 128), F32), struct((128, width), BF16)],
        in_specs=[VMEM] * 4,
        out_specs=[VMEM] * 2,
        scratch_shapes=[
            pltpu.VMEM((2,) * grid.nd + (own_rows, width), F32),
            DMA((grid.nd,)),
            DMA((grid.nd,)),
        ],
        compiler_params=pltpu.CompilerParams(
            collective_id=collective_id, has_side_effects=True, vmem_limit_bytes=VMEM_LIMIT
        ),
    )(pool, len_col, pair_col, pair_row)


def feed_back_kernel(
    tiles, lens, dp_ref, n2_ref, i2_ref, slope_ref, n1_ref, i1_ref, wd, wi, wo, g2, g1,
    dfeed_ref, dinner_ref, dbranch_ref, dpre1_ref, datt_ref, sums_ref, wide_ref,
):
    t = pl.program_id(0)
    rows = n2_ref.shape[0]

    @pl.when(t == 0)
    def _():
        sums_ref[...] = jnp.zeros_like(sums_ref)
        wide_ref[...] = jnp.zeros_like(wide_ref)

    def columns(v):
        return jnp.sum(v, axis=0, keepdims=True)

    def norm_back(g, n, inv):
        return inv * (
            g - jnp.mean(g, axis=-1, keepdims=True) - n * jnp.mean(g * n, axis=-1, keepdims=True)
        )

    r = t // tiles
    seg = segment_of(lens, r, (rows, 1), 0, (t % tiles) * rows)
    slot = jnp.where(seg < SEGS, r * SEGS + seg, -1)
    lane = lax.broadcasted_iota(jnp.int32, (rows, 128), 1)
    members = (lane % 64 == slot).astype(F32).astype(BF16)
    dh2 = dot(members, dp_ref[...])
    n2 = n2_ref[...].astype(F32)
    sums_ref[0:1] += columns(dh2 * n2)
    sums_ref[1:2] += columns(dh2)
    dpre2 = norm_back(dh2 * g2[...], n2, i2_ref[:, :1])
    dfeed = dpre2.astype(BF16)
    dfeed_ref[...] = dfeed
    sums_ref[2:3] += columns(dfeed.astype(F32))
    chunk = wd.shape[1]
    dh1 = dpre2
    for lo in range(0, wi.shape[1], chunk):
        sl = slice(lo, lo + chunk)
        dinner = (dot(dfeed, wd[sl, :], 1, 1) * slope_ref[:, sl].astype(F32)).astype(BF16)
        dinner_ref[:, sl] = dinner
        wide_ref[0:1, sl] += columns(dinner.astype(F32))
        dh1 = dh1 + dot(dinner, wi[:, sl], 1, 1)
    n1 = n1_ref[...].astype(F32)
    sums_ref[3:4] += columns(dh1 * n1)
    sums_ref[4:5] += columns(dh1)
    dpre1 = norm_back(dh1 * g1[...], n1, i1_ref[:, :1])
    dpre1_ref[...] = dpre1
    dbranch = dpre1.astype(BF16)
    dbranch_ref[...] = dbranch
    sums_ref[5:6] += columns(dbranch.astype(F32))
    datt_ref[...] = dot(dbranch, wo[...], 1, 1).astype(BF16)


def feed_back(lens, dp, n2, i2, slope, n1, i1, wd, wi, wo, g2, g1, tile_rows):
    count, width = n2.shape
    rows = lens.shape[0]
    ff = wi.shape[1]
    tiles = count // rows // tile_rows
    tile = lambda w: pl.BlockSpec((tile_rows, w), lambda t: (t, 0))
    full = lambda *s: pl.BlockSpec(s, lambda t: (0,) * len(s))
    low = struct((count, width), BF16)
    return pl.pallas_call(
        functools.partial(feed_back_kernel, tiles),
        grid=(count // tile_rows,),
        out_shape=[low, struct((count, ff), BF16), low, struct((count, width), F32), low]
        + [struct((8, width), F32), struct((8, ff), F32)],
        in_specs=[SMEM, full(128, width), tile(width), tile(128), tile(ff), tile(width), tile(128)]
        + [full(ff, width), full(width, ff), full(width, width), full(1, width), full(1, width)],
        out_specs=[tile(width), tile(ff), tile(width), tile(width), tile(width)]
        + [full(8, width), full(8, ff)],
        compiler_params=pltpu.CompilerParams(vmem_limit_bytes=VMEM_LIMIT),
    )(lens, dp, n2, i2, slope, n1, i1, wd, wi, wo, g2, g1)


def outer_kernel(a_ref, b_ref, o_ref):
    o_ref[...] = dot(a_ref[...], b_ref[...], 0, 0).astype(o_ref.dtype)


def outer(a, b, bm, bn):
    count, m = a.shape
    n = b.shape[1]
    return pl.pallas_call(
        outer_kernel,
        grid=(m // bm, n // bn),
        out_shape=struct((m, n), BF16),
        in_specs=[
            pl.BlockSpec((count, bm), lambda i, j: (0, i)),
            pl.BlockSpec((count, bn), lambda i, j: (0, j)),
        ],
        out_specs=pl.BlockSpec((bm, bn), lambda i, j: (i, j)),
        compiler_params=pltpu.CompilerParams(vmem_limit_bytes=VMEM_LIMIT),
    )(a, b)


def attention_back_kernel(q_ref, k_ref, v_ref, p_ref, do_ref, dq_ref, dk_ref, dv_ref, kt_ref, dqt_ref):
    kt_ref[...] = k_ref[0].T
    lane = lax.broadcasted_iota(jnp.int32, (1, 128), 1)

    def pair(p, carry):
        sl = pl.ds(pl.multiple_of(p * 128, 128), 128)
        qp, vp, dop = q_ref[0, :, sl], v_ref[0, :, sl], do_ref[0, :, sl]
        zero = jnp.zeros_like(vp)
        dv = dk = None
        for h in range(2):
            mine = lane // HEAD_DIM == h
            vm, dom, qm = (jnp.where(mine, u, zero) for u in (vp, dop, qp))
            hs = pl.ds(pl.multiple_of(p * 128 + h * HEAD_DIM, HEAD_DIM), HEAD_DIM)
            pt = p_ref[0, p * 2 + h]
            probs = pt.astype(F32)
            weighted = probs * dot(vm, dop, 1, 1)
            ds = (weighted - probs * jnp.sum(weighted, axis=0, keepdims=True)).astype(BF16)
            dv_h, dk_h = dot(pt, dom), dot(ds, qm)
            dv = dv_h if dv is None else dv + dv_h
            dk = dk_h if dk is None else dk + dk_h
            dqt_ref[hs, :] = (dot(kt_ref[hs, :], ds) * HEAD_DIM ** (-0.5)).astype(BF16)
        dv_ref[0, :, sl] = dv.astype(BF16)
        dk_ref[0, :, sl] = dk.astype(BF16)
        return carry

    lax.fori_loop(0, HEADS // 2, pair, 0)
    dq_ref[0] = dqt_ref[...].T


def attention_back(q, k, v, p, do):
    rows, length, width = q.shape
    row = lambda *s: pl.BlockSpec((1,) + s, lambda r: (r,) + (0,) * len(s))
    return pl.pallas_call(
        attention_back_kernel,
        grid=(rows,),
        out_shape=[struct((rows, length, width), BF16)] * 3,
        in_specs=[row(length, width)] * 3 + [row(HEADS, length, length), row(length, width)],
        out_specs=[row(length, width)] * 3,
        scratch_shapes=[pltpu.VMEM((width, length), BF16), pltpu.VMEM((width, length), BF16)],
        compiler_params=pltpu.CompilerParams(vmem_limit_bytes=VMEM_LIMIT),
    )(q, k, v, p, do)


def input_back_kernel(dpre1_ref, dq_ref, dk_ref, dv_ref, wq, wk, wv, out_ref, sums_ref):
    @pl.when(pl.program_id(0) == 0)
    def _():
        sums_ref[...] = jnp.zeros_like(sums_ref)

    sums_ref[0:1] += jnp.sum(dq_ref[...].astype(F32), axis=0, keepdims=True)
    sums_ref[1:2] += jnp.sum(dv_ref[...].astype(F32), axis=0, keepdims=True)
    total = dpre1_ref[...] + dot(dq_ref[...], wq[...], 1, 1)
    total += dot(dk_ref[...], wk[...], 1, 1) + dot(dv_ref[...], wv[...], 1, 1)
    out_ref[...] = total.astype(out_ref.dtype)


def input_back(dpre1, dq, dk, dv, wq, wk, wv, tile_rows):
    count, width = dpre1.shape
    tile = pl.BlockSpec((tile_rows, width), lambda t: (t, 0))
    full = lambda *s: pl.BlockSpec(s, lambda t: (0,) * len(s))
    return pl.pallas_call(
        input_back_kernel,
        grid=(count // tile_rows,),
        out_shape=[struct((count, width), BF16), struct((8, width), F32)],
        in_specs=[tile] * 4 + [full(width, width)] * 3,
        out_specs=[tile, full(8, width)],
        compiler_params=pltpu.CompilerParams(vmem_limit_bytes=VMEM_LIMIT),
    )(dpre1, dq, dk, dv, wq, wk, wv)


class Turned:
    def __init__(self, ref):
        self.ref = ref

    def __getitem__(self, at):
        return self.ref[at[1], at[0]]


def gelu_gate(v):
    return 0.5 + 0.5 * lax.erf(v * (0.5**0.5))


def gelu_slope(v):
    return gelu_gate(v) + v * (jnp.exp(-0.5 * v * v) * 0.3989422804014327)


class Gatherer:
    def __init__(self, grid, flat, partners, my, blocks, fulls, own_sem, send_sem, recv_sem):
        self.grid, self.flat, self.partners, self.my = grid, flat, partners, my
        self.blocks, self.fulls = blocks, fulls
        self.own_sem, self.send_sem, self.recv_sem = own_sem, send_sem, recv_sem

    def own(self, i):
        a, lo, ln, _ = self.flat[i]
        return pltpu.make_async_copy(
            self.blocks[a].at[:, pl.ds(lo, ln)],
            self.fulls[a].at[tuple(self.my) + (slice(None), pl.ds(lo, ln))],
            self.own_sem.at[i],
        )

    def copy(self, i, k):
        a, lo, ln, flavour = self.flat[i]
        order = self.grid.order(flavour)
        done = order[:k]
        ix = tuple(slice(None) if e in done else self.my[e] for e in range(self.grid.nd))
        dst = self.fulls[a].at[ix + (slice(None), pl.ds(lo, ln))]
        src = self.blocks[a].at[:, pl.ds(lo, ln)] if k == 0 else dst
        return remote(
            src, dst, self.send_sem.at[i, k], self.recv_sem.at[i, k], self.partners[order[k]]
        )

    def step(self, i, k):
        if k == 0:
            self.own(i).start()
        elif k == 1:
            self.own(i).wait()
        if k > 0:
            self.copy(i, k - 1).wait_recv()
        if k < self.grid.nd:
            self.copy(i, k).start()

    def finish(self):
        for i in range(len(self.flat)):
            for k in range(self.grid.nd):
                self.copy(i, k).wait_send()


def forward_kernel(grid, groups, tile_rows, *refs):
    it = iter(refs)
    take = lambda n: [next(it) for _ in range(n)]
    lens, tok = take(2)
    lens = Turned(lens)
    vectors = take(9)
    blocks = take(6)
    x_out, q_out, k_out, v_out, p_out, o_out = take(6)
    n1_out, i1_out, h1_out, act_out, inner_out, n2_out, i2_out, hid_out = take(8)
    full_out = take(7)
    pool, vecs = take(2)
    fulls = take(7)
    x_s, q_s, k_s, v_s, vt_s, mask_s, h_s, bi_s, packed = take(9)
    own_sem, send_sem, recv_sem, tok_own, tok_send, tok_recv, out_sem = take(7)

    b, sq = grid.here()
    nd, ns = grid.nd, grid.seq_size
    my = grid.digits(b, sq)
    partners = [grid.partner(b, sq, d) for d in range(nd)]
    others = [lax.rem(sq + j, ns) for j in range(1, ns)]
    flat = [c for g in groups for c in g]
    members, first = [], 0
    for g in groups:
        members.append(range(first, first + len(g)))
        first += len(g)
    packed[...] = jnp.zeros_like(packed)
    for i, u in enumerate(vectors):
        packed[i : i + 1, : u.shape[0]] = u[...].astype(F32).reshape(1, u.shape[0])
    blocks = [packed] + blocks
    ga = Gatherer(grid, flat, partners, my, blocks, fulls, own_sem, send_sem, recv_sem)
    rows, length, width = x_s.shape
    lt = length // ns
    tiles = length // tile_rows
    grid.greet(b, sq, partners, others)

    def row_copy(r, j):
        at = pl.ds(pl.multiple_of(sq * lt, lt), lt)
        if j == 0:
            return pltpu.make_async_copy(tok.at[sq * rows + r], x_s.at[r, at], tok_own.at[r])
        o = others[j - 1]
        return remote(
            tok.at[o * rows + r], x_s.at[r, at], tok_send.at[r, j - 1], tok_recv.at[r, j - 1], (b, o)
        )

    plan = forward_plan(nd, len(groups), ns)

    def run_at(point):
        for g, k in plan.get(point, ()):
            if k < 0:
                row_copy(g, -k).start()
            else:
                for i in members[g]:
                    ga.step(i, k)

    def hook(name, steps):
        def run():
            now = pl.program_id(0)
            for c in range(steps):
                if (name, c) in plan:
                    pl.when(now == c)(functools.partial(run_at, (name, c)))

        return run

    def arrived(*which):
        for g in which:
            for i in members[g]:
                ga.step(i, nd)

    out_copies = []

    def put(src, dst):
        c = pltpu.make_async_copy(src, dst, out_sem.at[len(out_copies)])
        c.start()
        out_copies.append(c)

    for r in range(rows):
        row_copy(r, 0).start()
    run_at("start")
    arrived(0, 1, 2)
    part = blocks[1].shape[0]
    wide_part = bi_s.shape[1] >> nd
    smalls = fulls[0][...].reshape((1 << nd,) + blocks[0].shape)

    def unpacked(i, size, first, lanes):
        col = lax.broadcasted_iota(jnp.int32, (1, lanes), 1) + first
        device = jnp.floor((col.astype(F32) + 0.5) * (1.0 / size)).astype(jnp.int32)
        at = lax.broadcasted_iota(jnp.int32, (128, lanes), 0)
        spread = (at == col - device * size).astype(F32).astype(BF16)
        owner = lax.broadcasted_iota(jnp.int32, (1 << nd, lanes), 0) == device
        values = dot(smalls[:, i, :].astype(BF16), spread)
        return jnp.sum(jnp.where(owner, values, 0.0), axis=0, keepdims=True)

    for i in range(8):
        vecs[i : i + 1] = unpacked(i, part, 0, width)
    for lo in range(0, bi_s.shape[1], width):
        bi_s[:, lo : lo + width] = unpacked(8, wide_part, lo, width)
    bq, bv, bo, g1, s1, bd, g2, s2 = (vecs[i : i + 1] for i in range(8))
    lane = lax.broadcasted_iota(jnp.int32, (1, 128), 1)

    def square(ref):
        return ref[...].reshape(width, width)

    for r in range(rows):
        run_at(("row", r))
        for j in range(ns):
            c = row_copy(r, j)
            if j == 0:
                c.wait()
            else:
                c.wait_recv()
        put(x_s.at[r], x_out.at[r])
        x = x_s[r]
        q_s[r] = ((dot(x, square(fulls[1])) + bq) * HEAD_DIM ** (-0.5)).astype(BF16)
        k_s[r] = dot(x, square(fulls[2])).astype(BF16)
        v = dot(x, square(fulls[3])) + bv
        v_s[r] = v.astype(BF16)
        vt_s[...] = v.T.astype(BF16)
        for src, dst in ((q_s, q_out), (k_s, k_out), (v_s, v_out)):
            put(src.at[r], dst.at[r])
        seg_k = segment_of(lens, sq * rows + r, (length, 1), 0)
        seg_q = segment_of(lens, sq * rows + r, (1, length), 1)
        mask_s[...] = jnp.where(seg_k == seg_q, 0.0, MASKED)
        att_hook = hook(("attention", r), HEADS // 2)

        def att_body(p_t, o_t, r=r):
            att_hook()
            p = pl.program_id(0)
            sl = pl.ds(pl.multiple_of(p * 128, 128), 128)
            qp, kp = q_s[r, :, sl], k_s[r, :, sl]
            zero = jnp.zeros_like(kp)
            scores = [
                dot(jnp.where(lane // HEAD_DIM == h, kp, zero), qp, 1, 1) + mask_s[...]
                for h in range(2)
            ]
            probs = []
            for h, s in enumerate(scores):
                e = jnp.exp(s - jnp.max(s, axis=0, keepdims=True))
                probs.append((e * (1.0 / jnp.sum(e, axis=0, keepdims=True))).astype(BF16))
                p_t[0, h] = probs[h]
            out = []
            for h in range(2):
                hs = pl.ds(pl.multiple_of(p * 128 + h * HEAD_DIM, HEAD_DIM), HEAD_DIM)
                out.append(dot(vt_s[hs, :], probs[h]))
            o_t[0] = jnp.concatenate(out, axis=0).T.astype(BF16)

        pltpu.emit_pipeline(
            att_body,
            grid=(HEADS // 2,),
            out_specs=[
                pl.BlockSpec((1, 2, length, length), lambda s, r=r: (r, s, 0, 0)),
                pl.BlockSpec((1, length, 128), lambda s, r=r: (r, 0, s)),
            ],
        )(p_out, o_out)

    run_at("in")
    down_groups = width // 256
    arrived(*range(3, len(groups) - down_groups))
    for a in range(6):
        put(fulls[a], full_out[a])
    ff = bi_s.shape[1]
    tile = lambda w: pl.BlockSpec((tile_rows, w), lambda t: (t, 0))

    def tile_at():
        t = pl.program_id(0)
        start = lax.rem(t, tiles) * tile_rows
        return t // tiles, start, pl.ds(pl.multiple_of(start, tile_rows), tile_rows)

    in_hook = hook("in", rows * tiles)

    def in_body(o_t, n1_t, i1_t, h1_t, act_t, inner_t):
        in_hook()
        r, _, at = tile_at()
        pre1 = x_s[r, at].astype(F32) + dot(o_t[0], square(fulls[4])) + bo
        n1, i1 = layer_norm(pre1)
        h1 = n1 * g1 + s1
        low = h1.astype(BF16)
        h_s[r, at] = h1
        n1_t[...] = n1.astype(BF16)
        i1_t[...] = jnp.broadcast_to(i1, i1_t.shape)
        h1_t[...] = low
        for lo in range(0, ff, width):
            w = fulls[5][(slice(None),) * (nd + 1) + (slice(lo, lo + width),)]
            inner = dot(low, w.reshape(width, width)) + bi_s[:, lo : lo + width]
            act_t[:, lo : lo + width] = (inner * gelu_gate(inner)).astype(BF16)
            inner_t[:, lo : lo + width] = inner.astype(BF16)

    pltpu.emit_pipeline(
        in_body,
        grid=(rows * tiles,),
        in_specs=[pl.BlockSpec((1, tile_rows, width), lambda t: (t // tiles, t % tiles, 0))],
        out_specs=[tile(width), tile(128), tile(width), tile(ff), tile(ff)],
    )(o_out, n1_out, i1_out, h1_out, act_out, inner_out)

    run_at("down")
    arrived(*range(len(groups) - down_groups, len(groups)))
    put(fulls[6], full_out[6])
    pool[...] = jnp.zeros_like(pool)
    down_rows = blocks[6].shape[0]
    top = nd - ((width // down_rows).bit_length() - 1)

    def down_body(act_t, hid_t, n2_t, i2_t):
        r, start, at = tile_at()
        acc = h_s[r, at] + bd
        for c, lo in enumerate(range(0, ff, width)):
            ix = tuple((c >> (top - 1 - e)) % 2 for e in range(top))
            acc = acc + dot(act_t[:, lo : lo + width], fulls[6][ix].reshape(width, width))
        n2, i2 = layer_norm(acc)
        high, low = split_two(n2 * g2 + s2)
        hid_t[...] = high
        n2_t[...] = n2.astype(BF16)
        i2_t[...] = jnp.broadcast_to(i2, i2_t.shape)
        seg = segment_of(lens, sq * rows + r, (1, tile_rows), 1, start)
        slot = jnp.where(seg < SEGS, r * SEGS + seg, -1)
        mine = lax.broadcasted_iota(jnp.int32, (pool.shape[0], tile_rows), 0) == slot
        mine = mine.astype(F32).astype(BF16)
        pool[...] += dot(mine, high) + dot(mine, low)

    pltpu.emit_pipeline(
        down_body,
        grid=(rows * tiles,),
        in_specs=[tile(ff)],
        out_specs=[tile(width), tile(width), tile(128)],
    )(act_out, hid_out, n2_out, i2_out)

    ga.finish()
    for r in range(rows):
        for j in range(1, ns):
            row_copy(r, j).wait_send()
    for c in out_copies:
        c.wait()


FORWARD_PLAN = {
    "start": (
        (1, 0), (2, 0), (0, 0), (6, 0), (1, 1), (5, 0), (4, 0), (0, 1), (2, 1), (8, 0),
        (1, 2), (7, 0), (0, 2), (2, 2), (3, 0), (1, 3), (4, 1), (5, 1), (8, 1), (0, 3),
        (0, -2), (4, 2), (1, 4), (3, 1), (7, 1), (6, 1), (0, -3), (0, -1), (2, 3), (0, 4),
        (8, 2), (1, -1), (1, -3), (5, 2), (3, 2), (1, -2), (2, 4), (7, 2), (6, 2), (5, 3),
        (8, 3), (3, 3), (9, 0), (10, 0), (4, 3), (7, 3),
    ),
    (("attention", 0), 3): (
        (8, 4),
    ),
    ("row", 1): (
        (5, 4), (4, 4), (3, 4), (6, 3),
    ),
    (("attention", 1), 0): (
        (10, 1),
    ),
    (("attention", 1), 1): (
        (9, 1),
    ),
    (("attention", 1), 2): (
        (7, 4), (10, 2), (6, 4),
    ),
    (("attention", 1), 4): (
        (9, 2),
    ),
    (("attention", 1), 5): (
        (10, 3),
    ),
    ("in", 3): (
        (10, 4), (9, 4),
    ),
    "in": (
        (9, 3),
    ),
}
def forward_plan(nd, groups, ns):
    if nd == 5 and groups == 11 and ns == 4:
        return FORWARD_PLAN
    ops = []
    for t in range(groups + 2 * nd):
        ops += [(t - 2 * k, k) for k in range(nd - 1, -1, -1) if 0 <= t - 2 * k < groups]
        if t == nd:
            ops += [(r, -j) for r in range(2) for j in range(1, ns)]
    return {"start": tuple(ops)}


def forward(grid, lens, tokens, vectors, weights, tile_rows, collective_id):
    blocks = [struct((16, 128), F32), *weights]
    nd, ns = grid.nd, grid.seq_size
    total, lt, width = tokens.shape
    rows, length = total // ns, lt * ns
    count = rows * length
    ff = blocks[5].shape[1]
    dev = (2,) * nd
    groups = pieces([x.shape for x in blocks])
    groups = [groups[0] + groups[1]] + groups[2:]
    n = sum(len(g) for g in groups)
    seq3 = struct((rows, length, width), BF16)
    low, stat = struct((count, width), BF16), struct((count, 128), F32)
    wide = struct((count, ff), BF16)
    out_shape = [seq3] * 4 + [struct((rows, HEADS, length, length), BF16), seq3]
    out_shape += [low, stat, low, wide, wide, low, stat, low]
    out_shape += [struct(dev + x.shape, x.dtype) for x in blocks]
    out_shape += [struct((rows * SEGS, width), F32), struct((8, width), F32)]
    res = pl.pallas_call(
        functools.partial(forward_kernel, grid, groups, tile_rows),
        out_shape=out_shape,
        in_specs=[SMEM] + [VMEM] * (1 + len(vectors) + len(weights)),
        out_specs=[ANY] * (len(out_shape) - 2) + [VMEM] * 2,
        scratch_shapes=[pltpu.VMEM(dev + x.shape, x.dtype) for x in blocks]
        + [pltpu.VMEM((rows, length, width), BF16)] * 4
        + [pltpu.VMEM((width, length), BF16), pltpu.VMEM((length, length), F32)]
        + [pltpu.VMEM((rows, length, width), F32), pltpu.VMEM((1, ff), F32)]
        + [pltpu.VMEM((16, 128), F32)]
        + [DMA((n,)), DMA((n, nd)), DMA((n, nd))]
        + [DMA((rows,)), DMA((rows, ns - 1)), DMA((rows, ns - 1)), DMA((7 + 4 * rows,))],
        compiler_params=pltpu.CompilerParams(
            collective_id=collective_id, has_side_effects=True, vmem_limit_bytes=VMEM_LIMIT
        ),
    )(lens, tokens, *vectors, *weights)
    return res


class Reducer:
    def __init__(self, grid, flat, partners, my, sources, outs, send_sem, recv_sem, bufs):
        self.grid, self.flat, self.partners, self.my = grid, flat, partners, my
        self.sources, self.outs = sources, outs
        self.send_sem, self.recv_sem = send_sem, recv_sem
        self.bufs = bufs

    def buf(self, i, k):
        return self.bufs[i * self.grid.nd + k]

    def place(self, i, k):
        order = self.grid.order(self.flat[i][4])[::-1]
        free = [d for d in range(self.grid.nd) if d not in order[:k]]
        return order[k], free.index(order[k])

    def copy(self, i, k):
        a, lo, ln, _, _ = self.flat[i]
        d, pos = self.place(i, k)
        ix = (slice(None),) * pos + (1 - self.my[d],) + (slice(None),) * (self.grid.nd - k - pos - 1)
        if k == 0:
            src = self.sources[a].at[ix + (slice(None), pl.ds(lo, ln))]
        else:
            src = self.buf(i, k - 1).at[ix]
        return remote(
            src, self.buf(i, k), self.send_sem.at[i, k], self.recv_sem.at[i, k], self.partners[d]
        )

    def add(self, i, k):
        nd = self.grid.nd
        a, lo, ln, out_lo, _ = self.flat[i]
        d, pos = self.place(i, k)
        self.copy(i, k).wait_recv()
        into = self.buf(i, k)
        left = nd - k - 1
        if left == 0:
            total = self.buf(i, k - 1)[self.my[d]].astype(F32) + into[...].astype(F32)
            out, at = self.outs[i]
            out[:, at : at + ln] = total
            return

        def one(j, carry):
            ix = tuple((j // (1 << (left - 1 - e))) % 2 for e in range(left))
            mine_at = ix[:pos] + (self.my[d],) + ix[pos:]
            if k == 0:
                mine = self.sources[a][mine_at + (slice(None), slice(lo, lo + ln))]
            else:
                mine = self.buf(i, k - 1)[mine_at]
            into[ix] = (mine.astype(F32) + into[ix].astype(F32)).astype(into.dtype)
            return carry

        lax.fori_loop(0, 1 << left, one, 0, unroll=min(4, 1 << left))

    def step(self, i, k):
        if k > 0:
            self.add(i, k - 1)
        if k < self.grid.nd:
            self.copy(i, k).start()

    def sent(self, i, k):
        self.copy(i, k).wait_send()


SMALL_ROWS = 16
ROW_BQ, ROW_BV, ROW_BO, ROW_G1, ROW_S1, ROW_BD, ROW_G2, ROW_S2, ROW_BI = range(9)
EMB_PAD = 128


def backward_kernel(grid, flat, groups, n_bufs, tile_rows, *refs):
    it = iter(refs)
    take = lambda n: [next(it) for _ in range(n)]
    lens, pairs, vecs, pool = take(4)
    lens = Turned(lens)
    n2, i2, inner, n1, i1, act, h1, o, q, k, v, p, x, hid = take(14)
    weights = take(6)
    g_in, g_down, g_out, g_query, g_key, g_value = take(6)
    small, loss, hid_back, gx_back = take(4)
    wd, wi, wo, wq, wk, wv = take(6)
    big1, big2, t_h1, t_o, t_feed, t_br, t_att, i1_s, i2_s, p_s = take(10)
    small_recv, emb, dp = take(3)
    send_sem, recv_sem, ex_own, ex_send, ex_recv, load_sem, p_sem, sm_send, sm_recv = take(9)
    emb_send, emb_recv, near_send, near_recv = take(4)
    bufs = take(n_bufs)

    b, sq = grid.here()
    nd, ns = grid.nd, grid.seq_size
    my = grid.digits(b, sq)
    partners = [grid.partner(b, sq, d) for d in range(nd)]
    others = [lax.rem(sq + j, ns) for j in range(1, ns)]
    rows, length, width = x.shape
    count = rows * length
    ff = big1.shape[1]
    chunks = ff // width
    lt = length // ns
    tiles = length // tile_rows
    base = sq * rows
    row_at = lambda r: pl.ds(r * length, length)
    lanes = lambda c: pl.ds(c * width, width)

    loads = []

    def load(src, dst):
        c = pltpu.make_async_copy(src, dst, load_sem.at[len(loads)])
        c.start()
        loads.append(c)
        return c

    inner_load = load(inner, big1)
    first = [load(s, d) for s, d in zip(weights[:3], (wd, wi, wo), strict=True)]
    first += [load(s, d) for s, d in ((n2, t_att), (i2, i2_s), (n1, t_br), (i1, i1_s))]
    second = [load(h1, t_h1), load(act, big2)]
    second += [load(o.at[r], t_o.at[row_at(r)]) for r in range(rows)]
    third = [load(s, d) for s, d in zip(weights[3:], (wq, wk, wv), strict=True)]
    grid.greet(b, sq, partners, others)

    def row_back(e, src, dst, r, j):
        o_ = sq if j == 0 else others[j - 1]
        start = pl.multiple_of(o_ * lt, lt)
        if e == 0:
            part = src.at[r, pl.ds(start, lt)]
        else:
            part = src.at[pl.ds(r * length + start, lt)]
        into = dst.at[sq * rows + r]
        if j == 0:
            return pltpu.make_async_copy(part, into, ex_own.at[e, r])
        return remote(part, into, ex_send.at[e, r, j - 1], ex_recv.at[e, r, j - 1], (b, o_))

    backs = ((hid, hid_back), (t_att, gx_back))

    own_rows = rows * SEGS
    total_rows = own_rows << nd
    at_row = lax.broadcasted_iota(jnp.int32, (own_rows, 1), 0)
    len_col = jnp.ones((own_rows, 1), F32)
    pair_col = jnp.full((own_rows, 1), -1, jnp.int32)
    for r in range(rows):
        for s in range(SEGS):
            here = at_row == r * SEGS + s
            len_col = jnp.where(here, lens[base + r, s].astype(F32), len_col)
            if s < NQ:
                pair_col = jnp.where(here, pairs[r * NQ + s], pair_col)
    avg = pool[...] / len_col
    inv = lax.rsqrt(jnp.sum(avg * avg, axis=-1, keepdims=True) + NORM_EPSILON)
    own = avg * inv
    emb[tuple(my) + (slice(None), slice(0, width))] = own
    emb[tuple(my) + (slice(None), slice(width, width + EMB_PAD))] = jnp.broadcast_to(
        pair_col.astype(F32), (own_rows, EMB_PAD)
    )
    half = width // 2
    emb_pieces = ((0, half, 0), (half, width + EMB_PAD - half, 1))

    def emb_copy(f, kk):
        lo, ln, flavour = emb_pieces[f]
        order = grid.order(flavour)
        ix = tuple(slice(None) if e in order[:kk] else my[e] for e in range(nd))
        ref = emb.at[ix + (slice(None), pl.ds(lo, ln))]
        return remote(ref, ref, emb_send.at[f, kk], emb_recv.at[f, kk], partners[order[kk]])

    def emb_near(j):
        ref = emb.at[tuple(my)]
        return remote(ref, ref, near_send.at[j - 1], near_recv.at[j - 1], (b, others[j - 1]))

    for j in range(1, ns):
        emb_near(j).start()
    for j in range(1, ns):
        emb_near(j).wait_recv()
    inner_load.wait()
    hops = nd - grid.ks
    share = count // hops // 64 * 64
    for kk in range(grid.ks, nd):
        for f in range(2):
            if kk > grid.ks:
                emb_copy(f, kk - 1).wait_recv()
            emb_copy(f, kk).start()
        lo = (kk - grid.ks) * share
        hi = lo + share if kk < nd - 1 else count

        def slopes(t, carry, lo=lo):
            at = pl.ds(pl.multiple_of(lo + t * 64, 64), 64)
            big1[at] = gelu_slope(big1[at].astype(F32)).astype(BF16)
            return carry

        lax.fori_loop(0, (hi - lo) // 64, slopes, 0)
    for r in range(rows):
        for j in range(ns):
            row_back(0, *backs[0], r, j).start()
    for f in range(2):
        emb_copy(f, nd - 1).wait_recv()
    every = emb[...].reshape(total_rows, width + EMB_PAD)
    high, low = split_two(every[:, :width])
    pair_row = every[:, width:].T[:1].astype(jnp.int32)
    own_high, own_low = split_two(own)
    scale = 1.0 / TEMPERATURE

    def product(ah, al, bh, bl, cb):
        return dot(ah, bh, 1, cb) + dot(ah, bl, 1, cb) + dot(al, bh, 1, cb)

    total = jnp.zeros((1, total_rows), F32)
    block = min(total_rows, 256)
    for lo in range(0, total_rows, block):
        sim = product(high[lo : lo + block], low[lo : lo + block], high, low, 1) * scale
        at = lax.broadcasted_iota(jnp.int32, (block, 1), 0)
        total += jnp.sum(jnp.where(at % SEGS >= NQ, jnp.exp(sim - scale), 0.0), axis=0, keepdims=True)
    lse_cols = scale + jnp.log(total)
    sim = product(own_high, own_low, high, low, 1) * scale
    col = lax.broadcasted_iota(jnp.int32, (1, total_rows), 1)
    row = at_row + (b * ns + sq) * own_rows
    col_doc, row_doc = col % SEGS >= NQ, row % SEGS >= NQ
    number = lambda at: (at // SEGS) * NQ + at % SEGS - NQ
    lse_rows = scale + jnp.log(
        jnp.sum(jnp.where(col_doc, jnp.exp(sim - scale), 0.0), axis=1, keepdims=True)
    )
    chosen = col_doc & (number(col) == pair_col)
    positive = jnp.sum(jnp.where(chosen, sim, 0.0), axis=1, keepdims=True)
    loss[...] = jnp.broadcast_to(lse_rows - positive, loss.shape)
    as_query = jnp.exp(sim - lse_rows) - chosen.astype(F32)
    chosen_by = number(row) == pair_row
    as_doc = jnp.exp(jnp.where(col_doc, MASKED, sim - lse_cols)) - chosen_by.astype(F32)
    grad = jnp.where(row_doc, jnp.where(col_doc, 0.0, as_doc), jnp.where(col_doc, as_query, 0.0))
    grad_high, grad_low = split_two(grad)
    demb = product(grad_high, grad_low, high, low, 0) * scale
    dpool = inv * demb - inv * inv * inv * avg * jnp.sum(avg * demb, axis=-1, keepdims=True)
    dpool_high, dpool_low = split_two(dpool / len_col)
    pad = jnp.zeros((64 - own_rows, width), F32)
    stacked = jnp.concatenate([dpool_high.astype(F32), pad, dpool_low.astype(F32), pad], axis=0)
    dp[...] = stacked.astype(BF16)

    members, at = [], 0
    for g in groups:
        members.append(range(at, at + len(g)))
        at += len(g)
    square_outs = {2: g_out}
    outs = {}
    late = len(groups) - 3
    for g, ix in enumerate(members):
        for i in ix:
            a, _, _, out_lo, _ = flat[i]
            if g >= late:
                out = (g_query, g_key, g_value)[g - late]
            else:
                out = (g_in, g_down, g_out)[a]
            outs[i] = (out, out_lo)
    red = Reducer(grid, flat, partners, my, (wi, wd, wo), outs, send_sem, recv_sem, bufs)
    plan = backward_plan(nd, len(groups), rows, ns)
    small_order = grid.order(0)[::-1]

    def small_copy(kk):
        return remote(
            small, small_recv.at[kk], sm_send.at[kk], sm_recv.at[kk], partners[small_order[kk]]
        )

    def run_at(point):
        for kind, *what in plan.get(point, ()):
            if kind == "g":
                g, kk = what
                for i in members[g]:
                    red.step(i, kk)
            elif kind == "x":
                r, j = what
                row_back(1, *backs[1], r, j).start()
            else:
                (kk,) = what
                if kk > 0:
                    small_copy(kk - 1).wait()
                    small[...] += small_recv[kk - 1]
                if kk < nd:
                    small_copy(kk).start()

    def run_in(name, now, steps):
        for c in range(steps):
            if (name, c) in plan:
                pl.when(now == c)(functools.partial(run_at, (name, c)))

    def columns(u):
        return jnp.sum(u, axis=0, keepdims=True)

    def norm_back(g, n, inv_std):
        return inv_std * (
            g - jnp.mean(g, axis=-1, keepdims=True) - n * jnp.mean(g * n, axis=-1, keepdims=True)
        )

    for c in first:
        c.wait()
    small[...] = jnp.zeros_like(small)
    g1, g2 = vecs[ROW_G1 : ROW_G1 + 1], vecs[ROW_G2 : ROW_G2 + 1]
    down_rows = wd.shape[-2]
    low_digits = (width // down_rows).bit_length() - 1
    top = nd - low_digits
    down_ix = lambda c: tuple((c >> (top - 1 - e)) % 2 for e in range(top))
    dev = (slice(None),) * (nd + 1)

    def bump(at, u):
        small[at : at + 1] += u

    def feed_tile(t, carry):
        r = t // tiles
        start = lax.rem(t, tiles) * tile_rows
        at = pl.ds(pl.multiple_of(t * tile_rows, tile_rows), tile_rows)
        seg = segment_of(lens, base + r, (tile_rows, 1), 0, start)
        place = jnp.where(seg < SEGS, r * SEGS + seg, -1)
        lane = lax.broadcasted_iota(jnp.int32, (tile_rows, 128), 1)
        mine = (lane % 64 == place).astype(F32).astype(BF16)
        dh2 = dot(mine, dp[...])
        m2 = t_att[at].astype(F32)
        bump(ROW_G2, columns(dh2 * m2))
        bump(ROW_S2, columns(dh2))
        dpre2 = norm_back(dh2 * g2, m2, i2_s[at, :1])
        dfeed = dpre2.astype(BF16)
        t_feed[at] = dfeed
        bump(ROW_BD, columns(dfeed.astype(F32)))
        dh1 = dpre2
        for c in range(chunks):
            w = wd[down_ix(c)].reshape(width, width)
            din = (dot(dfeed, w, 1, 1) * big1[at, lanes(c)].astype(F32)).astype(BF16)
            big1[at, lanes(c)] = din
            bump(ROW_BI + c, columns(din.astype(F32)))
            dh1 = dh1 + dot(din, wi[dev + (lanes(c),)].reshape(width, width), 1, 1)
        m1 = t_br[at].astype(F32)
        bump(ROW_G1, columns(dh1 * m1))
        bump(ROW_S1, columns(dh1))
        dbranch = norm_back(dh1 * g1, m1, i1_s[at, :1]).astype(BF16)
        t_br[at] = dbranch
        bump(ROW_BO, columns(dbranch.astype(F32)))
        t_att[at] = dot(dbranch, wo[...].reshape(width, width), 1, 1).astype(BF16)
        return carry

    lax.fori_loop(0, rows * tiles, feed_tile, 0)

    square = (2,) * nd + wo.shape[-2:]

    def outer(lhs, rhs):
        return dot(lhs, rhs, 0, 0)

    fourth = []

    def phase_in():
        for c in second[:1]:
            c.wait()
        for c in range(chunks):
            run_at(("in", c))
            res = outer(t_h1[...], big1[:, lanes(c)])
            wi[dev + (lanes(c),)] = res.reshape(square).astype(BF16)
        for r in range(rows):
            for c, u in enumerate((q, k, v)):
                fourth.append(load(u.at[r], big1.at[row_at(r), lanes(c)]))
            fourth.append(load(x.at[r], t_h1.at[row_at(r)]))

    def phase_down():
        second[1].wait()
        for c in range(chunks):
            run_at(("down", c))
            res = outer(big2[:, lanes(c)], t_feed[...])
            wd[down_ix(c)] = res.reshape((2,) * low_digits + (down_rows, width)).astype(BF16)

    def phase_out():
        for c in second[2:]:
            c.wait()
        run_at("out")
        wo[...] = outer(t_o[...], t_br[...]).reshape(square).astype(BF16)

    n_pairs = HEADS // 2
    slots = p_s.shape[0]
    lane = lax.broadcasted_iota(jnp.int32, (1, 128), 1)

    def probs_copy(s):
        slot = lax.rem(s, slots)
        pair = pl.ds(lax.rem(s, n_pairs) * 2, 2)
        return pltpu.make_async_copy(p.at[s // n_pairs, pair], p_s.at[slot], p_sem.at[slot])

    for s in range(slots - 1):
        probs_copy(s).start()

    def phase_attention(r):
        if r == 0:
            for c in fourth:
                c.wait()

        def pair_step(s, carry):
            run_in(("attention", r), s, n_pairs)
            g = r * n_pairs + s
            probs_copy(g).wait()

            @pl.when(g + slots - 1 < rows * n_pairs)
            def _():
                probs_copy(g + slots - 1).start()

            slot = lax.rem(g, slots)
            at = lambda c: pl.ds(pl.multiple_of(c * width + s * 128, 128), 128)
            qp, kp, vp = (big1[row_at(r), at(c)] for c in range(3))
            dop = t_att[row_at(r), at(0)]
            kt = kp.T
            zero = jnp.zeros_like(vp)
            head = lambda u, h: jnp.where(lane // HEAD_DIM == h, u, zero)
            dprobs = [dot(head(vp, h), dop, 1, 1) for h in range(2)]
            dv = dot(p_s[slot, 0], head(dop, 0)) + dot(p_s[slot, 1], head(dop, 1))
            ds = []
            for h in range(2):
                probs = p_s[slot, h].astype(F32)
                weighted = probs * dprobs[h]
                ds.append((weighted - probs * jnp.sum(weighted, axis=0, keepdims=True)).astype(BF16))
            dk = dot(ds[0], head(qp, 0)) + dot(ds[1], head(qp, 1))
            dqt = [
                dot(kt[h * HEAD_DIM : (h + 1) * HEAD_DIM], ds[h]) * HEAD_DIM ** (-0.5)
                for h in range(2)
            ]
            big1[row_at(r), at(0)] = jnp.concatenate(dqt, axis=0).T.astype(BF16)
            big1[row_at(r), at(1)] = dk.astype(BF16)
            big1[row_at(r), at(2)] = dv.astype(BF16)
            return carry

        lax.fori_loop(0, n_pairs, pair_step, 0)

    def phase_input(r):
        if r == 0:
            for c in third:
                c.wait()
        run_at(("input", r))
        dq, dk, dv = (big1[row_at(r), lanes(c)] for c in range(3))
        bump(ROW_BQ, columns(dq.astype(F32)))
        bump(ROW_BV, columns(dv.astype(F32)))
        gx = t_br[row_at(r)].astype(F32)
        for d, w in ((dq, wq), (dk, wk), (dv, wv)):
            gx = gx + dot(d, w[...].reshape(width, width), 1, 1)
        t_att[row_at(r)] = gx.astype(BF16)
        row_back(1, *backs[1], r, 0).start()

    def phase_projection(c):
        run_at(("projection", c))
        for i in members[c]:
            red.sent(i, 0)
        wi[dev + (lanes(c),)] = outer(t_h1[...], big1[:, lanes(c)]).reshape(square).astype(BF16)

    phases = {"in": phase_in, "down": phase_down, "out": phase_out, "attention": phase_attention}
    phases.update({"input": phase_input, "projection": phase_projection})
    for name, *which in BACKWARD_ORDER:
        phases[name](*which)
    run_at("end")

    for g, ix in enumerate(members):
        for i in ix:
            for kk in range(nd):
                if not (kk == 0 and g < 3):
                    red.sent(i, kk)
    for j in range(1, ns):
        emb_near(j).wait_send()
    for f in range(2):
        for kk in range(grid.ks, nd):
            emb_copy(f, kk).wait_send()
    for r in range(rows):
        for e, (src, dst) in enumerate(backs):
            for j in range(ns):
                row_back(e, src, dst, r, j).wait()


BACKWARD_ORDER = (
    ("in",), ("down",), ("out",), ("attention", 0), ("input", 0),
    ("attention", 1), ("input", 1), ("projection", 0), ("projection", 1), ("projection", 2),
)
BACKWARD_PLAN = {
    ("in", 1): (
        ("g", 0, 0),
    ),
    ("in", 2): (
        ("g", 1, 0),
    ),
    ("in", 3): (
        ("g", 2, 0),
    ),
    ("down", 0): (
        ("g", 0, 1), ("g", 1, 1), ("g", 3, 0),
    ),
    ("down", 1): (
        ("g", 2, 1),
    ),
    ("down", 3): (
        ("g", 3, 1), ("g", 0, 2),
    ),
    "out": (
        ("g", 4, 0), ("g", 5, 0), ("g", 6, 0),
    ),
    (("attention", 0), 0): (
        ("g", 1, 2), ("g", 7, 0),
    ),
    (("attention", 0), 1): (
        ("g", 2, 2), ("g", 4, 1), ("g", 5, 1), ("g", 6, 1), ("g", 3, 2), ("g", 7, 1),
    ),
    (("attention", 0), 2): (
        ("g", 0, 3), ("g", 1, 3),
    ),
    (("attention", 0), 3): (
        ("g", 2, 3),
    ),
    (("attention", 0), 5): (
        ("g", 0, 4), ("g", 1, 4), ("g", 4, 2),
    ),
    ("input", 0): (
        ("g", 2, 4),
    ),
    (("attention", 1), 0): (
        ("g", 0, 5), ("g", 5, 2), ("g", 1, 5), ("x", 0, 2), ("x", 0, 1), ("x", 0, 3),
    ),
    (("attention", 1), 1): (
        ("g", 2, 5), ("g", 6, 2),
    ),
    (("attention", 1), 2): (
        ("g", 3, 3),
    ),
    (("attention", 1), 3): (
        ("g", 7, 2),
    ),
    (("attention", 1), 4): (
        ("g", 4, 3),
    ),
    (("attention", 1), 5): (
        ("g", 5, 3),
    ),
    ("input", 1): (
        ("g", 6, 3),
    ),
    ("projection", 0): (
        ("g", 7, 3), ("s", 0), ("x", 1, 2), ("x", 1, 1), ("x", 1, 3),
    ),
    ("projection", 1): (
        ("g", 3, 4), ("g", 8, 0),
    ),
    ("projection", 2): (
        ("g", 4, 4), ("g", 9, 0), ("s", 1),
    ),
    "end": (
        ("g", 5, 4), ("g", 8, 1), ("g", 10, 0), ("g", 6, 4), ("g", 9, 1), ("s", 2), ("g", 7, 4),
        ("g", 10, 1), ("g", 8, 2), ("g", 9, 2), ("s", 3), ("g", 10, 2), ("g", 8, 3), ("g", 3, 5),
        ("g", 9, 3), ("g", 4, 5), ("g", 10, 3), ("g", 5, 5), ("s", 4), ("g", 6, 5), ("g", 8, 4),
        ("g", 7, 5), ("g", 9, 4), ("s", 5), ("g", 10, 4), ("g", 8, 5), ("g", 9, 5), ("g", 10, 5),
    ),
}


def backward_plan(nd, groups, rows, ns):
    if nd == 5 and groups == 11 and rows == 2 and ns == 4:
        return BACKWARD_PLAN
    late = groups - 3
    ops = [("g", g, k) for k in range(nd + 1) for g in range(late)]
    ops += [("x", r, j) for r in range(rows) for j in range(1, ns)]
    ops += [("s", k) for k in range(nd + 1)]
    plan = {("projection", 0): tuple(ops)}
    plan["end"] = tuple(("g", g, k) for k in range(nd + 1) for g in range(late, groups))
    return plan


def backward(grid, lens, pairs, vecs, pool, kept, weights, tile_rows, collective_id):
    nd, ns = grid.nd, grid.seq_size
    x = kept[-2]
    rows, length, width = x.shape
    count = rows * length
    ff = weights[1].shape[-1]
    part, down_part = weights[1].shape[-2], weights[0].shape[-2]
    groups = []
    half = width // 2
    for c in range(ff // width):
        groups.append([(0, c * width + f * half, half, c * width + f * half, f) for f in range(2)])
    for lo in range(0, width, 256):
        groups.append([(1, lo + f * 128, 128, lo + f * 128, f) for f in range(2)])
    groups.append([(2, f * half, half, f * half, f) for f in range(2)])
    for c in range(3):
        groups.append([(0, c * width + f * half, half, f * half, f) for f in range(2)])
    flat = [c for g in groups for c in g]
    n = len(flat)
    bufs = []
    for a, _, ln, _, _ in flat:
        shape = ((down_part if a == 1 else part), ln)
        bufs += [pltpu.VMEM((2,) * (nd - 1 - kk) + shape, BF16) for kk in range(nd)]
    back = struct((rows * ns, length // ns, width), BF16)
    out_shape = [struct((part, ff), F32), struct((down_part, width), F32)]
    out_shape += [struct((part, width), F32)] * 4
    out_shape += [struct((SMALL_ROWS, width), F32), struct((rows * SEGS, 128), F32), back, back]
    low, wide = pltpu.VMEM((count, width), BF16), pltpu.VMEM((count, ff), BF16)
    stat = pltpu.VMEM((count, 128), F32)
    n_loads = 10 + rows + 3 + 4 * rows
    return pl.pallas_call(
        functools.partial(backward_kernel, grid, flat, groups, len(bufs), tile_rows),
        out_shape=out_shape,
        in_specs=[SMEM, SMEM, VMEM, VMEM] + [ANY] * (len(kept) + len(weights)),
        out_specs=[VMEM] * 8 + [ANY] * 2,
        scratch_shapes=[pltpu.VMEM(w.shape, BF16) for w in weights]
        + [wide, wide, low, low, low, low, low, stat, stat]
        + [pltpu.VMEM((3, 2, length, length), BF16)]
        + [pltpu.VMEM((nd, SMALL_ROWS, width), F32)]
        + [pltpu.VMEM((2,) * nd + (rows * SEGS, width + EMB_PAD), F32), pltpu.VMEM((128, width), BF16)]
        + [DMA((n, nd)), DMA((n, nd))]
        + [DMA((2, rows)), DMA((2, rows, ns - 1)), DMA((2, rows, ns - 1))]
        + [DMA((n_loads,)), DMA((3,)), DMA((nd,)), DMA((nd,)), DMA((2, nd)), DMA((2, nd))]
        + [DMA((ns - 1,)), DMA((ns - 1,))]
        + bufs,
        compiler_params=pltpu.CompilerParams(
            collective_id=collective_id, has_side_effects=True, vmem_limit_bytes=BACK_VMEM
        ),
    )(lens, pairs, vecs, pool, *kept, *weights)


BACK_VMEM = 63 * 2**20


def finish_kernel(grid, gx_ref, hid_ref, small_ref, loss_ref, *refs):
    n = 6
    gx_out, hid_out, loss_out, wide_out = refs[n : n + 4]
    vec_outs, outs = refs[n + 4 : n + 12], refs[n + 12 :]
    gx_out[...] = gx_ref[...].astype(F32)
    hid_out[...] = hid_ref[...]

    @pl.when(pl.program_id(0) == 0)
    def _():
        for src, dst in zip(refs[:n], outs, strict=True):
            dst[...] = src[...]
        number = loss_out.shape[0]
        lane = lax.broadcasted_iota(jnp.int32, (1, 128), 1)
        at = lax.broadcasted_iota(jnp.int32, (loss_ref.shape[0], 1), 0)
        mine = at == (lane // NQ) * SEGS + lane % NQ
        row = jnp.sum(jnp.where(mine, loss_ref[...], 0.0), axis=0, keepdims=True)
        loss_out[...] = row[:, :number].reshape(number)
        b, q = grid.here()
        me = b * grid.seq_size + q
        sums = small_ref[...]
        width = sums.shape[1]
        part, wide = vec_outs[0].shape[0], wide_out.shape[0]

        def pick(first, lanes):
            at = lax.broadcasted_iota(jnp.int32, (width, lanes), 0)
            lane = lax.broadcasted_iota(jnp.int32, (width, lanes), 1)
            chosen = (at - first == lane).astype(F32).astype(BF16)
            out, rest = jnp.zeros((sums.shape[0], lanes), F32), sums
            for _ in range(3):
                top = rest.astype(BF16)
                out += dot(top, chosen)
                rest = rest - top.astype(F32)
            return out

        own = pick(me * part, 128)
        for i, out in enumerate(vec_outs):
            out[...] = own[i : i + 1, :part].reshape(part)
        own = pick(lax.rem(me * wide, width), -(-wide // 128) * 128)
        at = lax.broadcasted_iota(jnp.int32, (sums.shape[0], 1), 0)
        own = jnp.where(at == ROW_BI + (me * wide) // width, own, 0.0)
        wide_out[...] = jnp.sum(own, axis=0, keepdims=True)[:, :wide].reshape(wide)


def finish(grid, gx, hid, small, loss, grads):
    rows, lt, width = gx.shape
    wide = grads[0].shape[1] >> grid.nd
    step = rows // 2
    row = pl.BlockSpec((step, lt, width), lambda r: (r, 0, 0))
    full = lambda a: pl.BlockSpec(a.shape, lambda r: (0,) * len(a.shape))
    extra = [struct((loss.shape[0] // SEGS * NQ,), F32), struct((wide,), F32)]
    extra += [struct((width >> grid.nd,), F32)] * 8
    same = [struct(g.shape, F32) for g in grads]
    return pl.pallas_call(
        functools.partial(finish_kernel, grid),
        grid=(rows // step,),
        out_shape=[struct(gx.shape, F32), struct(hid.shape, BF16)] + extra + same,
        in_specs=[row, row, full(small), full(loss)] + [full(g) for g in grads],
        out_specs=[row, row] + [full(e) for e in extra] + [full(g) for g in grads],
        compiler_params=pltpu.CompilerParams(vmem_limit_bytes=VMEM_LIMIT),
    )(gx, hid, small, loss, *grads)


def pack_small(vectors, wide, extra):
    rows = [jnp.pad(v.astype(F32), (0, 128 - v.shape[0])) for v in (*vectors, wide, extra)]
    rows += [jnp.zeros((128,), F32)] * (16 - len(rows))
    return jnp.stack(rows)


def per_device(
    tokens, lengths, pair_ids, w_query, b_query, w_key, w_value, b_value, w_out, b_out,
    norm1_gain, norm1_bias, w_in, b_in, w_down, b_down, norm2_gain, norm2_bias,
):
    blk_size, seq_size = lax.axis_size("blk"), lax.axis_size("seq")
    grid = Grid(blk_size, seq_size)
    devices = blk_size * seq_size
    group_rows, local_len, width = tokens.shape
    rows = group_rows // seq_size
    length = local_len * seq_size
    count = rows * length
    ff = w_in.shape[1]
    part, wide_part, pairs = b_query.shape[0], b_in.shape[0], pair_ids.shape[0]

    vectors = (b_query, b_value, b_out, norm1_gain, norm1_bias, b_down, norm2_gain, norm2_bias)
    if part % 8 == 0:
        res = forward(
            grid, lengths.T, tokens, vectors + (b_in,),
            (w_query, w_key, w_value, w_out, w_in, w_down), 256, 4,
        )
        x, q, k, v, p, o, n1, i1, h1, act, slope, n2, i2, hid = res[:14]
        wq, wk, wv, wo, wi, wd = res[15:21]
        pool, vecs = res[21:]
        kept = (n2, i2, slope, n1, i1, act, h1, o, q, k, v, p, x, hid.reshape(x.shape))
        weights = (wd, wi, wo, wq, wk, wv)
        res = backward(grid, lengths.T, pair_ids, vecs, pool, kept, weights, min(512, length), 3)
        sums, losses, hid_back, gx_back = res[6:]
        out = finish(grid, gx_back, hid_back, sums, losses, res[:6])
        grad_tokens, hidden_out, query_loss, g_wide = out[:4]
        gv, grads = out[4:12], out[12:]
        g_in, g_down, g_out, g_query, g_key, g_value = grads
        return (
            hidden_out, query_loss, grad_tokens, g_query, gv[0], g_key, g_value, gv[1],
            g_out, gv[2], gv[3], gv[4], g_in, g_wide, g_down, gv[5], gv[6], gv[7],
        )

    lens = lax.dynamic_slice_in_dim(lengths, lax.axis_index("seq") * rows, rows, 0)
    small = pack_small(vectors, b_in, pair_ids)
    full, x = gather_all(grid, (w_query, w_key, w_value, small, w_out, w_in, w_down), tokens, 1)
    wq, wk, wv, smalls, wo, wi, wd = full
    smalls = smalls.reshape(devices, 16, 128)
    vecs = smalls[:, : len(vectors), :part].transpose(1, 0, 2).reshape(len(vectors), 1, width)
    bq, bv, bo, g1, s1, bd, g2, s2 = (vecs[i] for i in range(len(vectors)))
    bi = smalls[:, len(vectors), :wide_part].reshape(1, ff)

    q, k, v, p, o = attention(lens, x, wq, wk, wv, bq, bv)
    x2, o2 = x.reshape(count, width), o.reshape(count, width)
    hid, n1, i1, h1, act, slope, n2, i2, pool = feed(
        lens, x2, o2, wo, bo, g1, s1, wi, bi, wd, bd, g2, s2, 256
    )
    all_pairs = smalls[:, len(vectors) + 1, :pairs].reshape(-1, NQ).astype(jnp.int32)

    none = jnp.full((all_pairs.shape[0], SEGS - NQ), -1, jnp.int32)
    pair_row = jnp.concatenate([all_pairs, none], axis=1).reshape(1, -1)
    own_pairs = jnp.concatenate([pair_ids.reshape(rows, NQ), none[:rows]], axis=1).reshape(-1, 1)
    pair_col = jnp.broadcast_to(own_pairs, (rows * SEGS, 128))
    len_col = jnp.broadcast_to(lens.reshape(-1, 1).astype(F32), (rows * SEGS, 128))
    losses, dpool = contrast(grid, pool, len_col, pair_col, pair_row, 2)
    query_loss = losses[:, 0].reshape(rows, SEGS)[:, :NQ].reshape(-1)

    dfeed, dinner, dbranch, dpre1, datt, sums, wide_sums = feed_back(
        lens, dpool, n2, i2, slope, n1, i1, wd, wi, wo, g2, g1, 256
    )
    grad_w_down = outer(act, dfeed, width, width)
    grad_w_in = outer(h1, dinner, width, width)
    grad_w_out = outer(o2, dbranch, width, width)
    dq, dk, dv = attention_back(q, k, v, p, datt.reshape(rows, length, width))
    dq, dk, dv = (d.reshape(count, width) for d in (dq, dk, dv))
    grad_x, sums_in = input_back(dpre1, dq, dk, dv, wq, wk, wv, 256)
    grad_w_query = outer(x2, dq, width, width)
    grad_w_key = outer(x2, dk, width, width)
    grad_w_value = outer(x2, dv, width, width)

    vec_grads = jnp.stack(
        [sums_in[0], sums_in[1], sums[5], sums[3], sums[4], sums[2], sums[0], sums[1]]
    )
    packed = jnp.pad(
        vec_grads.reshape(8, devices, part).transpose(1, 0, 2), ((0, 0), (0, 0), (0, 128 - part))
    )
    wide_grads = jnp.pad(
        wide_sums[0].reshape(devices, 1, wide_part), ((0, 0), (0, 7), (0, 128 - wide_part))
    )
    packed = jnp.concatenate([packed, wide_grads], axis=1).reshape(devices * 16, 128)
    grads, back = scatter_all(
        grid,
        (grad_w_down, grad_w_in, grad_w_out, packed, grad_w_query, grad_w_key, grad_w_value),
        (hid.reshape(rows, length, width), grad_x.reshape(rows, length, width)),
        3,
    )
    g_down, g_in, g_out, g_small, g_query, g_key, g_value = grads
    hidden_out, grad_tokens = back
    gv = [g_small[i, :part] for i in range(8)]
    return (
        hidden_out,
        query_loss,
        grad_tokens.astype(F32),
        g_query,
        gv[0],
        g_key,
        g_value,
        gv[1],
        g_out,
        gv[2],
        gv[3],
        gv[4],
        g_in,
        g_small[8, :wide_part],
        g_down,
        gv[5],
        gv[6],
        gv[7],
    )


def solution(mesh):
    both = ("blk", "seq")
    vec, mat, tok = P(both), P(both, None), P("blk", "seq", None)
    in_specs = (
        tok, P("blk", None), vec, mat, vec, mat, mat, vec, mat, vec, vec, vec, mat, vec, mat, vec,
        vec, vec,
    )
    out_specs = (
        tok, vec, tok, mat, vec, mat, mat, vec, mat, vec, vec, vec, mat, vec, mat, vec, vec, vec,
    )
    return jax.shard_map(
        per_device, mesh=mesh, in_specs=in_specs, out_specs=out_specs, check_vma=False
    )
```
